32 devices in a mesh: section: 2 (over core), dp: 4 (over y, x), mp: 4 (over z).
Axes of the slice: x: 2, y: 2, z: 4, core: 2. Of those that a mesh axis runs over, the one named last changes fastest.
Arguments:
- block_input: bfloat16 [2, 1536, 2048], P(None, 'dp', 'mp'), may hold values from -6 to 6
- image_sides: int32 [2, 4, 96], P(None, 'dp'), may hold values from 0 to 7, as said below
- w_reduce: float32 [2, 2048, 512], P('section', 'mp', 'dp'), may hold values from -0.125 to 0.125
- w_spatial: float32 [2, 9, 512, 512], P('section', None, 'dp', 'mp'), may hold values from -0.09375 to 0.09375
- w_expand: float32 [2, 512, 2048], P('section', 'dp', 'mp'), may hold values from -0.25 to 0.25
- gain_inner: float32 [2, 2, 512], P('section', None, 'mp'), may hold values from 0.5 to 1.5
- shift_inner: float32 [2, 2, 512], P('section', None, 'mp'), may hold values from -1.8 to 1.8
- gain_outer: float32 [2, 2048], P('section', 'mp'), may hold values from 0.5 to 1.5
- shift_outer: float32 [2, 2048], P('section', 'mp'), may hold values from -1.8 to 1.8
- head_weight: float32 [3, 2048, 128], P(None, 'mp', ('section', 'dp')), may hold values from -0.3 to 0.3
- labels: int32 [3, 2, 1536], P(None, None, 'dp'), may hold values from 0 to 127
- thresholds: float32 [2, 1536, 2048], P(None, 'dp', 'mp'), may hold values from 0 to 1
Outputs:
- activations: bfloat16 [2, 2, 1536, 2048], P('section', None, 'dp', 'mp')
- input_grads: float32 [2, 2, 1536, 2048], P('section', None, 'dp', 'mp')
- grad_reduce: float32 [2, 2048, 512], P('section', 'mp', 'dp')
- grad_spatial: float32 [2, 9, 512, 512], P('section', None, 'dp', 'mp')
- grad_expand: float32 [2, 512, 2048], P('section', 'dp', 'mp')
- grad_gain_inner: float32 [2, 2, 4, 128], P('section', None, 'mp', 'dp')
- grad_shift_inner: float32 [2, 2, 4, 128], P('section', None, 'mp', 'dp')
- grad_gain_outer: float32 [2, 4, 512], P('section', 'mp', 'dp')
- grad_shift_outer: float32 [2, 4, 512], P('section', 'mp', 'dp')
- grad_head: float32 [3, 2048, 128], P(None, 'mp', ('section', 'dp'))
The draws below stay inside these ranges and needn't reach their ends.
Inputs may be any that keep to these rules, and one draw needn't show every extreme that they name: `image_sides`: each nonzero entry is 7 or 2. The live pixels (sum of squared sides) of one data group in one micro-batch number at most 384, and in every micro-batch some group has exactly 384.
All inputs are finite; a program needn't handle non-finite values.
Results may differ from the reference program's by a relative error of at most 0.02.
Values may be sent and summed in bfloat16 or wider, within the bound.
A program may use at most 192 MiB of HBM per device.

```python
from functools import partial
import jax
import jax.numpy as jnp
from jax import lax

WIDE = 2048
MID = 512
CLASSES = 128
MICRO = 2
ROWS = 384
SLOTS = 96
ROWS_ALL = 1536
N_DP = 4
N_MP = 4


def draw_image_sides(key, part):
    key = jax.random.fold_in(key, 11)
    key_list = jax.random.split(key, 5)
    most_big = ROWS // 49
    big_count = jax.random.randint(key_list[0], (MICRO, N_DP), 0, most_big + 1)
    full_device = jax.random.randint(key_list[1], (MICRO,), 0, N_DP)
    full_big = 4 * jax.random.randint(key_list[2], (MICRO,), 0, most_big // 4 + 1)
    is_full = jnp.arange(N_DP)[None, :] == full_device[:, None]
    big_count = jnp.where(is_full, full_big[:, None], big_count)
    spare_rows = (ROWS - 49 * big_count) // 4
    small_count = jax.random.randint(key_list[3], (MICRO, N_DP), 0, spare_rows + 1)
    small_count = jnp.where(is_full, spare_rows, small_count)
    scores = jax.random.randint(key_list[4], (MICRO, N_DP, SLOTS), 0, 1 << 20) * SLOTS + jnp.arange(SLOTS)[None, None, :]
    ranking = jnp.argsort(jnp.argsort(scores, axis=-1), axis=-1)
    sides_out = jnp.where(ranking < big_count[..., None], 7, jnp.where(ranking < (big_count + small_count)[..., None], 2, 0))
    return sides_out.astype(jnp.int32)


def with_ends(values, key, low, largest):
    place = [jax.random.randint(jax.random.fold_in(key, axis), (), 0, length) for axis, length in enumerate(values.shape)]
    longest = values.shape.index(max(values.shape))
    beside = place[:longest] + [(place[longest] + 1) % values.shape[longest]] + place[longest + 1:]
    return values.at[tuple(place)].set(low).at[tuple(beside)].set(largest)


def block_scale(stream_key, shape, pieces, least, top_value):
    factor_of, own = 1.0, jax.random.fold_in(stream_key, 6)
    for dim, blocks in pieces:
        heights = jnp.exp(jax.random.uniform(jax.random.fold_in(own, dim), (blocks,), jnp.float32, least / len(pieces), top_value / len(pieces)))
        factor_of = factor_of * jnp.repeat(heights, shape[dim] // blocks).reshape([-1 if axis == dim else 1 for axis in range(len(shape))])
    return factor_of


def centred(key, shape, width, bound, cuts=(), held_as=jnp.bfloat16):
    entries = width * jax.random.normal(key, shape, jnp.float32)
    if cuts:
        entries = entries * block_scale(key, shape, cuts, -0.22, 0.18)
    return jnp.clip(entries, -bound, bound).astype(held_as)


def setup_inputs(seed: int = 0) -> dict:
    splits = jax.random.split(jax.random.key(seed), 13)
    block_input = centred(splits[0], (MICRO, ROWS_ALL, WIDE), 1.0, 6.0, ((1, 4), (2, 4)))
    image_sides = draw_image_sides(jax.random.fold_in(splits[12], 71), 0)
    w_reduce = centred(splits[2], (2, WIDE, MID), WIDE ** -0.5, 0.125, ((0, 2), (1, 4), (2, 4)), jnp.float32)
    w_spatial = centred(splits[3], (2, 9, MID, MID), (9 * MID) ** -0.5, 0.09375, ((0, 2), (2, 4), (3, 4)), jnp.float32)
    w_expand = centred(splits[4], (2, MID, WIDE), MID ** -0.5, 0.25, ((0, 2), (1, 4), (2, 4)), jnp.float32)
    gain_inner = jnp.clip(1.0 + 0.1 * jax.random.normal(splits[5], (2, 2, MID), jnp.float32), 0.5, 1.5)
    shift_inner = centred(splits[6], (2, 2, MID), 0.3, 1.8, ((0, 2), (2, 4)), jnp.float32)
    gain_outer = jnp.clip(1.0 + 0.1 * jax.random.normal(splits[7], (2, WIDE), jnp.float32), 0.5, 1.5)
    shift_outer = centred(splits[8], (2, WIDE), 0.3, 1.8, ((0, 2), (1, 4)), jnp.float32)
    head_weight = centred(splits[9], (3, WIDE, CLASSES), 0.05, 0.3, ((1, 4), (2, 8)), jnp.float32)
    labels = with_ends(jax.random.randint(splits[10], (3, MICRO, ROWS_ALL), 0, CLASSES), jax.random.fold_in(splits[10], 1), 0, CLASSES - 1).astype(jnp.int32)
    thresholds = jnp.clip(1.0 * jax.random.uniform(splits[11], (MICRO, ROWS_ALL, WIDE), jnp.float32) ** block_scale(splits[11], (MICRO, ROWS_ALL, WIDE), ((1, 4), (2, 4)), -0.2, 0.2), 0.0, 1.0)
    return dict(block_input=block_input, image_sides=image_sides, w_reduce=w_reduce, w_spatial=w_spatial, w_expand=w_expand, gain_inner=gain_inner, shift_inner=shift_inner, gain_outer=gain_outer, shift_outer=shift_outer, head_weight=head_weight, labels=labels, thresholds=thresholds)


NORM_EPS = 1e-05
LOSS_WEIGHT = 20.0
SIGN_FLOOR = 0.1
KEEP_TEMPER = 0.2

@jax.custom_vjp
def low(v):
    return lax.optimization_barrier(v.astype(jnp.bfloat16)).astype(jnp.float32)

@jax.custom_vjp
def low_back(v):
    return v

def low_keep(v):
    return (low(v), None)

def low_pass(kept, grad):
    return (grad,)

def back_keep(v):
    return (v, None)

def back_low(kept, grad):
    return (low(grad),)
low.defvjp(low_keep, low_pass)
low_back.defvjp(back_keep, back_low)

def geometry(img_sides, row_count):
    img_sizes = (img_sides * img_sides).astype(jnp.int32)
    img_ends = jnp.cumsum(img_sizes).astype(jnp.int32)
    img_starts = (img_ends - img_sizes).astype(jnp.int32)
    row_pos = jnp.arange(row_count, dtype=jnp.int32)[:, None]
    inside = (row_pos >= img_starts[None, :]) & (row_pos < img_ends[None, :])
    first_row = lax.optimization_barrier(jnp.sum(jnp.where(inside, img_starts[None, :], 0), axis=1)).astype(jnp.int32)
    side_len = lax.optimization_barrier(jnp.sum(jnp.where(inside, img_sides[None, :], 0), axis=1)).astype(jnp.int32)
    live_rows = jnp.any(inside, axis=1)
    offset = (row_pos[:, 0] - first_row).astype(jnp.int32)
    safe_side = jnp.maximum(side_len, 1)
    row_in = (offset // safe_side).astype(jnp.int32)
    col_in = (offset % safe_side).astype(jnp.int32)
    index_list = []
    valid_list = []
    for row_step in (-1, 0, 1):
        for col_step in (-1, 0, 1):
            new_row = row_in + row_step
            new_col = col_in + col_step
            valid = live_rows & (new_row >= 0) & (new_row < side_len) & (new_col >= 0) & (new_col < side_len)
            index_list.append(jnp.where(valid, first_row + new_row * side_len + new_col, 0).astype(jnp.int32))
            valid_list.append(valid)
    return (jnp.stack(index_list), jnp.stack(valid_list).astype(jnp.float32), live_rows.astype(jnp.float32))

def group_geometry(sides_all):
    indices, valids, live_rows = jax.vmap(partial(geometry, row_count=ROWS))(sides_all)
    offsets = (jnp.arange(N_DP, dtype=jnp.int32) * ROWS)[:, None, None]
    indices = jnp.transpose((indices + offsets).astype(jnp.int32), (1, 0, 2)).reshape(9, N_DP * ROWS)
    valids = jnp.transpose(valids, (1, 0, 2)).reshape(9, N_DP * ROWS)
    return (indices, valids, live_rows.reshape(N_DP * ROWS))

def matmul_hi(left, right):
    return jnp.dot(left, right, precision=lax.Precision.HIGHEST, preferred_element_type=jnp.float32)

def smooth_act(values):
    return jax.nn.gelu(values, approximate=True)

def batch_norm(values, live_rows, gain_vec, shift_vec, live_total):
    mean_val = lax.optimization_barrier(jnp.sum(values * live_rows[:, None], axis=0)) / live_total
    centered = values - mean_val
    var_val = lax.optimization_barrier(jnp.sum(live_rows[:, None] * centered * centered, axis=0)) / live_total
    return live_rows[:, None] * (gain_vec * centered * lax.rsqrt(var_val + NORM_EPS) + shift_vec)

def block(x_in, w_red, w_spa, w_exp, g_in, s_in, g_out, s_out, layout):
    indices, valids, live_rows, live_total = layout
    x_low = low(x_in)
    first_pre = low_back(matmul_hi(x_low, low(w_red)))
    hidden_a = low(smooth_act(batch_norm(first_pre, live_rows, g_in[0], s_in[0], live_total)))
    spatial = low(w_spa)
    second_pre = matmul_hi(hidden_a[indices[0]] * valids[0][:, None], spatial[0])
    for tap_idx in range(1, 9):
        second_pre = second_pre + matmul_hi(hidden_a[indices[tap_idx]] * valids[tap_idx][:, None], spatial[tap_idx])
    second_pre = low_back(second_pre)
    hidden_b = low(smooth_act(batch_norm(second_pre, live_rows, g_in[1], s_in[1], live_total)))
    third_pre = low_back(matmul_hi(hidden_b, low(w_exp)))
    pre_out = batch_norm(third_pre, live_rows, g_out, s_out, live_total) + x_low
    return smooth_act(pre_out) * live_rows[:, None]

def heads(features, head_w, labels_now, live_rows):
    feat_low = low(features)
    class_ids = jnp.arange(CLASSES, dtype=jnp.int32)[None, :]
    losses = []
    for task_idx in range(3):
        logits = low_back(matmul_hi(feat_low, low(head_w[task_idx])))
        peak_val = lax.optimization_barrier(jnp.max(logits, axis=1, keepdims=True))
        log_total = jnp.log(lax.optimization_barrier(jnp.sum(jnp.exp(logits - peak_val), axis=1))) + peak_val[:, 0]
        picked = lax.optimization_barrier(jnp.sum(jnp.where(class_ids == labels_now[task_idx][:, None], logits, 0.0), axis=1))
        losses.append(LOSS_WEIGHT * jnp.sum(live_rows * (log_total - picked)))
    return jnp.stack(losses)

def sign_merge(task_grads, thresh):
    soft_abs = jnp.sqrt(task_grads * task_grads + SIGN_FLOOR * SIGN_FLOOR) - SIGN_FLOOR
    purity = 0.5 * (1.0 + lax.optimization_barrier(jnp.sum(task_grads, axis=0)) / (lax.optimization_barrier(jnp.sum(soft_abs, axis=0)) + SIGN_FLOOR))
    keep_frac = jax.nn.sigmoid((purity - thresh) / KEEP_TEMPER)
    upper = 0.5 * lax.optimization_barrier(jnp.sum(task_grads + soft_abs, axis=0))
    lower = 0.5 * lax.optimization_barrier(jnp.sum(task_grads - soft_abs, axis=0))
    return keep_frac * upper + (1.0 - keep_frac) * lower

def reference(block_input, image_sides, w_reduce, w_spatial, w_expand, gain_inner, shift_inner, gain_outer, shift_outer, head_weight, labels, thresholds):

    def params_of(section_idx):
        return (w_reduce[section_idx], w_spatial[section_idx], w_expand[section_idx], gain_inner[section_idx], shift_inner[section_idx], gain_outer[section_idx], shift_outer[section_idx])
    grad_totals = [jnp.zeros((2,) + leaf.shape, jnp.float32) for leaf in params_of(0)]
    head_total = jnp.zeros(head_weight.shape, jnp.float32)
    act_list = [[], []]
    grad_list = [[], []]
    for micro_idx in range(MICRO):
        indices, valids, live_rows = group_geometry(image_sides[micro_idx])
        layout = (indices, valids, live_rows, jnp.sum(live_rows))

        def first_block(x_in, *params):
            return block(x_in, *params, layout)

        def second_block(sent, *params):
            return block(low_back(sent), *params, layout)

        def task_heads(features, head_w):
            return heads(features, head_w, labels[:, micro_idx], live_rows)
        x_in = block_input[micro_idx].astype(jnp.float32)
        out_a, pull_a = jax.vjp(first_block, x_in, *params_of(0))
        sent = low(out_a)
        out_b, pull_b = jax.vjp(second_block, sent, *params_of(1))
        losses, pull_h = jax.vjp(task_heads, out_b, head_weight)
        task_grads = []
        for task_idx in range(3):
            feat_grad, head_grad = pull_h(jnp.zeros((3,), jnp.float32).at[task_idx].set(1.0))
            task_grads.append(feat_grad)
            head_total = head_total + head_grad
        merged = sign_merge(jnp.stack(task_grads), thresholds[micro_idx])
        grads_b = pull_b(merged)
        grads_a = pull_a(grads_b[0])
        act_list[0].append(out_a.astype(jnp.bfloat16))
        act_list[1].append(out_b.astype(jnp.bfloat16))
        grad_list[0].append(grads_a[0])
        grad_list[1].append(grads_b[0])
        for slot_idx in range(7):
            grad_totals[slot_idx] = grad_totals[slot_idx] + jnp.stack([grads_a[slot_idx + 1], grads_b[slot_idx + 1]])
    activations = jnp.stack([jnp.stack(act_list[0]), jnp.stack(act_list[1])])
    input_grads = jnp.stack([jnp.stack(grad_list[0]), jnp.stack(grad_list[1])])
    return (activations, input_grads, grad_totals[0], grad_totals[1], grad_totals[2], grad_totals[3].reshape(2, 2, N_MP, MID // N_MP), grad_totals[4].reshape(2, 2, N_MP, MID // N_MP), grad_totals[5].reshape(2, N_MP, WIDE // N_MP), grad_totals[6].reshape(2, N_MP, WIDE // N_MP), head_total)
```

```python
import math

import jax
import jax.numpy as jnp
from jax import lax
from jax.experimental import pallas as pl
from jax.experimental.pallas import tpu as pltpu
from jax.sharding import PartitionSpec as P

NORM_EPS = 1e-05
LOSS_WEIGHT = 20.0
SIGN_FLOOR = 0.1
KEEP_TEMPER = 0.2


def shifted(value, axis, steps):
    count = lax.axis_size(axis)
    leading, last = (max(0, -steps), min(count, count - steps))
    return lax.ppermute(value, axis, [(source, source + steps) for source in range(leading, last)])


def geometry(img_sides, row_count):
    img_sizes = img_sides * img_sides
    img_ends = jnp.cumsum(img_sizes)
    img_starts = img_ends - img_sizes
    row_pos = jnp.arange(row_count, dtype=jnp.int32)[:, None]
    inside = (row_pos >= img_starts[None, :]) & (row_pos < img_ends[None, :])
    first_row = jnp.sum(jnp.where(inside, img_starts[None, :], 0), axis=1)
    side_len = jnp.sum(jnp.where(inside, img_sides[None, :], 0), axis=1)
    live_rows = jnp.any(inside, axis=1)
    offset = row_pos[:, 0] - first_row
    safe_side = jnp.maximum(side_len, 1)
    row_in = offset // safe_side
    col_in = offset % safe_side
    index_list = []
    valid_list = []
    for row_step in (-1, 0, 1):
        for col_step in (-1, 0, 1):
            new_row = row_in + row_step
            new_col = col_in + col_step
            valid = (
                live_rows
                & (new_row >= 0)
                & (new_row < side_len)
                & (new_col >= 0)
                & (new_col < side_len)
            )
            index_list.append(jnp.where(valid, first_row + new_row * side_len + new_col, 0))
            valid_list.append(valid)
    return (
        jnp.stack(index_list),
        jnp.stack(valid_list).astype(jnp.float32),
        live_rows.astype(jnp.float32),
    )


def smooth_act(values):
    return jax.nn.gelu(values, approximate=True)


def take_block(store, micro_idx):
    return lax.dynamic_index_in_dim(store, micro_idx, 0, keepdims=False)


def put_block(store, update, micro_idx, active):
    previous = take_block(store, micro_idx)
    return lax.dynamic_update_index_in_dim(store, jnp.where(active, update, previous), micro_idx, 0)


def channel_gather(values):
    return lax.all_gather(values, "mp", axis=1, tiled=True)


def channel_sum(values):
    return lax.psum_scatter(values, "mp", scatter_dimension=1, tiled=True)


def norm_stats(values, live_rows):
    masked = values * live_rows[:, None]
    total_sum, live_total = lax.psum((jnp.sum(masked, axis=0), jnp.sum(live_rows)), "dp")
    mean_val = total_sum / live_total
    centered = (values - mean_val) * live_rows[:, None]
    var_val = lax.psum(jnp.sum(centered * centered, axis=0), "dp") / live_total
    return (mean_val, lax.rsqrt(var_val + NORM_EPS), live_total)


def normalize(values, stats, live_rows, gain_vec, shift_vec):
    mean_val, inv_std, live_total = stats
    return live_rows[:, None] * (gain_vec * (values - mean_val) * inv_std + shift_vec)


def norm_backward(values, stats, live_rows, gain_vec, grad_norm):
    mean_val, inv_std, live_total = stats
    normed = (values - mean_val) * inv_std
    grad_live = grad_norm * live_rows[:, None]
    local_shift = jnp.sum(grad_live, axis=0)
    local_gain = jnp.sum(grad_live * normed, axis=0)
    sum_shift, sum_gain = lax.psum((local_shift, local_gain), "dp")
    grad_values = (
        live_rows[:, None]
        * inv_std
        * gain_vec
        * (grad_live - sum_shift / live_total - normed * sum_gain / live_total)
    )
    return (grad_values, local_gain, local_shift)


def gather_taps(values, indices, valids, tap_idx):
    return values[indices[tap_idx]] * valids[tap_idx][:, None].astype(values.dtype)


def act_backward(pre_values, grad_values):
    return jax.vjp(smooth_act, pre_values)[1](grad_values)[0]


def block_forward(x_in, layout, weights):
    indices, valids, live_rows = layout
    w_red, w_spa, w_exp, g_in, s_in, g_out, s_out = weights
    first_pre = channel_sum(jnp.dot(x_in, w_red, preferred_element_type=jnp.float32))
    stats_a = norm_stats(first_pre, live_rows)
    full_a = channel_gather(
        smooth_act(normalize(first_pre, stats_a, live_rows, g_in[0], s_in[0])).astype(jnp.bfloat16)
    )
    second_pre = jnp.zeros((x_in.shape[0], w_spa.shape[2]), jnp.float32)
    for tap_idx in range(9):
        second_pre = second_pre + jnp.dot(
            gather_taps(full_a, indices, valids, tap_idx),
            w_spa[tap_idx],
            preferred_element_type=jnp.float32,
        )
    stats_b = norm_stats(second_pre, live_rows)
    full_b = channel_gather(
        smooth_act(normalize(second_pre, stats_b, live_rows, g_in[1], s_in[1])).astype(jnp.bfloat16)
    )
    third_pre = jnp.dot(full_b, w_exp, preferred_element_type=jnp.float32)
    stats_c = norm_stats(third_pre, live_rows)
    pre_out = normalize(third_pre, stats_c, live_rows, g_out, s_out) + x_in.astype(jnp.float32)
    result = smooth_act(pre_out) * live_rows[:, None]
    return (result, (first_pre, stats_a, full_a, second_pre, stats_b, full_b, third_pre, stats_c))


def block_backward(d_out, x_in, layout, weights, saved_state):
    indices, valids, live_rows = layout
    w_red, w_spa, w_exp, g_in, s_in, g_out, s_out = weights
    first_pre, stats_a, full_a, second_pre, stats_b, full_b, third_pre, stats_c = saved_state
    pre_out = normalize(third_pre, stats_c, live_rows, g_out, s_out) + x_in.astype(jnp.float32)
    d_pre = act_backward(pre_out, d_out * live_rows[:, None])
    d_third, gain_c, shift_c = norm_backward(third_pre, stats_c, live_rows, g_out, d_pre)
    d_third = d_third.astype(jnp.bfloat16)
    grad_exp = jnp.einsum("rc,ro->co", full_b, d_third, preferred_element_type=jnp.float32)
    d_full_b = channel_sum(
        jnp.einsum("ro,co->rc", d_third, w_exp, preferred_element_type=jnp.float32)
    )
    pre_b = normalize(second_pre, stats_b, live_rows, g_in[1], s_in[1])
    d_second, gain_b, shift_b = norm_backward(
        second_pre, stats_b, live_rows, g_in[1], act_backward(pre_b, d_full_b)
    )
    d_second = d_second.astype(jnp.bfloat16)
    grad_spa = []
    back_total = jnp.zeros((x_in.shape[0], w_spa.shape[1]), jnp.float32)
    for tap_idx in range(9):
        grad_spa.append(
            jnp.einsum(
                "rc,ro->co",
                gather_taps(full_a, indices, valids, tap_idx),
                d_second,
                preferred_element_type=jnp.float32,
            )
        )
        spread = jnp.einsum(
            "ro,co->rc", d_second, w_spa[8 - tap_idx], preferred_element_type=jnp.float32
        )
        back_total = back_total + spread[indices[tap_idx]] * valids[tap_idx][:, None]
    d_full_a = channel_sum(back_total)
    pre_a = normalize(first_pre, stats_a, live_rows, g_in[0], s_in[0])
    d_first, gain_a, shift_a = norm_backward(
        first_pre, stats_a, live_rows, g_in[0], act_backward(pre_a, d_full_a)
    )
    d_first_full = channel_gather(d_first.astype(jnp.bfloat16))
    grad_red = jnp.einsum("rc,ro->co", x_in, d_first_full, preferred_element_type=jnp.float32)
    d_in = jnp.einsum("ro,co->rc", d_first_full, w_red, preferred_element_type=jnp.float32) + d_pre
    return (
        d_in,
        (
            grad_red,
            jnp.stack(grad_spa),
            grad_exp,
            jnp.stack([gain_a, gain_b]),
            jnp.stack([shift_a, shift_b]),
            gain_c,
            shift_c,
        ),
    )


def sign_merge(task_grads, thresh):
    soft_abs = jnp.sqrt(task_grads * task_grads + SIGN_FLOOR * SIGN_FLOOR) - SIGN_FLOOR
    purity = 0.5 * (1.0 + jnp.sum(task_grads, axis=0) / (jnp.sum(soft_abs, axis=0) + SIGN_FLOOR))
    keep_frac = jax.nn.sigmoid((purity - thresh) / KEEP_TEMPER)
    upper = 0.5 * jnp.sum(task_grads + soft_abs, axis=0)
    lower = 0.5 * jnp.sum(task_grads - soft_abs, axis=0)
    return keep_frac * upper + (1.0 - keep_frac) * lower


def plain_device(
    block_input,
    image_sides,
    w_reduce,
    w_spatial,
    w_expand,
    gain_inner,
    shift_inner,
    gain_outer,
    shift_outer,
    head_weight,
    labels,
    thresholds,
):
    section_idx = lax.axis_index("section")
    micro_count = block_input.shape[0]
    row_count = block_input.shape[1]
    w_red, w_spa, w_exp = (
        lax.all_gather(w_reduce[0].astype(jnp.bfloat16), "dp", axis=1, tiled=True),
        lax.all_gather(w_spatial[0].astype(jnp.bfloat16), "dp", axis=1, tiled=True),
        lax.all_gather(w_expand[0].astype(jnp.bfloat16), "dp", axis=0, tiled=True),
    )
    weights = (w_red, w_spa, w_exp, gain_inner[0], shift_inner[0], gain_outer[0], shift_outer[0])
    heads_all = lax.all_gather(
        head_weight.astype(jnp.bfloat16), ("section", "dp"), axis=2, tiled=True
    )
    class_total = heads_all.shape[2]
    class_ids = jnp.arange(class_total, dtype=jnp.int32)[None, None, :]

    def layout_for(micro_idx):
        return geometry(take_block(image_sides, micro_idx)[0], row_count)

    received = jnp.zeros(block_input.shape[1:], jnp.bfloat16)
    kept_inputs = jnp.zeros(block_input.shape, jnp.bfloat16)
    activ_store = jnp.zeros(block_input.shape, jnp.bfloat16)
    cotangents = jnp.zeros(block_input.shape, jnp.float32)
    head_grad = jnp.zeros(heads_all.shape, jnp.float32)
    for turn_idx in range(micro_count + 1):
        micro_idx = jnp.clip(turn_idx - section_idx, 0, micro_count - 1)
        active = (turn_idx - section_idx >= 0) & (turn_idx - section_idx < micro_count)
        x_in = jnp.where(section_idx == 0, block_input[min(turn_idx, micro_count - 1)], received)
        layout = layout_for(micro_idx)
        live_rows = layout[2]
        result, saved_state = block_forward(x_in, layout, weights)
        result_low = result.astype(jnp.bfloat16)
        kept_inputs = put_block(kept_inputs, x_in, micro_idx, active)
        activ_store = put_block(activ_store, result_low, micro_idx, active)
        labels_now = lax.dynamic_index_in_dim(labels, micro_idx, 1, keepdims=False)
        logits = lax.psum(
            jnp.einsum("rc,tco->tro", result_low, heads_all, preferred_element_type=jnp.float32),
            "mp",
        )
        peak_val = jnp.max(logits, axis=2, keepdims=True)
        expo = jnp.exp(logits - peak_val)
        soft_p = expo / jnp.sum(expo, axis=2, keepdims=True)
        picked = (class_ids == labels_now[:, :, None]).astype(jnp.float32)
        delta_low = (LOSS_WEIGHT * live_rows[None, :, None] * (soft_p - picked)).astype(
            jnp.bfloat16
        )
        task_grads = jnp.einsum(
            "tro,tco->trc", delta_low, heads_all, preferred_element_type=jnp.float32
        )
        merged = sign_merge(task_grads, take_block(thresholds, micro_idx))
        use_head = active & (section_idx == 1)
        head_grad = head_grad + jnp.where(
            use_head,
            jnp.einsum("rc,tro->tco", result_low, delta_low, preferred_element_type=jnp.float32),
            0.0,
        )
        cotangents = put_block(cotangents, merged, micro_idx, use_head)
        received = shifted(result_low, "section", 1)
    grad_recv = jnp.zeros(block_input.shape[1:], jnp.bfloat16)
    input_store = jnp.zeros(block_input.shape, jnp.float32)
    grad_total = None
    for turn_idx in range(micro_count + 1):
        micro_idx = jnp.clip(turn_idx - 1 + section_idx, 0, micro_count - 1)
        active = (turn_idx - 1 + section_idx >= 0) & (turn_idx - 1 + section_idx < micro_count)
        d_out = jnp.where(
            section_idx == 1, take_block(cotangents, micro_idx), grad_recv.astype(jnp.float32)
        )
        x_in = take_block(kept_inputs, micro_idx)
        layout = layout_for(micro_idx)
        saved_state = block_forward(x_in, layout, weights)[1]
        d_in, grad_set = block_backward(d_out, x_in, layout, weights, saved_state)
        masked = jax.tree.map(lambda leaf: jnp.where(active, leaf, 0.0), grad_set)
        grad_total = masked if grad_total is None else jax.tree.map(jnp.add, grad_total, masked)
        d_send = d_in.astype(jnp.bfloat16)
        input_store = put_block(
            input_store,
            jnp.where(section_idx == 1, d_send.astype(jnp.float32), d_in),
            micro_idx,
            active,
        )
        grad_recv = shifted(d_send, "section", -1)
    g_red, g_spa, g_exp, g_gain_in, g_shift_in, g_gain_out, g_shift_out = grad_total
    out_red, out_spa, out_exp, out_gain_in, out_shift_in, out_gain_out, out_shift_out = (
        lax.psum_scatter(g_red[None], "dp", scatter_dimension=2, tiled=True),
        lax.psum_scatter(g_spa[None], "dp", scatter_dimension=2, tiled=True),
        lax.psum_scatter(g_exp[None], "dp", scatter_dimension=1, tiled=True),
        lax.psum_scatter(g_gain_in[None, :, None, :], "dp", scatter_dimension=3, tiled=True),
        lax.psum_scatter(g_shift_in[None, :, None, :], "dp", scatter_dimension=3, tiled=True),
        lax.psum_scatter(g_gain_out[None, None, :], "dp", scatter_dimension=2, tiled=True),
        lax.psum_scatter(g_shift_out[None, None, :], "dp", scatter_dimension=2, tiled=True),
    )
    head_out = lax.psum_scatter(head_grad, ("section", "dp"), scatter_dimension=2, tiled=True)
    return (
        activ_store[None],
        input_store[None],
        out_red,
        out_spa,
        out_exp,
        out_gain_in,
        out_shift_in,
        out_gain_out,
        out_shift_out,
        head_out,
    )


K0 = math.sqrt(2.0 / math.pi)
K1 = 0.044715
MESH = pl.DeviceIdType.MESH
F32 = jnp.float32
BF16 = jnp.bfloat16
SIDES = (2, 7)
TAPS = [(a, b) for a in (-1, 0, 1) for b in (-1, 0, 1)]
PAD = 8
NN = (((1,), (0,)), ((), ()))
NT = (((1,), (1,)), ((), ()))
TN = (((0,), (0,)), ((), ()))


def tap_masks():
    found = []
    for tap_idx, (a, b) in enumerate(TAPS):
        for side in SIDES:
            found.append((tap_idx, a, b, side, a * side + b))
    return found


MASKS = tap_masks()


def dot(left, right, dims):
    return lax.dot_general(left, right, dims, preferred_element_type=F32)


def gelu(v):
    return 0.5 * v * (1.0 + jnp.tanh(K0 * v * (1.0 + K1 * v * v)))


def gelu_grad(v):
    sq = v * v
    t = jnp.tanh(K0 * v * (1.0 + K1 * sq))
    return 0.5 * (1.0 + t) + (0.5 * K0) * v * (1.0 - t * t) * (1.0 + 3.0 * K1 * sq)


def fold(x):
    return jnp.sum(x.reshape(x.shape[0] // 8, 8, x.shape[1]), axis=0)


def wide(x, width):
    times = width // x.shape[1]
    return x if times == 1 else jnp.concatenate([x] * times, axis=1)


def loop(total, chunk, body, init=None):
    def one(i, carry):
        return body(pl.ds(pl.multiple_of(i * chunk, chunk), chunk), carry)

    return lax.fori_loop(0, total // chunk, one, 0 if init is None else init)


def rows_tile(first, second, third):
    width = first.shape[1]
    place = lax.broadcasted_iota(jnp.int32, (8, width), 0)
    wide_of = lambda v: jnp.broadcast_to(v, (8, width))
    return jnp.where(
        place == 0, wide_of(first), jnp.where(place == 1, wide_of(second), wide_of(third))
    )


class Sems:
    def __init__(self, ref):
        self.ref, self.used, self.size = ref, 0, ref.shape[0]

    def take(self, count=1):
        first = self.used
        self.used += count
        assert self.used <= self.size, self.used
        return first


def make_kernel(sizes):
    n_dp, n_mp, R, Wd, M, C, Cd, classes, tasks, piece = sizes
    n_sec = 2
    W9 = 9 * C

    def kernel(*refs):
        (
            x_hbm, sides_ref, wred_hbm, wspa_hbm, wexp_hbm, gin_ref, sin_ref, gout_ref, sout_ref,
            head_hbm, lab_ref, thr_hbm,
            act_hbm, ig_hbm, ored, ospa, oexp, ovec, ohead,
            ssems, rsems, lsems,
            sred, sspa, sexp, shead, thr, xin, wr, wsp, we, hd, par,
            live, geo, masks, labc,
            rs_s, rs_r, ag_a, ag_b, ag_d, st, keep, first, second, third, ppad, dpad, dbuf,
            lg_s, lg_r, dl, act1, tg, dpre, evec, dth, hbuf, ig,
            gred, gspa, gexp, sibred, sibspa, sibexp, rred, rspa, rexp, ghead, rhead, vec, vsib,
        ) = refs
        s = lax.axis_index("section")
        d = lax.axis_index("dp")
        m = lax.axis_index("mp")
        o = 1 - s
        send, recv, local = Sems(ssems), Sems(rsems), Sems(lsems)
        pending = {None: [], 0: [], 1: []}
        rem = lax.rem
        dp_dev = lambda t: (s, t, m)
        mp_dev = lambda t: (s, d, t)
        sib_dev = (o, d, m)

        def rcopy(src, dst, rsem, dev, when=None):
            ssem = send.take()
            pltpu.make_async_remote_copy(
                src_ref=src(),
                dst_ref=dst(),
                send_sem=ssems.at[ssem],
                recv_sem=rsems.at[rsem],
                device_id=dev,
                device_id_type=MESH,
            ).start()

            def sent():
                pltpu.make_async_remote_copy(
                    src_ref=src(),
                    dst_ref=src(),
                    send_sem=ssems.at[ssem],
                    recv_sem=rsems.at[0],
                    device_id=sib_dev,
                    device_id_type=MESH,
                ).wait_send()

            pending[when].append(sent)

        def arrive(dst, rsem):
            pltpu.make_async_remote_copy(
                src_ref=dst,
                dst_ref=dst,
                send_sem=ssems.at[0],
                recv_sem=rsems.at[rsem],
                device_id=sib_dev,
                device_id_type=MESH,
            ).wait_recv()

        def load(src, dst):
            cp = pltpu.make_async_copy(src, dst, lsems.at[local.take()])
            cp.start()
            return cp

        axes = {"dp": (n_dp, d, dp_dev), "mp": (n_mp, m, mp_dev)}

        def spread(axis, src_of, dst, when=None, base=None):
            n, me, dev = axes[axis]
            base = recv.take(n) if base is None else base
            for k in range(1, n):
                rcopy(lambda k=k: src_of(rem(me + k, n)), dst, base + me, dev(rem(me + k, n)), when)
            return base

        def gathered(axis, slot_of, base):
            n, me, _ = axes[axis]
            for k in range(1, n):
                src = rem(me + n - k, n)
                arrive(slot_of(src), base + src)

        l_red = load(wred_hbm.at[0], sred)
        l_x = load(x_hbm.at[s], xin.at[0])
        l_spa = load(wspa_hbm.at[0], sspa)
        l_exp = load(wexp_hbm.at[0], sexp)
        l_head = load(head_hbm, shead)
        l_thr = load(thr_hbm.at[s], thr)

        barrier = pltpu.get_barrier_semaphore()
        greeted = 0
        for ds_ in range(n_sec):
            for k in range(n_dp):
                if ds_ == 0 and k == 0:
                    continue
                pl.semaphore_signal(
                    barrier, inc=1,
                    device_id=(rem(s + ds_, n_sec), rem(d + k, n_dp), m),
                    device_id_type=MESH,
                )
                greeted += 1
        for k in range(1, n_mp):
            pl.semaphore_signal(
                barrier, inc=1, device_id=(s, d, rem(m + k, n_mp)), device_id_type=MESH
            )
            greeted += 1

        l_red.wait()
        wr[s, d] = sred[...].astype(BF16)
        par[s] = jnp.zeros(par.shape[1:], F32)
        for i in range(2):
            par[s, i:i + 1, :C] = gin_ref[0, i:i + 1, :]
            par[s, 2 + i:3 + i, :C] = sin_ref[0, i:i + 1, :]
        par[s, 4:5, :] = gout_ref[...]
        par[s, 5:6, :] = sout_ref[...]
        pl.semaphore_wait(barrier, greeted)

        b_red, b_spa, b_exp = [[recv.take(n_dp) for _ in range(2)] for _ in range(3)]
        f_red, f_spa, f_exp = [[recv.take() for _ in range(2)] for _ in range(3)]

        def send_own(buf, bases, j):
            spread("dp", lambda t: buf.at[j, d], lambda: buf.at[j, d], when=j, base=bases[j])

        def pass_on(buf, bases, fsems, j):
            @pl.when(s == j)
            def _():
                gathered("dp", lambda src: buf.at[j, src], bases[j])
                rcopy(lambda: buf.at[j], lambda: buf.at[j], fsems[j], sib_dev, when=j)

        def from_sib(buf, fsems, j):
            @pl.when(s != j)
            def _():
                arrive(buf.at[j], fsems[j])

        par_sem = recv.take()
        rcopy(lambda: par.at[s], lambda: par.at[s], par_sem, sib_dev)

        @pl.when(s == 0)
        def _():
            send_own(wr, b_red, 0)

        l_spa.wait()
        for k in range(9):
            wsp[s, d, :, k * C:(k + 1) * C] = sspa[k].astype(BF16)

        @pl.when(s == 0)
        def _():
            send_own(wsp, b_spa, 0)

        l_exp.wait()
        we[s, d] = sexp[...].astype(BF16)

        @pl.when(s == 0)
        def _():
            send_own(we, b_exp, 0)

        sides = jnp.where(s == 0, sides_ref[0], sides_ref[1]).astype(F32)
        slots = sides.shape[1]
        sq = jnp.broadcast_to(sides * sides, (8, slots)).astype(BF16)
        upper = (
            lax.broadcasted_iota(jnp.int32, (slots, slots), 0)
            <= lax.broadcasted_iota(jnp.int32, (slots, slots), 1)
        ).astype(BF16)
        ends = dot(sq, upper, NN)[0:1]
        starts = ends - sides * sides
        nloc = jnp.broadcast_to(jnp.max(ends, axis=1, keepdims=True), (1, 128))
        shape = (R, 128)
        pos = lax.broadcasted_iota(jnp.int32, (R, slots), 0).astype(F32)
        inside = (pos >= starts) & (pos < ends)
        origin = jnp.sum(jnp.where(inside, starts, 0.0), axis=1, keepdims=True)
        side = jnp.sum(jnp.where(inside, sides, 0.0), axis=1, keepdims=True)
        geo[0] = jnp.broadcast_to(origin, shape)
        geo[1] = jnp.broadcast_to(side, shape)

        def make_masks(rows, carry):
            side_b = geo[1, rows]
            here = lax.broadcasted_iota(jnp.int32, side_b.shape, 0) + rows.start
            offset = here.astype(F32) - geo[0, rows]
            row_in = jnp.floor((offset + 0.5) / jnp.maximum(side_b, 1.0))
            col_in = offset - row_in * side_b
            live[rows] = (side_b > 0.0).astype(F32)
            for idx, (_, a, b, q, _) in enumerate(MASKS):
                ra, cb = row_in + a, col_in + b
                ok = (side_b == q) & (ra >= 0.0) & (ra < q) & (cb >= 0.0) & (cb < q)
                masks[idx, rows] = ok.astype(F32)
            return carry

        loop(R, 64, make_masks)
        for buf in (ppad, dpad):
            edge = jnp.zeros((PAD, buf.shape[1]), F32)
            buf[0:PAD] = edge
            buf[PAD + R:PAD + R + PAD] = edge
        lab2 = lab_ref[...]
        lab = jnp.where(s == 0, lab2[:, 0], lab2[:, 1]).astype(F32)
        lab = jnp.concatenate([lab, jnp.zeros((8 - tasks, R), F32)], axis=0)
        labc[...] = jnp.transpose(lab)

        l_head.wait()
        eye = (
            lax.broadcasted_iota(jnp.int32, (piece, piece), 0)
            == lax.broadcasted_iota(jnp.int32, (piece, piece), 1)
        ).astype(BF16)
        mine = s * n_dp + d
        for t in range(tasks):
            hd[mine, t] = dot(eye, shead[t].astype(BF16), NT).astype(BF16)
        b_head = recv.take(n_sec * n_dp)

        def to_all(src_of, dst, base):
            for ds_ in range(n_sec):
                for k in range(n_dp):
                    if ds_ == 0 and k == 0:
                        continue
                    place = lambda ds_=ds_, k=k: (rem(s + ds_, n_sec), rem(d + k, n_dp))

                    def src(place=place):
                        ts, td = place()
                        return src_of(ts * n_dp + td)

                    rcopy(src, dst, base + mine, place() + (m,))

        def from_all(slot_of, base):
            for ds_ in range(n_sec):
                for k in range(n_dp):
                    if ds_ == 0 and k == 0:
                        continue
                    src = rem(s + ds_, n_sec) * n_dp + rem(d + k, n_dp)
                    arrive(slot_of(src), base + src)

        def cat(buf, n):
            return jnp.concatenate([buf[i] for i in range(n)], axis=1)

        phase = {"rs": 0, "st": 0}

        def rs_start():
            p = phase["rs"]
            phase["rs"] += 1
            base = spread("mp", lambda t: rs_s.at[p, t], lambda: rs_r.at[p, m])
            return p, base

        def rs_finish(handle, dst):
            p, base = handle
            gathered("mp", lambda src: rs_r.at[p, src], base)

            def add(rows, carry):
                total = rs_s[p, m, rows].astype(F32)
                for k in range(1, n_mp):
                    total = total + rs_r[p, rem(m + k, n_mp), rows].astype(F32)
                dst[rows] = total
                return carry

            loop(R, 128, add)

        def product_to_rs(left, right_of, dims):
            p = phase["rs"]

            def part(rows, carry):
                out = dot(left[rows], right_of(), dims)
                for c in range(n_mp):
                    rs_s[p, c, rows] = out[:, c * C:(c + 1) * C].astype(BF16)
                return carry

            loop(R, 128, part)
            return rs_start()

        def exchange(tile):
            p = phase["st"]
            phase["st"] += 1
            width = tile.shape[1]
            view = st.at[p, :, :, 0:width]
            st[p, d, :, 0:width] = tile
            slot = lambda src: st.at[p, src, :, 0:width]
            base = spread("dp", lambda t: slot(d), lambda: slot(d))
            return p, width, base

        def collect(handle):
            p, width, base = handle
            gathered("dp", lambda src: st.at[p, src, :, 0:width], base)
            return [st[p, i, :, 0:width] for i in range(n_dp)]

        def stats_start(buf, width):
            chunk = 128 if width <= 128 else 32
            zero = jnp.zeros((8, width), F32)

            def sum_up(rows, carry):
                return carry + fold(buf[rows] * wide(live[rows], width))

            total = jnp.sum(loop(R, chunk, sum_up, zero), axis=0, keepdims=True)
            count = wide(nloc, width)
            mean = total / jnp.maximum(count, 1.0)

            def squares(rows, carry):
                off = (buf[rows] - mean) * wide(live[rows], width)
                return carry + fold(off * off)

            sqs = jnp.sum(loop(R, chunk, squares, zero), axis=0, keepdims=True)
            return exchange(rows_tile(total, sqs, count))

        def stats_finish(handle, j, i):
            tiles = collect(handle)
            width = handle[1]
            count = sum(t[2:3] for t in tiles)
            mean = sum(t[0:1] for t in tiles) / count
            sqs = 0.0
            for t in tiles:
                local_mean = t[0:1] / jnp.maximum(t[2:3], 1.0)
                sqs = sqs + t[1:2] + t[2:3] * (local_mean - mean) * (local_mean - mean)
            inv = lax.rsqrt(sqs / count + NORM_EPS)
            keep[j, i, :, 0:width] = rows_tile(mean, inv, count)

        def norm_of(j, i, width):
            tile = keep[j, i, :, 0:width]
            if i < 2:
                gain, shift = par[j, i:i + 1, 0:width], par[j, 2 + i:3 + i, 0:width]
            else:
                gain, shift = par[j, 4:5, 0:width], par[j, 5:6, 0:width]
            return tile[0:1], tile[1:2], tile[2:3], gain, shift

        def taps_sum(src, flip, put):
            for r0 in range(0, R, 128):
                put(r0, lambda idx_list, lanes: sum(
                    masks[(len(MASKS) - 2 - (idx // 2) * 2 + idx % 2) if flip else idx, r0:r0 + 128]
                    * src[
                        PAD + r0 + (-1 if flip else 1) * MASKS[idx][4]:
                        PAD + r0 + (-1 if flip else 1) * MASKS[idx][4] + 128,
                        lanes,
                    ]
                    for idx in idx_list
                ))

        nothing = lambda: None
        vec[...] = jnp.zeros(vec.shape, F32)

        def forward(j, hooks):
            x = xin.at[j]
            h = product_to_rs(x, lambda: cat(wr.at[j], n_dp), NN)
            hooks[0]()
            rs_finish(h, first.at[j])
            h = stats_start(first.at[j], C)
            stats_finish(h, j, 0)
            mu, inv, _, gain, shift = norm_of(j, 0, C)

            def act_a(rows, carry):
                y = live[rows] * (gain * ((first[j, rows] - mu) * inv) + shift)
                ag_a[j, m, rows] = gelu(y).astype(BF16)
                return carry

            loop(R, 128, act_a)
            base = spread("mp", lambda t: ag_a.at[j, m], lambda: ag_a.at[j, m])
            hooks[1]()
            gathered("mp", lambda src: ag_a.at[j, src], base)

            def conv(rows, carry):
                full = jnp.concatenate([ag_a[j, i, rows] for i in range(n_mp)], axis=1)
                weights = wsp[j].reshape(M, W9)
                start = pl.multiple_of(rows.start + PAD, 8)
                ppad[pl.ds(start, 128)] = dot(full, weights, NN)
                return carry

            loop(R, 128, conv)

            def put(r0, summed):
                second[j, r0:r0 + 128] = sum(
                    summed([2 * k, 2 * k + 1], slice(k * C, (k + 1) * C)) for k in range(9)
                )

            taps_sum(ppad, False, put)
            h = stats_start(second.at[j], C)
            stats_finish(h, j, 1)
            mu, inv, _, gain, shift = norm_of(j, 1, C)

            def act_b(rows, carry):
                y = live[rows] * (gain * ((second[j, rows] - mu) * inv) + shift)
                ag_b[j, m, rows] = gelu(y).astype(BF16)
                return carry

            loop(R, 128, act_b)
            base = spread("mp", lambda t: ag_b.at[j, m], lambda: ag_b.at[j, m])
            hooks[2]()
            gathered("mp", lambda src: ag_b.at[j, src], base)

            def expand(rows, carry):
                full = jnp.concatenate([ag_b[j, i, rows] for i in range(n_mp)], axis=1)
                third[j, rows] = dot(full, we[j].reshape(M, Wd), NN)
                return carry

            loop(R, 128, expand)
            h = stats_start(third.at[j], Wd)
            hooks[3]()
            stats_finish(h, j, 2)
            mu, inv, _, gain, shift = norm_of(j, 2, Wd)
            out = xin.at[1] if j == 0 else act1

            def act_c(rows, carry):
                lv = wide(live[rows], Wd)
                pre = lv * (gain * ((third[j, rows] - mu) * inv) + shift)
                pre = pre + xin[j, rows].astype(F32)
                out[rows] = (lv * gelu(pre)).astype(BF16)
                return carry

            loop(R, 32, act_c)

        def to_section(src, hbm, j, sem):
            @pl.when(s == j)
            def _():
                lsem = local.take()
                made = lambda: pltpu.make_async_copy(src(), hbm.at[0, s], lsems.at[lsem])
                made().start()
                pending[j].append(lambda: made().wait())

            @pl.when(s != j)
            def _():
                rcopy(src, lambda: hbm.at[0, s], sem, sib_dev, when=1 - j)

        out_sems = [[recv.take() for _ in range(2)] for _ in range(2)]

        g_sib = [recv.take() for _ in range(3)]
        g_dp = [recv.take(n_dp) for _ in range(3)]
        grads = ((gred, sibred, rred), (gspa, sibspa, rspa), (gexp, sibexp, rexp))

        def grad_to_sib(which, j):
            own, sib, _ = grads[which]

            @pl.when(s != j)
            def _():
                rcopy(lambda: own.at[j], lambda: sib, g_sib[which], sib_dev, when=1 - j)

        def grad_to_dp(which, j):
            own, sib, got = grads[which]

            @pl.when(s == j)
            def _():
                arrive(sib, g_sib[which])
                depth = own.shape[2]

                def add(rows, carry):
                    for i in range(n_dp):
                        own[j, i, rows] = (
                            own[j, i, rows].astype(F32) + sib[i, rows].astype(F32)
                        ).astype(BF16)
                    return carry

                loop(depth, 64, add)
                spread("dp", lambda t: own.at[j, t], lambda: got.at[d], when=j, base=g_dp[which])

        def backward(j, hooks):
            mu, inv, count, gain, shift = norm_of(j, 2, Wd)
            zero = (jnp.zeros((8, Wd), F32), jnp.zeros((8, Wd), F32))

            def top(rows, carry):
                sb, sg = carry
                lv = wide(live[rows], Wd)
                xhat = (third[j, rows] - mu) * inv
                pre = lv * (gain * xhat + shift) + xin[j, rows].astype(F32)
                dp_ = gelu_grad(pre) * lv * evec[rows]
                dpre[rows] = dp_
                return sb + fold(dp_), sg + fold(dp_ * xhat)

            sb, sg = loop(R, 32, top, zero)
            total = lambda v: jnp.sum(v, axis=0, keepdims=True)
            sb, sg = total(sb), total(sg)
            h = exchange(rows_tile(sb, sg, sg))
            hooks[0]()
            tile = sum(collect(h))
            vec[j, 4:5, :] = tile[1:2]
            vec[j, 5:6, :] = tile[0:1]
            sb_n, sg_n = tile[0:1] / count, tile[1:2] / count
            scale = gain * inv

            def d_third(rows, carry):
                lv = wide(live[rows], Wd)
                xhat = (third[j, rows] - mu) * inv
                dth[rows] = (lv * scale * (dpre[rows] - sb_n - xhat * sg_n)).astype(BF16)
                return carry

            loop(R, 32, d_third)
            h = product_to_rs(dth, lambda: we[j].reshape(M, Wd), NT)
            for i in range(n_dp):
                full = cat(ag_b.at[j], n_mp)[:, i * Cd:(i + 1) * Cd]
                gexp[j, i] = dot(full, dth[...], TN).astype(BF16)
            grad_to_sib(2, j)
            hooks[1]()
            rs_finish(h, hbuf)

            def inner(i, src):
                mu, inv, count, gain, shift = norm_of(j, i, C)
                zero = (jnp.zeros((8, C), F32), jnp.zeros((8, C), F32))

                def up(rows, carry):
                    sb, sg = carry
                    xhat = (src[j, rows] - mu) * inv
                    pre = live[rows] * (gain * xhat + shift)
                    g = live[rows] * gelu_grad(pre) * hbuf[rows]
                    hbuf[rows] = g
                    return sb + fold(g), sg + fold(g * xhat)

                sb, sg = loop(R, 128, up, zero)
                sb, sg = total(sb), total(sg)
                tile = sum(collect(exchange(rows_tile(sb, sg, sg))))
                vec[j, i:i + 1, 0:C] = tile[1:2]
                vec[j, 2 + i:3 + i, 0:C] = tile[0:1]
                sb_n, sg_n = tile[0:1] / count, tile[1:2] / count
                scale = gain * inv

                def grad_of(rows):
                    xhat = (src[j, rows] - mu) * inv
                    return live[rows] * scale * (hbuf[rows] - sb_n - xhat * sg_n)

                return grad_of

            grad_of = inner(1, second)

            def d_second(rows, carry):
                start = pl.multiple_of(rows.start + PAD, 8)
                dpad[pl.ds(start, 128)] = grad_of(rows).astype(BF16).astype(F32)
                return carry

            loop(R, 128, d_second)

            def put(r0, summed):
                for k in range(9):
                    dbuf[r0:r0 + 128, k * C:(k + 1) * C] = summed(
                        [2 * k, 2 * k + 1], slice(None)
                    ).astype(BF16)

            taps_sum(dpad, True, put)
            h = product_to_rs(dbuf, lambda: wsp[j].reshape(M, W9), NT)
            for i in range(n_dp):
                full = cat(ag_a.at[j], n_mp)[:, i * Cd:(i + 1) * Cd]
                gspa[j, i] = dot(full, dbuf[...], TN).astype(BF16)
            grad_to_sib(1, j)
            grad_to_dp(2, j)
            hooks[2]()
            rs_finish(h, hbuf)
            grad_of = inner(0, first)

            def d_first(rows, carry):
                ag_d[j, m, rows] = grad_of(rows).astype(BF16)
                return carry

            loop(R, 128, d_first)
            base = spread("mp", lambda t: ag_d.at[j, m], lambda: ag_d.at[j, m])
            grad_to_dp(1, j)
            hooks[3]()
            gathered("mp", lambda src: ag_d.at[j, src], base)

            def d_input():
                def body(rows, carry):
                    full = jnp.concatenate([ag_d[j, i, rows] for i in range(n_mp)], axis=1)
                    out = dot(full, cat(wr.at[j], n_dp), NT) + dpre[rows]
                    if j == 1:
                        out = out.astype(BF16).astype(F32)
                        evec[rows] = out
                    ig[j, rows] = out
                    return carry

                loop(R, 128, body)
                to_section(lambda: ig.at[j], ig_hbm, j, out_sems[1][j])

            def g_reduce():
                for i in range(n_dp):
                    full = cat(ag_d.at[j], n_mp)[:, i * Cd:(i + 1) * Cd]
                    gred[j, i] = dot(xin[j], full, TN).astype(BF16)
                grad_to_sib(0, j)

            return d_input, g_reduce

        pass_on(wr, b_red, f_red, 0)
        l_x.wait()
        from_sib(wr, f_red, 0)

        @pl.when(s == 1)
        def _():
            send_own(wr, b_red, 1)
            send_own(wsp, b_spa, 1)
            send_own(we, b_exp, 1)

        arrive(par.at[o], par_sem)

        def f00():
            pass_on(wsp, b_spa, f_spa, 0)
            to_all(lambda t: hd.at[mine], lambda: hd.at[mine], b_head)

        def f01():
            pass_on(we, b_exp, f_exp, 0)
            from_sib(wsp, f_spa, 0)

        def f02():
            pass_on(wr, b_red, f_red, 1)
            from_sib(we, f_exp, 0)

        def f03():
            pass_on(wsp, b_spa, f_spa, 1)
            from_sib(wr, f_red, 1)

        forward(0, (f00, f01, f02, f03))

        def f10():
            to_section(lambda: xin.at[1], act_hbm, 0, out_sems[0][0])
            pass_on(we, b_exp, f_exp, 1)

        def f11():
            from_sib(wsp, f_spa, 1)

        def f12():
            from_sib(we, f_exp, 1)

        forward(1, (f10, f11, f12, nothing))

        from_all(lambda src: hd.at[src], b_head)
        RM = R // n_mp
        n_cls = n_sec * n_dp

        def heads_of(t):
            return hd[:, t].reshape(classes, Wd)

        for c in range(n_mp):
            rows = act1[c * RM:(c + 1) * RM]
            for t in range(tasks):
                lg_s[c, :, t * classes:(t + 1) * classes] = dot(rows, heads_of(t), NT).astype(
                    lg_s.dtype
                )
        base = spread("mp", lambda t: lg_s.at[t], lambda: lg_r.at[m])
        to_section(lambda: act1, act_hbm, 1, out_sems[0][1])
        l_thr.wait()
        gathered("mp", lambda src: lg_r.at[src], base)
        here = pl.ds(pl.multiple_of(m * RM, RM), RM)
        lv = wide(live[here], classes)
        for t in range(tasks):
            lanes = slice(t * classes, (t + 1) * classes)
            logit = lg_s[m, :, lanes].astype(F32)
            for k in range(1, n_mp):
                logit = logit + lg_r[rem(m + k, n_mp), :, lanes].astype(F32)
            expo = jnp.exp(logit - jnp.max(logit, axis=1, keepdims=True))
            soft = expo / jnp.sum(expo, axis=1, keepdims=True)
            ids = lax.broadcasted_iota(jnp.int32, (RM, classes), 1).astype(F32)
            hot = (ids == labc[here, t:t + 1]).astype(F32)
            dl[m, :, lanes] = (LOSS_WEIGHT * lv * (soft - hot)).astype(BF16)
        base = spread("mp", lambda t: dl.at[m], lambda: dl.at[m])
        gathered("mp", lambda src: dl.at[src], base)

        def merge_block(c):
            for t in range(tasks):
                lanes = slice(t * classes, (t + 1) * classes)
                tg[t] = dot(dl[c, :, lanes], heads_of(t), NN)

            def merge(rows, carry):
                total = soft_sum = None
                for t in range(tasks):
                    g = tg[t, rows]
                    soft = jnp.sqrt(g * g + SIGN_FLOOR * SIGN_FLOOR) - SIGN_FLOOR
                    total = g if t == 0 else total + g
                    soft_sum = soft if t == 0 else soft_sum + soft
                purity = 0.5 * (1.0 + total / (soft_sum + SIGN_FLOOR))
                start = pl.multiple_of(rows.start + c * RM, 32)
                there = pl.ds(start, 32)
                frac = 1.0 / (1.0 + jnp.exp((thr[there] - purity) * (1.0 / KEEP_TEMPER)))
                upper, lower = 0.5 * (total + soft_sum), 0.5 * (total - soft_sum)
                evec[there] = frac * upper + (1.0 - frac) * lower
                return carry

            loop(RM, 32, merge)

        for c in range(n_mp):
            merge_block(c)

        def b10():
            b_gh = recv.take(n_cls)
            for t in range(tasks):
                lanes = slice(t * classes, (t + 1) * classes)
                delta = dl[:, :, lanes].reshape(R, classes)
                out = dot(delta, act1[...], TN).astype(BF16)
                ghead[:, t] = out.reshape(n_cls, piece, Wd)
            to_all(lambda t: ghead.at[t], lambda: rhead.at[mine], b_gh)
            hold["b_gh"] = b_gh

        hold = {}
        late1 = backward(1, (b10, nothing, nothing, nothing))
        late1[0]()

        def b00():
            late1[1]()

        def b01():
            grad_to_dp(0, 1)

        late0 = backward(0, (b00, b01, nothing, nothing))
        late0[1]()
        late0[0]()
        vec_sem = recv.take()
        rcopy(lambda: vec.at[o], lambda: vsib, vec_sem, sib_dev)

        from_all(lambda src: rhead.at[src], hold["b_gh"])
        for t in range(tasks):
            total = ghead[mine, t].astype(F32)
            for k in range(1, n_cls):
                total = total + rhead[rem(mine + k, n_cls), t].astype(F32)
            ohead[t] = total
        arrive(vsib, vec_sem)
        ovec[...] = vec[s] + vsib[...]
        grad_to_dp(0, 0)

        def total_of(own, got, rows):
            out = own[s, d, rows].astype(F32)
            for k in range(1, n_dp):
                out = out + got[rem(d + k, n_dp), rows].astype(F32)
            return out

        for which in (2, 1, 0):
            own, _, got = grads[which]
            gathered("dp", lambda src: got.at[src], g_dp[which])

            def finish(rows, carry):
                out = total_of(own, got, rows)
                if which == 1:
                    for k in range(9):
                        ospa[0, k, rows] = out[:, k * C:(k + 1) * C]
                else:
                    (ored if which == 0 else oexp)[0, rows] = out
                return carry

            loop(own.shape[2], 64, finish)

        for j in range(2):
            @pl.when(s == j)
            def _():
                for i, hbm in enumerate((act_hbm, ig_hbm)):
                    arrive(hbm.at[0, o], out_sems[i][j])

        for key, waits in pending.items():
            def finish_all(waits=waits):
                for wait in waits:
                    wait()

            if key is None:
                finish_all()
            else:
                pl.when(s == key)(finish_all)

    return kernel


def fused_device(sizes, *args):
    n_dp, n_mp, R, Wd, M, C, Cd, classes, tasks, piece = sizes
    W9, n_cls = 9 * C, 2 * n_dp
    RM = R // n_mp
    vmem = lambda shape, dtype: pltpu.VMEM(shape, dtype)
    scratch = [
        pltpu.SemaphoreType.DMA((300,)),
        pltpu.SemaphoreType.DMA((300,)),
        pltpu.SemaphoreType.DMA((16,)),
        vmem((Wd, Cd), F32),
        vmem((9, Cd, C), F32),
        vmem((Cd, Wd), F32),
        vmem((tasks, Wd, piece), F32),
        vmem((R, Wd), F32),
        vmem((2, R, Wd), BF16),
        vmem((2, n_dp, Wd, Cd), BF16),
        vmem((2, n_dp, Cd, W9), BF16),
        vmem((2, n_dp, Cd, Wd), BF16),
        vmem((n_cls, tasks, piece, Wd), BF16),
        vmem((2, 8, Wd), F32),
        vmem((R, 128), F32),
        vmem((2, R, 128), F32),
        vmem((len(MASKS), R, 128), F32),
        vmem((R, 8), F32),
        vmem((6, n_mp, R, C), BF16),
        vmem((6, n_mp, R, C), BF16),
        vmem((2, n_mp, R, C), BF16),
        vmem((2, n_mp, R, C), BF16),
        vmem((2, n_mp, R, C), BF16),
        vmem((12, n_dp, 8, Wd), F32),
        vmem((2, 3, 8, Wd), F32),
        vmem((2, R, C), F32),
        vmem((2, R, C), F32),
        vmem((2, R, Wd), F32),
        vmem((R + 2 * PAD, W9), F32),
        vmem((R + 2 * PAD, C), F32),
        vmem((R, W9), BF16),
        vmem((n_mp, RM, tasks * classes), BF16),
        vmem((n_mp, RM, tasks * classes), BF16),
        vmem((n_mp, RM, tasks * classes), BF16),
        vmem((R, Wd), BF16),
        vmem((tasks, RM, Wd), F32),
        vmem((R, Wd), F32),
        vmem((R, Wd), F32),
        vmem((R, Wd), BF16),
        vmem((R, C), F32),
        vmem((2, R, Wd), F32),
        vmem((2, n_dp, Wd, Cd), BF16),
        vmem((2, n_dp, Cd, W9), BF16),
        vmem((2, n_dp, Cd, Wd), BF16),
        vmem((n_dp, Wd, Cd), BF16),
        vmem((n_dp, Cd, W9), BF16),
        vmem((n_dp, Cd, Wd), BF16),
        vmem((n_dp, Wd, Cd), BF16),
        vmem((n_dp, Cd, W9), BF16),
        vmem((n_dp, Cd, Wd), BF16),
        vmem((n_cls, tasks, piece, Wd), BF16),
        vmem((n_cls, tasks, piece, Wd), BF16),
        vmem((2, 8, Wd), F32),
        vmem((8, Wd), F32),
    ]
    in_vmem = pl.BlockSpec(memory_space=pltpu.VMEM)
    in_any = pl.BlockSpec(memory_space=pl.ANY)
    whole = lambda shape, dtype=F32: jax.ShapeDtypeStruct(shape, dtype)
    out = pl.pallas_call(
        make_kernel(sizes),
        out_shape=(
            whole((1, 2, R, Wd), BF16),
            whole((1, 2, R, Wd)),
            whole((1, Wd, Cd)),
            whole((1, 9, Cd, C)),
            whole((1, Cd, Wd)),
            whole((8, Wd)),
            whole((tasks, piece, Wd)),
        ),
        in_specs=[
            in_any, in_vmem, in_any, in_any, in_any, in_vmem, in_vmem, in_vmem, in_vmem,
            in_any, in_vmem, in_any,
        ],
        out_specs=(in_any, in_any, in_vmem, in_vmem, in_vmem, in_vmem, in_vmem),
        scratch_shapes=scratch,
        compiler_params=pltpu.CompilerParams(
            collective_id=0, has_side_effects=True, vmem_limit_bytes=60 * 2**20
        ),
    )(*args)
    act, grads_in, g_red, g_spa, g_exp, vec, head = out
    d = lax.axis_index("dp")
    part = C // n_dp
    outer = Wd // n_dp
    inner = lambda rows: lax.dynamic_slice_in_dim(vec[rows, :C], d * part, part, 1)[None, :, None]
    outer_of = lambda row: lax.dynamic_slice_in_dim(vec[row, :], d * outer, outer, 0)[None, None]
    return (
        act,
        grads_in,
        g_red,
        g_spa,
        g_exp,
        inner(slice(0, 2)),
        inner(slice(2, 4)),
        outer_of(4),
        outer_of(5),
        jnp.transpose(head, (0, 2, 1)),
    )


def per_device(*args):
    block_input, _, w_reduce, w_spatial = args[:4]
    n_dp, n_mp = lax.axis_size("dp"), lax.axis_size("mp")
    R, Wd = block_input.shape[1:]
    Cd, C = w_reduce.shape[2], w_spatial.shape[3]
    tasks, _, piece = args[9].shape
    sizes = (n_dp, n_mp, R, Wd, C * n_mp, C, Cd, piece * 2 * n_dp, tasks, piece)
    whole_tiles = not (C % 128 or Cd % 128 or Wd % 128 or R % 128 or piece % 16 or (R // n_mp) % 32)
    if whole_tiles and block_input.shape[0] == lax.axis_size("section") == 2:
        return fused_device(sizes, *args)
    return plain_device(*args)


def solution(mesh):
    return jax.shard_map(
        per_device,
        mesh=mesh,
        in_specs=(
            P(None, "dp", "mp"),
            P(None, "dp", None),
            P("section", "mp", "dp"),
            P("section", None, "dp", "mp"),
            P("section", "dp", "mp"),
            P("section", None, "mp"),
            P("section", None, "mp"),
            P("section", "mp"),
            P("section", "mp"),
            P(None, "mp", ("section", "dp")),
            P(None, None, "dp"),
            P(None, "dp", "mp"),
        ),
        out_specs=(
            P("section", None, "dp", "mp"),
            P("section", None, "dp", "mp"),
            P("section", "mp", "dp"),
            P("section", None, "dp", "mp"),
            P("section", "dp", "mp"),
            P("section", None, "mp", "dp"),
            P("section", None, "mp", "dp"),
            P("section", "mp", "dp"),
            P("section", "mp", "dp"),
            P(None, "mp", ("section", "dp")),
        ),
        check_vma=False,
    )
```

```python
import math

import jax
import jax.numpy as jnp
from jax import lax
from jax.experimental import pallas as pl
from jax.experimental.pallas import tpu as pltpu
from jax.sharding import PartitionSpec as P

NORM_EPS = 1e-05
LOSS_WEIGHT = 20.0
SIGN_FLOOR = 0.1
KEEP_TEMPER = 0.2


def shifted(value, axis, steps):
    count = lax.axis_size(axis)
    leading, last = (max(0, -steps), min(count, count - steps))
    return lax.ppermute(value, axis, [(source, source + steps) for source in range(leading, last)])


def geometry(img_sides, row_count):
    img_sizes = img_sides * img_sides
    img_ends = jnp.cumsum(img_sizes)
    img_starts = img_ends - img_sizes
    row_pos = jnp.arange(row_count, dtype=jnp.int32)[:, None]
    inside = (row_pos >= img_starts[None, :]) & (row_pos < img_ends[None, :])
    first_row = jnp.sum(jnp.where(inside, img_starts[None, :], 0), axis=1)
    side_len = jnp.sum(jnp.where(inside, img_sides[None, :], 0), axis=1)
    live_rows = jnp.any(inside, axis=1)
    offset = row_pos[:, 0] - first_row
    safe_side = jnp.maximum(side_len, 1)
    row_in = offset // safe_side
    col_in = offset % safe_side
    index_list = []
    valid_list = []
    for row_step in (-1, 0, 1):
        for col_step in (-1, 0, 1):
            new_row = row_in + row_step
            new_col = col_in + col_step
            valid = (
                live_rows
                & (new_row >= 0)
                & (new_row < side_len)
                & (new_col >= 0)
                & (new_col < side_len)
            )
            index_list.append(jnp.where(valid, first_row + new_row * side_len + new_col, 0))
            valid_list.append(valid)
    return (
        jnp.stack(index_list),
        jnp.stack(valid_list).astype(jnp.float32),
        live_rows.astype(jnp.float32),
    )


def smooth_act(values):
    return jax.nn.gelu(values, approximate=True)


def take_block(store, micro_idx):
    return lax.dynamic_index_in_dim(store, micro_idx, 0, keepdims=False)


def put_block(store, update, micro_idx, active):
    previous = take_block(store, micro_idx)
    return lax.dynamic_update_index_in_dim(store, jnp.where(active, update, previous), micro_idx, 0)


def channel_gather(values):
    return lax.all_gather(values, "mp", axis=1, tiled=True)


def channel_sum(values):
    return lax.psum_scatter(values, "mp", scatter_dimension=1, tiled=True)


def norm_stats(values, live_rows):
    masked = values * live_rows[:, None]
    total_sum, live_total = lax.psum((jnp.sum(masked, axis=0), jnp.sum(live_rows)), "dp")
    mean_val = total_sum / live_total
    centered = (values - mean_val) * live_rows[:, None]
    var_val = lax.psum(jnp.sum(centered * centered, axis=0), "dp") / live_total
    return (mean_val, lax.rsqrt(var_val + NORM_EPS), live_total)


def normalize(values, stats, live_rows, gain_vec, shift_vec):
    mean_val, inv_std, live_total = stats
    return live_rows[:, None] * (gain_vec * (values - mean_val) * inv_std + shift_vec)


def norm_backward(values, stats, live_rows, gain_vec, grad_norm):
    mean_val, inv_std, live_total = stats
    normed = (values - mean_val) * inv_std
    grad_live = grad_norm * live_rows[:, None]
    local_shift = jnp.sum(grad_live, axis=0)
    local_gain = jnp.sum(grad_live * normed, axis=0)
    sum_shift, sum_gain = lax.psum((local_shift, local_gain), "dp")
    grad_values = (
        live_rows[:, None]
        * inv_std
        * gain_vec
        * (grad_live - sum_shift / live_total - normed * sum_gain / live_total)
    )
    return (grad_values, local_gain, local_shift)


def gather_taps(values, indices, valids, tap_idx):
    return values[indices[tap_idx]] * valids[tap_idx][:, None].astype(values.dtype)


def act_backward(pre_values, grad_values):
    return jax.vjp(smooth_act, pre_values)[1](grad_values)[0]


def block_forward(x_in, layout, weights):
    indices, valids, live_rows = layout
    w_red, w_spa, w_exp, g_in, s_in, g_out, s_out = weights
    first_pre = channel_sum(jnp.dot(x_in, w_red, preferred_element_type=jnp.float32))
    stats_a = norm_stats(first_pre, live_rows)
    full_a = channel_gather(
        smooth_act(normalize(first_pre, stats_a, live_rows, g_in[0], s_in[0])).astype(jnp.bfloat16)
    )
    second_pre = jnp.zeros((x_in.shape[0], w_spa.shape[2]), jnp.float32)
    for tap_idx in range(9):
        second_pre = second_pre + jnp.dot(
            gather_taps(full_a, indices, valids, tap_idx),
            w_spa[tap_idx],
            preferred_element_type=jnp.float32,
        )
    stats_b = norm_stats(second_pre, live_rows)
    full_b = channel_gather(
        smooth_act(normalize(second_pre, stats_b, live_rows, g_in[1], s_in[1])).astype(jnp.bfloat16)
    )
    third_pre = jnp.dot(full_b, w_exp, preferred_element_type=jnp.float32)
    stats_c = norm_stats(third_pre, live_rows)
    pre_out = normalize(third_pre, stats_c, live_rows, g_out, s_out) + x_in.astype(jnp.float32)
    result = smooth_act(pre_out) * live_rows[:, None]
    return (result, (first_pre, stats_a, full_a, second_pre, stats_b, full_b, third_pre, stats_c))


def block_backward(d_out, x_in, layout, weights, saved_state):
    indices, valids, live_rows = layout
    w_red, w_spa, w_exp, g_in, s_in, g_out, s_out = weights
    first_pre, stats_a, full_a, second_pre, stats_b, full_b, third_pre, stats_c = saved_state
    pre_out = normalize(third_pre, stats_c, live_rows, g_out, s_out) + x_in.astype(jnp.float32)
    d_pre = act_backward(pre_out, d_out * live_rows[:, None])
    d_third, gain_c, shift_c = norm_backward(third_pre, stats_c, live_rows, g_out, d_pre)
    d_third = d_third.astype(jnp.bfloat16)
    grad_exp = jnp.einsum("rc,ro->co", full_b, d_third, preferred_element_type=jnp.float32)
    d_full_b = channel_sum(
        jnp.einsum("ro,co->rc", d_third, w_exp, preferred_element_type=jnp.float32)
    )
    pre_b = normalize(second_pre, stats_b, live_rows, g_in[1], s_in[1])
    d_second, gain_b, shift_b = norm_backward(
        second_pre, stats_b, live_rows, g_in[1], act_backward(pre_b, d_full_b)
    )
    d_second = d_second.astype(jnp.bfloat16)
    grad_spa = []
    back_total = jnp.zeros((x_in.shape[0], w_spa.shape[1]), jnp.float32)
    for tap_idx in range(9):
        grad_spa.append(
            jnp.einsum(
                "rc,ro->co",
                gather_taps(full_a, indices, valids, tap_idx),
                d_second,
                preferred_element_type=jnp.float32,
            )
        )
        spread = jnp.einsum(
            "ro,co->rc", d_second, w_spa[8 - tap_idx], preferred_element_type=jnp.float32
        )
        back_total = back_total + spread[indices[tap_idx]] * valids[tap_idx][:, None]
    d_full_a = channel_sum(back_total)
    pre_a = normalize(first_pre, stats_a, live_rows, g_in[0], s_in[0])
    d_first, gain_a, shift_a = norm_backward(
        first_pre, stats_a, live_rows, g_in[0], act_backward(pre_a, d_full_a)
    )
    d_first_full = channel_gather(d_first.astype(jnp.bfloat16))
    grad_red = jnp.einsum("rc,ro->co", x_in, d_first_full, preferred_element_type=jnp.float32)
    d_in = jnp.einsum("ro,co->rc", d_first_full, w_red, preferred_element_type=jnp.float32) + d_pre
    return (
        d_in,
        (
            grad_red,
            jnp.stack(grad_spa),
            grad_exp,
            jnp.stack([gain_a, gain_b]),
            jnp.stack([shift_a, shift_b]),
            gain_c,
            shift_c,
        ),
    )


def sign_merge(task_grads, thresh):
    soft_abs = jnp.sqrt(task_grads * task_grads + SIGN_FLOOR * SIGN_FLOOR) - SIGN_FLOOR
    purity = 0.5 * (1.0 + jnp.sum(task_grads, axis=0) / (jnp.sum(soft_abs, axis=0) + SIGN_FLOOR))
    keep_frac = jax.nn.sigmoid((purity - thresh) / KEEP_TEMPER)
    upper = 0.5 * jnp.sum(task_grads + soft_abs, axis=0)
    lower = 0.5 * jnp.sum(task_grads - soft_abs, axis=0)
    return keep_frac * upper + (1.0 - keep_frac) * lower


def plain_device(
    block_input,
    image_sides,
    w_reduce,
    w_spatial,
    w_expand,
    gain_inner,
    shift_inner,
    gain_outer,
    shift_outer,
    head_weight,
    labels,
    thresholds,
):
    section_idx = lax.axis_index("section")
    micro_count = block_input.shape[0]
    row_count = block_input.shape[1]
    w_red, w_spa, w_exp = (
        lax.all_gather(w_reduce[0].astype(jnp.bfloat16), "dp", axis=1, tiled=True),
        lax.all_gather(w_spatial[0].astype(jnp.bfloat16), "dp", axis=1, tiled=True),
        lax.all_gather(w_expand[0].astype(jnp.bfloat16), "dp", axis=0, tiled=True),
    )
    weights = (w_red, w_spa, w_exp, gain_inner[0], shift_inner[0], gain_outer[0], shift_outer[0])
    heads_all = lax.all_gather(
        head_weight.astype(jnp.bfloat16), ("section", "dp"), axis=2, tiled=True
    )
    class_total = heads_all.shape[2]
    class_ids = jnp.arange(class_total, dtype=jnp.int32)[None, None, :]

    def layout_for(micro_idx):
        return geometry(take_block(image_sides, micro_idx)[0], row_count)

    received = jnp.zeros(block_input.shape[1:], jnp.bfloat16)
    kept_inputs = jnp.zeros(block_input.shape, jnp.bfloat16)
    activ_store = jnp.zeros(block_input.shape, jnp.bfloat16)
    cotangents = jnp.zeros(block_input.shape, jnp.float32)
    head_grad = jnp.zeros(heads_all.shape, jnp.float32)
    for turn_idx in range(micro_count + 1):
        micro_idx = jnp.clip(turn_idx - section_idx, 0, micro_count - 1)
        active = (turn_idx - section_idx >= 0) & (turn_idx - section_idx < micro_count)
        x_in = jnp.where(section_idx == 0, block_input[min(turn_idx, micro_count - 1)], received)
        layout = layout_for(micro_idx)
        live_rows = layout[2]
        result, saved_state = block_forward(x_in, layout, weights)
        result_low = result.astype(jnp.bfloat16)
        kept_inputs = put_block(kept_inputs, x_in, micro_idx, active)
        activ_store = put_block(activ_store, result_low, micro_idx, active)
        labels_now = lax.dynamic_index_in_dim(labels, micro_idx, 1, keepdims=False)
        logits = lax.psum(
            jnp.einsum("rc,tco->tro", result_low, heads_all, preferred_element_type=jnp.float32),
            "mp",
        )
        peak_val = jnp.max(logits, axis=2, keepdims=True)
        expo = jnp.exp(logits - peak_val)
        soft_p = expo / jnp.sum(expo, axis=2, keepdims=True)
        picked = (class_ids == labels_now[:, :, None]).astype(jnp.float32)
        delta_low = (LOSS_WEIGHT * live_rows[None, :, None] * (soft_p - picked)).astype(
            jnp.bfloat16
        )
        task_grads = jnp.einsum(
            "tro,tco->trc", delta_low, heads_all, preferred_element_type=jnp.float32
        )
        merged = sign_merge(task_grads, take_block(thresholds, micro_idx))
        use_head = active & (section_idx == 1)
        head_grad = head_grad + jnp.where(
            use_head,
            jnp.einsum("rc,tro->tco", result_low, delta_low, preferred_element_type=jnp.float32),
            0.0,
        )
        cotangents = put_block(cotangents, merged, micro_idx, use_head)
        received = shifted(result_low, "section", 1)
    grad_recv = jnp.zeros(block_input.shape[1:], jnp.bfloat16)
    input_store = jnp.zeros(block_input.shape, jnp.float32)
    grad_total = None
    for turn_idx in range(micro_count + 1):
        micro_idx = jnp.clip(turn_idx - 1 + section_idx, 0, micro_count - 1)
        active = (turn_idx - 1 + section_idx >= 0) & (turn_idx - 1 + section_idx < micro_count)
        d_out = jnp.where(
            section_idx == 1, take_block(cotangents, micro_idx), grad_recv.astype(jnp.float32)
        )
        x_in = take_block(kept_inputs, micro_idx)
        layout = layout_for(micro_idx)
        saved_state = block_forward(x_in, layout, weights)[1]
        d_in, grad_set = block_backward(d_out, x_in, layout, weights, saved_state)
        masked = jax.tree.map(lambda leaf: jnp.where(active, leaf, 0.0), grad_set)
        grad_total = masked if grad_total is None else jax.tree.map(jnp.add, grad_total, masked)
        d_send = d_in.astype(jnp.bfloat16)
        input_store = put_block(
            input_store,
            jnp.where(section_idx == 1, d_send.astype(jnp.float32), d_in),
            micro_idx,
            active,
        )
        grad_recv = shifted(d_send, "section", -1)
    g_red, g_spa, g_exp, g_gain_in, g_shift_in, g_gain_out, g_shift_out = grad_total
    out_red, out_spa, out_exp, out_gain_in, out_shift_in, out_gain_out, out_shift_out = (
        lax.psum_scatter(g_red[None], "dp", scatter_dimension=2, tiled=True),
        lax.psum_scatter(g_spa[None], "dp", scatter_dimension=2, tiled=True),
        lax.psum_scatter(g_exp[None], "dp", scatter_dimension=1, tiled=True),
        lax.psum_scatter(g_gain_in[None, :, None, :], "dp", scatter_dimension=3, tiled=True),
        lax.psum_scatter(g_shift_in[None, :, None, :], "dp", scatter_dimension=3, tiled=True),
        lax.psum_scatter(g_gain_out[None, None, :], "dp", scatter_dimension=2, tiled=True),
        lax.psum_scatter(g_shift_out[None, None, :], "dp", scatter_dimension=2, tiled=True),
    )
    head_out = lax.psum_scatter(head_grad, ("section", "dp"), scatter_dimension=2, tiled=True)
    return (
        activ_store[None],
        input_store[None],
        out_red,
        out_spa,
        out_exp,
        out_gain_in,
        out_shift_in,
        out_gain_out,
        out_shift_out,
        head_out,
    )


K0 = math.sqrt(2.0 / math.pi)
K1 = 0.044715
MESH = pl.DeviceIdType.MESH
F32 = jnp.float32
BF16 = jnp.bfloat16
SIDES = (2, 7)
TAPS = [(a, b) for a in (-1, 0, 1) for b in (-1, 0, 1)]
PAD = 8
NN = (((1,), (0,)), ((), ()))
NT = (((1,), (1,)), ((), ()))
TN = (((0,), (0,)), ((), ()))


def tap_masks():
    found = []
    for tap_idx, (a, b) in enumerate(TAPS):
        for side in SIDES:
            found.append((tap_idx, a, b, side, a * side + b))
    return found


MASKS = tap_masks()


def dot(left, right, dims):
    return lax.dot_general(left, right, dims, preferred_element_type=F32)


def gelu(v):
    return 0.5 * v * (1.0 + jnp.tanh(K0 * v * (1.0 + K1 * v * v)))


def gelu_grad(v):
    sq = v * v
    t = jnp.tanh(K0 * v * (1.0 + K1 * sq))
    return 0.5 * (1.0 + t) + (0.5 * K0) * v * (1.0 - t * t) * (1.0 + 3.0 * K1 * sq)


def fold(x):
    return jnp.sum(x.reshape(x.shape[0] // 8, 8, x.shape[1]), axis=0)


def wide(x, width):
    times = width // x.shape[1]
    return x if times == 1 else jnp.concatenate([x] * times, axis=1)


def loop(total, chunk, body, init=None):
    def one(i, carry):
        return body(pl.ds(pl.multiple_of(i * chunk, chunk), chunk), carry)

    return lax.fori_loop(0, total // chunk, one, 0 if init is None else init)


def rows_tile(first, second, third):
    width = first.shape[1]
    place = lax.broadcasted_iota(jnp.int32, (8, width), 0)
    wide_of = lambda v: jnp.broadcast_to(v, (8, width))
    return jnp.where(
        place == 0, wide_of(first), jnp.where(place == 1, wide_of(second), wide_of(third))
    )


class Sems:
    def __init__(self, ref):
        self.ref, self.used, self.size = ref, 0, ref.shape[0]

    def take(self, count=1):
        first = self.used
        self.used += count
        assert self.used <= self.size, self.used
        return first


def make_kernel(sizes):
    n_dp, n_mp, R, Wd, M, C, Cd, classes, tasks, piece = sizes
    n_sec = 2
    W9 = 9 * C

    def kernel(*refs):
        (
            x_hbm, sides_ref, wred_hbm, wspa_hbm, wexp_hbm, gin_ref, sin_ref, gout_ref, sout_ref,
            head_hbm, lab_ref, thr_hbm,
            act_hbm, ig_hbm, red_hbm, spa_hbm, exp_hbm, vec_hbm, head_out,
            ssems, rsems, lsems,
            sred, sspa, sexp, shead, thr, xin, wr, wsp, we, hd, par,
            live, geo, masks, labc,
            rs_s, rs_r, ag_a, ag_b, ag_d, fulla, fullb, dfull, co, st, keep, first, second, third, ppad, dpad, dbuf,
            lg_s, lg_r, dl, act1, tg, dpre, evec, dth, hbuf, ig,
            gred, gspa, gexp, sibred, sibspa, sibexp, rred, rspa, rexp, ghead, rhead, vec, vsib,
            ored, ospa, oexp, ovec, ohead,
        ) = refs
        s = lax.axis_index("section")
        d = lax.axis_index("dp")
        m = lax.axis_index("mp")
        o = 1 - s
        send, recv, local = Sems(ssems), Sems(rsems), Sems(lsems)
        pending = {None: [], 0: [], 1: []}
        rem = lax.rem
        dp_dev = lambda t: (s, t, m)
        mp_dev = lambda t: (s, d, t)
        sib_dev = (o, d, m)

        def put_to(src, dst, ssem, rsem, dev):
            pltpu.make_async_remote_copy(
                src_ref=src,
                dst_ref=dst,
                send_sem=ssems.at[ssem],
                recv_sem=rsems.at[rsem],
                device_id=dev,
                device_id_type=MESH,
            ).start()

        def waiter(ref, ssem, rsem):
            return pltpu.make_async_remote_copy(
                src_ref=ref,
                dst_ref=ref,
                send_sem=ssems.at[ssem],
                recv_sem=rsems.at[rsem],
                device_id=sib_dev,
                device_id_type=MESH,
            )

        def rcopy(src, dst, rsem, dev, when=None):
            ssem = send.take()
            put_to(src(), dst(), ssem, rsem, dev)
            pending[when].append(lambda: waiter(src(), ssem, 0).wait_send())

        def arrive(dst, rsem):
            waiter(dst, 0, rsem).wait_recv()

        axes = {"dp": (n_dp, d, dp_dev), "mp": (n_mp, m, mp_dev)}
        expected = {}

        def settle(key):
            expected.pop(key)()

        def load(src, dst):
            cp = pltpu.make_async_copy(src, dst, lsems.at[local.take()])
            cp.start()
            key = ("load", local.used)
            expected[key] = cp.wait
            return key

        def on(cond, what):
            return lambda: pl.when(cond())(what)

        class Group:
            def __init__(self, axis, all_of, when=None):
                self.n, self.me, self.dev = axes[axis]
                self.ssem, self.rsem = send.take(), recv.take()
                self.all_of, self.when = all_of, when

            def put(self, src_of, slot_of):
                for k in range(1, self.n):
                    t = rem(self.me + k, self.n)
                    put_to(src_of(t), slot_of(self.me), self.ssem, self.rsem, self.dev(t))

            def close(self):
                ssem, rsem, all_of, when = self.ssem, self.rsem, self.all_of, self.when
                pending[when].append(lambda: waiter(all_of(), ssem, 0).wait_send())
                wait = lambda: arrive(all_of(), rsem)
                expected[rsem] = wait if when is None else on(lambda: s == when, wait)
                return rsem

        def spread(axis, src_of, slot_of, all_of, when=None):
            group = Group(axis, all_of, when)
            group.put(src_of, slot_of)
            return group.close()

        l_red = load(wred_hbm.at[0], sred)
        l_x = load(x_hbm.at[s], xin.at[0])
        l_spa = load(wspa_hbm.at[0], sspa)
        l_exp = load(wexp_hbm.at[0], sexp)
        l_head = load(head_hbm, shead)
        l_thr = load(thr_hbm.at[s], thr)

        barrier = pltpu.get_barrier_semaphore()
        greeted = 0
        for ds_ in range(n_sec):
            for k in range(n_dp):
                if ds_ == 0 and k == 0:
                    continue
                pl.semaphore_signal(
                    barrier, inc=1,
                    device_id=(rem(s + ds_, n_sec), rem(d + k, n_dp), m),
                    device_id_type=MESH,
                )
                greeted += 1
        for k in range(1, n_mp):
            pl.semaphore_signal(
                barrier, inc=1, device_id=(s, d, rem(m + k, n_mp)), device_id_type=MESH
            )
            greeted += 1

        settle(l_red)
        wr[s, d] = sred[...].astype(BF16)
        par[s] = jnp.zeros(par.shape[1:], F32)
        for i in range(2):
            par[s, i:i + 1, :C] = gin_ref[0, i:i + 1, :]
            par[s, 2 + i:3 + i, :C] = sin_ref[0, i:i + 1, :]
        par[s, 4:5, :] = gout_ref[...]
        par[s, 5:6, :] = sout_ref[...]
        pl.semaphore_wait(barrier, greeted)

        by_dp, by_sib = {}, {}

        def send_own(buf, j):
            def go():
                by_dp[id(buf), j] = spread(
                    "dp",
                    lambda t: buf.at[j, d],
                    lambda src: buf.at[j, src],
                    lambda: buf.at[j, pl.ds(0, n_dp - 1)],
                    when=j,
                )

            pl.when(s == j)(go)

        def pass_on(buf, j):
            settle(by_dp[id(buf), j])
            sem = by_sib[id(buf), j] = recv.take()

            @pl.when(s == j)
            def _():
                rcopy(lambda: buf.at[j], lambda: buf.at[j], sem, sib_dev, when=j)

            expected[sem] = on(lambda: s != j, lambda: arrive(buf.at[j], sem))

        def from_sib(buf, j):
            settle(by_sib[id(buf), j])

        par_sem = recv.take()
        rcopy(lambda: par.at[s], lambda: par.at[s], par_sem, sib_dev)
        expected[par_sem] = lambda: arrive(par.at[o], par_sem)
        send_own(wr, 0)

        settle(l_spa)
        for k in range(9):
            wsp[s, d, :, k * C:(k + 1) * C] = sspa[k].astype(BF16)

        settle(l_exp)
        we[s, d] = sexp[...].astype(BF16)

        sides = jnp.where(s == 0, sides_ref[0], sides_ref[1]).astype(F32)
        slots = sides.shape[1]
        sq = jnp.broadcast_to(sides * sides, (8, slots)).astype(BF16)
        upper = (
            lax.broadcasted_iota(jnp.int32, (slots, slots), 0)
            <= lax.broadcasted_iota(jnp.int32, (slots, slots), 1)
        ).astype(BF16)
        ends = dot(sq, upper, NN)[0:1]
        starts = ends - sides * sides
        nloc = jnp.broadcast_to(jnp.max(ends, axis=1, keepdims=True), (1, 128))
        shape = (R, 128)
        pos = lax.broadcasted_iota(jnp.int32, (R, slots), 0).astype(F32)
        inside = (pos >= starts) & (pos < ends)
        origin = jnp.sum(jnp.where(inside, starts, 0.0), axis=1, keepdims=True)
        side = jnp.sum(jnp.where(inside, sides, 0.0), axis=1, keepdims=True)
        geo[0] = jnp.broadcast_to(origin, shape)
        geo[1] = jnp.broadcast_to(side, shape)

        def make_masks(rows, carry):
            side_b = geo[1, rows]
            here = lax.broadcasted_iota(jnp.int32, side_b.shape, 0) + rows.start
            offset = here.astype(F32) - geo[0, rows]
            row_in = jnp.floor((offset + 0.5) / jnp.maximum(side_b, 1.0))
            col_in = offset - row_in * side_b
            live[rows] = (side_b > 0.0).astype(F32)
            for idx, (_, a, b, q, _) in enumerate(MASKS):
                ra, cb = row_in + a, col_in + b
                ok = (side_b == q) & (ra >= 0.0) & (ra < q) & (cb >= 0.0) & (cb < q)
                masks[idx, rows] = ok.astype(F32)
            return carry

        loop(R, 64, make_masks)
        for buf in (ppad, dpad):
            edge = jnp.zeros((PAD, buf.shape[1]), F32)
            buf[0:PAD] = edge
            buf[PAD + R:PAD + R + PAD] = edge
        lab2 = lab_ref[...]
        lab = jnp.where(s == 0, lab2[:, 0], lab2[:, 1]).astype(F32)
        lab = jnp.concatenate([lab, jnp.zeros((8 - tasks, R), F32)], axis=0)
        labc[...] = jnp.transpose(lab)

        settle(l_head)
        mine = s * n_dp + d
        for t in range(tasks):
            hd[mine, t] = shead[t].astype(BF16)

        def to_all(src_of, buf):
            ssem, rsem = send.take(), recv.take()
            others = [(a, k) for a in range(n_sec) for k in range(n_dp) if a or k]
            for a, k in others:
                ts, td = rem(s + a, n_sec), rem(d + k, n_dp)
                put_to(src_of(ts * n_dp + td), buf.at[mine], ssem, rsem, (ts, td, m))
            rest = lambda: buf.at[pl.ds(0, len(others))]
            pending[None].append(lambda: waiter(rest(), ssem, 0).wait_send())
            expected[rsem] = lambda: arrive(rest(), rsem)
            return rsem

        def cat(buf, n):
            return jnp.concatenate([buf[i] for i in range(n)], axis=1)

        phase = {"rs": 0, "st": 0}

        def rs_open():
            p = phase["rs"]
            phase["rs"] += 1
            return p, Group("mp", lambda: rs_r.at[p, pl.ds(0, n_mp - 1)])

        def rs_rows(handle, rows, out):
            p, group = handle
            for c in range(n_mp):
                rs_s[p, c, rows] = out[:, c * C:(c + 1) * C].astype(BF16)
            group.put(lambda t: rs_s.at[p, t, rows], lambda src: rs_r.at[p, src, rows])

        def rs_finish(handle, dst):
            p, group = handle
            settle(group.rsem)

            def add(rows, carry):
                total = rs_s[p, m, rows].astype(F32)
                for k in range(1, n_mp):
                    total = total + rs_r[p, rem(m + k, n_mp), rows].astype(F32)
                dst[rows] = total
                return carry

            loop(R, 128, add)

        def product_to_rs(left, right_of, dims):
            handle = rs_open()

            def part(rows, carry):
                rs_rows(handle, rows, dot(left[rows], right_of(), dims))
                return carry

            loop(R, 128, part)
            handle[1].close()
            return handle

        def exchange(tile):
            p = phase["st"]
            phase["st"] += 1
            width = tile.shape[1]
            st[p, d, :, 0:width] = tile
            slot = lambda src: st.at[p, src, :, 0:width]
            rest = lambda: st.at[p, pl.ds(0, n_dp - 1), :, 0:width]
            return p, width, spread("dp", lambda t: slot(d), slot, rest)

        def collect(handle):
            p, width, base = handle
            settle(base)
            return [st[p, i, :, 0:width] for i in range(n_dp)]

        def stats_start(buf, width):
            chunk = 128 if width <= 128 else 32
            zero = jnp.zeros((8, width), F32)

            def sum_up(rows, carry):
                return carry + fold(buf[rows] * wide(live[rows], width))

            total = jnp.sum(loop(R, chunk, sum_up, zero), axis=0, keepdims=True)
            count = wide(nloc, width)
            mean = total / jnp.maximum(count, 1.0)

            def squares(rows, carry):
                off = (buf[rows] - mean) * wide(live[rows], width)
                return carry + fold(off * off)

            sqs = jnp.sum(loop(R, chunk, squares, zero), axis=0, keepdims=True)
            return exchange(rows_tile(total, sqs, count)), mean

        def stats_finish(handle, j, i):
            tiles = collect(handle)
            width = handle[1]
            count = sum(t[2:3] for t in tiles)
            mean = sum(t[0:1] for t in tiles) / count
            sqs = 0.0
            for t in tiles:
                local_mean = t[0:1] / jnp.maximum(t[2:3], 1.0)
                sqs = sqs + t[1:2] + t[2:3] * (local_mean - mean) * (local_mean - mean)
            inv = lax.rsqrt(sqs / count + NORM_EPS)
            keep[j, i, :, 0:width] = rows_tile(mean, inv, count)

        def slots_out(buf, at, values_of):
            group = Group("mp", lambda: buf.at[at, pl.ds(0, n_mp - 1)])

            def fill(rows, carry):
                buf[at, m, rows] = values_of(rows).astype(BF16)
                group.put(lambda t: buf.at[at, m, rows], lambda src: buf.at[at, src, rows])
                return carry

            loop(R, 128, fill)
            return group.close()

        def coeffs_out(at, *values):
            place = lax.broadcasted_iota(jnp.int32, (8, C), 0)
            tile = jnp.zeros((8, C), F32)
            for i, v in enumerate(values):
                tile = jnp.where(place == i, jnp.broadcast_to(v, (8, C)), tile)
            co[at, m] = tile
            slot = lambda src: co.at[at, src]
            return spread("mp", lambda t: slot(m), slot, lambda: co.at[at, pl.ds(0, n_mp - 1)])

        def inner_norm(j, i, src, raw, full, hook):
            at = 2 * j + i
            handle, mean_here = stats_start(src.at[j], C)
            group = slots_out(raw, j, lambda rows: src[j, rows] - mean_here)
            hook()
            stats_finish(handle, j, i)
            mu, inv, _, gain, shift = norm_of(j, i, C)
            moved = (mean_here - mu) * inv
            sent = coeffs_out(at, gain * inv, gain * moved + shift, inv, moved)
            settle(group)
            settle(sent)

            def act(rows, carry):
                for c in range(n_mp):
                    tile = co[at, c]
                    y = live[rows] * (raw[j, c, rows].astype(F32) * tile[0:1] + tile[1:2])
                    full[j, rows, c * C:(c + 1) * C] = gelu(y).astype(BF16)
                return carry

            loop(R, 64, act)

        def norm_of(j, i, width):
            tile = keep[j, i, :, 0:width]
            if i < 2:
                gain, shift = par[j, i:i + 1, 0:width], par[j, 2 + i:3 + i, 0:width]
            else:
                gain, shift = par[j, 4:5, 0:width], par[j, 5:6, 0:width]
            return tile[0:1], tile[1:2], tile[2:3], gain, shift

        def taps_sum(src, flip, put):
            for r0 in range(0, R, 128):
                put(r0, lambda idx_list, lanes: sum(
                    masks[(len(MASKS) - 2 - (idx // 2) * 2 + idx % 2) if flip else idx, r0:r0 + 128]
                    * src[
                        PAD + r0 + (-1 if flip else 1) * MASKS[idx][4]:
                        PAD + r0 + (-1 if flip else 1) * MASKS[idx][4] + 128,
                        lanes,
                    ]
                    for idx in idx_list
                ))

        nothing = lambda: None
        vec[...] = jnp.zeros(vec.shape, F32)

        def forward(j, hooks):
            x = xin.at[j]
            h = product_to_rs(x, lambda: cat(wr.at[j], n_dp), NN)
            hooks[0]()
            rs_finish(h, first.at[j])
            inner_norm(j, 0, first, ag_a, fulla, hooks[1])

            def conv(rows, carry):
                start = pl.multiple_of(rows.start + PAD, 8)
                ppad[pl.ds(start, 128)] = dot(fulla[j, rows], wsp[j].reshape(M, W9), NN)
                return carry

            loop(R, 128, conv)

            def put(r0, summed):
                second[j, r0:r0 + 128] = sum(
                    summed([2 * k, 2 * k + 1], slice(k * C, (k + 1) * C)) for k in range(9)
                )

            taps_sum(ppad, False, put)
            inner_norm(j, 1, second, ag_b, fullb, hooks[2])

            def expand(rows, carry):
                third[j, rows] = dot(fullb[j, rows], we[j].reshape(M, Wd), NN)
                return carry

            loop(R, 128, expand)
            h, _ = stats_start(third.at[j], Wd)
            hooks[3]()
            stats_finish(h, j, 2)
            mu, inv, _, gain, shift = norm_of(j, 2, Wd)
            out = xin.at[1] if j == 0 else act1

            def act_c(rows, carry):
                lv = wide(live[rows], Wd)
                pre = lv * (gain * ((third[j, rows] - mu) * inv) + shift)
                pre = pre + xin[j, rows].astype(F32)
                out[rows] = (lv * gelu(pre)).astype(BF16)
                return carry

            loop(R, 32, act_c)

        def to_section(src, hbm, j):
            sem = recv.take()

            @pl.when(s == j)
            def _():
                lsem = local.take()
                made = lambda: pltpu.make_async_copy(src(), hbm.at[0, s], lsems.at[lsem])
                made().start()
                pending[j].append(lambda: made().wait())

            @pl.when(s != j)
            def _():
                rcopy(src, lambda: hbm.at[0, s], sem, sib_dev, when=1 - j)

            expected[sem] = on(lambda: s == j, lambda: arrive(hbm.at[0, o], sem))

        grads = ((gred, sibred, rred), (gspa, sibspa, rspa), (gexp, sibexp, rexp))
        at_sib, at_dp = {}, {}

        def grad_to_sib(which, j):
            own, sib, _ = grads[which]
            sem = at_sib[which, j] = recv.take()

            @pl.when(s != j)
            def _():
                rcopy(lambda: own.at[j], lambda: sib, sem, sib_dev, when=1 - j)

            expected[sem] = on(lambda: s == j, lambda: arrive(sib, sem))

        def grad_to_dp(which, j):
            own, sib, got = grads[which]
            settle(at_sib[which, j])

            def go():
                def add(rows, carry):
                    for i in range(n_dp):
                        own[j, i, rows] = (
                            own[j, i, rows].astype(F32) + sib[i, rows].astype(F32)
                        ).astype(BF16)
                    return carry

                loop(own.shape[2], 64, add)
                base = spread(
                    "dp",
                    lambda t: own.at[j, t],
                    lambda src: got.at[src],
                    lambda: got.at[pl.ds(0, n_dp - 1)],
                    when=j,
                )
                at_dp.setdefault(which, []).append(base)

            pl.when(s == j)(go)

        def backward(j, hooks):
            mu, inv, count, gain, shift = norm_of(j, 2, Wd)
            zero = (jnp.zeros((8, Wd), F32), jnp.zeros((8, Wd), F32))

            def top(rows, carry):
                sb, sg = carry
                lv = wide(live[rows], Wd)
                xhat = (third[j, rows] - mu) * inv
                pre = lv * (gain * xhat + shift) + xin[j, rows].astype(F32)
                dp_ = gelu_grad(pre) * lv * evec[rows]
                dpre[rows] = dp_
                return sb + fold(dp_), sg + fold(dp_ * xhat)

            sb, sg = loop(R, 32, top, zero)
            total = lambda v: jnp.sum(v, axis=0, keepdims=True)
            sb, sg = total(sb), total(sg)
            h = exchange(rows_tile(sb, sg, sg))
            hooks[0]()
            tile = sum(collect(h))
            vec[j, 4:5, :] = tile[1:2]
            vec[j, 5:6, :] = tile[0:1]
            sb_n, sg_n = tile[0:1] / count, tile[1:2] / count
            scale = gain * inv

            def d_third(rows, carry):
                lv = wide(live[rows], Wd)
                xhat = (third[j, rows] - mu) * inv
                dth[rows] = (lv * scale * (dpre[rows] - sb_n - xhat * sg_n)).astype(BF16)
                return carry

            loop(R, 32, d_third)
            h = product_to_rs(dth, lambda: we[j].reshape(M, Wd), NT)
            for i in range(n_dp):
                full = fullb[j, :, i * Cd:(i + 1) * Cd]
                gexp[j, i] = dot(full, dth[...], TN).astype(BF16)
            grad_to_sib(2, j)
            hooks[1]()
            rs_finish(h, hbuf)

            def inner_sums(i, src):
                mu, inv, count, gain, shift = norm_of(j, i, C)
                zero = (jnp.zeros((8, C), F32), jnp.zeros((8, C), F32))

                def up(rows, carry):
                    sb, sg = carry
                    xhat = (src[j, rows] - mu) * inv
                    pre = live[rows] * (gain * xhat + shift)
                    g = live[rows] * gelu_grad(pre) * hbuf[rows]
                    hbuf[rows] = g
                    return sb + fold(g), sg + fold(g * xhat)

                sb, sg = loop(R, 128, up, zero)
                sb, sg = total(sb), total(sg)
                return exchange(rows_tile(sb, sg, sg)), sb

            def inner_coeffs(i, handle):
                _, inv, count, gain, _ = norm_of(j, i, C)
                tile = sum(collect(handle))
                vec[j, i:i + 1, 0:C] = tile[1:2]
                vec[j, 2 + i:3 + i, 0:C] = tile[0:1]
                return gain * inv, tile[0:1] / count, tile[1:2] / count

            scale_b, sb_b, sg_b = inner_coeffs(1, inner_sums(1, second)[0])
            mu_b, inv_b = norm_of(j, 1, C)[:2]

            def d_second(rows, carry):
                start = pl.multiple_of(rows.start + PAD, 8)
                xhat = (second[j, rows] - mu_b) * inv_b
                out = live[rows] * scale_b * (hbuf[rows] - sb_b - xhat * sg_b)
                dpad[pl.ds(start, 128)] = out.astype(BF16).astype(F32)
                return carry

            loop(R, 128, d_second)

            h = rs_open()

            def put(r0, summed):
                for k in range(9):
                    dbuf[r0:r0 + 128, k * C:(k + 1) * C] = summed(
                        [2 * k, 2 * k + 1], slice(None)
                    ).astype(BF16)
                rows = slice(r0, r0 + 128)
                rs_rows(h, rows, dot(dbuf[rows], wsp[j].reshape(M, W9), NT))

            taps_sum(dpad, True, put)
            h[1].close()
            for i in range(n_dp):
                full = fulla[j, :, i * Cd:(i + 1) * Cd]
                gspa[j, i] = dot(full, dbuf[...], TN).astype(BF16)
            grad_to_sib(1, j)
            grad_to_dp(2, j)
            hooks[2]()
            rs_finish(h, hbuf)
            handle, sb_here = inner_sums(0, first)
            here = sb_here / jnp.maximum(nloc, 1.0)
            group = slots_out(ag_d, j, lambda rows: hbuf[rows] - here)
            scale, sb_a, sg_a = inner_coeffs(0, handle)
            own = co[2 * j, m]
            sent = coeffs_out(
                4 + j,
                scale,
                -scale * sg_a * own[2:3],
                scale * (here - sb_a - sg_a * own[3:4]),
            )
            grad_to_dp(1, j)
            hooks[3]()
            settle(group)
            settle(sent)

            def d_first(rows, carry):
                for c in range(n_mp):
                    tile = co[4 + j, c]
                    out = live[rows] * (
                        ag_d[j, c, rows].astype(F32) * tile[0:1]
                        + ag_a[j, c, rows].astype(F32) * tile[1:2]
                        + tile[2:3]
                    )
                    dfull[j, rows, c * C:(c + 1) * C] = out.astype(BF16)
                return carry

            loop(R, 64, d_first)

            def d_input():
                def body(rows, carry):
                    out = dot(dfull[j, rows], cat(wr.at[j], n_dp), NT) + dpre[rows]
                    if j == 1:
                        out = out.astype(BF16).astype(F32)
                        evec[rows] = out
                    ig[j, rows] = out
                    return carry

                loop(R, 128, body)
                to_section(lambda: ig.at[j], ig_hbm, j)

            def g_reduce():
                for i in range(n_dp):
                    full = dfull[j, :, i * Cd:(i + 1) * Cd]
                    gred[j, i] = dot(xin[j], full, TN).astype(BF16)
                grad_to_sib(0, j)

            return d_input, g_reduce

        pass_on(wr, 0)
        settle(l_x)
        from_sib(wr, 0)
        settle(par_sem)

        def f00():
            send_own(wsp, 0)

        def f01():
            pass_on(wsp, 0)
            send_own(we, 0)
            send_own(wr, 1)
            from_sib(wsp, 0)

        def f02():
            pass_on(we, 0)
            pass_on(wr, 1)
            send_own(wsp, 1)
            from_sib(we, 0)

        def f03():
            from_sib(wr, 1)

        hold = {}
        forward(0, (f00, f01, f02, f03))

        def f10():
            pass_on(wsp, 1)
            send_own(we, 1)
            hold["heads"] = to_all(lambda t: hd.at[mine], hd)
            to_section(lambda: xin.at[1], act_hbm, 0)

        def f11():
            pass_on(we, 1)
            from_sib(wsp, 1)

        def f12():
            from_sib(we, 1)

        forward(1, (f10, f11, f12, nothing))

        settle(hold["heads"])
        RM = R // n_mp
        n_cls = n_sec * n_dp

        def heads_of(t):
            return hd[:, t].reshape(classes, Wd)

        for c in range(n_mp):
            rows = act1[c * RM:(c + 1) * RM]
            for t in range(tasks):
                lg_s[c, :, t * classes:(t + 1) * classes] = dot(rows, heads_of(t), NT).astype(
                    lg_s.dtype
                )
        base = spread(
            "mp", lambda t: lg_s.at[t], lambda src: lg_r.at[src], lambda: lg_r.at[pl.ds(0, n_mp - 1)]
        )
        to_section(lambda: act1, act_hbm, 1)
        settle(l_thr)
        settle(base)
        here = pl.ds(pl.multiple_of(m * RM, RM), RM)
        lv = wide(live[here], classes)
        for t in range(tasks):
            lanes = slice(t * classes, (t + 1) * classes)
            logit = lg_s[m, :, lanes].astype(F32)
            for k in range(1, n_mp):
                logit = logit + lg_r[rem(m + k, n_mp), :, lanes].astype(F32)
            expo = jnp.exp(logit - jnp.max(logit, axis=1, keepdims=True))
            soft = expo / jnp.sum(expo, axis=1, keepdims=True)
            ids = lax.broadcasted_iota(jnp.int32, (RM, classes), 1).astype(F32)
            hot = (ids == labc[here, t:t + 1]).astype(F32)
            dl[m, :, lanes] = (LOSS_WEIGHT * lv * (soft - hot)).astype(BF16)
        settle(spread(
            "mp", lambda t: dl.at[m], lambda src: dl.at[src], lambda: dl.at[pl.ds(0, n_mp - 1)]
        ))

        def merge_block(c):
            for t in range(tasks):
                lanes = slice(t * classes, (t + 1) * classes)
                tg[t] = dot(dl[c, :, lanes], heads_of(t), NN)

            def merge(rows, carry):
                total = soft_sum = None
                for t in range(tasks):
                    g = tg[t, rows]
                    soft = jnp.sqrt(g * g + SIGN_FLOOR * SIGN_FLOOR) - SIGN_FLOOR
                    total = g if t == 0 else total + g
                    soft_sum = soft if t == 0 else soft_sum + soft
                purity = 0.5 * (1.0 + total / (soft_sum + SIGN_FLOOR))
                start = pl.multiple_of(rows.start + c * RM, 32)
                there = pl.ds(start, 32)
                frac = 1.0 / (1.0 + jnp.exp((thr[there] - purity) * (1.0 / KEEP_TEMPER)))
                upper, lower = 0.5 * (total + soft_sum), 0.5 * (total - soft_sum)
                evec[there] = frac * upper + (1.0 - frac) * lower
                return carry

            loop(RM, 32, merge)

        for c in range(n_mp):
            merge_block(c)

        def b10():
            for t in range(tasks):
                lanes = slice(t * classes, (t + 1) * classes)
                delta = dl[:, :, lanes].reshape(R, classes)
                out = dot(delta, act1[...], TN).astype(BF16)
                ghead[:, t] = out.reshape(n_cls, piece, Wd)
            hold["ghead"] = to_all(lambda t: ghead.at[t], rhead)

        late1 = backward(1, (b10, nothing, nothing, nothing))
        late1[0]()

        def b00():
            late1[1]()

        def b01():
            grad_to_dp(0, 1)

        late0 = backward(0, (b00, b01, nothing, nothing))
        late0[1]()
        late0[0]()
        vec_sem = recv.take()
        rcopy(lambda: vec.at[o], lambda: vsib, vec_sem, sib_dev)
        expected[vec_sem] = lambda: arrive(vsib, vec_sem)

        settle(hold["ghead"])
        for t in range(tasks):
            total = ghead[mine, t].astype(F32)
            for k in range(1, n_cls):
                total = total + rhead[rem(mine + k, n_cls), t].astype(F32)
            ohead[t] = total
        load(ohead, head_out)
        settle(vec_sem)
        ovec[...] = vec[s] + vsib[...]
        load(ovec, vec_hbm)
        grad_to_dp(0, 0)

        def total_of(own, got, rows):
            out = own[s, d, rows].astype(F32)
            for k in range(1, n_dp):
                out = out + got[rem(d + k, n_dp), rows].astype(F32)
            return out

        def finish_grad(which):
            own, _, got = grads[which]
            for key in at_dp[which]:
                settle(key)

            def finish(rows, carry):
                out = total_of(own, got, rows)
                if which == 1:
                    for k in range(9):
                        ospa[0, k, rows] = out[:, k * C:(k + 1) * C]
                else:
                    (ored if which == 0 else oexp)[0, rows] = out
                return carry

            loop(own.shape[2], 64, finish)
            load((ored, ospa, oexp)[which], (red_hbm, spa_hbm, exp_hbm)[which])

        finish_grad(2)
        finish_grad(1)
        finish_grad(0)
        for key in list(expected):
            settle(key)

        for key, waits in pending.items():
            def finish_all(waits=waits):
                for wait in waits:
                    wait()

            if key is None:
                finish_all()
            else:
                pl.when(s == key)(finish_all)

    return kernel


def fused_device(sizes, *args):
    n_dp, n_mp, R, Wd, M, C, Cd, classes, tasks, piece = sizes
    W9, n_cls = 9 * C, 2 * n_dp
    RM = R // n_mp
    vmem = lambda shape, dtype: pltpu.VMEM(shape, dtype)
    scratch = [
        pltpu.SemaphoreType.DMA((64,)),
        pltpu.SemaphoreType.DMA((64,)),
        pltpu.SemaphoreType.DMA((15,)),
        vmem((Wd, Cd), F32),
        vmem((9, Cd, C), F32),
        vmem((Cd, Wd), F32),
        vmem((tasks, piece, Wd), F32),
        vmem((R, Wd), F32),
        vmem((2, R, Wd), BF16),
        vmem((2, n_dp, Wd, Cd), BF16),
        vmem((2, n_dp, Cd, W9), BF16),
        vmem((2, n_dp, Cd, Wd), BF16),
        vmem((n_cls, tasks, piece, Wd), BF16),
        vmem((2, 8, Wd), F32),
        vmem((R, 128), F32),
        vmem((2, R, 128), F32),
        vmem((len(MASKS), R, 128), F32),
        vmem((R, 8), F32),
        vmem((6, n_mp, R, C), BF16),
        vmem((6, n_mp, R, C), BF16),
        vmem((2, n_mp, R, C), BF16),
        vmem((2, n_mp, R, C), BF16),
        vmem((2, n_mp, R, C), BF16),
        vmem((2, R, M), BF16),
        vmem((2, R, M), BF16),
        vmem((2, R, M), BF16),
        vmem((6, n_mp, 8, C), F32),
        vmem((12, n_dp, 8, Wd), F32),
        vmem((2, 3, 8, Wd), F32),
        vmem((2, R, C), F32),
        vmem((2, R, C), F32),
        vmem((2, R, Wd), F32),
        vmem((R + 2 * PAD, W9), F32),
        vmem((R + 2 * PAD, C), F32),
        vmem((R, W9), BF16),
        vmem((n_mp, RM, tasks * classes), BF16),
        vmem((n_mp, RM, tasks * classes), BF16),
        vmem((n_mp, RM, tasks * classes), BF16),
        vmem((R, Wd), BF16),
        vmem((tasks, RM, Wd), F32),
        vmem((R, Wd), F32),
        vmem((R, Wd), F32),
        vmem((R, Wd), BF16),
        vmem((R, C), F32),
        vmem((2, R, Wd), F32),
        vmem((2, n_dp, Wd, Cd), BF16),
        vmem((2, n_dp, Cd, W9), BF16),
        vmem((2, n_dp, Cd, Wd), BF16),
        vmem((n_dp, Wd, Cd), BF16),
        vmem((n_dp, Cd, W9), BF16),
        vmem((n_dp, Cd, Wd), BF16),
        vmem((n_dp, Wd, Cd), BF16),
        vmem((n_dp, Cd, W9), BF16),
        vmem((n_dp, Cd, Wd), BF16),
        vmem((n_cls, tasks, piece, Wd), BF16),
        vmem((n_cls, tasks, piece, Wd), BF16),
        vmem((2, 8, Wd), F32),
        vmem((8, Wd), F32),
        vmem((1, Wd, Cd), F32),
        vmem((1, 9, Cd, C), F32),
        vmem((1, Cd, Wd), F32),
        vmem((8, Wd), F32),
        vmem((tasks, piece, Wd), F32),
    ]
    in_vmem = pl.BlockSpec(memory_space=pltpu.VMEM)
    in_any = pl.BlockSpec(memory_space=pl.ANY)
    whole = lambda shape, dtype=F32: jax.ShapeDtypeStruct(shape, dtype)
    out = pl.pallas_call(
        make_kernel(sizes),
        out_shape=(
            whole((1, 2, R, Wd), BF16),
            whole((1, 2, R, Wd)),
            whole((1, Wd, Cd)),
            whole((1, 9, Cd, C)),
            whole((1, Cd, Wd)),
            whole((8, Wd)),
            whole((tasks, piece, Wd)),
        ),
        in_specs=[
            in_any, in_vmem, in_any, in_any, in_any, in_vmem, in_vmem, in_vmem, in_vmem,
            in_any, in_vmem, in_any,
        ],
        out_specs=(in_any,) * 7,
        scratch_shapes=scratch,
        compiler_params=pltpu.CompilerParams(
            collective_id=0, has_side_effects=True, vmem_limit_bytes=60 * 2**20
        ),
    )(*args[:9], jnp.transpose(args[9], (0, 2, 1)), *args[10:])
    part, outer = C // n_dp, Wd // n_dp
    shapes = (
        whole((1, 2, R, Wd), BF16),
        whole((1, 2, R, Wd)),
        whole((1, Wd, Cd)),
        whole((1, 9, Cd, C)),
        whole((1, Cd, Wd)),
        whole((1, 2, 1, part)),
        whole((1, 2, 1, part)),
        whole((1, 1, outer)),
        whole((1, 1, outer)),
        whole((tasks, piece, Wd)),
    )
    done = pl.pallas_call(
        hand_out,
        out_shape=shapes,
        in_specs=[in_any] * 5 + [in_vmem, in_any],
        out_specs=(in_any,) * 5 + (in_vmem,) * 4 + (in_any,),
        scratch_shapes=[pltpu.VMEM(a.shape, a.dtype) for a in shapes[:5] + shapes[9:]]
        + [pltpu.SemaphoreType.DMA((16,)), pltpu.SemaphoreType.DMA((16,))],
    )(*out)
    return done[:9] + (jnp.transpose(done[9], (0, 2, 1)),)


def hand_out(*refs):
    given, outs, held, came, left = refs[:7], refs[7:17], refs[17:23], refs[23], refs[24]
    vec, gains, shifts, gain_out, shift_out = given[5], *outs[5:9]
    pieces = []
    for src, mid, dst in zip(given[:5] + given[6:], held, outs[:5] + outs[9:]):
        for i in range(src.shape[1]) if len(src.shape) == 4 else (None,):
            at = (lambda ref, i=i: ref) if i is None else (lambda ref, i=i: ref.at[0, i])
            n = len(pieces)
            pieces.append((
                pltpu.make_async_copy(at(src), at(mid), came.at[n]),
                pltpu.make_async_copy(at(mid), at(dst), left.at[n]),
            ))
    for fetch, _ in pieces:
        fetch.start()
    d = lax.axis_index("dp")
    part, outer = gains.shape[3], gain_out.shape[2]
    lanes = part * lax.axis_size("dp")
    rolled = pltpu.roll(vec[:, 0:lanes], lax.rem(lanes - d * part, lanes), 1)
    for i in range(2):
        gains[0, i] = rolled[i:i + 1, 0:part]
        shifts[0, i] = rolled[2 + i:3 + i, 0:part]
    mine = pl.ds(pl.multiple_of(d * outer, outer), outer)
    gain_out[0] = vec[4:5, mine]
    shift_out[0] = vec[5:6, mine]
    for fetch, store in pieces:
        fetch.wait()
        store.start()
    for _, store in pieces:
        store.wait()


def per_device(*args):
    block_input, _, w_reduce, w_spatial = args[:4]
    n_dp, n_mp = lax.axis_size("dp"), lax.axis_size("mp")
    R, Wd = block_input.shape[1:]
    Cd, C = w_reduce.shape[2], w_spatial.shape[3]
    tasks, _, piece = args[9].shape
    sizes = (n_dp, n_mp, R, Wd, C * n_mp, C, Cd, piece * 2 * n_dp, tasks, piece)
    whole_tiles = not (C % 128 or Cd % 128 or Wd % 128 or R % 128 or piece % 16 or (R // n_mp) % 32)
    if whole_tiles and block_input.shape[0] == lax.axis_size("section") == 2:
        return fused_device(sizes, *args)
    return plain_device(*args)


def solution(mesh):
    return jax.shard_map(
        per_device,
        mesh=mesh,
        in_specs=(
            P(None, "dp", "mp"),
            P(None, "dp", None),
            P("section", "mp", "dp"),
            P("section", None, "dp", "mp"),
            P("section", "dp", "mp"),
            P("section", None, "mp"),
            P("section", None, "mp"),
            P("section", "mp"),
            P("section", "mp"),
            P(None, "mp", ("section", "dp")),
            P(None, None, "dp"),
            P(None, "dp", "mp"),
        ),
        out_specs=(
            P("section", None, "dp", "mp"),
            P("section", None, "dp", "mp"),
            P("section", "mp", "dp"),
            P("section", None, "dp", "mp"),
            P("section", "dp", "mp"),
            P("section", None, "mp", "dp"),
            P("section", None, "mp", "dp"),
            P("section", "mp", "dp"),
            P("section", "mp", "dp"),
            P(None, "mp", ("section", "dp")),
        ),
        check_vma=False,
    )
```

```python
import math

import jax
import jax.numpy as jnp
from jax import lax
from jax.experimental import pallas as pl
from jax.experimental.pallas import tpu as pltpu
from jax.sharding import PartitionSpec as P

NORM_EPS = 1e-05
LOSS_WEIGHT = 20.0
SIGN_FLOOR = 0.1
KEEP_TEMPER = 0.2


def shifted(value, axis, steps):
    count = lax.axis_size(axis)
    leading, last = (max(0, -steps), min(count, count - steps))
    return lax.ppermute(value, axis, [(source, source + steps) for source in range(leading, last)])


def geometry(img_sides, row_count):
    img_sizes = img_sides * img_sides
    img_ends = jnp.cumsum(img_sizes)
    img_starts = img_ends - img_sizes
    row_pos = jnp.arange(row_count, dtype=jnp.int32)[:, None]
    inside = (row_pos >= img_starts[None, :]) & (row_pos < img_ends[None, :])
    first_row = jnp.sum(jnp.where(inside, img_starts[None, :], 0), axis=1)
    side_len = jnp.sum(jnp.where(inside, img_sides[None, :], 0), axis=1)
    live_rows = jnp.any(inside, axis=1)
    offset = row_pos[:, 0] - first_row
    safe_side = jnp.maximum(side_len, 1)
    row_in = offset // safe_side
    col_in = offset % safe_side
    index_list = []
    valid_list = []
    for row_step in (-1, 0, 1):
        for col_step in (-1, 0, 1):
            new_row = row_in + row_step
            new_col = col_in + col_step
            valid = (
                live_rows
                & (new_row >= 0)
                & (new_row < side_len)
                & (new_col >= 0)
                & (new_col < side_len)
            )
            index_list.append(jnp.where(valid, first_row + new_row * side_len + new_col, 0))
            valid_list.append(valid)
    return (
        jnp.stack(index_list),
        jnp.stack(valid_list).astype(jnp.float32),
        live_rows.astype(jnp.float32),
    )


def smooth_act(values):
    return jax.nn.gelu(values, approximate=True)


def take_block(store, micro_idx):
    return lax.dynamic_index_in_dim(store, micro_idx, 0, keepdims=False)


def put_block(store, update, micro_idx, active):
    previous = take_block(store, micro_idx)
    return lax.dynamic_update_index_in_dim(store, jnp.where(active, update, previous), micro_idx, 0)


def channel_gather(values):
    return lax.all_gather(values, "mp", axis=1, tiled=True)


def channel_sum(values):
    return lax.psum_scatter(values, "mp", scatter_dimension=1, tiled=True)


def norm_stats(values, live_rows):
    masked = values * live_rows[:, None]
    total_sum, live_total = lax.psum((jnp.sum(masked, axis=0), jnp.sum(live_rows)), "dp")
    mean_val = total_sum / live_total
    centered = (values - mean_val) * live_rows[:, None]
    var_val = lax.psum(jnp.sum(centered * centered, axis=0), "dp") / live_total
    return (mean_val, lax.rsqrt(var_val + NORM_EPS), live_total)


def normalize(values, stats, live_rows, gain_vec, shift_vec):
    mean_val, inv_std, live_total = stats
    return live_rows[:, None] * (gain_vec * (values - mean_val) * inv_std + shift_vec)


def norm_backward(values, stats, live_rows, gain_vec, grad_norm):
    mean_val, inv_std, live_total = stats
    normed = (values - mean_val) * inv_std
    grad_live = grad_norm * live_rows[:, None]
    local_shift = jnp.sum(grad_live, axis=0)
    local_gain = jnp.sum(grad_live * normed, axis=0)
    sum_shift, sum_gain = lax.psum((local_shift, local_gain), "dp")
    grad_values = (
        live_rows[:, None]
        * inv_std
        * gain_vec
        * (grad_live - sum_shift / live_total - normed * sum_gain / live_total)
    )
    return (grad_values, local_gain, local_shift)


def gather_taps(values, indices, valids, tap_idx):
    return values[indices[tap_idx]] * valids[tap_idx][:, None].astype(values.dtype)


def act_backward(pre_values, grad_values):
    return jax.vjp(smooth_act, pre_values)[1](grad_values)[0]


def block_forward(x_in, layout, weights):
    indices, valids, live_rows = layout
    w_red, w_spa, w_exp, g_in, s_in, g_out, s_out = weights
    first_pre = channel_sum(jnp.dot(x_in, w_red, preferred_element_type=jnp.float32))
    stats_a = norm_stats(first_pre, live_rows)
    full_a = channel_gather(
        smooth_act(normalize(first_pre, stats_a, live_rows, g_in[0], s_in[0])).astype(jnp.bfloat16)
    )
    second_pre = jnp.zeros((x_in.shape[0], w_spa.shape[2]), jnp.float32)
    for tap_idx in range(9):
        second_pre = second_pre + jnp.dot(
            gather_taps(full_a, indices, valids, tap_idx),
            w_spa[tap_idx],
            preferred_element_type=jnp.float32,
        )
    stats_b = norm_stats(second_pre, live_rows)
    full_b = channel_gather(
        smooth_act(normalize(second_pre, stats_b, live_rows, g_in[1], s_in[1])).astype(jnp.bfloat16)
    )
    third_pre = jnp.dot(full_b, w_exp, preferred_element_type=jnp.float32)
    stats_c = norm_stats(third_pre, live_rows)
    pre_out = normalize(third_pre, stats_c, live_rows, g_out, s_out) + x_in.astype(jnp.float32)
    result = smooth_act(pre_out) * live_rows[:, None]
    return (result, (first_pre, stats_a, full_a, second_pre, stats_b, full_b, third_pre, stats_c))


def block_backward(d_out, x_in, layout, weights, saved_state):
    indices, valids, live_rows = layout
    w_red, w_spa, w_exp, g_in, s_in, g_out, s_out = weights
    first_pre, stats_a, full_a, second_pre, stats_b, full_b, third_pre, stats_c = saved_state
    pre_out = normalize(third_pre, stats_c, live_rows, g_out, s_out) + x_in.astype(jnp.float32)
    d_pre = act_backward(pre_out, d_out * live_rows[:, None])
    d_third, gain_c, shift_c = norm_backward(third_pre, stats_c, live_rows, g_out, d_pre)
    d_third = d_third.astype(jnp.bfloat16)
    grad_exp = jnp.einsum("rc,ro->co", full_b, d_third, preferred_element_type=jnp.float32)
    d_full_b = channel_sum(
        jnp.einsum("ro,co->rc", d_third, w_exp, preferred_element_type=jnp.float32)
    )
    pre_b = normalize(second_pre, stats_b, live_rows, g_in[1], s_in[1])
    d_second, gain_b, shift_b = norm_backward(
        second_pre, stats_b, live_rows, g_in[1], act_backward(pre_b, d_full_b)
    )
    d_second = d_second.astype(jnp.bfloat16)
    grad_spa = []
    back_total = jnp.zeros((x_in.shape[0], w_spa.shape[1]), jnp.float32)
    for tap_idx in range(9):
        grad_spa.append(
            jnp.einsum(
                "rc,ro->co",
                gather_taps(full_a, indices, valids, tap_idx),
                d_second,
                preferred_element_type=jnp.float32,
            )
        )
        spread = jnp.einsum(
            "ro,co->rc", d_second, w_spa[8 - tap_idx], preferred_element_type=jnp.float32
        )
        back_total = back_total + spread[indices[tap_idx]] * valids[tap_idx][:, None]
    d_full_a = channel_sum(back_total)
    pre_a = normalize(first_pre, stats_a, live_rows, g_in[0], s_in[0])
    d_first, gain_a, shift_a = norm_backward(
        first_pre, stats_a, live_rows, g_in[0], act_backward(pre_a, d_full_a)
    )
    d_first_full = channel_gather(d_first.astype(jnp.bfloat16))
    grad_red = jnp.einsum("rc,ro->co", x_in, d_first_full, preferred_element_type=jnp.float32)
    d_in = jnp.einsum("ro,co->rc", d_first_full, w_red, preferred_element_type=jnp.float32) + d_pre
    return (
        d_in,
        (
            grad_red,
            jnp.stack(grad_spa),
            grad_exp,
            jnp.stack([gain_a, gain_b]),
            jnp.stack([shift_a, shift_b]),
            gain_c,
            shift_c,
        ),
    )


def sign_merge(task_grads, thresh):
    soft_abs = jnp.sqrt(task_grads * task_grads + SIGN_FLOOR * SIGN_FLOOR) - SIGN_FLOOR
    purity = 0.5 * (1.0 + jnp.sum(task_grads, axis=0) / (jnp.sum(soft_abs, axis=0) + SIGN_FLOOR))
    keep_frac = jax.nn.sigmoid((purity - thresh) / KEEP_TEMPER)
    upper = 0.5 * jnp.sum(task_grads + soft_abs, axis=0)
    lower = 0.5 * jnp.sum(task_grads - soft_abs, axis=0)
    return keep_frac * upper + (1.0 - keep_frac) * lower


def plain_device(
    block_input,
    image_sides,
    w_reduce,
    w_spatial,
    w_expand,
    gain_inner,
    shift_inner,
    gain_outer,
    shift_outer,
    head_weight,
    labels,
    thresholds,
):
    section_idx = lax.axis_index("section")
    micro_count = block_input.shape[0]
    row_count = block_input.shape[1]
    w_red, w_spa, w_exp = (
        lax.all_gather(w_reduce[0].astype(jnp.bfloat16), "dp", axis=1, tiled=True),
        lax.all_gather(w_spatial[0].astype(jnp.bfloat16), "dp", axis=1, tiled=True),
        lax.all_gather(w_expand[0].astype(jnp.bfloat16), "dp", axis=0, tiled=True),
    )
    weights = (w_red, w_spa, w_exp, gain_inner[0], shift_inner[0], gain_outer[0], shift_outer[0])
    heads_all = lax.all_gather(
        head_weight.astype(jnp.bfloat16), ("section", "dp"), axis=2, tiled=True
    )
    class_total = heads_all.shape[2]
    class_ids = jnp.arange(class_total, dtype=jnp.int32)[None, None, :]

    def layout_for(micro_idx):
        return geometry(take_block(image_sides, micro_idx)[0], row_count)

    received = jnp.zeros(block_input.shape[1:], jnp.bfloat16)
    kept_inputs = jnp.zeros(block_input.shape, jnp.bfloat16)
    activ_store = jnp.zeros(block_input.shape, jnp.bfloat16)
    cotangents = jnp.zeros(block_input.shape, jnp.float32)
    head_grad = jnp.zeros(heads_all.shape, jnp.float32)
    for turn_idx in range(micro_count + 1):
        micro_idx = jnp.clip(turn_idx - section_idx, 0, micro_count - 1)
        active = (turn_idx - section_idx >= 0) & (turn_idx - section_idx < micro_count)
        x_in = jnp.where(section_idx == 0, block_input[min(turn_idx, micro_count - 1)], received)
        layout = layout_for(micro_idx)
        live_rows = layout[2]
        result, saved_state = block_forward(x_in, layout, weights)
        result_low = result.astype(jnp.bfloat16)
        kept_inputs = put_block(kept_inputs, x_in, micro_idx, active)
        activ_store = put_block(activ_store, result_low, micro_idx, active)
        labels_now = lax.dynamic_index_in_dim(labels, micro_idx, 1, keepdims=False)
        logits = lax.psum(
            jnp.einsum("rc,tco->tro", result_low, heads_all, preferred_element_type=jnp.float32),
            "mp",
        )
        peak_val = jnp.max(logits, axis=2, keepdims=True)
        expo = jnp.exp(logits - peak_val)
        soft_p = expo / jnp.sum(expo, axis=2, keepdims=True)
        picked = (class_ids == labels_now[:, :, None]).astype(jnp.float32)
        delta_low = (LOSS_WEIGHT * live_rows[None, :, None] * (soft_p - picked)).astype(
            jnp.bfloat16
        )
        task_grads = jnp.einsum(
            "tro,tco->trc", delta_low, heads_all, preferred_element_type=jnp.float32
        )
        merged = sign_merge(task_grads, take_block(thresholds, micro_idx))
        use_head = active & (section_idx == 1)
        head_grad = head_grad + jnp.where(
            use_head,
            jnp.einsum("rc,tro->tco", result_low, delta_low, preferred_element_type=jnp.float32),
            0.0,
        )
        cotangents = put_block(cotangents, merged, micro_idx, use_head)
        received = shifted(result_low, "section", 1)
    grad_recv = jnp.zeros(block_input.shape[1:], jnp.bfloat16)
    input_store = jnp.zeros(block_input.shape, jnp.float32)
    grad_total = None
    for turn_idx in range(micro_count + 1):
        micro_idx = jnp.clip(turn_idx - 1 + section_idx, 0, micro_count - 1)
        active = (turn_idx - 1 + section_idx >= 0) & (turn_idx - 1 + section_idx < micro_count)
        d_out = jnp.where(
            section_idx == 1, take_block(cotangents, micro_idx), grad_recv.astype(jnp.float32)
        )
        x_in = take_block(kept_inputs, micro_idx)
        layout = layout_for(micro_idx)
        saved_state = block_forward(x_in, layout, weights)[1]
        d_in, grad_set = block_backward(d_out, x_in, layout, weights, saved_state)
        masked = jax.tree.map(lambda leaf: jnp.where(active, leaf, 0.0), grad_set)
        grad_total = masked if grad_total is None else jax.tree.map(jnp.add, grad_total, masked)
        d_send = d_in.astype(jnp.bfloat16)
        input_store = put_block(
            input_store,
            jnp.where(section_idx == 1, d_send.astype(jnp.float32), d_in),
            micro_idx,
            active,
        )
        grad_recv = shifted(d_send, "section", -1)
    g_red, g_spa, g_exp, g_gain_in, g_shift_in, g_gain_out, g_shift_out = grad_total
    out_red, out_spa, out_exp, out_gain_in, out_shift_in, out_gain_out, out_shift_out = (
        lax.psum_scatter(g_red[None], "dp", scatter_dimension=2, tiled=True),
        lax.psum_scatter(g_spa[None], "dp", scatter_dimension=2, tiled=True),
        lax.psum_scatter(g_exp[None], "dp", scatter_dimension=1, tiled=True),
        lax.psum_scatter(g_gain_in[None, :, None, :], "dp", scatter_dimension=3, tiled=True),
        lax.psum_scatter(g_shift_in[None, :, None, :], "dp", scatter_dimension=3, tiled=True),
        lax.psum_scatter(g_gain_out[None, None, :], "dp", scatter_dimension=2, tiled=True),
        lax.psum_scatter(g_shift_out[None, None, :], "dp", scatter_dimension=2, tiled=True),
    )
    head_out = lax.psum_scatter(head_grad, ("section", "dp"), scatter_dimension=2, tiled=True)
    return (
        activ_store[None],
        input_store[None],
        out_red,
        out_spa,
        out_exp,
        out_gain_in,
        out_shift_in,
        out_gain_out,
        out_shift_out,
        head_out,
    )


K0 = math.sqrt(2.0 / math.pi)
K1 = 0.044715
MESH = pl.DeviceIdType.MESH
F32 = jnp.float32
BF16 = jnp.bfloat16
SIDES = (2, 7)
TAPS = [(a, b) for a in (-1, 0, 1) for b in (-1, 0, 1)]
PAD = 8
NN = (((1,), (0,)), ((), ()))
NT = (((1,), (1,)), ((), ()))
TN = (((0,), (0,)), ((), ()))


def tap_masks():
    found = []
    for tap_idx, (a, b) in enumerate(TAPS):
        for side in SIDES:
            found.append((tap_idx, a, b, side, a * side + b))
    return found


MASKS = tap_masks()


def dot(left, right, dims):
    return lax.dot_general(left, right, dims, preferred_element_type=F32)


def gelu(v):
    return 0.5 * v * (1.0 + jnp.tanh(K0 * v * (1.0 + K1 * v * v)))


def gelu_grad(v):
    sq = v * v
    t = jnp.tanh(K0 * v * (1.0 + K1 * sq))
    return 0.5 * (1.0 + t) + (0.5 * K0) * v * (1.0 - t * t) * (1.0 + 3.0 * K1 * sq)


def fold(x):
    return jnp.sum(x.reshape(x.shape[0] // 8, 8, x.shape[1]), axis=0)


def wide(x, width):
    times = width // x.shape[1]
    return x if times == 1 else jnp.concatenate([x] * times, axis=1)


def loop(total, chunk, body, init=None):
    def one(i, carry):
        return body(pl.ds(pl.multiple_of(i * chunk, chunk), chunk), carry)

    return lax.fori_loop(0, total // chunk, one, 0 if init is None else init)


def rows_tile(first, second, third):
    width = first.shape[1]
    place = lax.broadcasted_iota(jnp.int32, (8, width), 0)
    wide_of = lambda v: jnp.broadcast_to(v, (8, width))
    return jnp.where(
        place == 0, wide_of(first), jnp.where(place == 1, wide_of(second), wide_of(third))
    )


class Sems:
    def __init__(self, ref):
        self.ref, self.used, self.size = ref, 0, ref.shape[0]

    def take(self, count=1):
        first = self.used
        self.used += count
        assert self.used <= self.size, self.used
        return first


def make_kernel(sizes):
    n_dp, n_mp, R, Wd, M, C, Cd, classes, tasks, piece = sizes
    n_sec = 2
    W9 = 9 * C

    def kernel(*refs):
        (
            x_hbm, sides_ref, wred_hbm, wspa_hbm, wexp_hbm, gin_ref, sin_ref, gout_ref, sout_ref,
            head_hbm, lab_ref, thr_hbm,
            act_hbm, ig_hbm, red_hbm, spa_hbm, exp_hbm, vec_hbm, head_out,
            ssems, rsems, lsems, go,
            sred, sspa, sexp, shead, thr, xin, wr, wsp, we, hd, par,
            live, geo, masks, labc,
            rs_s, rs_r, ag_a, ag_b, ag_d, fulla, fullb, co, sums_s, sums_r, st, keep, first, second, third, ppad, dpad, dbuf,
            lg_s, lg_r, dl, act1, tg, dpre, evec, dth, ig, slope, steep,
            gred, gspa, gexp, sibred, sibspa, sibexp, rred, rspa, rexp, ghead, rhead, vec, vsib,
            ored, ospa, oexp, ovec, ohead,
        ) = refs
        s = lax.axis_index("section")
        d = lax.axis_index("dp")
        m = lax.axis_index("mp")
        o = 1 - s
        send, recv, local = Sems(ssems), Sems(rsems), Sems(lsems)
        pending = {None: [], 0: [], 1: []}
        rem = lax.rem
        dp_dev = lambda t: (s, t, m)
        mp_dev = lambda t: (s, d, t)
        sib_dev = (o, d, m)

        def put_to(src, dst, ssem, rsem, dev):
            pltpu.make_async_remote_copy(
                src_ref=src,
                dst_ref=dst,
                send_sem=ssems.at[ssem],
                recv_sem=rsems.at[rsem],
                device_id=dev,
                device_id_type=MESH,
            ).start()

        def waiter(ref, ssem, rsem):
            return pltpu.make_async_remote_copy(
                src_ref=ref,
                dst_ref=ref,
                send_sem=ssems.at[ssem],
                recv_sem=rsems.at[rsem],
                device_id=sib_dev,
                device_id_type=MESH,
            )

        def rcopy(src, dst, rsem, dev, when=None):
            ssem = send.take()
            put_to(src(), dst(), ssem, rsem, dev)
            pending[when].append(lambda: waiter(src(), ssem, 0).wait_send())

        def arrive(dst, rsem):
            waiter(dst, 0, rsem).wait_recv()

        axes = {"dp": (n_dp, d, dp_dev), "mp": (n_mp, m, mp_dev)}
        expected = {}

        def settle(key):
            expected.pop(key)()

        def load(src, dst):
            cp = pltpu.make_async_copy(src, dst, lsems.at[local.take()])
            cp.start()
            key = ("load", local.used)
            expected[key] = cp.wait
            return key

        def on(cond, what):
            return lambda: pl.when(cond())(what)

        class Group:
            def __init__(self, axis, all_of, when=None, slot_of=None):
                self.n, self.me, self.dev = axes[axis]
                self.ssem = send.take()
                self.rsem = recv.take(1 if slot_of is None else self.n - 1)
                self.all_of, self.when, self.slot_of = all_of, when, slot_of

            def put(self, src_of, slot_of):
                for k in range(1, self.n):
                    t = rem(self.me + k, self.n)
                    rsem = self.rsem + (0 if self.slot_of is None else k - 1)
                    put_to(src_of(t), slot_of(self.me), self.ssem, rsem, self.dev(t))

            def came_from(self, k):
                return rem(self.me + self.n - k, self.n)

            def close(self):
                ssem, all_of, when = self.ssem, self.all_of, self.when
                pending[when].append(lambda: waiter(all_of(), ssem, 0).wait_send())
                if self.slot_of is None:
                    waits = {self.rsem: lambda: arrive(all_of(), self.rsem)}
                else:
                    waits = {
                        self.rsem + k - 1: lambda k=k: arrive(
                            self.slot_of(self.came_from(k)), self.rsem + k - 1
                        )
                        for k in range(1, self.n)
                    }
                for key, wait in waits.items():
                    expected[key] = wait if when is None else on(lambda: s == when, wait)
                return self.rsem

        def spread(axis, src_of, slot_of, all_of, when=None):
            group = Group(axis, all_of, when)
            group.put(src_of, slot_of)
            return group.close()

        l_red = load(wred_hbm.at[0], sred)
        l_x = load(x_hbm.at[s], xin.at[0])
        l_spa = load(wspa_hbm.at[0], sspa)
        l_exp = load(wexp_hbm.at[0], sexp)
        l_head = load(head_hbm, shead)
        l_thr = load(thr_hbm.at[s], thr)

        barrier = pltpu.get_barrier_semaphore()
        greeted = 0
        for ds_ in range(n_sec):
            for k in range(n_dp):
                if ds_ == 0 and k == 0:
                    continue
                pl.semaphore_signal(
                    barrier, inc=1,
                    device_id=(rem(s + ds_, n_sec), rem(d + k, n_dp), m),
                    device_id_type=MESH,
                )
                greeted += 1
        for k in range(1, n_mp):
            pl.semaphore_signal(
                barrier, inc=1, device_id=(s, d, rem(m + k, n_mp)), device_id_type=MESH
            )
            greeted += 1

        settle(l_red)
        wr[s, d] = sred[...].astype(BF16)
        par[s] = jnp.zeros(par.shape[1:], F32)
        for i in range(2):
            par[s, i:i + 1, :C] = gin_ref[0, i:i + 1, :]
            par[s, 2 + i:3 + i, :C] = sin_ref[0, i:i + 1, :]
        par[s, 4:5, :] = gout_ref[...]
        par[s, 5:6, :] = sout_ref[...]
        pl.semaphore_wait(barrier, greeted)

        by_dp, by_sib = {}, {}

        def send_own(buf, j):
            def go():
                by_dp[id(buf), j] = spread(
                    "dp",
                    lambda t: buf.at[j, d],
                    lambda src: buf.at[j, src],
                    lambda: buf.at[j, pl.ds(0, n_dp - 1)],
                    when=j,
                )

            pl.when(s == j)(go)

        def pass_on(buf, j):
            settle(by_dp[id(buf), j])
            sem = by_sib[id(buf), j] = recv.take()

            @pl.when(s == j)
            def _():
                rcopy(lambda: buf.at[j], lambda: buf.at[j], sem, sib_dev, when=j)

            expected[sem] = on(lambda: s != j, lambda: arrive(buf.at[j], sem))

        def from_sib(buf, j):
            settle(by_sib[id(buf), j])

        par_sem = recv.take()
        rcopy(lambda: par.at[s], lambda: par.at[s], par_sem, sib_dev)
        expected[par_sem] = lambda: arrive(par.at[o], par_sem)
        early = Group(
            "dp",
            lambda: wr.at[0, pl.ds(0, n_dp - 1)],
            when=0,
            slot_of=lambda src: wr.at[0, src],
        )

        @pl.when(s == 0)
        def _():
            early.put(lambda t: wr.at[0, d], lambda src: wr.at[0, src])

        early.close()

        settle(l_spa)
        for k in range(9):
            wsp[s, d, :, k * C:(k + 1) * C] = sspa[k].astype(BF16)

        settle(l_exp)
        we[s, d] = sexp[...].astype(BF16)

        sides = jnp.where(s == 0, sides_ref[0], sides_ref[1]).astype(F32)
        slots = sides.shape[1]
        sq = jnp.broadcast_to(sides * sides, (8, slots)).astype(BF16)
        upper = (
            lax.broadcasted_iota(jnp.int32, (slots, slots), 0)
            <= lax.broadcasted_iota(jnp.int32, (slots, slots), 1)
        ).astype(BF16)
        ends = dot(sq, upper, NN)[0:1]
        starts = ends - sides * sides
        nloc = jnp.broadcast_to(jnp.max(ends, axis=1, keepdims=True), (1, 128))
        shape = (R, 128)
        pos = lax.broadcasted_iota(jnp.int32, (R, slots), 0).astype(F32)
        inside = (pos >= starts) & (pos < ends)
        origin = jnp.sum(jnp.where(inside, starts, 0.0), axis=1, keepdims=True)
        side = jnp.sum(jnp.where(inside, sides, 0.0), axis=1, keepdims=True)
        geo[0] = jnp.broadcast_to(origin, shape)
        geo[1] = jnp.broadcast_to(side, shape)

        def make_masks(rows, carry):
            side_b = geo[1, rows]
            here = lax.broadcasted_iota(jnp.int32, side_b.shape, 0) + rows.start
            offset = here.astype(F32) - geo[0, rows]
            row_in = jnp.floor((offset + 0.5) / jnp.maximum(side_b, 1.0))
            col_in = offset - row_in * side_b
            live[rows] = (side_b > 0.0).astype(F32)
            for idx, (_, a, b, q, _) in enumerate(MASKS):
                ra, cb = row_in + a, col_in + b
                ok = (side_b == q) & (ra >= 0.0) & (ra < q) & (cb >= 0.0) & (cb < q)
                masks[idx, rows] = ok.astype(F32)
            return carry

        loop(R, 64, make_masks)
        for buf in (ppad, dpad):
            edge = jnp.zeros((PAD, buf.shape[1]), F32)
            buf[0:PAD] = edge
            buf[PAD + R:PAD + R + PAD] = edge
        lab2 = lab_ref[...]
        lab = jnp.where(s == 0, lab2[:, 0], lab2[:, 1]).astype(F32)
        lab = jnp.concatenate([lab, jnp.zeros((8 - tasks, R), F32)], axis=0)
        labc[...] = jnp.transpose(lab)

        settle(l_head)
        mine = s * n_dp + d
        for t in range(tasks):
            hd[mine, t] = shead[t].astype(BF16)

        def to_all(src_of, buf):
            ssem, rsem = send.take(), recv.take()
            others = [(a, k) for a in range(n_sec) for k in range(n_dp) if a or k]
            for a, k in others:
                ts, td = rem(s + a, n_sec), rem(d + k, n_dp)
                put_to(src_of(ts * n_dp + td), buf.at[mine], ssem, rsem, (ts, td, m))
            rest = lambda: buf.at[pl.ds(0, len(others))]
            pending[None].append(lambda: waiter(rest(), ssem, 0).wait_send())
            expected[rsem] = lambda: arrive(rest(), rsem)
            return rsem

        def cat(buf, n):
            return jnp.concatenate([buf[i] for i in range(n)], axis=1)

        phase = {"rs": 0, "st": 0}

        def rs_open():
            p = phase["rs"]
            phase["rs"] += 1
            return p, Group("mp", lambda: rs_r.at[p, pl.ds(0, n_mp - 1)])

        def rs_rows(handle, rows, out):
            p, group = handle
            for c in range(n_mp):
                rs_s[p, c, rows] = out[:, c * C:(c + 1) * C].astype(BF16)
            group.put(lambda t: rs_s.at[p, t, rows], lambda src: rs_r.at[p, src, rows])

        def rs_finish(handle, dst):
            p, group = handle
            settle(group.rsem)

            def add(rows, carry):
                dst[rows] = rs_sum(handle, rows)
                return carry

            loop(R, 128, add)

        def product_to_rs(left, right_of, dims):
            handle = rs_open()

            def part(rows, carry):
                rs_rows(handle, rows, dot(left[rows], right_of(), dims))
                return carry

            loop(R, 128, part)
            handle[1].close()
            return handle

        def exchange(tile):
            p = phase["st"]
            phase["st"] += 1
            width = tile.shape[1]
            st[p, d, :, 0:width] = tile
            slot = lambda src: st.at[p, src, :, 0:width]
            rest = lambda: st.at[p, pl.ds(0, n_dp - 1), :, 0:width]
            return p, width, spread("dp", lambda t: slot(d), slot, rest)

        def collect(handle):
            p, width, base = handle
            settle(base)
            return [st[p, i, :, 0:width] for i in range(n_dp)]

        def stats_start(buf, width, total=None):
            chunk = 128 if width <= 128 else 32
            zero = jnp.zeros((8, width), F32)

            def sum_up(rows, carry):
                return carry + fold(buf[rows] * wide(live[rows], width))

            if total is None:
                total = loop(R, chunk, sum_up, zero)
            total = jnp.sum(total, axis=0, keepdims=True)
            count = wide(nloc, width)
            mean = total / jnp.maximum(count, 1.0)

            def squares(rows, carry):
                off = (buf[rows] - mean) * wide(live[rows], width)
                return carry + fold(off * off)

            sqs = jnp.sum(loop(R, chunk, squares, zero), axis=0, keepdims=True)
            return exchange(rows_tile(total, sqs, count)), mean

        def stats_finish(handle, j, i):
            tiles = collect(handle)
            width = handle[1]
            count = sum(t[2:3] for t in tiles)
            mean = sum(t[0:1] for t in tiles) / count
            sqs = 0.0
            for t in tiles:
                local_mean = t[0:1] / jnp.maximum(t[2:3], 1.0)
                sqs = sqs + t[1:2] + t[2:3] * (local_mean - mean) * (local_mean - mean)
            inv = lax.rsqrt(sqs / count + NORM_EPS)
            keep[j, i, :, 0:width] = rows_tile(mean, inv, count)

        spans = [slice(r0, r0 + 128) for r0 in range(0, R, 128)]

        def rows_out(buf, at, rows, values):
            buf[at, m, rows] = values.astype(BF16)
            return spread(
                "mp",
                lambda t: buf.at[at, m, rows],
                lambda src: buf.at[at, src, rows],
                lambda: buf.at[at, pl.ds(0, n_mp - 1), rows],
            )

        def rs_rows_sums(handle, j, i, rows, out, carry):
            p, group = handle
            sb, sg = carry
            raw = (ag_a, ag_b)[i]
            for c in range(n_mp):
                part = out[:, c * C:(c + 1) * C]
                rs_s[p, c, rows] = part.astype(BF16)
                tile = co[2 * j + i, c]
                g = part * slope[j, i, c, rows]
                xhat = raw[j, c, rows].astype(F32) * tile[2:3] + tile[3:4]
                sb[c] = sb[c] + fold(g)
                sg[c] = sg[c] + fold(g * xhat)
            if rows is not spans[-1]:
                group.put(lambda t: rs_s.at[p, t, rows], lambda src: rs_r.at[p, src, rows])

        def rs_sums_out(handle, carry):
            p, group = handle
            sb, sg = carry
            total = lambda v: jnp.sum(v, axis=0, keepdims=True)
            for c in range(n_mp):
                b, g = total(sb[c]), total(sg[c])
                sums_s[p, c] = rows_tile(b, g, g)
            ssem, rsem = send.take(), recv.take()
            others = [(a, k) for a in range(n_mp) for k in range(n_dp) if a or k]
            me = m * n_dp + d
            for a, k in others:
                tz, td = rem(m + a, n_mp), rem(d + k, n_dp)
                put_to(sums_s.at[p, tz], sums_r.at[p, me], ssem, rsem, (s, td, tz))
            rows = spans[-1]
            group.put(lambda t: rs_s.at[p, t, rows], lambda src: rs_r.at[p, src, rows])
            group.close()
            rest = lambda: sums_r.at[p, pl.ds(0, len(others))]
            pending[None].append(lambda: waiter(rest(), ssem, 0).wait_send())
            expected[rsem] = lambda: arrive(rest(), rsem)

            def collect_sums():
                settle(rsem)
                tile = sums_s[p, m]
                for a, k in others:
                    tile = tile + sums_r[p, rem(m + a, n_mp) * n_dp + rem(d + k, n_dp)]
                return tile

            return collect_sums

        def rs_sum(handle, rows):
            p, _ = handle
            out = rs_s[p, m, rows].astype(F32)
            for k in range(1, n_mp):
                out = out + rs_r[p, rem(m + k, n_mp), rows].astype(F32)
            return out

        def coeffs_out(at, *values):
            place = lax.broadcasted_iota(jnp.int32, (8, C), 0)
            tile = jnp.zeros((8, C), F32)
            for i, v in enumerate(values):
                tile = jnp.where(place == i, jnp.broadcast_to(v, (8, C)), tile)
            co[at, m] = tile
            slot = lambda src: co.at[at, src]
            return spread("mp", lambda t: slot(m), slot, lambda: co.at[at, pl.ds(0, n_mp - 1)])

        def inner_norm(j, i, src, raw, full, hook, need, consume):
            at = 2 * j + i
            handle, mean_here = stats_start(src.at[j], C)
            push = lambda rows: rows_out(raw, j, rows, src[j, rows] - mean_here)
            groups = [push(rows) for rows in spans[:-1]]
            hook()
            stats_finish(handle, j, i)
            mu, inv, _, gain, shift = norm_of(j, i, C)
            moved = (mean_here - mu) * inv
            sent = coeffs_out(at, gain * inv, gain * moved + shift, inv, moved)
            groups.append(push(spans[-1]))
            need()
            settle(sent)
            for rows, group in zip(spans, groups):
                settle(group)
                for c in range(n_mp):
                    tile = co[at, c]
                    y = live[rows] * (raw[j, c, rows].astype(F32) * tile[0:1] + tile[1:2])
                    full[j, rows, c * C:(c + 1) * C] = gelu(y).astype(BF16)
                consume(rows)

        def norm_of(j, i, width):
            tile = keep[j, i, :, 0:width]
            if i < 2:
                gain, shift = par[j, i:i + 1, 0:width], par[j, 2 + i:3 + i, 0:width]
            else:
                gain, shift = par[j, 4:5, 0:width], par[j, 5:6, 0:width]
            return tile[0:1], tile[1:2], tile[2:3], gain, shift

        def taps_sum(src, flip, put):
            for r0 in range(0, R, 128):
                put(r0, lambda idx_list, lanes: sum(
                    masks[(len(MASKS) - 2 - (idx // 2) * 2 + idx % 2) if flip else idx, r0:r0 + 128]
                    * src[
                        PAD + r0 + (-1 if flip else 1) * MASKS[idx][4]:
                        PAD + r0 + (-1 if flip else 1) * MASKS[idx][4] + 128,
                        lanes,
                    ]
                    for idx in idx_list
                ))

        nothing = lambda: None
        vec[...] = jnp.zeros(vec.shape, F32)

        def prepare(j):
            for i, raw in enumerate((ag_a, ag_b)):
                def inner(rows, carry):
                    for c in range(n_mp):
                        tile = co[2 * j + i, c]
                        y = live[rows] * (raw[j, c, rows].astype(F32) * tile[0:1] + tile[1:2])
                        slope[j, i, c, rows] = live[rows] * gelu_grad(y)
                    return carry

                loop(R, 64, inner)
            mu, inv, _, gain, shift = norm_of(j, 2, Wd)

            def outer(rows, carry):
                lv = wide(live[rows], Wd)
                pre = lv * (gain * ((third[j, rows] - mu) * inv) + shift)
                steep[j, rows] = lv * gelu_grad(pre + xin[j, rows].astype(F32))
                return carry

            loop(R, 32, outer)

        def forward(j, h, hooks, needs):
            hooks[0]()
            rs_finish(h, first.at[j])

            def conv(rows):
                there = slice(PAD + rows.start, PAD + rows.stop)
                ppad[there] = dot(fulla[j, rows], wsp[j].reshape(M, W9), NN)

            inner_norm(j, 0, first, ag_a, fulla, hooks[1], needs[0], conv)

            def put(r0, summed):
                second[j, r0:r0 + 128] = sum(
                    summed([2 * k, 2 * k + 1], slice(k * C, (k + 1) * C)) for k in range(9)
                )

            taps_sum(ppad, False, put)
            if j == 0:
                pass_on(wr, 1)
            sums = []

            def expand(rows):
                out = dot(fullb[j, rows], we[j].reshape(M, Wd), NN)
                third[j, rows] = out
                sums.append(fold(out * wide(live[rows], Wd)))

            inner_norm(j, 1, second, ag_b, fullb, hooks[2], needs[1], expand)
            h, _ = stats_start(third.at[j], Wd, sum(sums))
            hooks[3]()
            stats_finish(h, j, 2)
            mu, inv, _, gain, shift = norm_of(j, 2, Wd)
            out = xin.at[1] if j == 0 else act1

            def act_c(rows, carry):
                lv = wide(live[rows], Wd)
                pre = lv * (gain * ((third[j, rows] - mu) * inv) + shift)
                pre = pre + xin[j, rows].astype(F32)
                out[rows] = (lv * gelu(pre)).astype(BF16)
                return carry

            loop(R, 32, act_c)

        def to_section(src, hbm, j):
            sem = recv.take()

            @pl.when(s == j)
            def _():
                lsem = local.take()
                made = lambda: pltpu.make_async_copy(src(), hbm.at[0, s], lsems.at[lsem])
                made().start()
                pending[j].append(lambda: made().wait())

            @pl.when(s != j)
            def _():
                rcopy(src, lambda: hbm.at[0, s], sem, sib_dev, when=1 - j)

            expected[sem] = on(lambda: s == j, lambda: arrive(hbm.at[0, o], sem))

        grads = ((gred, sibred, rred), (gspa, sibspa, rspa), (gexp, sibexp, rexp))
        at_sib, at_dp = {}, {}

        def grad_to_sib(which, j):
            own, sib, _ = grads[which]
            sem = at_sib[which, j] = recv.take()

            @pl.when(s != j)
            def _():
                rcopy(lambda: own.at[j], lambda: sib, sem, sib_dev, when=1 - j)

            expected[sem] = on(lambda: s == j, lambda: arrive(sib, sem))

        def grad_to_dp(which, j):
            own, sib, got = grads[which]
            settle(at_sib[which, j])

            def go():
                def add(rows, carry):
                    for i in range(n_dp):
                        own[j, i, rows] = (
                            own[j, i, rows].astype(F32) + sib[i, rows].astype(F32)
                        ).astype(BF16)
                    return carry

                loop(own.shape[2], 64, add)
                base = spread(
                    "dp",
                    lambda t: own.at[j, t],
                    lambda src: got.at[src],
                    lambda: got.at[pl.ds(0, n_dp - 1)],
                    when=j,
                )
                at_dp.setdefault(which, []).append(base)

            pl.when(s == j)(go)

        def reduce_to_sib(j):
            for i in range(n_dp):
                gred[j, i] = dot(xin[j], ag_d[j, i], TN).astype(BF16)
                sem = at_sib[0, j, i] = recv.take()

                @pl.when(s != j)
                def _():
                    rcopy(lambda: gred.at[j, i], lambda: sibred.at[i], sem, sib_dev, when=1 - j)

                expected[sem] = on(
                    lambda: s == j, lambda i=i, sem=sem: arrive(sibred.at[i], sem)
                )

        def reduce_to_dp(j):
            group = Group("dp", lambda: rred.at[pl.ds(0, n_dp - 1)], when=j)
            for i in range(n_dp):
                settle(at_sib[0, j, i])

                @pl.when(s == j)
                def _():
                    def add(rows, carry):
                        gred[j, i, rows] = (
                            gred[j, i, rows].astype(F32) + sibred[i, rows].astype(F32)
                        ).astype(BF16)
                        return carry

                    loop(Wd, 128, add)

                    @pl.when(d != i)
                    def _():
                        put_to(gred.at[j, i], rred.at[d], group.ssem, group.rsem, dp_dev(i))

            at_dp.setdefault(0, []).append(group.close())

        def steepest(j, rows, e, carry):
            mu, inv, _, _, _ = norm_of(j, 2, Wd)
            out = steep[j, rows] * e
            dpre[rows] = out
            return carry[0] + fold(out), carry[1] + fold(out * ((third[j, rows] - mu) * inv))

        def backward(j, sums, hooks):
            mu, inv, count, gain, shift = norm_of(j, 2, Wd)
            sb, sg = sums
            total = lambda v: jnp.sum(v, axis=0, keepdims=True)
            sb, sg = total(sb), total(sg)
            h = exchange(rows_tile(sb, sg, sg))
            hooks[0]()
            tile = sum(collect(h))
            vec[j, 4:5, :] = tile[1:2]
            vec[j, 5:6, :] = tile[0:1]
            sb_n, sg_n = tile[0:1] / count, tile[1:2] / count
            scale = gain * inv

            def d_third(rows, carry):
                lv = wide(live[rows], Wd)
                xhat = (third[j, rows] - mu) * inv
                dth[rows] = (lv * scale * (dpre[rows] - sb_n - xhat * sg_n)).astype(BF16)
                return carry

            none = lambda: ([jnp.zeros((8, C), F32)] * n_mp, [jnp.zeros((8, C), F32)] * n_mp)
            h, carry = rs_open(), none()
            for rows in spans:
                for r0 in range(rows.start, rows.stop, 32):
                    d_third(slice(r0, r0 + 32), 0)
                out = dot(dth[rows], we[j].reshape(M, Wd), NT)
                rs_rows_sums(h, j, 1, rows, out, carry)
            sums_of = rs_sums_out(h, carry)
            for i in range(n_dp):
                full = fullb[j, :, i * Cd:(i + 1) * Cd]
                gexp[j, i] = dot(full, dth[...], TN).astype(BF16)
            grad_to_sib(2, j)
            hooks[1]()
            settle(h[1].rsem)

            def norm_grad(i, src, tile):
                mu, inv, count, gain, _ = norm_of(j, i, C)
                vec[j, i:i + 1, 0:C] = tile[1:2]
                vec[j, 2 + i:3 + i, 0:C] = tile[0:1]
                sb_n, sg_n, scale = tile[0:1] / count, tile[1:2] / count, gain * inv

                def grad_of(rows, h):
                    xhat = (src[j, rows] - mu) * inv
                    g = slope[j, i, m, rows] * rs_sum(h, rows)
                    return live[rows] * scale * (g - sb_n - xhat * sg_n)

                return grad_of

            grad_of = norm_grad(1, second, sums_of())
            for rows in spans:
                there = slice(PAD + rows.start, PAD + rows.stop)
                dpad[there] = grad_of(rows, h).astype(BF16).astype(F32)

            h, carry = rs_open(), none()

            def put(r0, summed):
                for k in range(9):
                    dbuf[r0:r0 + 128, k * C:(k + 1) * C] = summed(
                        [2 * k, 2 * k + 1], slice(None)
                    ).astype(BF16)
                rows = spans[r0 // 128]
                out = dot(dbuf[rows], wsp[j].reshape(M, W9), NT)
                rs_rows_sums(h, j, 0, rows, out, carry)

            taps_sum(dpad, True, put)
            sums_of = rs_sums_out(h, carry)
            for i in range(n_dp):
                full = fulla[j, :, i * Cd:(i + 1) * Cd]
                gspa[j, i] = dot(full, dbuf[...], TN).astype(BF16)
            grad_to_sib(1, j)
            grad_to_dp(2, j)
            hooks[2]()
            settle(h[1].rsem)
            grad_of = norm_grad(0, first, sums_of())
            groups = [rows_out(ag_d, j, rows, grad_of(rows, h)) for rows in spans]
            hooks[3]()
            grad_to_dp(1, j)

            def d_input(rows):
                full = jnp.concatenate([ag_d[j, c, rows] for c in range(n_mp)], axis=1)
                out = dot(full, cat(wr.at[j], n_dp), NT) + dpre[rows]
                if j == 1:
                    out = out.astype(BF16).astype(F32)
                    evec[rows] = out
                ig[j, rows] = out

            for rows, group in zip(spans, groups):
                settle(group)
                if j == 1:
                    d_input(rows)
            if j == 0:
                reduce_to_sib(j)
                for rows in spans:
                    d_input(rows)
            to_section(lambda: ig.at[j], ig_hbm, j)

        settle(l_x)
        hold = {}

        def first_product():
            handle = rs_open()
            p, group = handle
            for k in range(n_dp):
                src = early.came_from(k) if k else d
                if k:
                    settle(early.rsem + k - 1)
                sem = recv.take()

                @pl.when(s == 0)
                def _():
                    rcopy(lambda: wr.at[0, src], lambda: wr.at[0, src], sem, sib_dev, when=0)

                expected[sem] = on(lambda: s != 0, lambda: arrive(wr.at[0, src], sem))
                settle(sem)

                def part(rows, carry):
                    rs_s[p, src, rows] = dot(xin[0, rows], wr[0, src], NN).astype(BF16)
                    return carry

                loop(R, 128, part)

                @pl.when(src != m)
                def _():
                    put_to(rs_s.at[p, src], rs_r.at[p, m], group.ssem, group.rsem, mp_dev(src))

            group.close()
            return handle

        @pl.when(s == 1)
        def _():
            pl.semaphore_wait(go, 1)

        start = first_product()
        settle(par_sem)

        def w_next():
            send_own(we, 0)
            send_own(wr, 1)

        def w_head():
            hold["heads"] = to_all(lambda t: hd.at[mine], hd)

        def f00():
            send_own(wsp, 0)
            pending[None].pop()()

            @pl.when(s == 0)
            def _():
                pl.semaphore_signal(go, inc=1, device_id=sib_dev, device_id_type=MESH)

        hooks = (f00, w_next, lambda: send_own(wsp, 1), nothing)

        def n00():
            pass_on(wsp, 0)
            from_sib(wsp, 0)

        def n01():
            pass_on(we, 0)
            from_sib(we, 0)

        forward(0, start, hooks, (n00, n01))
        from_sib(wr, 1)
        start = product_to_rs(xin.at[1], lambda: cat(wr.at[1], n_dp), NN)

        def f10():
            send_own(we, 1)
            pass_on(wsp, 1)
            to_section(lambda: xin.at[1], act_hbm, 0)
            prepare(0)

        def n10():
            pass_on(we, 1)
            from_sib(wsp, 1)

        hooks = (f10, w_head, nothing, nothing)
        forward(1, start, hooks, (n10, lambda: from_sib(we, 1)))

        settle(hold["heads"])
        RM = R // n_mp
        n_cls = n_sec * n_dp

        def heads_of(t):
            return hd[:, t].reshape(classes, Wd)

        for c in range(n_mp):
            rows = act1[c * RM:(c + 1) * RM]
            for t in range(tasks):
                lg_s[c, :, t * classes:(t + 1) * classes] = dot(rows, heads_of(t), NT).astype(
                    lg_s.dtype
                )
        base = spread(
            "mp", lambda t: lg_s.at[t], lambda src: lg_r.at[src], lambda: lg_r.at[pl.ds(0, n_mp - 1)]
        )
        to_section(lambda: act1, act_hbm, 1)
        settle(l_thr)
        prepare(1)
        settle(base)
        here = pl.ds(pl.multiple_of(m * RM, RM), RM)
        lv = wide(live[here], classes)
        for t in range(tasks):
            lanes = slice(t * classes, (t + 1) * classes)
            logit = lg_s[m, :, lanes].astype(F32)
            for k in range(1, n_mp):
                logit = logit + lg_r[rem(m + k, n_mp), :, lanes].astype(F32)
            expo = jnp.exp(logit - jnp.max(logit, axis=1, keepdims=True))
            soft = expo / jnp.sum(expo, axis=1, keepdims=True)
            ids = lax.broadcasted_iota(jnp.int32, (RM, classes), 1).astype(F32)
            hot = (ids == labc[here, t:t + 1]).astype(F32)
            dl[m, :, lanes] = (LOSS_WEIGHT * lv * (soft - hot)).astype(BF16)
        group = Group(
            "mp", lambda: dl.at[pl.ds(0, n_mp - 1)], slot_of=lambda src: dl.at[src]
        )
        group.put(lambda t: dl.at[m], lambda src: dl.at[src])
        group.close()

        def merge_block(c, sums):
            for t in range(tasks):
                lanes = slice(t * classes, (t + 1) * classes)
                tg[t] = dot(dl[c, :, lanes], heads_of(t), NN)

            def merge(rows, carry):
                total = soft_sum = None
                for t in range(tasks):
                    g = tg[t, rows]
                    soft = jnp.sqrt(g * g + SIGN_FLOOR * SIGN_FLOOR) - SIGN_FLOOR
                    total = g if t == 0 else total + g
                    soft_sum = soft if t == 0 else soft_sum + soft
                purity = 0.5 * (1.0 + total / (soft_sum + SIGN_FLOOR))
                start = pl.multiple_of(rows.start + c * RM, 32)
                there = pl.ds(start, 32)
                frac = 1.0 / (1.0 + jnp.exp((thr[there] - purity) * (1.0 / KEEP_TEMPER)))
                upper, lower = 0.5 * (total + soft_sum), 0.5 * (total - soft_sum)
                return steepest(1, there, frac * upper + (1.0 - frac) * lower, carry)

            return loop(RM, 32, merge, sums)

        zero = (jnp.zeros((8, Wd), F32), jnp.zeros((8, Wd), F32))
        sums = merge_block(m, zero)
        for k in [1] + list(range(n_mp - 1, 1, -1)):
            settle(group.rsem + k - 1)
            sums = merge_block(group.came_from(k), sums)

        def b10():
            for t in range(tasks):
                lanes = slice(t * classes, (t + 1) * classes)
                delta = dl[:, :, lanes].reshape(R, classes)
                out = dot(delta, act1[...], TN).astype(BF16)
                ghead[:, t] = out.reshape(n_cls, piece, Wd)
            hold["ghead"] = to_all(lambda t: ghead.at[t], rhead)

        backward(1, sums, (nothing, b10, nothing, nothing))
        sums = loop(R, 32, lambda rows, carry: steepest(0, rows, evec[rows], carry), zero)

        def b03():
            hold["vec"] = recv.take()
            rcopy(lambda: vec.at[o], lambda: vsib, hold["vec"], sib_dev)
            expected[hold["vec"]] = lambda: arrive(vsib, hold["vec"])

        backward(0, sums, (lambda: reduce_to_sib(1), lambda: reduce_to_dp(1), nothing, b03))
        reduce_to_dp(0)

        settle(hold["ghead"])
        for t in range(tasks):
            total = ghead[mine, t].astype(F32)
            for k in range(1, n_cls):
                total = total + rhead[rem(mine + k, n_cls), t].astype(F32)
            ohead[t] = total
        load(ohead, head_out)
        settle(hold["vec"])
        ovec[...] = vec[s] + vsib[...]
        load(ovec, vec_hbm)

        def total_of(own, got, rows):
            out = own[s, d, rows].astype(F32)
            for k in range(1, n_dp):
                out = out + got[rem(d + k, n_dp), rows].astype(F32)
            return out

        def finish_grad(which):
            own, _, got = grads[which]
            for key in at_dp[which]:
                settle(key)

            def finish(rows, carry):
                out = total_of(own, got, rows)
                if which == 1:
                    for k in range(9):
                        ospa[0, k, rows] = out[:, k * C:(k + 1) * C]
                else:
                    (ored if which == 0 else oexp)[0, rows] = out
                return carry

            loop(own.shape[2], 64, finish)
            load((ored, ospa, oexp)[which], (red_hbm, spa_hbm, exp_hbm)[which])

        finish_grad(2)
        finish_grad(1)
        finish_grad(0)
        for key in list(expected):
            settle(key)

        for key, waits in pending.items():
            def finish_all(waits=waits):
                for wait in waits:
                    wait()

            if key is None:
                finish_all()
            else:
                pl.when(s == key)(finish_all)

    return kernel


def fused_device(sizes, *args):
    n_dp, n_mp, R, Wd, M, C, Cd, classes, tasks, piece = sizes
    W9, n_cls = 9 * C, 2 * n_dp
    RM = R // n_mp
    vmem = lambda shape, dtype: pltpu.VMEM(shape, dtype)
    scratch = [
        pltpu.SemaphoreType.DMA((83,)),
        pltpu.SemaphoreType.DMA((87,)),
        pltpu.SemaphoreType.DMA((15,)),
        pltpu.SemaphoreType.REGULAR,
        vmem((Wd, Cd), F32),
        vmem((9, Cd, C), F32),
        vmem((Cd, Wd), F32),
        vmem((tasks, piece, Wd), F32),
        vmem((R, Wd), F32),
        vmem((2, R, Wd), BF16),
        vmem((2, n_dp, Wd, Cd), BF16),
        vmem((2, n_dp, Cd, W9), BF16),
        vmem((2, n_dp, Cd, Wd), BF16),
        vmem((n_cls, tasks, piece, Wd), BF16),
        vmem((2, 8, Wd), F32),
        vmem((R, 128), F32),
        vmem((2, R, 128), F32),
        vmem((len(MASKS), R, 128), F32),
        vmem((R, 8), F32),
        vmem((6, n_mp, R, C), BF16),
        vmem((6, n_mp, R, C), BF16),
        vmem((2, n_mp, R, C), BF16),
        vmem((2, n_mp, R, C), BF16),
        vmem((2, n_mp, R, C), BF16),
        vmem((2, R, M), BF16),
        vmem((2, R, M), BF16),
        vmem((4, n_mp, 8, C), F32),
        vmem((6, n_mp, 8, C), F32),
        vmem((6, n_mp * n_dp, 8, C), F32),
        vmem((12, n_dp, 8, Wd), F32),
        vmem((2, 3, 8, Wd), F32),
        vmem((2, R, C), F32),
        vmem((2, R, C), F32),
        vmem((2, R, Wd), F32),
        vmem((R + 2 * PAD, W9), F32),
        vmem((R + 2 * PAD, C), F32),
        vmem((R, W9), BF16),
        vmem((n_mp, RM, tasks * classes), BF16),
        vmem((n_mp, RM, tasks * classes), BF16),
        vmem((n_mp, RM, tasks * classes), BF16),
        vmem((R, Wd), BF16),
        vmem((tasks, RM, Wd), F32),
        vmem((R, Wd), F32),
        vmem((R, Wd), F32),
        vmem((R, Wd), BF16),
        vmem((2, R, Wd), F32),
        vmem((2, 2, n_mp, R, C), F32),
        vmem((2, R, Wd), F32),
        vmem((2, n_dp, Wd, Cd), BF16),
        vmem((2, n_dp, Cd, W9), BF16),
        vmem((2, n_dp, Cd, Wd), BF16),
        vmem((n_dp, Wd, Cd), BF16),
        vmem((n_dp, Cd, W9), BF16),
        vmem((n_dp, Cd, Wd), BF16),
        vmem((n_dp, Wd, Cd), BF16),
        vmem((n_dp, Cd, W9), BF16),
        vmem((n_dp, Cd, Wd), BF16),
        vmem((n_cls, tasks, piece, Wd), BF16),
        vmem((n_cls, tasks, piece, Wd), BF16),
        vmem((2, 8, Wd), F32),
        vmem((8, Wd), F32),
        vmem((1, Wd, Cd), F32),
        vmem((1, 9, Cd, C), F32),
        vmem((1, Cd, Wd), F32),
        vmem((8, Wd), F32),
        vmem((tasks, piece, Wd), F32),
    ]
    in_vmem = pl.BlockSpec(memory_space=pltpu.VMEM)
    in_any = pl.BlockSpec(memory_space=pl.ANY)
    whole = lambda shape, dtype=F32: jax.ShapeDtypeStruct(shape, dtype)
    out = pl.pallas_call(
        make_kernel(sizes),
        out_shape=(
            whole((1, 2, R, Wd), BF16),
            whole((1, 2, R, Wd)),
            whole((1, Wd, Cd)),
            whole((1, 9, Cd, C)),
            whole((1, Cd, Wd)),
            whole((8, Wd)),
            whole((tasks, piece, Wd)),
        ),
        in_specs=[
            in_any, in_vmem, in_any, in_any, in_any, in_vmem, in_vmem, in_vmem, in_vmem,
            in_any, in_vmem, in_any,
        ],
        out_specs=(in_any,) * 7,
        scratch_shapes=scratch,
        compiler_params=pltpu.CompilerParams(
            collective_id=0, has_side_effects=True, vmem_limit_bytes=60 * 2**20
        ),
    )(*args[:9], jnp.transpose(args[9], (0, 2, 1)), *args[10:])
    part, outer = C // n_dp, Wd // n_dp
    shapes = (
        whole((1, 2, R, Wd), BF16),
        whole((1, 2, R, Wd)),
        whole((1, Wd, Cd)),
        whole((1, 9, Cd, C)),
        whole((1, Cd, Wd)),
        whole((1, 2, 1, part)),
        whole((1, 2, 1, part)),
        whole((1, 1, outer)),
        whole((1, 1, outer)),
        whole((tasks, piece, Wd)),
    )
    done = pl.pallas_call(
        hand_out,
        out_shape=shapes,
        in_specs=[in_any] * 5 + [in_vmem, in_any],
        out_specs=(in_any,) * 5 + (in_vmem,) * 4 + (in_any,),
        scratch_shapes=[pltpu.VMEM(a.shape, a.dtype) for a in shapes[:5] + shapes[9:]]
        + [pltpu.SemaphoreType.DMA((16,)), pltpu.SemaphoreType.DMA((16,))],
    )(*out)
    return done[:9] + (jnp.transpose(done[9], (0, 2, 1)),)


def hand_out(*refs):
    given, outs, held, came, left = refs[:7], refs[7:17], refs[17:23], refs[23], refs[24]
    vec, gains, shifts, gain_out, shift_out = given[5], *outs[5:9]
    pieces = []
    for src, mid, dst in zip(given[:5] + given[6:], held, outs[:5] + outs[9:]):
        for i in range(src.shape[1]) if len(src.shape) == 4 else (None,):
            at = (lambda ref, i=i: ref) if i is None else (lambda ref, i=i: ref.at[0, i])
            n = len(pieces)
            pieces.append((
                pltpu.make_async_copy(at(src), at(mid), came.at[n]),
                pltpu.make_async_copy(at(mid), at(dst), left.at[n]),
            ))
    for fetch, _ in pieces:
        fetch.start()
    d = lax.axis_index("dp")
    part, outer = gains.shape[3], gain_out.shape[2]
    lanes = part * lax.axis_size("dp")
    rolled = pltpu.roll(vec[:, 0:lanes], lax.rem(lanes - d * part, lanes), 1)
    for i in range(2):
        gains[0, i] = rolled[i:i + 1, 0:part]
        shifts[0, i] = rolled[2 + i:3 + i, 0:part]
    mine = pl.ds(pl.multiple_of(d * outer, outer), outer)
    gain_out[0] = vec[4:5, mine]
    shift_out[0] = vec[5:6, mine]
    for fetch, store in pieces:
        fetch.wait()
        store.start()
    for _, store in pieces:
        store.wait()


def per_device(*args):
    block_input, _, w_reduce, w_spatial = args[:4]
    n_dp, n_mp = lax.axis_size("dp"), lax.axis_size("mp")
    R, Wd = block_input.shape[1:]
    Cd, C = w_reduce.shape[2], w_spatial.shape[3]
    tasks, _, piece = args[9].shape
    sizes = (n_dp, n_mp, R, Wd, C * n_mp, C, Cd, piece * 2 * n_dp, tasks, piece)
    whole_tiles = not (C % 128 or Cd % 128 or Wd % 128 or R % 128 or piece % 16 or (R // n_mp) % 32)
    if whole_tiles and C == Cd and block_input.shape[0] == lax.axis_size("section") == 2:
        return fused_device(sizes, *args)
    return plain_device(*args)


def solution(mesh):
    return jax.shard_map(
        per_device,
        mesh=mesh,
        in_specs=(
            P(None, "dp", "mp"),
            P(None, "dp", None),
            P("section", "mp", "dp"),
            P("section", None, "dp", "mp"),
            P("section", "dp", "mp"),
            P("section", None, "mp"),
            P("section", None, "mp"),
            P("section", "mp"),
            P("section", "mp"),
            P(None, "mp", ("section", "dp")),
            P(None, None, "dp"),
            P(None, "dp", "mp"),
        ),
        out_specs=(
            P("section", None, "dp", "mp"),
            P("section", None, "dp", "mp"),
            P("section", "mp", "dp"),
            P("section", None, "dp", "mp"),
            P("section", "dp", "mp"),
            P("section", None, "mp", "dp"),
            P("section", None, "mp", "dp"),
            P("section", "mp", "dp"),
            P("section", "mp", "dp"),
            P(None, "mp", ("section", "dp")),
        ),
        check_vma=False,
    )
```

```python
import math

import jax
import jax.numpy as jnp
from jax import lax
from jax.experimental import pallas as pl
from jax.experimental.pallas import tpu as pltpu
from jax.sharding import PartitionSpec as P

NORM_EPS = 1e-05
LOSS_WEIGHT = 20.0
SIGN_FLOOR = 0.1
KEEP_TEMPER = 0.2


def shifted(value, axis, steps):
    count = lax.axis_size(axis)
    leading, last = (max(0, -steps), min(count, count - steps))
    return lax.ppermute(value, axis, [(source, source + steps) for source in range(leading, last)])


def geometry(img_sides, row_count):
    img_sizes = img_sides * img_sides
    img_ends = jnp.cumsum(img_sizes)
    img_starts = img_ends - img_sizes
    row_pos = jnp.arange(row_count, dtype=jnp.int32)[:, None]
    inside = (row_pos >= img_starts[None, :]) & (row_pos < img_ends[None, :])
    first_row = jnp.sum(jnp.where(inside, img_starts[None, :], 0), axis=1)
    side_len = jnp.sum(jnp.where(inside, img_sides[None, :], 0), axis=1)
    live_rows = jnp.any(inside, axis=1)
    offset = row_pos[:, 0] - first_row
    safe_side = jnp.maximum(side_len, 1)
    row_in = offset // safe_side
    col_in = offset % safe_side
    index_list = []
    valid_list = []
    for row_step in (-1, 0, 1):
        for col_step in (-1, 0, 1):
            new_row = row_in + row_step
            new_col = col_in + col_step
            valid = (
                live_rows
                & (new_row >= 0)
                & (new_row < side_len)
                & (new_col >= 0)
                & (new_col < side_len)
            )
            index_list.append(jnp.where(valid, first_row + new_row * side_len + new_col, 0))
            valid_list.append(valid)
    return (
        jnp.stack(index_list),
        jnp.stack(valid_list).astype(jnp.float32),
        live_rows.astype(jnp.float32),
    )


def smooth_act(values):
    return jax.nn.gelu(values, approximate=True)


def take_block(store, micro_idx):
    return lax.dynamic_index_in_dim(store, micro_idx, 0, keepdims=False)


def put_block(store, update, micro_idx, active):
    previous = take_block(store, micro_idx)
    return lax.dynamic_update_index_in_dim(store, jnp.where(active, update, previous), micro_idx, 0)


def channel_gather(values):
    return lax.all_gather(values, "mp", axis=1, tiled=True)


def channel_sum(values):
    return lax.psum_scatter(values, "mp", scatter_dimension=1, tiled=True)


def norm_stats(values, live_rows):
    masked = values * live_rows[:, None]
    total_sum, live_total = lax.psum((jnp.sum(masked, axis=0), jnp.sum(live_rows)), "dp")
    mean_val = total_sum / live_total
    centered = (values - mean_val) * live_rows[:, None]
    var_val = lax.psum(jnp.sum(centered * centered, axis=0), "dp") / live_total
    return (mean_val, lax.rsqrt(var_val + NORM_EPS), live_total)


def normalize(values, stats, live_rows, gain_vec, shift_vec):
    mean_val, inv_std, live_total = stats
    return live_rows[:, None] * (gain_vec * (values - mean_val) * inv_std + shift_vec)


def norm_backward(values, stats, live_rows, gain_vec, grad_norm):
    mean_val, inv_std, live_total = stats
    normed = (values - mean_val) * inv_std
    grad_live = grad_norm * live_rows[:, None]
    local_shift = jnp.sum(grad_live, axis=0)
    local_gain = jnp.sum(grad_live * normed, axis=0)
    sum_shift, sum_gain = lax.psum((local_shift, local_gain), "dp")
    grad_values = (
        live_rows[:, None]
        * inv_std
        * gain_vec
        * (grad_live - sum_shift / live_total - normed * sum_gain / live_total)
    )
    return (grad_values, local_gain, local_shift)


def gather_taps(values, indices, valids, tap_idx):
    return values[indices[tap_idx]] * valids[tap_idx][:, None].astype(values.dtype)


def act_backward(pre_values, grad_values):
    return jax.vjp(smooth_act, pre_values)[1](grad_values)[0]


def block_forward(x_in, layout, weights):
    indices, valids, live_rows = layout
    w_red, w_spa, w_exp, g_in, s_in, g_out, s_out = weights
    first_pre = channel_sum(jnp.dot(x_in, w_red, preferred_element_type=jnp.float32))
    stats_a = norm_stats(first_pre, live_rows)
    full_a = channel_gather(
        smooth_act(normalize(first_pre, stats_a, live_rows, g_in[0], s_in[0])).astype(jnp.bfloat16)
    )
    second_pre = jnp.zeros((x_in.shape[0], w_spa.shape[2]), jnp.float32)
    for tap_idx in range(9):
        second_pre = second_pre + jnp.dot(
            gather_taps(full_a, indices, valids, tap_idx),
            w_spa[tap_idx],
            preferred_element_type=jnp.float32,
        )
    stats_b = norm_stats(second_pre, live_rows)
    full_b = channel_gather(
        smooth_act(normalize(second_pre, stats_b, live_rows, g_in[1], s_in[1])).astype(jnp.bfloat16)
    )
    third_pre = jnp.dot(full_b, w_exp, preferred_element_type=jnp.float32)
    stats_c = norm_stats(third_pre, live_rows)
    pre_out = normalize(third_pre, stats_c, live_rows, g_out, s_out) + x_in.astype(jnp.float32)
    result = smooth_act(pre_out) * live_rows[:, None]
    return (result, (first_pre, stats_a, full_a, second_pre, stats_b, full_b, third_pre, stats_c))


def block_backward(d_out, x_in, layout, weights, saved_state):
    indices, valids, live_rows = layout
    w_red, w_spa, w_exp, g_in, s_in, g_out, s_out = weights
    first_pre, stats_a, full_a, second_pre, stats_b, full_b, third_pre, stats_c = saved_state
    pre_out = normalize(third_pre, stats_c, live_rows, g_out, s_out) + x_in.astype(jnp.float32)
    d_pre = act_backward(pre_out, d_out * live_rows[:, None])
    d_third, gain_c, shift_c = norm_backward(third_pre, stats_c, live_rows, g_out, d_pre)
    d_third = d_third.astype(jnp.bfloat16)
    grad_exp = jnp.einsum("rc,ro->co", full_b, d_third, preferred_element_type=jnp.float32)
    d_full_b = channel_sum(
        jnp.einsum("ro,co->rc", d_third, w_exp, preferred_element_type=jnp.float32)
    )
    pre_b = normalize(second_pre, stats_b, live_rows, g_in[1], s_in[1])
    d_second, gain_b, shift_b = norm_backward(
        second_pre, stats_b, live_rows, g_in[1], act_backward(pre_b, d_full_b)
    )
    d_second = d_second.astype(jnp.bfloat16)
    grad_spa = []
    back_total = jnp.zeros((x_in.shape[0], w_spa.shape[1]), jnp.float32)
    for tap_idx in range(9):
        grad_spa.append(
            jnp.einsum(
                "rc,ro->co",
                gather_taps(full_a, indices, valids, tap_idx),
                d_second,
                preferred_element_type=jnp.float32,
            )
        )
        spread = jnp.einsum(
            "ro,co->rc", d_second, w_spa[8 - tap_idx], preferred_element_type=jnp.float32
        )
        back_total = back_total + spread[indices[tap_idx]] * valids[tap_idx][:, None]
    d_full_a = channel_sum(back_total)
    pre_a = normalize(first_pre, stats_a, live_rows, g_in[0], s_in[0])
    d_first, gain_a, shift_a = norm_backward(
        first_pre, stats_a, live_rows, g_in[0], act_backward(pre_a, d_full_a)
    )
    d_first_full = channel_gather(d_first.astype(jnp.bfloat16))
    grad_red = jnp.einsum("rc,ro->co", x_in, d_first_full, preferred_element_type=jnp.float32)
    d_in = jnp.einsum("ro,co->rc", d_first_full, w_red, preferred_element_type=jnp.float32) + d_pre
    return (
        d_in,
        (
            grad_red,
            jnp.stack(grad_spa),
            grad_exp,
            jnp.stack([gain_a, gain_b]),
            jnp.stack([shift_a, shift_b]),
            gain_c,
            shift_c,
        ),
    )


def sign_merge(task_grads, thresh):
    soft_abs = jnp.sqrt(task_grads * task_grads + SIGN_FLOOR * SIGN_FLOOR) - SIGN_FLOOR
    purity = 0.5 * (1.0 + jnp.sum(task_grads, axis=0) / (jnp.sum(soft_abs, axis=0) + SIGN_FLOOR))
    keep_frac = jax.nn.sigmoid((purity - thresh) / KEEP_TEMPER)
    upper = 0.5 * jnp.sum(task_grads + soft_abs, axis=0)
    lower = 0.5 * jnp.sum(task_grads - soft_abs, axis=0)
    return keep_frac * upper + (1.0 - keep_frac) * lower


def plain_device(
    block_input,
    image_sides,
    w_reduce,
    w_spatial,
    w_expand,
    gain_inner,
    shift_inner,
    gain_outer,
    shift_outer,
    head_weight,
    labels,
    thresholds,
):
    section_idx = lax.axis_index("section")
    micro_count = block_input.shape[0]
    row_count = block_input.shape[1]
    w_red, w_spa, w_exp = (
        lax.all_gather(w_reduce[0].astype(jnp.bfloat16), "dp", axis=1, tiled=True),
        lax.all_gather(w_spatial[0].astype(jnp.bfloat16), "dp", axis=1, tiled=True),
        lax.all_gather(w_expand[0].astype(jnp.bfloat16), "dp", axis=0, tiled=True),
    )
    weights = (w_red, w_spa, w_exp, gain_inner[0], shift_inner[0], gain_outer[0], shift_outer[0])
    heads_all = lax.all_gather(
        head_weight.astype(jnp.bfloat16), ("section", "dp"), axis=2, tiled=True
    )
    class_total = heads_all.shape[2]
    class_ids = jnp.arange(class_total, dtype=jnp.int32)[None, None, :]

    def layout_for(micro_idx):
        return geometry(take_block(image_sides, micro_idx)[0], row_count)

    received = jnp.zeros(block_input.shape[1:], jnp.bfloat16)
    kept_inputs = jnp.zeros(block_input.shape, jnp.bfloat16)
    activ_store = jnp.zeros(block_input.shape, jnp.bfloat16)
    cotangents = jnp.zeros(block_input.shape, jnp.float32)
    head_grad = jnp.zeros(heads_all.shape, jnp.float32)
    for turn_idx in range(micro_count + 1):
        micro_idx = jnp.clip(turn_idx - section_idx, 0, micro_count - 1)
        active = (turn_idx - section_idx >= 0) & (turn_idx - section_idx < micro_count)
        x_in = jnp.where(section_idx == 0, block_input[min(turn_idx, micro_count - 1)], received)
        layout = layout_for(micro_idx)
        live_rows = layout[2]
        result, saved_state = block_forward(x_in, layout, weights)
        result_low = result.astype(jnp.bfloat16)
        kept_inputs = put_block(kept_inputs, x_in, micro_idx, active)
        activ_store = put_block(activ_store, result_low, micro_idx, active)
        labels_now = lax.dynamic_index_in_dim(labels, micro_idx, 1, keepdims=False)
        logits = lax.psum(
            jnp.einsum("rc,tco->tro", result_low, heads_all, preferred_element_type=jnp.float32),
            "mp",
        )
        peak_val = jnp.max(logits, axis=2, keepdims=True)
        expo = jnp.exp(logits - peak_val)
        soft_p = expo / jnp.sum(expo, axis=2, keepdims=True)
        picked = (class_ids == labels_now[:, :, None]).astype(jnp.float32)
        delta_low = (LOSS_WEIGHT * live_rows[None, :, None] * (soft_p - picked)).astype(
            jnp.bfloat16
        )
        task_grads = jnp.einsum(
            "tro,tco->trc", delta_low, heads_all, preferred_element_type=jnp.float32
        )
        merged = sign_merge(task_grads, take_block(thresholds, micro_idx))
        use_head = active & (section_idx == 1)
        head_grad = head_grad + jnp.where(
            use_head,
            jnp.einsum("rc,tro->tco", result_low, delta_low, preferred_element_type=jnp.float32),
            0.0,
        )
        cotangents = put_block(cotangents, merged, micro_idx, use_head)
        received = shifted(result_low, "section", 1)
    grad_recv = jnp.zeros(block_input.shape[1:], jnp.bfloat16)
    input_store = jnp.zeros(block_input.shape, jnp.float32)
    grad_total = None
    for turn_idx in range(micro_count + 1):
        micro_idx = jnp.clip(turn_idx - 1 + section_idx, 0, micro_count - 1)
        active = (turn_idx - 1 + section_idx >= 0) & (turn_idx - 1 + section_idx < micro_count)
        d_out = jnp.where(
            section_idx == 1, take_block(cotangents, micro_idx), grad_recv.astype(jnp.float32)
        )
        x_in = take_block(kept_inputs, micro_idx)
        layout = layout_for(micro_idx)
        saved_state = block_forward(x_in, layout, weights)[1]
        d_in, grad_set = block_backward(d_out, x_in, layout, weights, saved_state)
        masked = jax.tree.map(lambda leaf: jnp.where(active, leaf, 0.0), grad_set)
        grad_total = masked if grad_total is None else jax.tree.map(jnp.add, grad_total, masked)
        d_send = d_in.astype(jnp.bfloat16)
        input_store = put_block(
            input_store,
            jnp.where(section_idx == 1, d_send.astype(jnp.float32), d_in),
            micro_idx,
            active,
        )
        grad_recv = shifted(d_send, "section", -1)
    g_red, g_spa, g_exp, g_gain_in, g_shift_in, g_gain_out, g_shift_out = grad_total
    out_red, out_spa, out_exp, out_gain_in, out_shift_in, out_gain_out, out_shift_out = (
        lax.psum_scatter(g_red[None], "dp", scatter_dimension=2, tiled=True),
        lax.psum_scatter(g_spa[None], "dp", scatter_dimension=2, tiled=True),
        lax.psum_scatter(g_exp[None], "dp", scatter_dimension=1, tiled=True),
        lax.psum_scatter(g_gain_in[None, :, None, :], "dp", scatter_dimension=3, tiled=True),
        lax.psum_scatter(g_shift_in[None, :, None, :], "dp", scatter_dimension=3, tiled=True),
        lax.psum_scatter(g_gain_out[None, None, :], "dp", scatter_dimension=2, tiled=True),
        lax.psum_scatter(g_shift_out[None, None, :], "dp", scatter_dimension=2, tiled=True),
    )
    head_out = lax.psum_scatter(head_grad, ("section", "dp"), scatter_dimension=2, tiled=True)
    return (
        activ_store[None],
        input_store[None],
        out_red,
        out_spa,
        out_exp,
        out_gain_in,
        out_shift_in,
        out_gain_out,
        out_shift_out,
        head_out,
    )


K0 = math.sqrt(2.0 / math.pi)
K1 = 0.044715
MESH = pl.DeviceIdType.MESH
F32 = jnp.float32
BF16 = jnp.bfloat16
SIDES = (2, 7)
TAPS = [(a, b) for a in (-1, 0, 1) for b in (-1, 0, 1)]
PAD = 8
NN = (((1,), (0,)), ((), ()))
NT = (((1,), (1,)), ((), ()))
TN = (((0,), (0,)), ((), ()))


def tap_masks():
    found = []
    for tap_idx, (a, b) in enumerate(TAPS):
        for side in SIDES:
            found.append((tap_idx, a, b, side, a * side + b))
    return found


MASKS = tap_masks()


def dot(left, right, dims):
    return lax.dot_general(left, right, dims, preferred_element_type=F32)


def gelu(v):
    return 0.5 * v * (1.0 + jnp.tanh(K0 * v * (1.0 + K1 * v * v)))


def gelu_grad(v):
    sq = v * v
    t = jnp.tanh(K0 * v * (1.0 + K1 * sq))
    return 0.5 * (1.0 + t) + (0.5 * K0) * v * (1.0 - t * t) * (1.0 + 3.0 * K1 * sq)


def fold(x):
    return jnp.sum(x.reshape(x.shape[0] // 8, 8, x.shape[1]), axis=0)


def wide(x, width):
    times = width // x.shape[1]
    return x if times == 1 else jnp.concatenate([x] * times, axis=1)


def loop(total, chunk, body, init=None):
    def one(i, carry):
        return body(pl.ds(pl.multiple_of(i * chunk, chunk), chunk), carry)

    return lax.fori_loop(0, total // chunk, one, 0 if init is None else init)


def rows_tile(first, second, third):
    width = first.shape[1]
    place = lax.broadcasted_iota(jnp.int32, (8, width), 0)
    wide_of = lambda v: jnp.broadcast_to(v, (8, width))
    return jnp.where(
        place == 0, wide_of(first), jnp.where(place == 1, wide_of(second), wide_of(third))
    )


class Sems:
    def __init__(self, ref):
        self.ref, self.used, self.size = ref, 0, ref.shape[0]

    def take(self, count=1):
        first = self.used
        self.used += count
        assert self.used <= self.size, self.used
        return first


def make_kernel(sizes):
    n_dp, n_mp, R, Wd, M, C, Cd, classes, tasks, piece = sizes
    n_sec = 2
    W9 = 9 * C

    def kernel(*refs):
        (
            x_hbm, sides_hbm, wred_hbm, wspa_hbm, wexp_hbm, gin_hbm, sin_hbm, gout_hbm, sout_hbm,
            head_hbm, lab_hbm, thr_hbm,
            act_hbm, ig_hbm, red_hbm, spa_hbm, exp_hbm, vec_hbm, head_out,
            ssems, rsems, lsems, go,
            sred, sspa, sexp, shead, thr, xin, wr, wsp, we, hd, par,
            live, geo, masks, labc,
            rs_s, rs_r, ag_a, ag_b, ag_d, fulla, fullb, dfull, co, sums_s, sums_r, sums_t, st, keep, first, second, third, ppad, dpad, dbuf,
            lg_s, lg_r, dl, act1, tg, dpre, evec, dth, ig, slope, steep,
            gred, gspa, gexp, sibred, sibspa, sibexp, rred, rspa, rexp, ghead, rhead, vec, vsib,
            ored, ospa, oexp, ovec, ohead,
            sides_ref, gin_ref, sin_ref, gout_ref, sout_ref, lab_ref,
        ) = refs
        s = lax.axis_index("section")
        d = lax.axis_index("dp")
        m = lax.axis_index("mp")
        o = 1 - s
        recv, local = Sems(rsems), Sems(lsems)
        pending = {None: [], 0: [], 1: []}
        sends = {None: 0, 0: 1, 1: 2}
        rem = lax.rem
        dp_dev = lambda t: (s, t, m)
        mp_dev = lambda t: (s, d, t)
        sib_dev = (o, d, m)

        def put_to(src, dst, ssem, rsem, dev):
            pltpu.make_async_remote_copy(
                src_ref=src,
                dst_ref=dst,
                send_sem=ssems.at[ssem],
                recv_sem=rsems.at[rsem],
                device_id=dev,
                device_id_type=MESH,
            ).start()

        def waiter(ref, ssem, rsem):
            return pltpu.make_async_remote_copy(
                src_ref=ref,
                dst_ref=ref,
                send_sem=ssems.at[ssem],
                recv_sem=rsems.at[rsem],
                device_id=sib_dev,
                device_id_type=MESH,
            )

        def rcopy(src, dst, rsem, dev, when=None):
            ssem = sends[when]
            put_to(src(), dst(), ssem, rsem, dev)
            pending[when].append(lambda: waiter(src(), ssem, 0).wait_send())

        def arrive(dst, rsem):
            waiter(dst, 0, rsem).wait_recv()

        axes = {"dp": (n_dp, d, dp_dev), "mp": (n_mp, m, mp_dev)}
        expected, hold = {}, {}

        def settle(key):
            expected.pop(key)()

        def load(src, dst):
            cp = pltpu.make_async_copy(src, dst, lsems.at[local.take()])
            cp.start()
            key = ("load", local.used)
            expected[key] = cp.wait
            return key

        def on(cond, what):
            return lambda: pl.when(cond())(what)

        class Group:
            def __init__(self, axis, all_of, when=None, slot_of=None):
                self.n, self.me, self.dev = axes[axis]
                self.ssem = sends[when]
                self.rsem = recv.take(1 if slot_of is None else self.n - 1)
                self.all_of, self.when, self.slot_of = all_of, when, slot_of

            def put(self, src_of, slot_of):
                for k in range(1, self.n):
                    t = rem(self.me + k, self.n)
                    rsem = self.rsem + (0 if self.slot_of is None else k - 1)
                    put_to(src_of(t), slot_of(self.me), self.ssem, rsem, self.dev(t))

            def came_from(self, k):
                return rem(self.me + self.n - k, self.n)

            def close(self):
                ssem, all_of, when = self.ssem, self.all_of, self.when
                pending[when].append(lambda: waiter(all_of(), ssem, 0).wait_send())
                if self.slot_of is None:
                    waits = {self.rsem: lambda: arrive(all_of(), self.rsem)}
                else:
                    waits = {
                        self.rsem + k - 1: lambda k=k: arrive(
                            self.slot_of(self.came_from(k)), self.rsem + k - 1
                        )
                        for k in range(1, self.n)
                    }
                for key, wait in waits.items():
                    expected[key] = wait if when is None else on(lambda: s == when, wait)
                return self.rsem

        def spread(axis, src_of, slot_of, all_of, when=None):
            group = Group(axis, all_of, when)
            group.put(src_of, slot_of)
            return group.close()

        barrier = pltpu.get_barrier_semaphore()
        greeted = 0
        for ds_ in range(n_sec):
            for k in range(n_dp):
                if ds_ == 0 and k == 0:
                    continue
                pl.semaphore_signal(
                    barrier, inc=1,
                    device_id=(rem(s + ds_, n_sec), rem(d + k, n_dp), m),
                    device_id_type=MESH,
                )
                greeted += 1
        for k in range(1, n_mp):
            pl.semaphore_signal(
                barrier, inc=1, device_id=(s, d, rem(m + k, n_mp)), device_id_type=MESH
            )
            greeted += 1


        l_red = load(wred_hbm.at[0], sred)
        l_par = [
            load(src, dst)
            for src, dst in (
                (gin_hbm, gin_ref), (sin_hbm, sin_ref), (gout_hbm, gout_ref), (sout_hbm, sout_ref)
            )
        ]
        l_x = load(x_hbm.at[s], xin.at[0])
        l_spa = load(wspa_hbm.at[0], sspa)
        l_exp = load(wexp_hbm.at[0], sexp)
        l_small = [load(sides_hbm, sides_ref), load(lab_hbm, lab_ref)]
        l_head = load(head_hbm, shead)
        l_thr = load(thr_hbm.at[s], thr)

        settle(l_red)
        wr[s, d] = sred[...].astype(BF16)
        for key in l_par:
            settle(key)
        par[s] = jnp.zeros(par.shape[1:], F32)
        for i in range(2):
            par[s, i:i + 1, :C] = gin_ref[0, i:i + 1, :]
            par[s, 2 + i:3 + i, :C] = sin_ref[0, i:i + 1, :]
        par[s, 4:5, :] = gout_ref[...]
        par[s, 5:6, :] = sout_ref[...]
        pl.semaphore_wait(barrier, greeted)

        by_dp, by_sib = {}, {}

        def send_own(buf, j):
            def go():
                by_dp[id(buf), j] = spread(
                    "dp",
                    lambda t: buf.at[j, d],
                    lambda src: buf.at[j, src],
                    lambda: buf.at[j, pl.ds(0, n_dp - 1)],
                    when=j,
                )

            pl.when(s == j)(go)

        def pass_on(buf, j):
            settle(by_dp[id(buf), j])
            sem = by_sib[id(buf), j] = recv.take()

            @pl.when(s == j)
            def _():
                rcopy(lambda: buf.at[j], lambda: buf.at[j], sem, sib_dev, when=j)

            expected[sem] = on(lambda: s != j, lambda: arrive(buf.at[j], sem))

        def from_sib(buf, j):
            settle(by_sib[id(buf), j])

        par_sem = recv.take()
        rcopy(lambda: par.at[s], lambda: par.at[s], par_sem, sib_dev)
        expected[par_sem] = lambda: arrive(par.at[o], par_sem)
        early = Group(
            "dp",
            lambda: wr.at[0, pl.ds(0, n_dp - 1)],
            when=0,
            slot_of=lambda src: wr.at[0, src],
        )

        @pl.when(s == 0)
        def _():
            early.put(lambda t: wr.at[0, d], lambda src: wr.at[0, src])

        early.close()

        settle(l_spa)
        for k in range(9):
            wsp[s, d, :, k * C:(k + 1) * C] = sspa[k].astype(BF16)

        settle(l_exp)
        we[s, d] = sexp[...].astype(BF16)

        for key in l_small:
            settle(key)
        sides = jnp.where(s == 0, sides_ref[0], sides_ref[1]).astype(F32)
        slots = sides.shape[1]
        sq = jnp.broadcast_to(sides * sides, (8, slots)).astype(BF16)
        upper = (
            lax.broadcasted_iota(jnp.int32, (slots, slots), 0)
            <= lax.broadcasted_iota(jnp.int32, (slots, slots), 1)
        ).astype(BF16)
        ends = dot(sq, upper, NN)[0:1]
        starts = ends - sides * sides
        nloc = jnp.broadcast_to(jnp.max(ends, axis=1, keepdims=True), (1, 128))
        shape = (R, 128)
        pos = lax.broadcasted_iota(jnp.int32, (R, slots), 0).astype(F32)
        inside = (pos >= starts) & (pos < ends)
        origin = jnp.sum(jnp.where(inside, starts, 0.0), axis=1, keepdims=True)
        side = jnp.sum(jnp.where(inside, sides, 0.0), axis=1, keepdims=True)
        geo[0] = jnp.broadcast_to(origin, shape)
        geo[1] = jnp.broadcast_to(side, shape)

        def make_masks(rows, carry):
            side_b = geo[1, rows]
            here = lax.broadcasted_iota(jnp.int32, side_b.shape, 0) + rows.start
            offset = here.astype(F32) - geo[0, rows]
            row_in = jnp.floor((offset + 0.5) / jnp.maximum(side_b, 1.0))
            col_in = offset - row_in * side_b
            live[rows] = (side_b > 0.0).astype(F32)
            for idx, (_, a, b, q, _) in enumerate(MASKS):
                ra, cb = row_in + a, col_in + b
                ok = (side_b == q) & (ra >= 0.0) & (ra < q) & (cb >= 0.0) & (cb < q)
                masks[idx, rows] = ok.astype(F32)
            return carry

        loop(R, 64, make_masks)
        for buf in (ppad, dpad):
            edge = jnp.zeros((PAD, buf.shape[1]), F32)
            buf[0:PAD] = edge
            buf[PAD + R:PAD + R + PAD] = edge
        lab2 = lab_ref[...]
        lab = jnp.where(s == 0, lab2[:, 0], lab2[:, 1]).astype(F32)
        lab = jnp.concatenate([lab, jnp.zeros((8 - tasks, R), F32)], axis=0)
        labc[...] = jnp.transpose(lab)

        settle(l_head)
        mine = s * n_dp + d
        for t in range(tasks):
            hd[mine, t] = shead[t].astype(BF16)

        def to_all(src_of, buf):
            ssem, rsem = sends[None], recv.take()
            others = [(a, k) for a in range(n_sec) for k in range(n_dp) if a or k]
            for a, k in others:
                ts, td = rem(s + a, n_sec), rem(d + k, n_dp)
                put_to(src_of(ts * n_dp + td), buf.at[mine], ssem, rsem, (ts, td, m))
            rest = lambda: buf.at[pl.ds(0, len(others))]
            pending[None].append(lambda: waiter(rest(), ssem, 0).wait_send())
            expected[rsem] = lambda: arrive(rest(), rsem)
            return rsem

        def cat(buf, n):
            return jnp.concatenate([buf[i] for i in range(n)], axis=1)

        phase = {"rs": 0, "st": 0}

        def rs_open():
            p = phase["rs"]
            phase["rs"] += 1
            return p, Group("mp", lambda: rs_r.at[p, pl.ds(0, n_mp - 1)])

        def rs_rows(handle, rows, out):
            p, group = handle
            for c in range(n_mp):
                rs_s[p, c, rows] = out[:, c * C:(c + 1) * C].astype(BF16)
            group.put(lambda t: rs_s.at[p, t, rows], lambda src: rs_r.at[p, src, rows])

        def rs_finish(handle, dst):
            p, group = handle
            settle(group.rsem)

            def add(rows, carry):
                dst[rows] = rs_sum(handle, rows)
                return carry

            loop(R, 128, add)

        def exchange(tile):
            p = phase["st"]
            phase["st"] += 1
            width = tile.shape[1]
            st[p, d, :, 0:width] = tile
            slot = lambda src: st.at[p, src, :, 0:width]
            rest = lambda: st.at[p, pl.ds(0, n_dp - 1), :, 0:width]
            return p, width, spread("dp", lambda t: slot(d), slot, rest)

        def collect(handle):
            p, width, base = handle
            settle(base)
            return [st[p, i, :, 0:width] for i in range(n_dp)]

        def stats_start(buf, width, total=None):
            chunk = 128 if width <= 128 else 32
            zero = jnp.zeros((8, width), F32)

            def sum_up(rows, carry):
                return carry + fold(buf[rows] * wide(live[rows], width))

            if total is None:
                total = loop(R, chunk, sum_up, zero)
            total = jnp.sum(total, axis=0, keepdims=True)
            count = wide(nloc, width)
            mean = total / jnp.maximum(count, 1.0)

            def squares(rows, carry):
                off = (buf[rows] - mean) * wide(live[rows], width)
                return carry + fold(off * off)

            sqs = jnp.sum(loop(R, chunk, squares, zero), axis=0, keepdims=True)
            return exchange(rows_tile(total, sqs, count)), mean

        def stats_finish(handle, j, i):
            tiles = collect(handle)
            width = handle[1]
            count = sum(t[2:3] for t in tiles)
            mean = sum(t[0:1] for t in tiles) / count
            sqs = 0.0
            for t in tiles:
                local_mean = t[0:1] / jnp.maximum(t[2:3], 1.0)
                sqs = sqs + t[1:2] + t[2:3] * (local_mean - mean) * (local_mean - mean)
            inv = lax.rsqrt(sqs / count + NORM_EPS)
            keep[j, i, :, 0:width] = rows_tile(mean, inv, count)

        spans = [slice(r0, r0 + 128) for r0 in range(0, R, 128)]

        def rows_out(buf, at, rows, values):
            buf[at, m, rows] = values.astype(BF16)
            return spread(
                "mp",
                lambda t: buf.at[at, m, rows],
                lambda src: buf.at[at, src, rows],
                lambda: buf.at[at, pl.ds(0, n_mp - 1), rows],
            )

        def rs_rows_sums(handle, j, i, rows, out, carry):
            p, groups = handle
            sb, sg = carry
            raw = (ag_a, ag_b)[i]
            for c in range(n_mp):
                part = out[:, c * C:(c + 1) * C]
                rs_s[p, c, rows] = part.astype(BF16)
                tile = co[2 * j + i, c]
                g = part * slope[j, i, c, rows]
                xhat = raw[j, c, rows].astype(F32) * tile[2:3] + tile[3:4]
                sb[c] = sb[c] + fold(g)
                sg[c] = sg[c] + fold(g * xhat)
            if rows is spans[-1]:
                sums = sums_out(p, sb + sg)
            group = Group("mp", lambda: rs_r.at[p, pl.ds(0, n_mp - 1), rows])
            group.put(lambda t: rs_s.at[p, t, rows], lambda src: rs_r.at[p, src, rows])
            groups.append(group.close())
            return sums if rows is spans[-1] else None

        def sums_out(p, parts):
            place = lax.broadcasted_iota(jnp.int32, (2 * n_mp, C), 0)
            tile = jnp.zeros((2 * n_mp, C), F32)
            for i, part in enumerate(parts):
                tile = jnp.where(place == i, jnp.sum(part, axis=0, keepdims=True), tile)
            sums_s[p] = tile
            ssem, rsem = sends[None], recv.take()
            others = [(a, k) for a in range(n_mp) for k in range(n_dp) if a or k]
            me = m * n_dp + d
            for a, k in others:
                tz, td = rem(m + a, n_mp), rem(d + k, n_dp)
                put_to(sums_s.at[p], sums_r.at[p, me], ssem, rsem, (s, td, tz))
            rest = lambda: sums_r.at[p, pl.ds(0, len(others))]
            pending[None].append(lambda: waiter(rest(), ssem, 0).wait_send())
            expected[rsem] = lambda: arrive(rest(), rsem)

            def collect_sums():
                settle(rsem)
                total = sums_s[p]
                for a, k in others:
                    total = total + sums_r[p, rem(m + a, n_mp) * n_dp + rem(d + k, n_dp)]
                sums_t[p] = total
                return total

            return collect_sums

        def rs_parts():
            p = phase["rs"]
            phase["rs"] += 1
            return p, []

        def rs_sum(handle, rows):
            p, _ = handle
            out = rs_s[p, m, rows].astype(F32)
            for k in range(1, n_mp):
                out = out + rs_r[p, rem(m + k, n_mp), rows].astype(F32)
            return out

        def coeffs_out(at, *values):
            place = lax.broadcasted_iota(jnp.int32, (8, C), 0)
            tile = jnp.zeros((8, C), F32)
            for i, v in enumerate(values):
                tile = jnp.where(place == i, jnp.broadcast_to(v, (8, C)), tile)
            co[at, m] = tile
            slot = lambda src: co.at[at, src]
            return spread("mp", lambda t: slot(m), slot, lambda: co.at[at, pl.ds(0, n_mp - 1)])

        def inner_norm(j, i, src, raw, full, hook, need, consume):
            at = 2 * j + i
            handle, mean_here = stats_start(src.at[j], C)
            push = lambda rows: rows_out(raw, j, rows, src[j, rows] - mean_here)
            groups = [push(rows) for rows in spans[:-1]]
            hook()
            stats_finish(handle, j, i)
            mu, inv, _, gain, shift = norm_of(j, i, C)
            moved = (mean_here - mu) * inv
            sent = coeffs_out(at, gain * inv, gain * moved + shift, inv, moved)
            groups.append(push(spans[-1]))
            need()
            settle(sent)
            for rows, group in zip(spans, groups):
                settle(group)
                for c in range(n_mp):
                    tile = co[at, c]
                    y = live[rows] * (raw[j, c, rows].astype(F32) * tile[0:1] + tile[1:2])
                    full[j, rows, c * C:(c + 1) * C] = gelu(y).astype(BF16)
                consume(rows)

        def norm_of(j, i, width):
            tile = keep[j, i, :, 0:width]
            if i < 2:
                gain, shift = par[j, i:i + 1, 0:width], par[j, 2 + i:3 + i, 0:width]
            else:
                gain, shift = par[j, 4:5, 0:width], par[j, 5:6, 0:width]
            return tile[0:1], tile[1:2], tile[2:3], gain, shift

        def taps_sum(src, flip, put):
            for r0 in range(0, R, 128):
                put(r0, lambda idx_list, lanes: sum(
                    masks[(len(MASKS) - 2 - (idx // 2) * 2 + idx % 2) if flip else idx, r0:r0 + 128]
                    * src[
                        PAD + r0 + (-1 if flip else 1) * MASKS[idx][4]:
                        PAD + r0 + (-1 if flip else 1) * MASKS[idx][4] + 128,
                        lanes,
                    ]
                    for idx in idx_list
                ))

        nothing = lambda: None
        vec[...] = jnp.zeros(vec.shape, F32)

        def prepare(j):
            for i, raw in enumerate((ag_a, ag_b)):
                def inner(rows, carry):
                    for c in range(n_mp):
                        tile = co[2 * j + i, c]
                        y = live[rows] * (raw[j, c, rows].astype(F32) * tile[0:1] + tile[1:2])
                        slope[j, i, c, rows] = live[rows] * gelu_grad(y)
                    return carry

                loop(R, 64, inner)
            mu, inv, _, gain, shift = norm_of(j, 2, Wd)

            def outer(rows, carry):
                lv = wide(live[rows], Wd)
                pre = lv * (gain * ((third[j, rows] - mu) * inv) + shift)
                steep[j, rows] = lv * gelu_grad(pre + xin[j, rows].astype(F32))
                return carry

            loop(R, 32, outer)

        def forward(j, h, hooks, needs):
            hooks[0]()
            rs_finish(h, first.at[j])

            def conv(rows):
                there = slice(PAD + rows.start, PAD + rows.stop)
                ppad[there] = dot(fulla[j, rows], wsp[j].reshape(M, W9), NN)

            inner_norm(j, 0, first, ag_a, fulla, hooks[1], needs[0], conv)

            def put(r0, summed):
                second[j, r0:r0 + 128] = sum(
                    summed([2 * k, 2 * k + 1], slice(k * C, (k + 1) * C)) for k in range(9)
                )

            taps_sum(ppad, False, put)
            if j == 0:
                pass_on(wr, 1)
            sums = []

            def expand(rows):
                out = dot(fullb[j, rows], we[j].reshape(M, Wd), NN)
                third[j, rows] = out
                sums.append(fold(out * wide(live[rows], Wd)))

            inner_norm(j, 1, second, ag_b, fullb, hooks[2], needs[1], expand)
            h, _ = stats_start(third.at[j], Wd, sum(sums))
            hooks[3]()
            stats_finish(h, j, 2)
            mu, inv, _, gain, shift = norm_of(j, 2, Wd)
            out = xin.at[1] if j == 0 else act1

            def act_c(rows):
                for r0 in range(rows.start, rows.stop, 32):
                    there = slice(r0, r0 + 32)
                    lv = wide(live[there], Wd)
                    pre = lv * (gain * ((third[j, there] - mu) * inv) + shift)
                    pre = pre + xin[j, there].astype(F32)
                    out[there] = (lv * gelu(pre)).astype(BF16)

            return act_c

        def to_section(src, hbm, j):
            sem = recv.take()

            @pl.when(s == j)
            def _():
                lsem = local.take()
                made = lambda: pltpu.make_async_copy(src(), hbm.at[0, s], lsems.at[lsem])
                made().start()
                pending[j].append(lambda: made().wait())

            @pl.when(s != j)
            def _():
                rcopy(src, lambda: hbm.at[0, s], sem, sib_dev, when=1 - j)

            expected[sem] = on(lambda: s == j, lambda: arrive(hbm.at[0, o], sem))

        grads = ((gred, sibred, rred), (gspa, sibspa, rspa), (gexp, sibexp, rexp))
        at_sib, at_dp = {}, {}

        def grad_to_sib(which, j):
            own, sib, _ = grads[which]
            sem = at_sib[which, j] = recv.take()

            @pl.when(s != j)
            def _():
                rcopy(lambda: own.at[j], lambda: sib, sem, sib_dev, when=1 - j)

            expected[sem] = on(lambda: s == j, lambda: arrive(sib, sem))

        def grad_to_dp(which, j):
            own, sib, got = grads[which]
            settle(at_sib[which, j])

            def go():
                def add(rows, carry):
                    for i in range(n_dp):
                        own[j, i, rows] = (
                            own[j, i, rows].astype(F32) + sib[i, rows].astype(F32)
                        ).astype(BF16)
                    return carry

                loop(own.shape[2], 64, add)
                base = spread(
                    "dp",
                    lambda t: own.at[j, t],
                    lambda src: got.at[src],
                    lambda: got.at[pl.ds(0, n_dp - 1)],
                    when=j,
                )
                at_dp.setdefault(which, []).append(base)

            pl.when(s == j)(go)

        def reduce_to_sib(j):
            for i in range(n_dp):
                full = dfull[j, :, i * Cd:(i + 1) * Cd]
                gred[j, i] = dot(xin[j], full, TN).astype(BF16)
                sem = at_sib[0, j, i] = recv.take()

                @pl.when(s != j)
                def _():
                    rcopy(lambda: gred.at[j, i], lambda: sibred.at[i], sem, sib_dev, when=1 - j)

                expected[sem] = on(
                    lambda: s == j, lambda i=i, sem=sem: arrive(sibred.at[i], sem)
                )

        def reduce_to_dp(j):
            group = Group("dp", lambda: rred.at[pl.ds(0, n_dp - 1)], when=j)
            for i in range(n_dp):
                settle(at_sib[0, j, i])

                @pl.when(s == j)
                def _():
                    def add(rows, carry):
                        gred[j, i, rows] = (
                            gred[j, i, rows].astype(F32) + sibred[i, rows].astype(F32)
                        ).astype(BF16)
                        return carry

                    loop(Wd, 128, add)

                    @pl.when(d != i)
                    def _():
                        put_to(gred.at[j, i], rred.at[d], group.ssem, group.rsem, dp_dev(i))

            at_dp.setdefault(0, []).append(group.close())

        def steepest(j, rows, e, carry):
            mu, inv, _, _, _ = norm_of(j, 2, Wd)
            out = steep[j, rows] * e
            dpre[rows] = out
            return carry[0] + fold(out), carry[1] + fold(out * ((third[j, rows] - mu) * inv))

        def backward(j, sums, hooks):
            mu, inv, count, gain, shift = norm_of(j, 2, Wd)
            sb, sg = sums
            total = lambda v: jnp.sum(v, axis=0, keepdims=True)
            sb, sg = total(sb), total(sg)
            h = exchange(rows_tile(sb, sg, sg))
            hooks[0]()
            tile = sum(collect(h))
            vec[j, 4:5, :] = tile[1:2]
            vec[j, 5:6, :] = tile[0:1]
            sb_n, sg_n = tile[0:1] / count, tile[1:2] / count
            scale = gain * inv

            def d_third(rows, carry):
                lv = wide(live[rows], Wd)
                xhat = (third[j, rows] - mu) * inv
                dth[rows] = (lv * scale * (dpre[rows] - sb_n - xhat * sg_n)).astype(BF16)
                return carry

            none = lambda: ([jnp.zeros((8, C), F32)] * n_mp, [jnp.zeros((8, C), F32)] * n_mp)
            h, carry = rs_parts(), none()
            for rows in spans:
                for r0 in range(rows.start, rows.stop, 32):
                    d_third(slice(r0, r0 + 32), 0)
                out = dot(dth[rows], we[j].reshape(M, Wd), NT)
                sums_of = rs_rows_sums(h, j, 1, rows, out, carry)
            for i in range(n_dp):
                full = fullb[j, :, i * Cd:(i + 1) * Cd]
                gexp[j, i] = dot(full, dth[...], TN).astype(BF16)
            grad_to_sib(2, j)
            hooks[1]()
            for group in h[1]:
                settle(group)

            def norm_sums(i, sums):
                p = sums[0]
                place = lax.broadcasted_iota(jnp.int32, (2 * n_mp, C), 0)
                row = lambda i: jnp.sum(
                    jnp.where(place == i, sums_t[p], 0.0), axis=0, keepdims=True
                )
                sb, sg = row(m), row(n_mp + m)
                vec[j, i:i + 1, 0:C] = sg
                vec[j, 2 + i:3 + i, 0:C] = sb
                return sb, sg

            sums_of()
            sb_b, sg_b = norm_sums(1, h)
            mu_b, inv_b, count_b, gain_b, _ = norm_of(j, 1, C)
            scale_b, sb_b, sg_b = gain_b * inv_b, sb_b / count_b, sg_b / count_b
            for rows in spans:
                there = slice(PAD + rows.start, PAD + rows.stop)
                xhat = (second[j, rows] - mu_b) * inv_b
                g = slope[j, 1, m, rows] * rs_sum(h, rows)
                out = live[rows] * scale_b * (g - sb_b - xhat * sg_b)
                dpad[there] = out.astype(BF16).astype(F32)

            h, carry = rs_parts(), none()
            sums_a = []

            def put(r0, summed):
                for k in range(9):
                    dbuf[r0:r0 + 128, k * C:(k + 1) * C] = summed(
                        [2 * k, 2 * k + 1], slice(None)
                    ).astype(BF16)
                rows = spans[r0 // 128]
                out = dot(dbuf[rows], wsp[j].reshape(M, W9), NT)
                sums_a.append(rs_rows_sums(h, j, 0, rows, out, carry))

            taps_sum(dpad, True, put)
            for i in range(n_dp):
                full = fulla[j, :, i * Cd:(i + 1) * Cd]
                gspa[j, i] = dot(full, dbuf[...], TN).astype(BF16)
            grad_to_sib(1, j)
            grad_to_dp(2, j)
            hooks[2]()
            groups = []
            for rows, part in zip(spans, h[1]):
                settle(part)
                g = slope[j, 0, m, rows] * rs_sum(h, rows)
                if not groups:
                    pivot = jnp.sum(g, axis=0, keepdims=True) / jnp.maximum(
                        jnp.sum(live[rows], axis=0, keepdims=True), 1.0
                    )
                    sent = coeffs_out(4 + j, pivot)
                groups.append(rows_out(ag_d, j, rows, g - pivot))
            hooks[3]()
            grad_to_dp(1, j)

            def d_input(rows):
                out = dot(dfull[j, rows], cat(wr.at[j], n_dp), NT) + dpre[rows]
                if j == 1:
                    out = out.astype(BF16).astype(F32)
                    evec[rows] = out
                ig[j, rows] = out

            sums = sums_a[-1]()
            norm_sums(0, h)
            if j == 0:
                hold["vec"] = recv.take()
                rcopy(lambda: vec.at[o], lambda: vsib, hold["vec"], sib_dev)
                expected[hold["vec"]] = lambda: arrive(vsib, hold["vec"])
            settle(sent)
            count = keep[j, 0, 2:3, 0:C]
            terms = []
            for c in range(n_mp):
                tile = co[2 * j, c]
                sb_n, sg_n = sums[c:c + 1] / count, sums[n_mp + c:n_mp + c + 1] / count
                scale, inv, moved = tile[0:1], tile[2:3], tile[3:4]
                offset = scale * (co[4 + j, c, 0:1] - sb_n - moved * sg_n)
                terms.append((scale, -scale * sg_n * inv, offset))
            for rows, group in zip(spans, groups):
                settle(group)
                for c, (scale, slant, offset) in enumerate(terms):
                    out = live[rows] * (
                        ag_d[j, c, rows].astype(F32) * scale
                        + ag_a[j, c, rows].astype(F32) * slant
                        + offset
                    )
                    dfull[j, rows, c * C:(c + 1) * C] = out.astype(BF16)
                if j == 1:
                    d_input(rows)
            if j == 0:
                reduce_to_sib(j)
                d_input(spans[0])
                d_input(spans[1])
                reduce_to_dp(j)
                for rows in spans[2:]:
                    d_input(rows)
            to_section(lambda: ig.at[j], ig_hbm, j)

        settle(l_x)

        def first_product():
            handle = rs_open()
            p, group = handle
            for k in range(n_dp):
                src = early.came_from(k) if k else d
                if k:
                    settle(early.rsem + k - 1)
                sem = recv.take()

                @pl.when(s == 0)
                def _():
                    rcopy(lambda: wr.at[0, src], lambda: wr.at[0, src], sem, sib_dev, when=0)

                expected[sem] = on(lambda: s != 0, lambda: arrive(wr.at[0, src], sem))
                settle(sem)

                def part(rows, carry):
                    rs_s[p, src, rows] = dot(xin[0, rows], wr[0, src], NN).astype(BF16)
                    return carry

                loop(R, 128, part)

                @pl.when(src != m)
                def _():
                    put_to(rs_s.at[p, src], rs_r.at[p, m], group.ssem, group.rsem, mp_dev(src))

            group.close()
            return handle

        @pl.when(s == 1)
        def _():
            pl.semaphore_wait(go, 1)

        start = first_product()
        settle(par_sem)

        def w_next():
            send_own(we, 0)
            send_own(wr, 1)

        def w_head():
            hold["heads"] = to_all(lambda t: hd.at[mine], hd)

        def f00():
            send_own(wsp, 0)

            @pl.when(s == 0)
            def _():
                pl.semaphore_signal(go, inc=1, device_id=sib_dev, device_id_type=MESH)

        hooks = (f00, w_next, lambda: send_own(wsp, 1), nothing)

        def n00():
            pass_on(wsp, 0)
            from_sib(wsp, 0)

        def n01():
            pass_on(we, 0)
            from_sib(we, 0)

        act_c = forward(0, start, hooks, (n00, n01))
        from_sib(wr, 1)
        start = rs_open()
        for rows in spans:
            act_c(rows)
            rs_rows(start, rows, dot(xin[1, rows], cat(wr.at[1], n_dp), NN))
        start[1].close()

        def f10():
            send_own(we, 1)
            pass_on(wsp, 1)
            to_section(lambda: xin.at[1], act_hbm, 0)
            prepare(0)

        def n10():
            pass_on(we, 1)
            from_sib(wsp, 1)

        hooks = (f10, w_head, nothing, nothing)
        act_c = forward(1, start, hooks, (n10, lambda: from_sib(we, 1)))

        settle(hold["heads"])
        RM = R // n_mp
        n_cls = n_sec * n_dp

        def heads_of(t):
            return hd[:, t].reshape(classes, Wd)

        for c in range(n_mp):
            act_c(slice(c * RM, (c + 1) * RM))
            rows = act1[c * RM:(c + 1) * RM]
            for t in range(tasks):
                lg_s[c, :, t * classes:(t + 1) * classes] = dot(rows, heads_of(t), NT).astype(
                    lg_s.dtype
                )
        base = spread(
            "mp", lambda t: lg_s.at[t], lambda src: lg_r.at[src], lambda: lg_r.at[pl.ds(0, n_mp - 1)]
        )
        to_section(lambda: act1, act_hbm, 1)
        settle(l_thr)
        prepare(1)
        settle(base)
        here = pl.ds(pl.multiple_of(m * RM, RM), RM)
        lv = wide(live[here], classes)
        for t in range(tasks):
            lanes = slice(t * classes, (t + 1) * classes)
            logit = lg_s[m, :, lanes].astype(F32)
            for k in range(1, n_mp):
                logit = logit + lg_r[rem(m + k, n_mp), :, lanes].astype(F32)
            expo = jnp.exp(logit - jnp.max(logit, axis=1, keepdims=True))
            soft = expo / jnp.sum(expo, axis=1, keepdims=True)
            ids = lax.broadcasted_iota(jnp.int32, (RM, classes), 1).astype(F32)
            hot = (ids == labc[here, t:t + 1]).astype(F32)
            dl[m, :, lanes] = (LOSS_WEIGHT * lv * (soft - hot)).astype(BF16)
        group = Group(
            "mp", lambda: dl.at[pl.ds(0, n_mp - 1)], slot_of=lambda src: dl.at[src]
        )
        group.put(lambda t: dl.at[m], lambda src: dl.at[src])
        group.close()

        def merge_block(c, sums):
            for t in range(tasks):
                lanes = slice(t * classes, (t + 1) * classes)
                tg[t] = dot(dl[c, :, lanes], heads_of(t), NN)

            def merge(rows, carry):
                total = soft_sum = None
                for t in range(tasks):
                    g = tg[t, rows]
                    soft = jnp.sqrt(g * g + SIGN_FLOOR * SIGN_FLOOR) - SIGN_FLOOR
                    total = g if t == 0 else total + g
                    soft_sum = soft if t == 0 else soft_sum + soft
                purity = 0.5 * (1.0 + total / (soft_sum + SIGN_FLOOR))
                start = pl.multiple_of(rows.start + c * RM, 32)
                there = pl.ds(start, 32)
                frac = 1.0 / (1.0 + jnp.exp((thr[there] - purity) * (1.0 / KEEP_TEMPER)))
                upper, lower = 0.5 * (total + soft_sum), 0.5 * (total - soft_sum)
                return steepest(1, there, frac * upper + (1.0 - frac) * lower, carry)

            return loop(RM, 32, merge, sums)

        zero = (jnp.zeros((8, Wd), F32), jnp.zeros((8, Wd), F32))
        sums = merge_block(m, zero)
        for k in [1] + list(range(n_mp - 1, 1, -1)):
            settle(group.rsem + k - 1)
            sums = merge_block(group.came_from(k), sums)

        def b10():
            for t in range(tasks):
                lanes = slice(t * classes, (t + 1) * classes)
                delta = dl[:, :, lanes].reshape(R, classes)
                out = dot(delta, act1[...], TN).astype(BF16)
                ghead[:, t] = out.reshape(n_cls, piece, Wd)
            hold["ghead"] = to_all(lambda t: ghead.at[t], rhead)

        backward(1, sums, (nothing, b10, nothing, nothing))
        sums = loop(R, 32, lambda rows, carry: steepest(0, rows, evec[rows], carry), zero)

        backward(0, sums, (lambda: reduce_to_sib(1), lambda: reduce_to_dp(1), nothing, nothing))

        settle(hold["ghead"])
        for t in range(tasks):
            total = ghead[mine, t].astype(F32)
            for k in range(1, n_cls):
                total = total + rhead[rem(mine + k, n_cls), t].astype(F32)
            ohead[t] = total
        load(ohead, head_out)
        settle(hold["vec"])
        ovec[...] = vec[s] + vsib[...]
        load(ovec, vec_hbm)

        def total_of(own, got, rows):
            out = own[s, d, rows].astype(F32)
            for k in range(1, n_dp):
                out = out + got[rem(d + k, n_dp), rows].astype(F32)
            return out

        def finish_grad(which):
            own, _, got = grads[which]
            for key in at_dp[which]:
                settle(key)

            def finish(rows, carry):
                out = total_of(own, got, rows)
                if which == 1:
                    for k in range(9):
                        ospa[0, k, rows] = out[:, k * C:(k + 1) * C]
                else:
                    (ored if which == 0 else oexp)[0, rows] = out
                return carry

            loop(own.shape[2], 64, finish)
            load((ored, ospa, oexp)[which], (red_hbm, spa_hbm, exp_hbm)[which])

        finish_grad(2)
        finish_grad(1)
        finish_grad(0)
        for key in list(expected):
            settle(key)

        for key, waits in pending.items():
            def finish_all(waits=waits):
                for wait in waits:
                    wait()

            if key is None:
                finish_all()
            else:
                pl.when(s == key)(finish_all)

    return kernel


def fused_device(sizes, *args):
    n_dp, n_mp, R, Wd, M, C, Cd, classes, tasks, piece = sizes
    W9, n_cls = 9 * C, 2 * n_dp
    RM = R // n_mp
    vmem = lambda shape, dtype: pltpu.VMEM(shape, dtype)
    scratch = [
        pltpu.SemaphoreType.DMA((3,)),
        pltpu.SemaphoreType.DMA((97,)),
        pltpu.SemaphoreType.DMA((21,)),
        pltpu.SemaphoreType.REGULAR,
        vmem((Wd, Cd), F32),
        vmem((9, Cd, C), F32),
        vmem((Cd, Wd), F32),
        vmem((tasks, piece, Wd), F32),
        vmem((R, Wd), F32),
        vmem((2, R, Wd), BF16),
        vmem((2, n_dp, Wd, Cd), BF16),
        vmem((2, n_dp, Cd, W9), BF16),
        vmem((2, n_dp, Cd, Wd), BF16),
        vmem((n_cls, tasks, piece, Wd), BF16),
        vmem((2, 8, Wd), F32),
        vmem((R, 128), F32),
        vmem((2, R, 128), F32),
        vmem((len(MASKS), R, 128), F32),
        vmem((R, 8), F32),
        vmem((6, n_mp, R, C), BF16),
        vmem((6, n_mp, R, C), BF16),
        vmem((2, n_mp, R, C), BF16),
        vmem((2, n_mp, R, C), BF16),
        vmem((2, n_mp, R, C), BF16),
        vmem((2, R, M), BF16),
        vmem((2, R, M), BF16),
        vmem((2, R, M), BF16),
        vmem((6, n_mp, 8, C), F32),
        vmem((6, 2 * n_mp, C), F32),
        vmem((6, n_mp * n_dp, 2 * n_mp, C), F32),
        vmem((6, 2 * n_mp, C), F32),
        vmem((12, n_dp, 8, Wd), F32),
        vmem((2, 3, 8, Wd), F32),
        vmem((2, R, C), F32),
        vmem((2, R, C), F32),
        vmem((2, R, Wd), F32),
        vmem((R + 2 * PAD, W9), F32),
        vmem((R + 2 * PAD, C), F32),
        vmem((R, W9), BF16),
        vmem((n_mp, RM, tasks * classes), BF16),
        vmem((n_mp, RM, tasks * classes), BF16),
        vmem((n_mp, RM, tasks * classes), BF16),
        vmem((R, Wd), BF16),
        vmem((tasks, RM, Wd), F32),
        vmem((R, Wd), F32),
        vmem((R, Wd), F32),
        vmem((R, Wd), BF16),
        vmem((2, R, Wd), F32),
        vmem((2, 2, n_mp, R, C), F32),
        vmem((2, R, Wd), F32),
        vmem((2, n_dp, Wd, Cd), BF16),
        vmem((2, n_dp, Cd, W9), BF16),
        vmem((2, n_dp, Cd, Wd), BF16),
        vmem((n_dp, Wd, Cd), BF16),
        vmem((n_dp, Cd, W9), BF16),
        vmem((n_dp, Cd, Wd), BF16),
        vmem((n_dp, Wd, Cd), BF16),
        vmem((n_dp, Cd, W9), BF16),
        vmem((n_dp, Cd, Wd), BF16),
        vmem((n_cls, tasks, piece, Wd), BF16),
        vmem((n_cls, tasks, piece, Wd), BF16),
        vmem((2, 8, Wd), F32),
        vmem((8, Wd), F32),
        vmem((1, Wd, Cd), F32),
        vmem((1, 9, Cd, C), F32),
        vmem((1, Cd, Wd), F32),
        vmem((8, Wd), F32),
        vmem((tasks, piece, Wd), F32),
    ] + [vmem(args[i].shape, args[i].dtype) for i in (1, 5, 6, 7, 8, 10)]
    in_any = pl.BlockSpec(memory_space=pl.ANY)
    whole = lambda shape, dtype=F32: jax.ShapeDtypeStruct(shape, dtype)
    out = pl.pallas_call(
        make_kernel(sizes),
        out_shape=(
            whole((1, 2, R, Wd), BF16),
            whole((1, 2, R, Wd)),
            whole((1, Wd, Cd)),
            whole((1, 9, Cd, C)),
            whole((1, Cd, Wd)),
            whole((8, Wd)),
            whole((tasks, piece, Wd)),
        ),
        in_specs=[in_any] * len(args),
        out_specs=(in_any,) * 7,
        scratch_shapes=scratch,
        compiler_params=pltpu.CompilerParams(
            collective_id=0, has_side_effects=True, vmem_limit_bytes=60 * 2**20
        ),
    )(*args[:9], jnp.transpose(args[9], (0, 2, 1)), *args[10:])
    part, outer = C // n_dp, Wd // n_dp
    shapes = (
        whole((1, 2, R, Wd), BF16),
        whole((1, 2, R, Wd)),
        whole((1, Wd, Cd)),
        whole((1, 9, Cd, C)),
        whole((1, Cd, Wd)),
        whole((1, 2, 1, part)),
        whole((1, 2, 1, part)),
        whole((1, 1, outer)),
        whole((1, 1, outer)),
        whole((tasks, piece, Wd)),
    )
    done = pl.pallas_call(
        hand_out,
        out_shape=shapes,
        in_specs=[in_any] * 7,
        out_specs=(in_any,) * 10,
        scratch_shapes=[pltpu.VMEM(a.shape, a.dtype) for a in shapes]
        + [vmem((8, Wd), F32), pltpu.SemaphoreType.DMA((9,)), pltpu.SemaphoreType.DMA((12,))],
    )(*out)
    return done[:9] + (jnp.transpose(done[9], (0, 2, 1)),)


def hand_out(*refs):
    given, outs, held, vec, came, left = refs[:7], refs[7:17], refs[17:27], *refs[27:]
    gains, shifts, gain_out, shift_out = held[5:9]
    load_vec = pltpu.make_async_copy(given[5], vec, came.at[8])
    load_vec.start()
    pieces = []
    for src, mid, dst in zip(given[:5] + given[6:], held[:5] + held[9:], outs[:5] + outs[9:]):
        for i in range(src.shape[1]) if src.shape[1] == 2 else (None,):
            at = (lambda ref, i=i: ref) if i is None else (lambda ref, i=i: ref.at[0, i])
            n = len(pieces)
            pieces.append((
                pltpu.make_async_copy(at(src), at(mid), came.at[n]),
                pltpu.make_async_copy(at(mid), at(dst), left.at[n]),
            ))
    for fetch, _ in pieces:
        fetch.start()
    d = lax.axis_index("dp")
    part, outer = gains.shape[3], gain_out.shape[2]
    lanes = part * lax.axis_size("dp")
    load_vec.wait()
    rolled = pltpu.roll(vec[:, 0:lanes], lax.rem(lanes - d * part, lanes), 1)
    for i in range(2):
        gains[0, i] = rolled[i:i + 1, 0:part]
        shifts[0, i] = rolled[2 + i:3 + i, 0:part]
    mine = pl.ds(pl.multiple_of(d * outer, outer), outer)
    gain_out[0] = vec[4:5, mine]
    shift_out[0] = vec[5:6, mine]
    stores = [
        pltpu.make_async_copy(held[i], outs[i], left.at[len(pieces) + i - 5]) for i in range(5, 9)
    ]
    for store in stores:
        store.start()
    for fetch, store in pieces:
        fetch.wait()
        store.start()
    for store in stores + [store for _, store in pieces]:
        store.wait()


def per_device(*args):
    block_input, _, w_reduce, w_spatial = args[:4]
    n_dp, n_mp = lax.axis_size("dp"), lax.axis_size("mp")
    R, Wd = block_input.shape[1:]
    Cd, C = w_reduce.shape[2], w_spatial.shape[3]
    tasks, _, piece = args[9].shape
    sizes = (n_dp, n_mp, R, Wd, C * n_mp, C, Cd, piece * 2 * n_dp, tasks, piece)
    whole_tiles = not (C % 128 or Cd % 128 or Wd % 128 or R % 128 or piece % 16 or (R // n_mp) % 32)
    if whole_tiles and C == Cd and block_input.shape[0] == lax.axis_size("section") == 2:
        return fused_device(sizes, *args)
    return plain_device(*args)


def solution(mesh):
    return jax.shard_map(
        per_device,
        mesh=mesh,
        in_specs=(
            P(None, "dp", "mp"),
            P(None, "dp", None),
            P("section", "mp", "dp"),
            P("section", None, "dp", "mp"),
            P("section", "dp", "mp"),
            P("section", None, "mp"),
            P("section", None, "mp"),
            P("section", "mp"),
            P("section", "mp"),
            P(None, "mp", ("section", "dp")),
            P(None, None, "dp"),
            P(None, "dp", "mp"),
        ),
        out_specs=(
            P("section", None, "dp", "mp"),
            P("section", None, "dp", "mp"),
            P("section", "mp", "dp"),
            P("section", None, "dp", "mp"),
            P("section", "dp", "mp"),
            P("section", None, "mp", "dp"),
            P("section", None, "mp", "dp"),
            P("section", "mp", "dp"),
            P("section", "mp", "dp"),
            P(None, "mp", ("section", "dp")),
        ),
        check_vma=False,
    )
```

```python
import math

import jax
import jax.numpy as jnp
from jax import lax
from jax.experimental import pallas as pl
from jax.experimental.pallas import tpu as pltpu
from jax.sharding import PartitionSpec as P

NORM_EPS = 1e-05
LOSS_WEIGHT = 20.0
SIGN_FLOOR = 0.1
KEEP_TEMPER = 0.2


def shifted(value, axis, steps):
    count = lax.axis_size(axis)
    leading, last = (max(0, -steps), min(count, count - steps))
    return lax.ppermute(value, axis, [(source, source + steps) for source in range(leading, last)])


def geometry(img_sides, row_count):
    img_sizes = img_sides * img_sides
    img_ends = jnp.cumsum(img_sizes)
    img_starts = img_ends - img_sizes
    row_pos = jnp.arange(row_count, dtype=jnp.int32)[:, None]
    inside = (row_pos >= img_starts[None, :]) & (row_pos < img_ends[None, :])
    first_row = jnp.sum(jnp.where(inside, img_starts[None, :], 0), axis=1)
    side_len = jnp.sum(jnp.where(inside, img_sides[None, :], 0), axis=1)
    live_rows = jnp.any(inside, axis=1)
    offset = row_pos[:, 0] - first_row
    safe_side = jnp.maximum(side_len, 1)
    row_in = offset // safe_side
    col_in = offset % safe_side
    index_list = []
    valid_list = []
    for row_step in (-1, 0, 1):
        for col_step in (-1, 0, 1):
            new_row = row_in + row_step
            new_col = col_in + col_step
            valid = (
                live_rows
                & (new_row >= 0)
                & (new_row < side_len)
                & (new_col >= 0)
                & (new_col < side_len)
            )
            index_list.append(jnp.where(valid, first_row + new_row * side_len + new_col, 0))
            valid_list.append(valid)
    return (
        jnp.stack(index_list),
        jnp.stack(valid_list).astype(jnp.float32),
        live_rows.astype(jnp.float32),
    )


def smooth_act(values):
    return jax.nn.gelu(values, approximate=True)


def take_block(store, micro_idx):
    return lax.dynamic_index_in_dim(store, micro_idx, 0, keepdims=False)


def put_block(store, update, micro_idx, active):
    previous = take_block(store, micro_idx)
    return lax.dynamic_update_index_in_dim(store, jnp.where(active, update, previous), micro_idx, 0)


def channel_gather(values):
    return lax.all_gather(values, "mp", axis=1, tiled=True)


def channel_sum(values):
    return lax.psum_scatter(values, "mp", scatter_dimension=1, tiled=True)


def norm_stats(values, live_rows):
    masked = values * live_rows[:, None]
    total_sum, live_total = lax.psum((jnp.sum(masked, axis=0), jnp.sum(live_rows)), "dp")
    mean_val = total_sum / live_total
    centered = (values - mean_val) * live_rows[:, None]
    var_val = lax.psum(jnp.sum(centered * centered, axis=0), "dp") / live_total
    return (mean_val, lax.rsqrt(var_val + NORM_EPS), live_total)


def normalize(values, stats, live_rows, gain_vec, shift_vec):
    mean_val, inv_std, live_total = stats
    return live_rows[:, None] * (gain_vec * (values - mean_val) * inv_std + shift_vec)


def norm_backward(values, stats, live_rows, gain_vec, grad_norm):
    mean_val, inv_std, live_total = stats
    normed = (values - mean_val) * inv_std
    grad_live = grad_norm * live_rows[:, None]
    local_shift = jnp.sum(grad_live, axis=0)
    local_gain = jnp.sum(grad_live * normed, axis=0)
    sum_shift, sum_gain = lax.psum((local_shift, local_gain), "dp")
    grad_values = (
        live_rows[:, None]
        * inv_std
        * gain_vec
        * (grad_live - sum_shift / live_total - normed * sum_gain / live_total)
    )
    return (grad_values, local_gain, local_shift)


def gather_taps(values, indices, valids, tap_idx):
    return values[indices[tap_idx]] * valids[tap_idx][:, None].astype(values.dtype)


def act_backward(pre_values, grad_values):
    return jax.vjp(smooth_act, pre_values)[1](grad_values)[0]


def block_forward(x_in, layout, weights):
    indices, valids, live_rows = layout
    w_red, w_spa, w_exp, g_in, s_in, g_out, s_out = weights
    first_pre = channel_sum(jnp.dot(x_in, w_red, preferred_element_type=jnp.float32))
    stats_a = norm_stats(first_pre, live_rows)
    full_a = channel_gather(
        smooth_act(normalize(first_pre, stats_a, live_rows, g_in[0], s_in[0])).astype(jnp.bfloat16)
    )
    second_pre = jnp.zeros((x_in.shape[0], w_spa.shape[2]), jnp.float32)
    for tap_idx in range(9):
        second_pre = second_pre + jnp.dot(
            gather_taps(full_a, indices, valids, tap_idx),
            w_spa[tap_idx],
            preferred_element_type=jnp.float32,
        )
    stats_b = norm_stats(second_pre, live_rows)
    full_b = channel_gather(
        smooth_act(normalize(second_pre, stats_b, live_rows, g_in[1], s_in[1])).astype(jnp.bfloat16)
    )
    third_pre = jnp.dot(full_b, w_exp, preferred_element_type=jnp.float32)
    stats_c = norm_stats(third_pre, live_rows)
    pre_out = normalize(third_pre, stats_c, live_rows, g_out, s_out) + x_in.astype(jnp.float32)
    result = smooth_act(pre_out) * live_rows[:, None]
    return (result, (first_pre, stats_a, full_a, second_pre, stats_b, full_b, third_pre, stats_c))


def block_backward(d_out, x_in, layout, weights, saved_state):
    indices, valids, live_rows = layout
    w_red, w_spa, w_exp, g_in, s_in, g_out, s_out = weights
    first_pre, stats_a, full_a, second_pre, stats_b, full_b, third_pre, stats_c = saved_state
    pre_out = normalize(third_pre, stats_c, live_rows, g_out, s_out) + x_in.astype(jnp.float32)
    d_pre = act_backward(pre_out, d_out * live_rows[:, None])
    d_third, gain_c, shift_c = norm_backward(third_pre, stats_c, live_rows, g_out, d_pre)
    d_third = d_third.astype(jnp.bfloat16)
    grad_exp = jnp.einsum("rc,ro->co", full_b, d_third, preferred_element_type=jnp.float32)
    d_full_b = channel_sum(
        jnp.einsum("ro,co->rc", d_third, w_exp, preferred_element_type=jnp.float32)
    )
    pre_b = normalize(second_pre, stats_b, live_rows, g_in[1], s_in[1])
    d_second, gain_b, shift_b = norm_backward(
        second_pre, stats_b, live_rows, g_in[1], act_backward(pre_b, d_full_b)
    )
    d_second = d_second.astype(jnp.bfloat16)
    grad_spa = []
    back_total = jnp.zeros((x_in.shape[0], w_spa.shape[1]), jnp.float32)
    for tap_idx in range(9):
        grad_spa.append(
            jnp.einsum(
                "rc,ro->co",
                gather_taps(full_a, indices, valids, tap_idx),
                d_second,
                preferred_element_type=jnp.float32,
            )
        )
        spread = jnp.einsum(
            "ro,co->rc", d_second, w_spa[8 - tap_idx], preferred_element_type=jnp.float32
        )
        back_total = back_total + spread[indices[tap_idx]] * valids[tap_idx][:, None]
    d_full_a = channel_sum(back_total)
    pre_a = normalize(first_pre, stats_a, live_rows, g_in[0], s_in[0])
    d_first, gain_a, shift_a = norm_backward(
        first_pre, stats_a, live_rows, g_in[0], act_backward(pre_a, d_full_a)
    )
    d_first_full = channel_gather(d_first.astype(jnp.bfloat16))
    grad_red = jnp.einsum("rc,ro->co", x_in, d_first_full, preferred_element_type=jnp.float32)
    d_in = jnp.einsum("ro,co->rc", d_first_full, w_red, preferred_element_type=jnp.float32) + d_pre
    return (
        d_in,
        (
            grad_red,
            jnp.stack(grad_spa),
            grad_exp,
            jnp.stack([gain_a, gain_b]),
            jnp.stack([shift_a, shift_b]),
            gain_c,
            shift_c,
        ),
    )


def sign_merge(task_grads, thresh):
    soft_abs = jnp.sqrt(task_grads * task_grads + SIGN_FLOOR * SIGN_FLOOR) - SIGN_FLOOR
    purity = 0.5 * (1.0 + jnp.sum(task_grads, axis=0) / (jnp.sum(soft_abs, axis=0) + SIGN_FLOOR))
    keep_frac = jax.nn.sigmoid((purity - thresh) / KEEP_TEMPER)
    upper = 0.5 * jnp.sum(task_grads + soft_abs, axis=0)
    lower = 0.5 * jnp.sum(task_grads - soft_abs, axis=0)
    return keep_frac * upper + (1.0 - keep_frac) * lower


def plain_device(
    block_input,
    image_sides,
    w_reduce,
    w_spatial,
    w_expand,
    gain_inner,
    shift_inner,
    gain_outer,
    shift_outer,
    head_weight,
    labels,
    thresholds,
):
    section_idx = lax.axis_index("section")
    micro_count = block_input.shape[0]
    row_count = block_input.shape[1]
    w_red, w_spa, w_exp = (
        lax.all_gather(w_reduce[0].astype(jnp.bfloat16), "dp", axis=1, tiled=True),
        lax.all_gather(w_spatial[0].astype(jnp.bfloat16), "dp", axis=1, tiled=True),
        lax.all_gather(w_expand[0].astype(jnp.bfloat16), "dp", axis=0, tiled=True),
    )
    weights = (w_red, w_spa, w_exp, gain_inner[0], shift_inner[0], gain_outer[0], shift_outer[0])
    heads_all = lax.all_gather(
        head_weight.astype(jnp.bfloat16), ("section", "dp"), axis=2, tiled=True
    )
    class_total = heads_all.shape[2]
    class_ids = jnp.arange(class_total, dtype=jnp.int32)[None, None, :]

    def layout_for(micro_idx):
        return geometry(take_block(image_sides, micro_idx)[0], row_count)

    received = jnp.zeros(block_input.shape[1:], jnp.bfloat16)
    kept_inputs = jnp.zeros(block_input.shape, jnp.bfloat16)
    activ_store = jnp.zeros(block_input.shape, jnp.bfloat16)
    cotangents = jnp.zeros(block_input.shape, jnp.float32)
    head_grad = jnp.zeros(heads_all.shape, jnp.float32)
    for turn_idx in range(micro_count + 1):
        micro_idx = jnp.clip(turn_idx - section_idx, 0, micro_count - 1)
        active = (turn_idx - section_idx >= 0) & (turn_idx - section_idx < micro_count)
        x_in = jnp.where(section_idx == 0, block_input[min(turn_idx, micro_count - 1)], received)
        layout = layout_for(micro_idx)
        live_rows = layout[2]
        result, saved_state = block_forward(x_in, layout, weights)
        result_low = result.astype(jnp.bfloat16)
        kept_inputs = put_block(kept_inputs, x_in, micro_idx, active)
        activ_store = put_block(activ_store, result_low, micro_idx, active)
        labels_now = lax.dynamic_index_in_dim(labels, micro_idx, 1, keepdims=False)
        logits = lax.psum(
            jnp.einsum("rc,tco->tro", result_low, heads_all, preferred_element_type=jnp.float32),
            "mp",
        )
        peak_val = jnp.max(logits, axis=2, keepdims=True)
        expo = jnp.exp(logits - peak_val)
        soft_p = expo / jnp.sum(expo, axis=2, keepdims=True)
        picked = (class_ids == labels_now[:, :, None]).astype(jnp.float32)
        delta_low = (LOSS_WEIGHT * live_rows[None, :, None] * (soft_p - picked)).astype(
            jnp.bfloat16
        )
        task_grads = jnp.einsum(
            "tro,tco->trc", delta_low, heads_all, preferred_element_type=jnp.float32
        )
        merged = sign_merge(task_grads, take_block(thresholds, micro_idx))
        use_head = active & (section_idx == 1)
        head_grad = head_grad + jnp.where(
            use_head,
            jnp.einsum("rc,tro->tco", result_low, delta_low, preferred_element_type=jnp.float32),
            0.0,
        )
        cotangents = put_block(cotangents, merged, micro_idx, use_head)
        received = shifted(result_low, "section", 1)
    grad_recv = jnp.zeros(block_input.shape[1:], jnp.bfloat16)
    input_store = jnp.zeros(block_input.shape, jnp.float32)
    grad_total = None
    for turn_idx in range(micro_count + 1):
        micro_idx = jnp.clip(turn_idx - 1 + section_idx, 0, micro_count - 1)
        active = (turn_idx - 1 + section_idx >= 0) & (turn_idx - 1 + section_idx < micro_count)
        d_out = jnp.where(
            section_idx == 1, take_block(cotangents, micro_idx), grad_recv.astype(jnp.float32)
        )
        x_in = take_block(kept_inputs, micro_idx)
        layout = layout_for(micro_idx)
        saved_state = block_forward(x_in, layout, weights)[1]
        d_in, grad_set = block_backward(d_out, x_in, layout, weights, saved_state)
        masked = jax.tree.map(lambda leaf: jnp.where(active, leaf, 0.0), grad_set)
        grad_total = masked if grad_total is None else jax.tree.map(jnp.add, grad_total, masked)
        d_send = d_in.astype(jnp.bfloat16)
        input_store = put_block(
            input_store,
            jnp.where(section_idx == 1, d_send.astype(jnp.float32), d_in),
            micro_idx,
            active,
        )
        grad_recv = shifted(d_send, "section", -1)
    g_red, g_spa, g_exp, g_gain_in, g_shift_in, g_gain_out, g_shift_out = grad_total
    out_red, out_spa, out_exp, out_gain_in, out_shift_in, out_gain_out, out_shift_out = (
        lax.psum_scatter(g_red[None], "dp", scatter_dimension=2, tiled=True),
        lax.psum_scatter(g_spa[None], "dp", scatter_dimension=2, tiled=True),
        lax.psum_scatter(g_exp[None], "dp", scatter_dimension=1, tiled=True),
        lax.psum_scatter(g_gain_in[None, :, None, :], "dp", scatter_dimension=3, tiled=True),
        lax.psum_scatter(g_shift_in[None, :, None, :], "dp", scatter_dimension=3, tiled=True),
        lax.psum_scatter(g_gain_out[None, None, :], "dp", scatter_dimension=2, tiled=True),
        lax.psum_scatter(g_shift_out[None, None, :], "dp", scatter_dimension=2, tiled=True),
    )
    head_out = lax.psum_scatter(head_grad, ("section", "dp"), scatter_dimension=2, tiled=True)
    return (
        activ_store[None],
        input_store[None],
        out_red,
        out_spa,
        out_exp,
        out_gain_in,
        out_shift_in,
        out_gain_out,
        out_shift_out,
        head_out,
    )


K0 = math.sqrt(2.0 / math.pi)
K1 = 0.044715
MESH = pl.DeviceIdType.MESH
F32 = jnp.float32
BF16 = jnp.bfloat16
SIDES = (2, 7)
TAPS = [(a, b) for a in (-1, 0, 1) for b in (-1, 0, 1)]
PAD = 8
NN = (((1,), (0,)), ((), ()))
NT = (((1,), (1,)), ((), ()))
TN = (((0,), (0,)), ((), ()))


def tap_masks():
    found = []
    for tap_idx, (a, b) in enumerate(TAPS):
        for side in SIDES:
            found.append((tap_idx, a, b, side, a * side + b))
    return found


MASKS = tap_masks()


def dot(left, right, dims):
    return lax.dot_general(left, right, dims, preferred_element_type=F32)


def gelu(v):
    return 0.5 * v * (1.0 + jnp.tanh(K0 * v * (1.0 + K1 * v * v)))


def gelu_grad(v):
    sq = v * v
    t = jnp.tanh(K0 * v * (1.0 + K1 * sq))
    return 0.5 * (1.0 + t) + (0.5 * K0) * v * (1.0 - t * t) * (1.0 + 3.0 * K1 * sq)


def fold(x):
    return jnp.sum(x.reshape(x.shape[0] // 8, 8, x.shape[1]), axis=0)


def wide(x, width):
    times = width // x.shape[1]
    return x if times == 1 else jnp.concatenate([x] * times, axis=1)


def loop(total, chunk, body, init=None):
    def one(i, carry):
        return body(pl.ds(pl.multiple_of(i * chunk, chunk), chunk), carry)

    return lax.fori_loop(0, total // chunk, one, 0 if init is None else init)


def rows_tile(first, second, third):
    width = first.shape[1]
    place = lax.broadcasted_iota(jnp.int32, (8, width), 0)
    wide_of = lambda v: jnp.broadcast_to(v, (8, width))
    return jnp.where(
        place == 0, wide_of(first), jnp.where(place == 1, wide_of(second), wide_of(third))
    )


class Sems:
    def __init__(self, ref):
        self.ref, self.used, self.size = ref, 0, ref.shape[0]

    def take(self, count=1):
        first = self.used
        self.used += count
        assert self.used <= self.size, self.used
        return first


def make_kernel(sizes):
    n_dp, n_mp, R, Wd, M, C, Cd, classes, tasks, piece = sizes
    n_sec = 2
    W9 = 9 * C

    def kernel(*refs):
        (
            x_hbm, sides_hbm, wred_hbm, wspa_hbm, wexp_hbm, gin_hbm, sin_hbm, gout_hbm, sout_hbm,
            head_hbm, lab_hbm, thr_hbm,
            act_hbm, ig_hbm, red_hbm, spa_hbm, exp_hbm, vec_hbm, head_out,
            ssems, rsems, lsems, go,
            sred, sspa, sexp, shead, thr, xin, wr, wsp, we, hd, par,
            live, geo, masks, labc,
            rs_s, rs_r, ag_a, ag_b, ag_d, fulla, fullb, dfull, co, sums_s, sums_r, sums_t, st, keep, first, second, third, ppad, dpad, dbuf,
            lg_s, lg_r, dl, act1, tg, dpre, evec, dth, ig, slope, steep,
            gred, gspa, gexp, sibred, sibspa, sibexp, rred, rspa, rexp, ghead, rhead, vec, vsib,
            ored, ospa, oexp, ovec, ohead,
            sides_ref, gin_ref, sin_ref, gout_ref, sout_ref, lab_ref,
        ) = refs
        s = lax.axis_index("section")
        d = lax.axis_index("dp")
        m = lax.axis_index("mp")
        o = 1 - s
        recv, local = Sems(rsems), Sems(lsems)
        pending = {None: [], 0: [], 1: []}
        sends = {None: 0, 0: 1, 1: 2}
        rem = lax.rem
        dp_dev = lambda t: (s, t, m)
        mp_dev = lambda t: (s, d, t)
        sib_dev = (o, d, m)

        def put_to(src, dst, ssem, rsem, dev):
            pltpu.make_async_remote_copy(
                src_ref=src,
                dst_ref=dst,
                send_sem=ssems.at[ssem],
                recv_sem=rsems.at[rsem],
                device_id=dev,
                device_id_type=MESH,
            ).start()

        def waiter(ref, ssem, rsem):
            return pltpu.make_async_remote_copy(
                src_ref=ref,
                dst_ref=ref,
                send_sem=ssems.at[ssem],
                recv_sem=rsems.at[rsem],
                device_id=sib_dev,
                device_id_type=MESH,
            )

        def rcopy(src, dst, rsem, dev, when=None):
            ssem = sends[when]
            put_to(src(), dst(), ssem, rsem, dev)
            pending[when].append(lambda: waiter(src(), ssem, 0).wait_send())

        def arrive(dst, rsem):
            waiter(dst, 0, rsem).wait_recv()

        axes = {"dp": (n_dp, d, dp_dev), "mp": (n_mp, m, mp_dev)}
        expected, hold = {}, {}

        def settle(key):
            expected.pop(key)()

        def load(src, dst):
            cp = pltpu.make_async_copy(src, dst, lsems.at[local.take()])
            cp.start()
            key = ("load", local.used)
            expected[key] = cp.wait
            return key

        def on(cond, what):
            return lambda: pl.when(cond())(what)

        class Group:
            def __init__(self, axis, all_of, when=None, slot_of=None):
                self.n, self.me, self.dev = axes[axis]
                self.ssem = sends[when]
                self.rsem = recv.take(1 if slot_of is None else self.n - 1)
                self.all_of, self.when, self.slot_of = all_of, when, slot_of

            def put(self, src_of, slot_of):
                for k in range(1, self.n):
                    t = rem(self.me + k, self.n)
                    rsem = self.rsem + (0 if self.slot_of is None else k - 1)
                    put_to(src_of(t), slot_of(self.me), self.ssem, rsem, self.dev(t))

            def came_from(self, k):
                return rem(self.me + self.n - k, self.n)

            def close(self):
                ssem, all_of, when = self.ssem, self.all_of, self.when
                pending[when].append(lambda: waiter(all_of(), ssem, 0).wait_send())
                if self.slot_of is None:
                    waits = {self.rsem: lambda: arrive(all_of(), self.rsem)}
                else:
                    waits = {
                        self.rsem + k - 1: lambda k=k: arrive(
                            self.slot_of(self.came_from(k)), self.rsem + k - 1
                        )
                        for k in range(1, self.n)
                    }
                for key, wait in waits.items():
                    expected[key] = wait if when is None else on(lambda: s == when, wait)
                return self.rsem

        def spread(axis, src_of, slot_of, all_of, when=None):
            group = Group(axis, all_of, when)
            group.put(src_of, slot_of)
            return group.close()

        barrier = pltpu.get_barrier_semaphore()
        greeted = 0
        for ds_ in range(n_sec):
            for k in range(n_dp):
                if ds_ == 0 and k == 0:
                    continue
                pl.semaphore_signal(
                    barrier, inc=1,
                    device_id=(rem(s + ds_, n_sec), rem(d + k, n_dp), m),
                    device_id_type=MESH,
                )
                greeted += 1
        for k in range(1, n_mp):
            pl.semaphore_signal(
                barrier, inc=1, device_id=(s, d, rem(m + k, n_mp)), device_id_type=MESH
            )
            greeted += 1


        l_red = load(wred_hbm.at[0], sred)
        l_par = [
            load(src, dst)
            for src, dst in (
                (gin_hbm, gin_ref), (sin_hbm, sin_ref), (gout_hbm, gout_ref), (sout_hbm, sout_ref)
            )
        ]
        l_x = load(x_hbm.at[s], xin.at[0])
        l_spa = load(wspa_hbm.at[0], sspa)
        l_exp = load(wexp_hbm.at[0], sexp)
        l_small = [load(sides_hbm, sides_ref), load(lab_hbm, lab_ref)]
        l_head = load(head_hbm, shead)
        l_thr = load(thr_hbm.at[s], thr)

        settle(l_red)
        wr[s, d] = sred[...].astype(BF16)
        for key in l_par:
            settle(key)
        par[s] = jnp.zeros(par.shape[1:], F32)
        for i in range(2):
            par[s, i:i + 1, :C] = gin_ref[0, i:i + 1, :]
            par[s, 2 + i:3 + i, :C] = sin_ref[0, i:i + 1, :]
        par[s, 4:5, :] = gout_ref[...]
        par[s, 5:6, :] = sout_ref[...]
        pl.semaphore_wait(barrier, greeted)

        by_dp, by_sib = {}, {}

        def send_own(buf, j):
            def go():
                by_dp[id(buf), j] = spread(
                    "dp",
                    lambda t: buf.at[j, d],
                    lambda src: buf.at[j, src],
                    lambda: buf.at[j, pl.ds(0, n_dp - 1)],
                    when=j,
                )

            pl.when(s == j)(go)

        def pass_on(buf, j):
            settle(by_dp[id(buf), j])
            sem = by_sib[id(buf), j] = recv.take()

            @pl.when(s == j)
            def _():
                rcopy(lambda: buf.at[j], lambda: buf.at[j], sem, sib_dev, when=j)

            expected[sem] = on(lambda: s != j, lambda: arrive(buf.at[j], sem))

        def from_sib(buf, j):
            settle(by_sib[id(buf), j])

        par_sem = recv.take()
        rcopy(lambda: par.at[s], lambda: par.at[s], par_sem, sib_dev)
        expected[par_sem] = lambda: arrive(par.at[o], par_sem)
        early = Group(
            "dp",
            lambda: wr.at[0, pl.ds(0, n_dp - 1)],
            when=0,
            slot_of=lambda src: wr.at[0, src],
        )

        @pl.when(s == 0)
        def _():
            early.put(lambda t: wr.at[0, d], lambda src: wr.at[0, src])

        early.close()

        settle(l_spa)
        for k in range(9):
            wsp[s, d, :, k * C:(k + 1) * C] = sspa[k].astype(BF16)

        settle(l_exp)
        we[s, d] = sexp[...].astype(BF16)

        for key in l_small:
            settle(key)
        sides = jnp.where(s == 0, sides_ref[0], sides_ref[1]).astype(F32)
        slots = sides.shape[1]
        sq = jnp.broadcast_to(sides * sides, (8, slots)).astype(BF16)
        upper = (
            lax.broadcasted_iota(jnp.int32, (slots, slots), 0)
            <= lax.broadcasted_iota(jnp.int32, (slots, slots), 1)
        ).astype(BF16)
        ends = dot(sq, upper, NN)[0:1]
        starts = ends - sides * sides
        nloc = jnp.broadcast_to(jnp.max(ends, axis=1, keepdims=True), (1, 128))
        shape = (R, 128)
        pos = lax.broadcasted_iota(jnp.int32, (R, slots), 0).astype(F32)
        inside = (pos >= starts) & (pos < ends)
        origin = jnp.sum(jnp.where(inside, starts, 0.0), axis=1, keepdims=True)
        side = jnp.sum(jnp.where(inside, sides, 0.0), axis=1, keepdims=True)
        geo[0] = jnp.broadcast_to(origin, shape)
        geo[1] = jnp.broadcast_to(side, shape)

        def make_masks(rows, carry):
            side_b = geo[1, rows]
            here = lax.broadcasted_iota(jnp.int32, side_b.shape, 0) + rows.start
            offset = here.astype(F32) - geo[0, rows]
            row_in = jnp.floor((offset + 0.5) / jnp.maximum(side_b, 1.0))
            col_in = offset - row_in * side_b
            live[rows] = (side_b > 0.0).astype(F32)
            for idx, (_, a, b, q, _) in enumerate(MASKS):
                ra, cb = row_in + a, col_in + b
                ok = (side_b == q) & (ra >= 0.0) & (ra < q) & (cb >= 0.0) & (cb < q)
                masks[idx, rows] = ok.astype(F32)
            return carry

        loop(R, 64, make_masks)
        for buf in (ppad, dpad):
            edge = jnp.zeros((PAD, buf.shape[1]), F32)
            buf[0:PAD] = edge
            buf[PAD + R:PAD + R + PAD] = edge
        lab2 = lab_ref[...]
        lab = jnp.where(s == 0, lab2[:, 0], lab2[:, 1]).astype(F32)
        lab = jnp.concatenate([lab, jnp.zeros((8 - tasks, R), F32)], axis=0)
        labc[...] = jnp.transpose(lab)

        settle(l_head)
        mine = s * n_dp + d
        for t in range(tasks):
            hd[mine, t] = shead[t].astype(BF16)

        def to_all(src_of, buf):
            ssem, rsem = sends[None], recv.take()
            others = [(a, k) for a in range(n_sec) for k in range(n_dp) if a or k]
            for a, k in others:
                ts, td = rem(s + a, n_sec), rem(d + k, n_dp)
                put_to(src_of(ts * n_dp + td), buf.at[mine], ssem, rsem, (ts, td, m))
            rest = lambda: buf.at[pl.ds(0, len(others))]
            pending[None].append(lambda: waiter(rest(), ssem, 0).wait_send())
            expected[rsem] = lambda: arrive(rest(), rsem)
            return rsem

        def cat(buf, n):
            return jnp.concatenate([buf[i] for i in range(n)], axis=1)

        phase = {"rs": 0, "st": 0}

        def rs_open():
            p = phase["rs"]
            phase["rs"] += 1
            return p, Group("mp", lambda: rs_r.at[p, pl.ds(0, n_mp - 1)])

        def rs_rows(handle, rows, out):
            p, group = handle
            for c in range(n_mp):
                rs_s[p, c, rows] = out[:, c * C:(c + 1) * C].astype(BF16)
            group.put(lambda t: rs_s.at[p, t, rows], lambda src: rs_r.at[p, src, rows])

        def rs_finish(handle, dst):
            p, group = handle
            settle(group.rsem)

            def add(rows, carry):
                dst[rows] = rs_sum(handle, rows)
                return carry

            loop(R, 128, add)

        def exchange(tile):
            p = phase["st"]
            phase["st"] += 1
            width = tile.shape[1]
            st[p, d, :, 0:width] = tile
            slot = lambda src: st.at[p, src, :, 0:width]
            rest = lambda: st.at[p, pl.ds(0, n_dp - 1), :, 0:width]
            return p, width, spread("dp", lambda t: slot(d), slot, rest)

        def collect(handle):
            p, width, base = handle
            settle(base)
            return [st[p, i, :, 0:width] for i in range(n_dp)]

        def stats_start(buf, width, total=None):
            chunk = 128 if width <= 128 else 32
            zero = jnp.zeros((8, width), F32)

            def sum_up(rows, carry):
                return carry + fold(buf[rows] * wide(live[rows], width))

            if total is None:
                total = loop(R, chunk, sum_up, zero)
            total = jnp.sum(total, axis=0, keepdims=True)
            count = wide(nloc, width)
            mean = total / jnp.maximum(count, 1.0)

            def squares(rows, carry):
                off = (buf[rows] - mean) * wide(live[rows], width)
                return carry + fold(off * off)

            sqs = jnp.sum(loop(R, chunk, squares, zero), axis=0, keepdims=True)
            return exchange(rows_tile(total, sqs, count)), mean

        def stats_finish(handle, j, i):
            tiles = collect(handle)
            width = handle[1]
            count = sum(t[2:3] for t in tiles)
            mean = sum(t[0:1] for t in tiles) / count
            sqs = 0.0
            for t in tiles:
                local_mean = t[0:1] / jnp.maximum(t[2:3], 1.0)
                sqs = sqs + t[1:2] + t[2:3] * (local_mean - mean) * (local_mean - mean)
            inv = lax.rsqrt(sqs / count + NORM_EPS)
            keep[j, i, :, 0:width] = rows_tile(mean, inv, count)

        def parted(*twelfths):
            at = [max(32, R * n // 12 // 32 * 32) for n in twelfths]
            return [slice(a, b) for a, b in zip([0] + at, at + [R])]

        spans, halves = parted(2, 7), parted(6)

        def rows_out(buf, at, rows, values):
            buf[at, m, rows] = values.astype(BF16)
            return spread(
                "mp",
                lambda t: buf.at[at, m, rows],
                lambda src: buf.at[at, src, rows],
                lambda: buf.at[at, pl.ds(0, n_mp - 1), rows],
            )

        def rs_rows_sums(handle, j, i, rows, out, carry):
            p, groups = handle
            sb, sg = carry
            raw = (ag_a, ag_b)[i]
            for c in range(n_mp):
                part = out[:, c * C:(c + 1) * C]
                rs_s[p, c, rows] = part.astype(BF16)
                tile = co[2 * j + i, c]
                g = part * slope[j, i, c, rows]
                xhat = raw[j, c, rows].astype(F32) * tile[2:3] + tile[3:4]
                sb[c] = sb[c] + fold(g)
                sg[c] = sg[c] + fold(g * xhat)
            last = rows.stop == R
            if last:
                sums = sums_out(p, sb + sg)
            group = Group("mp", lambda: rs_r.at[p, pl.ds(0, n_mp - 1), rows])
            group.put(lambda t: rs_s.at[p, t, rows], lambda src: rs_r.at[p, src, rows])
            groups.append(group.close())
            return sums if last else None

        def sums_out(p, parts):
            place = lax.broadcasted_iota(jnp.int32, (2 * n_mp, C), 0)
            tile = jnp.zeros((2 * n_mp, C), F32)
            for i, part in enumerate(parts):
                tile = jnp.where(place == i, jnp.sum(part, axis=0, keepdims=True), tile)
            sums_s[p] = tile
            ssem, rsem = sends[None], recv.take()
            others = [(a, k) for a in range(n_mp) for k in range(n_dp) if a or k]
            me = m * n_dp + d
            for a, k in others:
                tz, td = rem(m + a, n_mp), rem(d + k, n_dp)
                put_to(sums_s.at[p], sums_r.at[p, me], ssem, rsem, (s, td, tz))
            rest = lambda: sums_r.at[p, pl.ds(0, len(others))]
            pending[None].append(lambda: waiter(rest(), ssem, 0).wait_send())
            expected[rsem] = lambda: arrive(rest(), rsem)

            def collect_sums():
                settle(rsem)
                total = sums_s[p]
                for a, k in others:
                    total = total + sums_r[p, rem(m + a, n_mp) * n_dp + rem(d + k, n_dp)]
                sums_t[p] = total
                return total

            return collect_sums

        def rs_parts():
            p = phase["rs"]
            phase["rs"] += 1
            return p, []

        def rs_sum(handle, rows):
            p, _ = handle
            out = rs_s[p, m, rows].astype(F32)
            for k in range(1, n_mp):
                out = out + rs_r[p, rem(m + k, n_mp), rows].astype(F32)
            return out

        def coeffs_out(at, *values):
            place = lax.broadcasted_iota(jnp.int32, (8, C), 0)
            tile = jnp.zeros((8, C), F32)
            for i, v in enumerate(values):
                tile = jnp.where(place == i, jnp.broadcast_to(v, (8, C)), tile)
            co[at, m] = tile
            slot = lambda src: co.at[at, src]
            return spread("mp", lambda t: slot(m), slot, lambda: co.at[at, pl.ds(0, n_mp - 1)])

        def inner_norm(j, i, src, raw, full, hook, need, consume):
            at = 2 * j + i
            handle, mean_here = stats_start(src.at[j], C)
            push = lambda rows: rows_out(raw, j, rows, src[j, rows] - mean_here)
            groups = [push(rows) for rows in spans[:-1]]
            hook()
            stats_finish(handle, j, i)
            mu, inv, _, gain, shift = norm_of(j, i, C)
            moved = (mean_here - mu) * inv
            sent = coeffs_out(at, gain * inv, gain * moved + shift, inv, moved)
            groups.append(push(spans[-1]))
            need()
            settle(sent)
            for rows, group in zip(spans, groups):
                settle(group)
                for c in range(n_mp):
                    tile = co[at, c]
                    y = live[rows] * (raw[j, c, rows].astype(F32) * tile[0:1] + tile[1:2])
                    full[j, rows, c * C:(c + 1) * C] = gelu(y).astype(BF16)
                consume(rows)

        def norm_of(j, i, width):
            tile = keep[j, i, :, 0:width]
            if i < 2:
                gain, shift = par[j, i:i + 1, 0:width], par[j, 2 + i:3 + i, 0:width]
            else:
                gain, shift = par[j, 4:5, 0:width], par[j, 5:6, 0:width]
            return tile[0:1], tile[1:2], tile[2:3], gain, shift

        def taps_sum(src, flip, put):
            way = -1 if flip else 1
            for rows in spans:
                first_row, last_row = PAD + rows.start, PAD + rows.stop
                put(rows, lambda idx_list, lanes: sum(
                    masks[(len(MASKS) - 2 - (idx // 2) * 2 + idx % 2) if flip else idx, rows]
                    * src[first_row + way * MASKS[idx][4]:last_row + way * MASKS[idx][4], lanes]
                    for idx in idx_list
                ))

        nothing = lambda: None
        vec[...] = jnp.zeros(vec.shape, F32)

        def prepare(j):
            for i, raw in enumerate((ag_a, ag_b)):
                def inner(rows, carry):
                    for c in range(n_mp):
                        tile = co[2 * j + i, c]
                        y = live[rows] * (raw[j, c, rows].astype(F32) * tile[0:1] + tile[1:2])
                        slope[j, i, c, rows] = live[rows] * gelu_grad(y)
                    return carry

                loop(R, 64, inner)
            mu, inv, _, gain, shift = norm_of(j, 2, Wd)

            def outer(rows, carry):
                lv = wide(live[rows], Wd)
                pre = lv * (gain * ((third[j, rows] - mu) * inv) + shift)
                steep[j, rows] = lv * gelu_grad(pre + xin[j, rows].astype(F32))
                return carry

            loop(R, 32, outer)

        def forward(j, h, hooks, needs):
            hooks[0]()
            rs_finish(h, first.at[j])

            def conv(rows):
                there = slice(PAD + rows.start, PAD + rows.stop)
                ppad[there] = dot(fulla[j, rows], wsp[j].reshape(M, W9), NN)

            inner_norm(j, 0, first, ag_a, fulla, hooks[1], needs[0], conv)

            def put(rows, summed):
                second[j, rows] = sum(
                    summed([2 * k, 2 * k + 1], slice(k * C, (k + 1) * C)) for k in range(9)
                )

            taps_sum(ppad, False, put)
            if j == 0:
                pass_on(wr, 1)
            sums = []

            def expand(rows):
                out = dot(fullb[j, rows], we[j].reshape(M, Wd), NN)
                third[j, rows] = out
                sums.append(fold(out * wide(live[rows], Wd)))

            inner_norm(j, 1, second, ag_b, fullb, hooks[2], needs[1], expand)
            h, _ = stats_start(third.at[j], Wd, sum(sums))
            hooks[3]()
            stats_finish(h, j, 2)
            mu, inv, _, gain, shift = norm_of(j, 2, Wd)
            out = xin.at[1] if j == 0 else act1

            def act_c(rows):
                for r0 in range(rows.start, rows.stop, 32):
                    there = slice(r0, r0 + 32)
                    lv = wide(live[there], Wd)
                    pre = lv * (gain * ((third[j, there] - mu) * inv) + shift)
                    pre = pre + xin[j, there].astype(F32)
                    out[there] = (lv * gelu(pre)).astype(BF16)

            return act_c

        def to_section(src, hbm, j):
            sem = recv.take()

            @pl.when(s == j)
            def _():
                lsem = local.take()
                made = lambda: pltpu.make_async_copy(src(), hbm.at[0, s], lsems.at[lsem])
                made().start()
                pending[j].append(lambda: made().wait())

            @pl.when(s != j)
            def _():
                rcopy(src, lambda: hbm.at[0, s], sem, sib_dev, when=1 - j)

            expected[sem] = on(lambda: s == j, lambda: arrive(hbm.at[0, o], sem))

        grads = ((gred, sibred, rred), (gspa, sibspa, rspa), (gexp, sibexp, rexp))
        at_sib, at_dp = {}, {}

        def grad_to_sib(which, j):
            own, sib, _ = grads[which]
            sem = at_sib[which, j] = recv.take()

            @pl.when(s != j)
            def _():
                rcopy(lambda: own.at[j], lambda: sib, sem, sib_dev, when=1 - j)

            expected[sem] = on(lambda: s == j, lambda: arrive(sib, sem))

        def grad_to_dp(which, j):
            own, sib, got = grads[which]
            settle(at_sib[which, j])

            def go():
                def add(rows, carry):
                    for i in range(n_dp):
                        own[j, i, rows] = (
                            own[j, i, rows].astype(F32) + sib[i, rows].astype(F32)
                        ).astype(BF16)
                    return carry

                loop(own.shape[2], 64, add)
                base = spread(
                    "dp",
                    lambda t: own.at[j, t],
                    lambda src: got.at[src],
                    lambda: got.at[pl.ds(0, n_dp - 1)],
                    when=j,
                )
                at_dp.setdefault(which, []).append(base)

            pl.when(s == j)(go)

        def reduce_to_sib(j):
            for i in range(n_dp):
                full = dfull[j, :, i * Cd:(i + 1) * Cd]
                gred[j, i] = dot(xin[j], full, TN).astype(BF16)
                sem = at_sib[0, j, i] = recv.take()

                @pl.when(s != j)
                def _():
                    rcopy(lambda: gred.at[j, i], lambda: sibred.at[i], sem, sib_dev, when=1 - j)

                expected[sem] = on(
                    lambda: s == j, lambda i=i, sem=sem: arrive(sibred.at[i], sem)
                )

        def reduce_to_dp(j):
            group = Group("dp", lambda: rred.at[pl.ds(0, n_dp - 1)], when=j)
            for i in range(n_dp):
                settle(at_sib[0, j, i])

                @pl.when(s == j)
                def _():
                    def add(rows, carry):
                        gred[j, i, rows] = (
                            gred[j, i, rows].astype(F32) + sibred[i, rows].astype(F32)
                        ).astype(BF16)
                        return carry

                    loop(Wd, 128, add)

                    @pl.when(d != i)
                    def _():
                        put_to(gred.at[j, i], rred.at[d], group.ssem, group.rsem, dp_dev(i))

            at_dp.setdefault(0, []).append(group.close())

        def steepest(j, rows, e, carry):
            mu, inv, _, _, _ = norm_of(j, 2, Wd)
            out = steep[j, rows] * e
            dpre[rows] = out
            return carry[0] + fold(out), carry[1] + fold(out * ((third[j, rows] - mu) * inv))

        def backward(j, sums, hooks):
            mu, inv, count, gain, shift = norm_of(j, 2, Wd)
            sb, sg = sums
            total = lambda v: jnp.sum(v, axis=0, keepdims=True)
            sb, sg = total(sb), total(sg)
            h = exchange(rows_tile(sb, sg, sg))
            hooks[0]()
            tile = sum(collect(h))
            vec[j, 4:5, :] = tile[1:2]
            vec[j, 5:6, :] = tile[0:1]
            sb_n, sg_n = tile[0:1] / count, tile[1:2] / count
            scale = gain * inv

            def d_third(rows, carry):
                lv = wide(live[rows], Wd)
                xhat = (third[j, rows] - mu) * inv
                dth[rows] = (lv * scale * (dpre[rows] - sb_n - xhat * sg_n)).astype(BF16)
                return carry

            none = lambda: ([jnp.zeros((8, C), F32)] * n_mp, [jnp.zeros((8, C), F32)] * n_mp)
            h, carry = rs_parts(), none()
            for rows in halves:
                for r0 in range(rows.start, rows.stop, 32):
                    d_third(slice(r0, r0 + 32), 0)
                out = dot(dth[rows], we[j].reshape(M, Wd), NT)
                sums_of = rs_rows_sums(h, j, 1, rows, out, carry)
            for i in range(n_dp):
                full = fullb[j, :, i * Cd:(i + 1) * Cd]
                gexp[j, i] = dot(full, dth[...], TN).astype(BF16)
            grad_to_sib(2, j)
            hooks[1]()
            for group in h[1]:
                settle(group)

            def norm_sums(i, sums):
                p = sums[0]
                place = lax.broadcasted_iota(jnp.int32, (2 * n_mp, C), 0)
                row = lambda i: jnp.sum(
                    jnp.where(place == i, sums_t[p], 0.0), axis=0, keepdims=True
                )
                sb, sg = row(m), row(n_mp + m)
                vec[j, i:i + 1, 0:C] = sg
                vec[j, 2 + i:3 + i, 0:C] = sb
                return sb, sg

            sums_of()
            sb_b, sg_b = norm_sums(1, h)
            mu_b, inv_b, count_b, gain_b, _ = norm_of(j, 1, C)
            scale_b, sb_b, sg_b = gain_b * inv_b, sb_b / count_b, sg_b / count_b
            for rows in spans:
                there = slice(PAD + rows.start, PAD + rows.stop)
                xhat = (second[j, rows] - mu_b) * inv_b
                g = slope[j, 1, m, rows] * rs_sum(h, rows)
                out = live[rows] * scale_b * (g - sb_b - xhat * sg_b)
                dpad[there] = out.astype(BF16).astype(F32)

            h, carry = rs_parts(), none()
            sums_a = []

            def put(rows, summed):
                for k in range(9):
                    dbuf[rows, k * C:(k + 1) * C] = summed([2 * k, 2 * k + 1], slice(None)).astype(BF16)
                out = dot(dbuf[rows], wsp[j].reshape(M, W9), NT)
                sums_a.append(rs_rows_sums(h, j, 0, rows, out, carry))

            taps_sum(dpad, True, put)
            for i in range(n_dp):
                full = fulla[j, :, i * Cd:(i + 1) * Cd]
                gspa[j, i] = dot(full, dbuf[...], TN).astype(BF16)
            grad_to_sib(1, j)
            grad_to_dp(2, j)
            hooks[2]()
            groups = []
            for rows, part in zip(spans, h[1]):
                settle(part)
                g = slope[j, 0, m, rows] * rs_sum(h, rows)
                if not groups:
                    pivot = jnp.sum(g, axis=0, keepdims=True) / jnp.maximum(
                        jnp.sum(live[rows], axis=0, keepdims=True), 1.0
                    )
                    sent = coeffs_out(4 + j, pivot)
                groups.append(rows_out(ag_d, j, rows, g - pivot))
            hooks[3]()
            grad_to_dp(1, j)

            def d_input(rows):
                out = dot(dfull[j, rows], cat(wr.at[j], n_dp), NT) + dpre[rows]
                if j == 1:
                    out = out.astype(BF16).astype(F32)
                    evec[rows] = out
                ig[j, rows] = out

            sums = sums_a[-1]()
            norm_sums(0, h)
            if j == 0:
                hold["vec"] = recv.take()
                rcopy(lambda: vec.at[o], lambda: vsib, hold["vec"], sib_dev)
                expected[hold["vec"]] = lambda: arrive(vsib, hold["vec"])
            settle(sent)
            count = keep[j, 0, 2:3, 0:C]
            terms = []
            for c in range(n_mp):
                tile = co[2 * j, c]
                sb_n, sg_n = sums[c:c + 1] / count, sums[n_mp + c:n_mp + c + 1] / count
                scale, inv, moved = tile[0:1], tile[2:3], tile[3:4]
                offset = scale * (co[4 + j, c, 0:1] - sb_n - moved * sg_n)
                terms.append((scale, -scale * sg_n * inv, offset))
            for rows, group in zip(spans, groups):
                settle(group)
                for c, (scale, slant, offset) in enumerate(terms):
                    out = live[rows] * (
                        ag_d[j, c, rows].astype(F32) * scale
                        + ag_a[j, c, rows].astype(F32) * slant
                        + offset
                    )
                    dfull[j, rows, c * C:(c + 1) * C] = out.astype(BF16)
                if j == 1:
                    d_input(rows)
            if j == 0:
                reduce_to_sib(j)
                for rows in spans[:-1]:
                    d_input(rows)
                reduce_to_dp(j)
                for rows in spans[-1:]:
                    d_input(rows)
            to_section(lambda: ig.at[j], ig_hbm, j)

        settle(l_x)

        def first_product():
            handle = rs_open()
            p, group = handle
            for k in range(n_dp):
                src = early.came_from(k) if k else d
                if k:
                    settle(early.rsem + k - 1)
                sem = recv.take()

                @pl.when(s == 0)
                def _():
                    rcopy(lambda: wr.at[0, src], lambda: wr.at[0, src], sem, sib_dev, when=0)

                expected[sem] = on(lambda: s != 0, lambda: arrive(wr.at[0, src], sem))
                settle(sem)

                def part(rows, carry):
                    rs_s[p, src, rows] = dot(xin[0, rows], wr[0, src], NN).astype(BF16)
                    return carry

                loop(R, 128, part)

                @pl.when(src != m)
                def _():
                    put_to(rs_s.at[p, src], rs_r.at[p, m], group.ssem, group.rsem, mp_dev(src))

            group.close()
            return handle

        @pl.when(s == 1)
        def _():
            pl.semaphore_wait(go, 1)

        start = first_product()
        settle(par_sem)

        def w_next():
            send_own(we, 0)
            send_own(wr, 1)

        def w_head():
            hold["heads"] = to_all(lambda t: hd.at[mine], hd)

        def f00():
            send_own(wsp, 0)

            @pl.when(s == 0)
            def _():
                pl.semaphore_signal(go, inc=1, device_id=sib_dev, device_id_type=MESH)

        hooks = (f00, w_next, lambda: send_own(wsp, 1), nothing)

        def n00():
            pass_on(wsp, 0)
            from_sib(wsp, 0)

        def n01():
            pass_on(we, 0)
            from_sib(we, 0)

        act_c = forward(0, start, hooks, (n00, n01))
        from_sib(wr, 1)
        start = rs_open()
        for rows in spans:
            act_c(rows)
            rs_rows(start, rows, dot(xin[1, rows], cat(wr.at[1], n_dp), NN))
        start[1].close()

        def f10():
            send_own(we, 1)
            pass_on(wsp, 1)
            to_section(lambda: xin.at[1], act_hbm, 0)
            prepare(0)

        def n10():
            pass_on(we, 1)
            from_sib(wsp, 1)

        hooks = (f10, w_head, nothing, nothing)
        act_c = forward(1, start, hooks, (n10, lambda: from_sib(we, 1)))

        settle(hold["heads"])
        RM = R // n_mp
        n_cls = n_sec * n_dp

        def heads_of(t):
            return hd[:, t].reshape(classes, Wd)

        for c in range(n_mp):
            act_c(slice(c * RM, (c + 1) * RM))
            rows = act1[c * RM:(c + 1) * RM]
            for t in range(tasks):
                lg_s[c, :, t * classes:(t + 1) * classes] = dot(rows, heads_of(t), NT).astype(
                    lg_s.dtype
                )
        base = spread(
            "mp", lambda t: lg_s.at[t], lambda src: lg_r.at[src], lambda: lg_r.at[pl.ds(0, n_mp - 1)]
        )
        to_section(lambda: act1, act_hbm, 1)
        settle(l_thr)
        prepare(1)
        settle(base)
        here = pl.ds(pl.multiple_of(m * RM, RM), RM)
        lv = wide(live[here], classes)
        for t in range(tasks):
            lanes = slice(t * classes, (t + 1) * classes)
            logit = lg_s[m, :, lanes].astype(F32)
            for k in range(1, n_mp):
                logit = logit + lg_r[rem(m + k, n_mp), :, lanes].astype(F32)
            expo = jnp.exp(logit - jnp.max(logit, axis=1, keepdims=True))
            soft = expo / jnp.sum(expo, axis=1, keepdims=True)
            ids = lax.broadcasted_iota(jnp.int32, (RM, classes), 1).astype(F32)
            hot = (ids == labc[here, t:t + 1]).astype(F32)
            dl[m, :, lanes] = (LOSS_WEIGHT * lv * (soft - hot)).astype(BF16)
        group = Group(
            "mp", lambda: dl.at[pl.ds(0, n_mp - 1)], slot_of=lambda src: dl.at[src]
        )
        group.put(lambda t: dl.at[m], lambda src: dl.at[src])
        group.close()

        def merge_block(c, sums):
            for t in range(tasks):
                lanes = slice(t * classes, (t + 1) * classes)
                tg[t] = dot(dl[c, :, lanes], heads_of(t), NN)

            def merge(rows, carry):
                total = soft_sum = None
                for t in range(tasks):
                    g = tg[t, rows]
                    soft = jnp.sqrt(g * g + SIGN_FLOOR * SIGN_FLOOR) - SIGN_FLOOR
                    total = g if t == 0 else total + g
                    soft_sum = soft if t == 0 else soft_sum + soft
                purity = 0.5 * (1.0 + total / (soft_sum + SIGN_FLOOR))
                start = pl.multiple_of(rows.start + c * RM, 32)
                there = pl.ds(start, 32)
                frac = 1.0 / (1.0 + jnp.exp((thr[there] - purity) * (1.0 / KEEP_TEMPER)))
                upper, lower = 0.5 * (total + soft_sum), 0.5 * (total - soft_sum)
                return steepest(1, there, frac * upper + (1.0 - frac) * lower, carry)

            return loop(RM, 32, merge, sums)

        zero = (jnp.zeros((8, Wd), F32), jnp.zeros((8, Wd), F32))
        sums = merge_block(m, zero)
        for k in [1] + list(range(n_mp - 1, 1, -1)):
            settle(group.rsem + k - 1)
            sums = merge_block(group.came_from(k), sums)

        def b10():
            for t in range(tasks):
                lanes = slice(t * classes, (t + 1) * classes)
                delta = dl[:, :, lanes].reshape(R, classes)
                out = dot(delta, act1[...], TN).astype(BF16)
                ghead[:, t] = out.reshape(n_cls, piece, Wd)
            hold["ghead"] = to_all(lambda t: ghead.at[t], rhead)

        backward(1, sums, (nothing, b10, nothing, nothing))
        sums = loop(R, 32, lambda rows, carry: steepest(0, rows, evec[rows], carry), zero)

        backward(0, sums, (lambda: reduce_to_sib(1), lambda: reduce_to_dp(1), nothing, nothing))

        settle(hold["ghead"])
        for t in range(tasks):
            total = ghead[mine, t].astype(F32)
            for k in range(1, n_cls):
                total = total + rhead[rem(mine + k, n_cls), t].astype(F32)
            ohead[t] = total
        load(ohead, head_out)
        settle(hold["vec"])
        ovec[...] = vec[s] + vsib[...]
        load(ovec, vec_hbm)

        def total_of(own, got, rows):
            out = own[s, d, rows].astype(F32)
            for k in range(1, n_dp):
                out = out + got[rem(d + k, n_dp), rows].astype(F32)
            return out

        def finish_grad(which):
            own, _, got = grads[which]
            for key in at_dp[which]:
                settle(key)

            def finish(rows, carry):
                out = total_of(own, got, rows)
                if which == 1:
                    for k in range(9):
                        ospa[0, k, rows] = out[:, k * C:(k + 1) * C]
                else:
                    (ored if which == 0 else oexp)[0, rows] = out
                return carry

            loop(own.shape[2], 64, finish)
            load((ored, ospa, oexp)[which], (red_hbm, spa_hbm, exp_hbm)[which])

        finish_grad(2)
        finish_grad(1)
        finish_grad(0)
        for key in list(expected):
            settle(key)

        for key, waits in pending.items():
            def finish_all(waits=waits):
                for wait in waits:
                    wait()

            if key is None:
                finish_all()
            else:
                pl.when(s == key)(finish_all)

    return kernel


def fused_device(sizes, *args):
    n_dp, n_mp, R, Wd, M, C, Cd, classes, tasks, piece = sizes
    W9, n_cls = 9 * C, 2 * n_dp
    RM = R // n_mp
    vmem = lambda shape, dtype: pltpu.VMEM(shape, dtype)
    scratch = [
        pltpu.SemaphoreType.DMA((3,)),
        pltpu.SemaphoreType.DMA((95,)),
        pltpu.SemaphoreType.DMA((21,)),
        pltpu.SemaphoreType.REGULAR,
        vmem((Wd, Cd), F32),
        vmem((9, Cd, C), F32),
        vmem((Cd, Wd), F32),
        vmem((tasks, piece, Wd), F32),
        vmem((R, Wd), F32),
        vmem((2, R, Wd), BF16),
        vmem((2, n_dp, Wd, Cd), BF16),
        vmem((2, n_dp, Cd, W9), BF16),
        vmem((2, n_dp, Cd, Wd), BF16),
        vmem((n_cls, tasks, piece, Wd), BF16),
        vmem((2, 8, Wd), F32),
        vmem((R, 128), F32),
        vmem((2, R, 128), F32),
        vmem((len(MASKS), R, 128), F32),
        vmem((R, 8), F32),
        vmem((6, n_mp, R, C), BF16),
        vmem((6, n_mp, R, C), BF16),
        vmem((2, n_mp, R, C), BF16),
        vmem((2, n_mp, R, C), BF16),
        vmem((2, n_mp, R, C), BF16),
        vmem((2, R, M), BF16),
        vmem((2, R, M), BF16),
        vmem((2, R, M), BF16),
        vmem((6, n_mp, 8, C), F32),
        vmem((6, 2 * n_mp, C), F32),
        vmem((6, n_mp * n_dp, 2 * n_mp, C), F32),
        vmem((6, 2 * n_mp, C), F32),
        vmem((12, n_dp, 8, Wd), F32),
        vmem((2, 3, 8, Wd), F32),
        vmem((2, R, C), F32),
        vmem((2, R, C), F32),
        vmem((2, R, Wd), F32),
        vmem((R + 2 * PAD, W9), F32),
        vmem((R + 2 * PAD, C), F32),
        vmem((R, W9), BF16),
        vmem((n_mp, RM, tasks * classes), BF16),
        vmem((n_mp, RM, tasks * classes), BF16),
        vmem((n_mp, RM, tasks * classes), BF16),
        vmem((R, Wd), BF16),
        vmem((tasks, RM, Wd), F32),
        vmem((R, Wd), F32),
        vmem((R, Wd), F32),
        vmem((R, Wd), BF16),
        vmem((2, R, Wd), F32),
        vmem((2, 2, n_mp, R, C), F32),
        vmem((2, R, Wd), F32),
        vmem((2, n_dp, Wd, Cd), BF16),
        vmem((2, n_dp, Cd, W9), BF16),
        vmem((2, n_dp, Cd, Wd), BF16),
        vmem((n_dp, Wd, Cd), BF16),
        vmem((n_dp, Cd, W9), BF16),
        vmem((n_dp, Cd, Wd), BF16),
        vmem((n_dp, Wd, Cd), BF16),
        vmem((n_dp, Cd, W9), BF16),
        vmem((n_dp, Cd, Wd), BF16),
        vmem((n_cls, tasks, piece, Wd), BF16),
        vmem((n_cls, tasks, piece, Wd), BF16),
        vmem((2, 8, Wd), F32),
        vmem((8, Wd), F32),
        vmem((1, Wd, Cd), F32),
        vmem((1, 9, Cd, C), F32),
        vmem((1, Cd, Wd), F32),
        vmem((8, Wd), F32),
        vmem((tasks, piece, Wd), F32),
    ] + [vmem(args[i].shape, args[i].dtype) for i in (1, 5, 6, 7, 8, 10)]
    in_any = pl.BlockSpec(memory_space=pl.ANY)
    whole = lambda shape, dtype=F32: jax.ShapeDtypeStruct(shape, dtype)
    out = pl.pallas_call(
        make_kernel(sizes),
        out_shape=(
            whole((1, 2, R, Wd), BF16),
            whole((1, 2, R, Wd)),
            whole((1, Wd, Cd)),
            whole((1, 9, Cd, C)),
            whole((1, Cd, Wd)),
            whole((8, Wd)),
            whole((tasks, piece, Wd)),
        ),
        in_specs=[in_any] * len(args),
        out_specs=(in_any,) * 7,
        scratch_shapes=scratch,
        compiler_params=pltpu.CompilerParams(
            collective_id=0, has_side_effects=True, vmem_limit_bytes=60 * 2**20
        ),
    )(*args[:9], jnp.transpose(args[9], (0, 2, 1)), *args[10:])
    part, outer = C // n_dp, Wd // n_dp
    shapes = (
        whole((1, 2, R, Wd), BF16),
        whole((1, 2, R, Wd)),
        whole((1, Wd, Cd)),
        whole((1, 9, Cd, C)),
        whole((1, Cd, Wd)),
        whole((1, 2, 1, part)),
        whole((1, 2, 1, part)),
        whole((1, 1, outer)),
        whole((1, 1, outer)),
        whole((tasks, piece, Wd)),
    )
    done = pl.pallas_call(
        hand_out,
        out_shape=shapes,
        in_specs=[in_any] * 7,
        out_specs=(in_any,) * 10,
        scratch_shapes=[pltpu.VMEM(a.shape, a.dtype) for a in shapes]
        + [vmem((8, Wd), F32), pltpu.SemaphoreType.DMA((9,)), pltpu.SemaphoreType.DMA((12,))],
    )(*out)
    return done[:9] + (jnp.transpose(done[9], (0, 2, 1)),)


def hand_out(*refs):
    given, outs, held, vec, came, left = refs[:7], refs[7:17], refs[17:27], *refs[27:]
    gains, shifts, gain_out, shift_out = held[5:9]
    load_vec = pltpu.make_async_copy(given[5], vec, came.at[8])
    load_vec.start()
    pieces = []
    for src, mid, dst in zip(given[:5] + given[6:], held[:5] + held[9:], outs[:5] + outs[9:]):
        for i in range(src.shape[1]) if src.shape[1] == 2 else (None,):
            at = (lambda ref, i=i: ref) if i is None else (lambda ref, i=i: ref.at[0, i])
            n = len(pieces)
            pieces.append((
                pltpu.make_async_copy(at(src), at(mid), came.at[n]),
                pltpu.make_async_copy(at(mid), at(dst), left.at[n]),
            ))
    for fetch, _ in pieces:
        fetch.start()
    d = lax.axis_index("dp")
    part, outer = gains.shape[3], gain_out.shape[2]
    lanes = part * lax.axis_size("dp")
    load_vec.wait()
    rolled = pltpu.roll(vec[:, 0:lanes], lax.rem(lanes - d * part, lanes), 1)
    for i in range(2):
        gains[0, i] = rolled[i:i + 1, 0:part]
        shifts[0, i] = rolled[2 + i:3 + i, 0:part]
    mine = pl.ds(pl.multiple_of(d * outer, outer), outer)
    gain_out[0] = vec[4:5, mine]
    shift_out[0] = vec[5:6, mine]
    stores = [
        pltpu.make_async_copy(held[i], outs[i], left.at[len(pieces) + i - 5]) for i in range(5, 9)
    ]
    for store in stores:
        store.start()
    for fetch, store in pieces:
        fetch.wait()
        store.start()
    for store in stores + [store for _, store in pieces]:
        store.wait()


def per_device(*args):
    block_input, _, w_reduce, w_spatial = args[:4]
    n_dp, n_mp = lax.axis_size("dp"), lax.axis_size("mp")
    R, Wd = block_input.shape[1:]
    Cd, C = w_reduce.shape[2], w_spatial.shape[3]
    tasks, _, piece = args[9].shape
    sizes = (n_dp, n_mp, R, Wd, C * n_mp, C, Cd, piece * 2 * n_dp, tasks, piece)
    whole_tiles = not (C % 128 or Cd % 128 or Wd % 128 or R % 128 or piece % 16 or (R // n_mp) % 32)
    if whole_tiles and C == Cd and block_input.shape[0] == lax.axis_size("section") == 2:
        return fused_device(sizes, *args)
    return plain_device(*args)


def solution(mesh):
    return jax.shard_map(
        per_device,
        mesh=mesh,
        in_specs=(
            P(None, "dp", "mp"),
            P(None, "dp", None),
            P("section", "mp", "dp"),
            P("section", None, "dp", "mp"),
            P("section", "dp", "mp"),
            P("section", None, "mp"),
            P("section", None, "mp"),
            P("section", "mp"),
            P("section", "mp"),
            P(None, "mp", ("section", "dp")),
            P(None, None, "dp"),
            P(None, "dp", "mp"),
        ),
        out_specs=(
            P("section", None, "dp", "mp"),
            P("section", None, "dp", "mp"),
            P("section", "mp", "dp"),
            P("section", None, "dp", "mp"),
            P("section", "dp", "mp"),
            P("section", None, "mp", "dp"),
            P("section", None, "mp", "dp"),
            P("section", "mp", "dp"),
            P("section", "mp", "dp"),
            P(None, "mp", ("section", "dp")),
        ),
        check_vma=False,
    )
```

```python
import math

import jax
import jax.numpy as jnp
from jax import lax
from jax.experimental import pallas as pl
from jax.experimental.pallas import tpu as pltpu
from jax.sharding import PartitionSpec as P

NORM_EPS = 1e-05
LOSS_WEIGHT = 20.0
SIGN_FLOOR = 0.1
KEEP_TEMPER = 0.2


def shifted(value, axis, steps):
    count = lax.axis_size(axis)
    leading, last = (max(0, -steps), min(count, count - steps))
    return lax.ppermute(value, axis, [(source, source + steps) for source in range(leading, last)])


def geometry(img_sides, row_count):
    img_sizes = img_sides * img_sides
    img_ends = jnp.cumsum(img_sizes)
    img_starts = img_ends - img_sizes
    row_pos = jnp.arange(row_count, dtype=jnp.int32)[:, None]
    inside = (row_pos >= img_starts[None, :]) & (row_pos < img_ends[None, :])
    first_row = jnp.sum(jnp.where(inside, img_starts[None, :], 0), axis=1)
    side_len = jnp.sum(jnp.where(inside, img_sides[None, :], 0), axis=1)
    live_rows = jnp.any(inside, axis=1)
    offset = row_pos[:, 0] - first_row
    safe_side = jnp.maximum(side_len, 1)
    row_in = offset // safe_side
    col_in = offset % safe_side
    index_list = []
    valid_list = []
    for row_step in (-1, 0, 1):
        for col_step in (-1, 0, 1):
            new_row = row_in + row_step
            new_col = col_in + col_step
            valid = (
                live_rows
                & (new_row >= 0)
                & (new_row < side_len)
                & (new_col >= 0)
                & (new_col < side_len)
            )
            index_list.append(jnp.where(valid, first_row + new_row * side_len + new_col, 0))
            valid_list.append(valid)
    return (
        jnp.stack(index_list),
        jnp.stack(valid_list).astype(jnp.float32),
        live_rows.astype(jnp.float32),
    )


def smooth_act(values):
    return jax.nn.gelu(values, approximate=True)


def take_block(store, micro_idx):
    return lax.dynamic_index_in_dim(store, micro_idx, 0, keepdims=False)


def put_block(store, update, micro_idx, active):
    previous = take_block(store, micro_idx)
    return lax.dynamic_update_index_in_dim(store, jnp.where(active, update, previous), micro_idx, 0)


def channel_gather(values):
    return lax.all_gather(values, "mp", axis=1, tiled=True)


def channel_sum(values):
    return lax.psum_scatter(values, "mp", scatter_dimension=1, tiled=True)


def norm_stats(values, live_rows):
    masked = values * live_rows[:, None]
    total_sum, live_total = lax.psum((jnp.sum(masked, axis=0), jnp.sum(live_rows)), "dp")
    mean_val = total_sum / live_total
    centered = (values - mean_val) * live_rows[:, None]
    var_val = lax.psum(jnp.sum(centered * centered, axis=0), "dp") / live_total
    return (mean_val, lax.rsqrt(var_val + NORM_EPS), live_total)


def normalize(values, stats, live_rows, gain_vec, shift_vec):
    mean_val, inv_std, live_total = stats
    return live_rows[:, None] * (gain_vec * (values - mean_val) * inv_std + shift_vec)


def norm_backward(values, stats, live_rows, gain_vec, grad_norm):
    mean_val, inv_std, live_total = stats
    normed = (values - mean_val) * inv_std
    grad_live = grad_norm * live_rows[:, None]
    local_shift = jnp.sum(grad_live, axis=0)
    local_gain = jnp.sum(grad_live * normed, axis=0)
    sum_shift, sum_gain = lax.psum((local_shift, local_gain), "dp")
    grad_values = (
        live_rows[:, None]
        * inv_std
        * gain_vec
        * (grad_live - sum_shift / live_total - normed * sum_gain / live_total)
    )
    return (grad_values, local_gain, local_shift)


def gather_taps(values, indices, valids, tap_idx):
    return values[indices[tap_idx]] * valids[tap_idx][:, None].astype(values.dtype)


def act_backward(pre_values, grad_values):
    return jax.vjp(smooth_act, pre_values)[1](grad_values)[0]


def block_forward(x_in, layout, weights):
    indices, valids, live_rows = layout
    w_red, w_spa, w_exp, g_in, s_in, g_out, s_out = weights
    first_pre = channel_sum(jnp.dot(x_in, w_red, preferred_element_type=jnp.float32))
    stats_a = norm_stats(first_pre, live_rows)
    full_a = channel_gather(
        smooth_act(normalize(first_pre, stats_a, live_rows, g_in[0], s_in[0])).astype(jnp.bfloat16)
    )
    second_pre = jnp.zeros((x_in.shape[0], w_spa.shape[2]), jnp.float32)
    for tap_idx in range(9):
        second_pre = second_pre + jnp.dot(
            gather_taps(full_a, indices, valids, tap_idx),
            w_spa[tap_idx],
            preferred_element_type=jnp.float32,
        )
    stats_b = norm_stats(second_pre, live_rows)
    full_b = channel_gather(
        smooth_act(normalize(second_pre, stats_b, live_rows, g_in[1], s_in[1])).astype(jnp.bfloat16)
    )
    third_pre = jnp.dot(full_b, w_exp, preferred_element_type=jnp.float32)
    stats_c = norm_stats(third_pre, live_rows)
    pre_out = normalize(third_pre, stats_c, live_rows, g_out, s_out) + x_in.astype(jnp.float32)
    result = smooth_act(pre_out) * live_rows[:, None]
    return (result, (first_pre, stats_a, full_a, second_pre, stats_b, full_b, third_pre, stats_c))


def block_backward(d_out, x_in, layout, weights, saved_state):
    indices, valids, live_rows = layout
    w_red, w_spa, w_exp, g_in, s_in, g_out, s_out = weights
    first_pre, stats_a, full_a, second_pre, stats_b, full_b, third_pre, stats_c = saved_state
    pre_out = normalize(third_pre, stats_c, live_rows, g_out, s_out) + x_in.astype(jnp.float32)
    d_pre = act_backward(pre_out, d_out * live_rows[:, None])
    d_third, gain_c, shift_c = norm_backward(third_pre, stats_c, live_rows, g_out, d_pre)
    d_third = d_third.astype(jnp.bfloat16)
    grad_exp = jnp.einsum("rc,ro->co", full_b, d_third, preferred_element_type=jnp.float32)
    d_full_b = channel_sum(
        jnp.einsum("ro,co->rc", d_third, w_exp, preferred_element_type=jnp.float32)
    )
    pre_b = normalize(second_pre, stats_b, live_rows, g_in[1], s_in[1])
    d_second, gain_b, shift_b = norm_backward(
        second_pre, stats_b, live_rows, g_in[1], act_backward(pre_b, d_full_b)
    )
    d_second = d_second.astype(jnp.bfloat16)
    grad_spa = []
    back_total = jnp.zeros((x_in.shape[0], w_spa.shape[1]), jnp.float32)
    for tap_idx in range(9):
        grad_spa.append(
            jnp.einsum(
                "rc,ro->co",
                gather_taps(full_a, indices, valids, tap_idx),
                d_second,
                preferred_element_type=jnp.float32,
            )
        )
        spread = jnp.einsum(
            "ro,co->rc", d_second, w_spa[8 - tap_idx], preferred_element_type=jnp.float32
        )
        back_total = back_total + spread[indices[tap_idx]] * valids[tap_idx][:, None]
    d_full_a = channel_sum(back_total)
    pre_a = normalize(first_pre, stats_a, live_rows, g_in[0], s_in[0])
    d_first, gain_a, shift_a = norm_backward(
        first_pre, stats_a, live_rows, g_in[0], act_backward(pre_a, d_full_a)
    )
    d_first_full = channel_gather(d_first.astype(jnp.bfloat16))
    grad_red = jnp.einsum("rc,ro->co", x_in, d_first_full, preferred_element_type=jnp.float32)
    d_in = jnp.einsum("ro,co->rc", d_first_full, w_red, preferred_element_type=jnp.float32) + d_pre
    return (
        d_in,
        (
            grad_red,
            jnp.stack(grad_spa),
            grad_exp,
            jnp.stack([gain_a, gain_b]),
            jnp.stack([shift_a, shift_b]),
            gain_c,
            shift_c,
        ),
    )


def sign_merge(task_grads, thresh):
    soft_abs = jnp.sqrt(task_grads * task_grads + SIGN_FLOOR * SIGN_FLOOR) - SIGN_FLOOR
    purity = 0.5 * (1.0 + jnp.sum(task_grads, axis=0) / (jnp.sum(soft_abs, axis=0) + SIGN_FLOOR))
    keep_frac = jax.nn.sigmoid((purity - thresh) / KEEP_TEMPER)
    upper = 0.5 * jnp.sum(task_grads + soft_abs, axis=0)
    lower = 0.5 * jnp.sum(task_grads - soft_abs, axis=0)
    return keep_frac * upper + (1.0 - keep_frac) * lower


def plain_device(
    block_input,
    image_sides,
    w_reduce,
    w_spatial,
    w_expand,
    gain_inner,
    shift_inner,
    gain_outer,
    shift_outer,
    head_weight,
    labels,
    thresholds,
):
    section_idx = lax.axis_index("section")
    micro_count = block_input.shape[0]
    row_count = block_input.shape[1]
    w_red, w_spa, w_exp = (
        lax.all_gather(w_reduce[0].astype(jnp.bfloat16), "dp", axis=1, tiled=True),
        lax.all_gather(w_spatial[0].astype(jnp.bfloat16), "dp", axis=1, tiled=True),
        lax.all_gather(w_expand[0].astype(jnp.bfloat16), "dp", axis=0, tiled=True),
    )
    weights = (w_red, w_spa, w_exp, gain_inner[0], shift_inner[0], gain_outer[0], shift_outer[0])
    heads_all = lax.all_gather(
        head_weight.astype(jnp.bfloat16), ("section", "dp"), axis=2, tiled=True
    )
    class_total = heads_all.shape[2]
    class_ids = jnp.arange(class_total, dtype=jnp.int32)[None, None, :]

    def layout_for(micro_idx):
        return geometry(take_block(image_sides, micro_idx)[0], row_count)

    received = jnp.zeros(block_input.shape[1:], jnp.bfloat16)
    kept_inputs = jnp.zeros(block_input.shape, jnp.bfloat16)
    activ_store = jnp.zeros(block_input.shape, jnp.bfloat16)
    cotangents = jnp.zeros(block_input.shape, jnp.float32)
    head_grad = jnp.zeros(heads_all.shape, jnp.float32)
    for turn_idx in range(micro_count + 1):
        micro_idx = jnp.clip(turn_idx - section_idx, 0, micro_count - 1)
        active = (turn_idx - section_idx >= 0) & (turn_idx - section_idx < micro_count)
        x_in = jnp.where(section_idx == 0, block_input[min(turn_idx, micro_count - 1)], received)
        layout = layout_for(micro_idx)
        live_rows = layout[2]
        result, saved_state = block_forward(x_in, layout, weights)
        result_low = result.astype(jnp.bfloat16)
        kept_inputs = put_block(kept_inputs, x_in, micro_idx, active)
        activ_store = put_block(activ_store, result_low, micro_idx, active)
        labels_now = lax.dynamic_index_in_dim(labels, micro_idx, 1, keepdims=False)
        logits = lax.psum(
            jnp.einsum("rc,tco->tro", result_low, heads_all, preferred_element_type=jnp.float32),
            "mp",
        )
        peak_val = jnp.max(logits, axis=2, keepdims=True)
        expo = jnp.exp(logits - peak_val)
        soft_p = expo / jnp.sum(expo, axis=2, keepdims=True)
        picked = (class_ids == labels_now[:, :, None]).astype(jnp.float32)
        delta_low = (LOSS_WEIGHT * live_rows[None, :, None] * (soft_p - picked)).astype(
            jnp.bfloat16
        )
        task_grads = jnp.einsum(
            "tro,tco->trc", delta_low, heads_all, preferred_element_type=jnp.float32
        )
        merged = sign_merge(task_grads, take_block(thresholds, micro_idx))
        use_head = active & (section_idx == 1)
        head_grad = head_grad + jnp.where(
            use_head,
            jnp.einsum("rc,tro->tco", result_low, delta_low, preferred_element_type=jnp.float32),
            0.0,
        )
        cotangents = put_block(cotangents, merged, micro_idx, use_head)
        received = shifted(result_low, "section", 1)
    grad_recv = jnp.zeros(block_input.shape[1:], jnp.bfloat16)
    input_store = jnp.zeros(block_input.shape, jnp.float32)
    grad_total = None
    for turn_idx in range(micro_count + 1):
        micro_idx = jnp.clip(turn_idx - 1 + section_idx, 0, micro_count - 1)
        active = (turn_idx - 1 + section_idx >= 0) & (turn_idx - 1 + section_idx < micro_count)
        d_out = jnp.where(
            section_idx == 1, take_block(cotangents, micro_idx), grad_recv.astype(jnp.float32)
        )
        x_in = take_block(kept_inputs, micro_idx)
        layout = layout_for(micro_idx)
        saved_state = block_forward(x_in, layout, weights)[1]
        d_in, grad_set = block_backward(d_out, x_in, layout, weights, saved_state)
        masked = jax.tree.map(lambda leaf: jnp.where(active, leaf, 0.0), grad_set)
        grad_total = masked if grad_total is None else jax.tree.map(jnp.add, grad_total, masked)
        d_send = d_in.astype(jnp.bfloat16)
        input_store = put_block(
            input_store,
            jnp.where(section_idx == 1, d_send.astype(jnp.float32), d_in),
            micro_idx,
            active,
        )
        grad_recv = shifted(d_send, "section", -1)
    g_red, g_spa, g_exp, g_gain_in, g_shift_in, g_gain_out, g_shift_out = grad_total
    out_red, out_spa, out_exp, out_gain_in, out_shift_in, out_gain_out, out_shift_out = (
        lax.psum_scatter(g_red[None], "dp", scatter_dimension=2, tiled=True),
        lax.psum_scatter(g_spa[None], "dp", scatter_dimension=2, tiled=True),
        lax.psum_scatter(g_exp[None], "dp", scatter_dimension=1, tiled=True),
        lax.psum_scatter(g_gain_in[None, :, None, :], "dp", scatter_dimension=3, tiled=True),
        lax.psum_scatter(g_shift_in[None, :, None, :], "dp", scatter_dimension=3, tiled=True),
        lax.psum_scatter(g_gain_out[None, None, :], "dp", scatter_dimension=2, tiled=True),
        lax.psum_scatter(g_shift_out[None, None, :], "dp", scatter_dimension=2, tiled=True),
    )
    head_out = lax.psum_scatter(head_grad, ("section", "dp"), scatter_dimension=2, tiled=True)
    return (
        activ_store[None],
        input_store[None],
        out_red,
        out_spa,
        out_exp,
        out_gain_in,
        out_shift_in,
        out_gain_out,
        out_shift_out,
        head_out,
    )


K0 = math.sqrt(2.0 / math.pi)
K1 = 0.044715
MESH = pl.DeviceIdType.MESH
F32 = jnp.float32
BF16 = jnp.bfloat16
SIDES = (2, 7)
TAPS = [(a, b) for a in (-1, 0, 1) for b in (-1, 0, 1)]
PAD = 8
NN = (((1,), (0,)), ((), ()))
NT = (((1,), (1,)), ((), ()))
TN = (((0,), (0,)), ((), ()))


def tap_masks():
    found = []
    for tap_idx, (a, b) in enumerate(TAPS):
        for side in SIDES:
            found.append((tap_idx, a, b, side, a * side + b))
    return found


MASKS = tap_masks()


def dot(left, right, dims):
    return lax.dot_general(left, right, dims, preferred_element_type=F32)


def gelu(v):
    return 0.5 * v * (1.0 + jnp.tanh(K0 * v * (1.0 + K1 * v * v)))


def gelu_grad(v):
    sq = v * v
    t = jnp.tanh(K0 * v * (1.0 + K1 * sq))
    return 0.5 * (1.0 + t) + (0.5 * K0) * v * (1.0 - t * t) * (1.0 + 3.0 * K1 * sq)


def fold(x):
    return jnp.sum(x.reshape(x.shape[0] // 8, 8, x.shape[1]), axis=0)


def wide(x, width):
    times = width // x.shape[1]
    return x if times == 1 else jnp.concatenate([x] * times, axis=1)


def loop(total, chunk, body, init=None):
    def one(i, carry):
        return body(pl.ds(pl.multiple_of(i * chunk, chunk), chunk), carry)

    return lax.fori_loop(0, total // chunk, one, 0 if init is None else init)


def rows_tile(first, second, third):
    width = first.shape[1]
    place = lax.broadcasted_iota(jnp.int32, (8, width), 0)
    wide_of = lambda v: jnp.broadcast_to(v, (8, width))
    return jnp.where(
        place == 0, wide_of(first), jnp.where(place == 1, wide_of(second), wide_of(third))
    )


class Sems:
    def __init__(self, ref):
        self.ref, self.used, self.size = ref, 0, ref.shape[0]

    def take(self, count=1):
        first = self.used
        self.used += count
        assert self.used <= self.size, self.used
        return first


def make_kernel(sizes):
    n_dp, n_mp, R, Wd, M, C, Cd, classes, tasks, piece = sizes
    n_sec = 2
    W9 = 9 * C

    def kernel(*refs):
        (
            x_hbm, sides_hbm, wred_hbm, wspa_hbm, wexp_hbm, gin_hbm, sin_hbm, gout_hbm, sout_hbm,
            head_hbm, lab_hbm, thr_hbm,
            act_hbm, ig_hbm, red_hbm, spa_hbm, exp_hbm, vec_hbm, head_out,
            ssems, rsems, lsems, go,
            sred, sspa, sexp, shead, thr, xin, wr, wsp, we, hd, par,
            live, geo, masks, labc,
            rs_s, rs_r, ag_a, ag_b, ag_d, fulla, fullb, dfull, co, sums_s, sums_r, sums_t, st, keep, first, second, third, ppad, dpad, dbuf,
            lg_s, lg_r, dl, act1, tg, dpre, evec, dth, ig, slope, steep,
            gred, gspa, gexp, sibred, sibspa, sibexp, rred, rspa, rexp, ghead, rhead, vec, vsib,
            ored, ospa, oexp, ovec, ohead,
            sides_ref, gin_ref, sin_ref, gout_ref, sout_ref, lab_ref,
        ) = refs
        s = lax.axis_index("section")
        d = lax.axis_index("dp")
        m = lax.axis_index("mp")
        o = 1 - s
        recv, local = Sems(rsems), Sems(lsems)
        pending = {None: [], 0: [], 1: []}
        sends = {None: 0, 0: 1, 1: 2}
        rem = lax.rem
        dp_dev = lambda t: (s, t, m)
        mp_dev = lambda t: (s, d, t)
        sib_dev = (o, d, m)

        def put_to(src, dst, ssem, rsem, dev):
            pltpu.make_async_remote_copy(
                src_ref=src,
                dst_ref=dst,
                send_sem=ssems.at[ssem],
                recv_sem=rsems.at[rsem],
                device_id=dev,
                device_id_type=MESH,
            ).start()

        def waiter(ref, ssem, rsem):
            return pltpu.make_async_remote_copy(
                src_ref=ref,
                dst_ref=ref,
                send_sem=ssems.at[ssem],
                recv_sem=rsems.at[rsem],
                device_id=sib_dev,
                device_id_type=MESH,
            )

        def rcopy(src, dst, rsem, dev, when=None):
            ssem = sends[when]
            put_to(src(), dst(), ssem, rsem, dev)
            pending[when].append(lambda: waiter(src(), ssem, 0).wait_send())

        def arrive(dst, rsem):
            waiter(dst, 0, rsem).wait_recv()

        axes = {"dp": (n_dp, d, dp_dev), "mp": (n_mp, m, mp_dev)}
        expected, hold = {}, {}

        def settle(key):
            expected.pop(key)()

        def load(src, dst):
            cp = pltpu.make_async_copy(src, dst, lsems.at[local.take()])
            cp.start()
            key = ("load", local.used)
            expected[key] = cp.wait
            return key

        def on(cond, what):
            return lambda: pl.when(cond())(what)

        class Group:
            def __init__(self, axis, all_of, when=None, slot_of=None):
                self.n, self.me, self.dev = axes[axis]
                self.ssem = sends[when]
                self.rsem = recv.take(1 if slot_of is None else self.n - 1)
                self.all_of, self.when, self.slot_of = all_of, when, slot_of

            def put(self, src_of, slot_of):
                for k in range(1, self.n):
                    t = rem(self.me + k, self.n)
                    rsem = self.rsem + (0 if self.slot_of is None else k - 1)
                    put_to(src_of(t), slot_of(self.me), self.ssem, rsem, self.dev(t))

            def came_from(self, k):
                return rem(self.me + self.n - k, self.n)

            def close(self):
                ssem, all_of, when = self.ssem, self.all_of, self.when
                pending[when].append(lambda: waiter(all_of(), ssem, 0).wait_send())
                if self.slot_of is None:
                    waits = {self.rsem: lambda: arrive(all_of(), self.rsem)}
                else:
                    waits = {
                        self.rsem + k - 1: lambda k=k: arrive(
                            self.slot_of(self.came_from(k)), self.rsem + k - 1
                        )
                        for k in range(1, self.n)
                    }
                for key, wait in waits.items():
                    expected[key] = wait if when is None else on(lambda: s == when, wait)
                return self.rsem

        def spread(axis, src_of, slot_of, all_of, when=None):
            group = Group(axis, all_of, when)
            group.put(src_of, slot_of)
            return group.close()

        barrier = pltpu.get_barrier_semaphore()
        greeted = 0
        for ds_ in range(n_sec):
            for k in range(n_dp):
                if ds_ == 0 and k == 0:
                    continue
                pl.semaphore_signal(
                    barrier, inc=1,
                    device_id=(rem(s + ds_, n_sec), rem(d + k, n_dp), m),
                    device_id_type=MESH,
                )
                greeted += 1
        for k in range(1, n_mp):
            pl.semaphore_signal(
                barrier, inc=1, device_id=(s, d, rem(m + k, n_mp)), device_id_type=MESH
            )
            greeted += 1


        l_red = load(wred_hbm.at[0], sred)
        l_par = [
            load(src, dst)
            for src, dst in (
                (gin_hbm, gin_ref), (sin_hbm, sin_ref), (gout_hbm, gout_ref), (sout_hbm, sout_ref)
            )
        ]
        l_x = load(x_hbm.at[s], xin.at[0])
        l_spa = load(wspa_hbm.at[0], sspa)
        l_exp = load(wexp_hbm.at[0], sexp)
        l_small = [load(sides_hbm, sides_ref), load(lab_hbm, lab_ref)]
        l_head = load(head_hbm, shead)
        l_thr = load(thr_hbm.at[s], thr)

        settle(l_red)
        wr[s, d] = sred[...].astype(BF16)
        for key in l_par:
            settle(key)
        par[s] = jnp.zeros(par.shape[1:], F32)
        for i in range(2):
            par[s, i:i + 1, :C] = gin_ref[0, i:i + 1, :]
            par[s, 2 + i:3 + i, :C] = sin_ref[0, i:i + 1, :]
        par[s, 4:5, :] = gout_ref[...]
        par[s, 5:6, :] = sout_ref[...]
        pl.semaphore_wait(barrier, greeted)

        by_dp, by_sib = {}, {}

        def send_own(buf, j):
            def go():
                by_dp[id(buf), j] = spread(
                    "dp",
                    lambda t: buf.at[j, d],
                    lambda src: buf.at[j, src],
                    lambda: buf.at[j, pl.ds(0, n_dp - 1)],
                    when=j,
                )

            pl.when(s == j)(go)

        def pass_on(buf, j):
            settle(by_dp[id(buf), j])
            sem = by_sib[id(buf), j] = recv.take()

            @pl.when(s == j)
            def _():
                rcopy(lambda: buf.at[j], lambda: buf.at[j], sem, sib_dev, when=j)

            expected[sem] = on(lambda: s != j, lambda: arrive(buf.at[j], sem))

        def from_sib(buf, j):
            settle(by_sib[id(buf), j])

        par_sem = recv.take()
        rcopy(lambda: par.at[s], lambda: par.at[s], par_sem, sib_dev)
        expected[par_sem] = lambda: arrive(par.at[o], par_sem)
        early = Group(
            "dp",
            lambda: wr.at[0, pl.ds(0, n_dp - 1)],
            when=0,
            slot_of=lambda src: wr.at[0, src],
        )

        @pl.when(s == 0)
        def _():
            early.put(lambda t: wr.at[0, d], lambda src: wr.at[0, src])

        early.close()

        settle(l_spa)
        for k in range(9):
            wsp[s, d, :, k * C:(k + 1) * C] = sspa[k].astype(BF16)

        settle(l_exp)
        we[s, d] = sexp[...].astype(BF16)

        for key in l_small:
            settle(key)
        sides = jnp.where(s == 0, sides_ref[0], sides_ref[1]).astype(F32)
        slots = sides.shape[1]
        sq = jnp.broadcast_to(sides * sides, (8, slots)).astype(BF16)
        upper = (
            lax.broadcasted_iota(jnp.int32, (slots, slots), 0)
            <= lax.broadcasted_iota(jnp.int32, (slots, slots), 1)
        ).astype(BF16)
        ends = dot(sq, upper, NN)[0:1]
        starts = ends - sides * sides
        nloc = jnp.broadcast_to(jnp.max(ends, axis=1, keepdims=True), (1, 128))
        shape = (R, 128)
        pos = lax.broadcasted_iota(jnp.int32, (R, slots), 0).astype(F32)
        inside = (pos >= starts) & (pos < ends)
        origin = jnp.sum(jnp.where(inside, starts, 0.0), axis=1, keepdims=True)
        side = jnp.sum(jnp.where(inside, sides, 0.0), axis=1, keepdims=True)
        geo[0] = jnp.broadcast_to(origin, shape)
        geo[1] = jnp.broadcast_to(side, shape)

        def make_masks(rows, carry):
            side_b = geo[1, rows]
            here = lax.broadcasted_iota(jnp.int32, side_b.shape, 0) + rows.start
            offset = here.astype(F32) - geo[0, rows]
            row_in = jnp.floor((offset + 0.5) / jnp.maximum(side_b, 1.0))
            col_in = offset - row_in * side_b
            live[rows] = (side_b > 0.0).astype(F32)
            for idx, (_, a, b, q, _) in enumerate(MASKS):
                ra, cb = row_in + a, col_in + b
                ok = (side_b == q) & (ra >= 0.0) & (ra < q) & (cb >= 0.0) & (cb < q)
                masks[idx, rows] = ok.astype(F32)
            return carry

        loop(R, 64, make_masks)
        for buf in (ppad, dpad):
            edge = jnp.zeros((PAD, buf.shape[1]), F32)
            buf[0:PAD] = edge
            buf[PAD + R:PAD + R + PAD] = edge
        lab2 = lab_ref[...]
        lab = jnp.where(s == 0, lab2[:, 0], lab2[:, 1]).astype(F32)
        lab = jnp.concatenate([lab, jnp.zeros((8 - tasks, R), F32)], axis=0)
        labc[...] = jnp.transpose(lab)

        settle(l_head)
        mine = s * n_dp + d
        for t in range(tasks):
            hd[mine, t] = shead[t].astype(BF16)

        def to_all(src_of, buf):
            ssem, rsem = sends[None], recv.take()
            others = [(a, k) for a in range(n_sec) for k in range(n_dp) if a or k]
            for a, k in others:
                ts, td = rem(s + a, n_sec), rem(d + k, n_dp)
                put_to(src_of(ts * n_dp + td), buf.at[mine], ssem, rsem, (ts, td, m))
            rest = lambda: buf.at[pl.ds(0, len(others))]
            pending[None].append(lambda: waiter(rest(), ssem, 0).wait_send())
            expected[rsem] = lambda: arrive(rest(), rsem)
            return rsem

        def cat(buf, n):
            return jnp.concatenate([buf[i] for i in range(n)], axis=1)

        phase = {"rs": 0, "st": 0}

        def rs_open():
            p = phase["rs"]
            phase["rs"] += 1
            return p, Group("mp", lambda: rs_r.at[p, pl.ds(0, n_mp - 1)])

        def rs_rows(handle, rows, out):
            p, group = handle
            for c in range(n_mp):
                rs_s[p, c, rows] = out[:, c * C:(c + 1) * C].astype(BF16)
            group.put(lambda t: rs_s.at[p, t, rows], lambda src: rs_r.at[p, src, rows])

        def rs_finish(handle, dst):
            p, group = handle
            settle(group.rsem)

            def add(rows, carry):
                dst[rows] = rs_sum(handle, rows)
                return carry

            loop(R, 128, add)

        def exchange(tile):
            p = phase["st"]
            phase["st"] += 1
            width = tile.shape[1]
            st[p, d, :, 0:width] = tile
            slot = lambda src: st.at[p, src, :, 0:width]
            rest = lambda: st.at[p, pl.ds(0, n_dp - 1), :, 0:width]
            return p, width, spread("dp", lambda t: slot(d), slot, rest)

        def collect(handle):
            p, width, base = handle
            settle(base)
            return [st[p, i, :, 0:width] for i in range(n_dp)]

        def stats_start(buf, width, total=None):
            chunk = 128 if width <= 128 else 32
            zero = jnp.zeros((8, width), F32)

            def sum_up(rows, carry):
                return carry + fold(buf[rows] * wide(live[rows], width))

            if total is None:
                total = loop(R, chunk, sum_up, zero)
            total = jnp.sum(total, axis=0, keepdims=True)
            count = wide(nloc, width)
            mean = total / jnp.maximum(count, 1.0)

            def squares(rows, carry):
                off = (buf[rows] - mean) * wide(live[rows], width)
                return carry + fold(off * off)

            sqs = jnp.sum(loop(R, chunk, squares, zero), axis=0, keepdims=True)
            return exchange(rows_tile(total, sqs, count)), mean

        def stats_finish(handle, j, i):
            tiles = collect(handle)
            width = handle[1]
            count = sum(t[2:3] for t in tiles)
            mean = sum(t[0:1] for t in tiles) / count
            sqs = 0.0
            for t in tiles:
                local_mean = t[0:1] / jnp.maximum(t[2:3], 1.0)
                sqs = sqs + t[1:2] + t[2:3] * (local_mean - mean) * (local_mean - mean)
            inv = lax.rsqrt(sqs / count + NORM_EPS)
            keep[j, i, :, 0:width] = rows_tile(mean, inv, count)

        def parted(*twelfths):
            at = [max(32, R * n // 12 // 32 * 32) for n in twelfths]
            return [slice(a, b) for a, b in zip([0] + at, at + [R])]

        spans, halves = parted(2, 7), parted(6)

        def rows_out(buf, at, rows, values):
            buf[at, m, rows] = values.astype(BF16)
            return spread(
                "mp",
                lambda t: buf.at[at, m, rows],
                lambda src: buf.at[at, src, rows],
                lambda: buf.at[at, pl.ds(0, n_mp - 1), rows],
            )

        def rs_rows_sums(handle, j, i, rows, out, carry):
            p, groups = handle
            sb, sg = carry
            raw = (ag_a, ag_b)[i]
            for c in range(n_mp):
                part = out[:, c * C:(c + 1) * C]
                rs_s[p, c, rows] = part.astype(BF16)
                tile = co[2 * j + i, c]
                g = part * slope[j, i, c, rows]
                xhat = raw[j, c, rows].astype(F32) * tile[2:3] + tile[3:4]
                sb[c] = sb[c] + fold(g)
                sg[c] = sg[c] + fold(g * xhat)
            last = rows.stop == R
            if last:
                sums = sums_out(p, sb + sg)
            group = Group("mp", lambda: rs_r.at[p, pl.ds(0, n_mp - 1), rows])
            group.put(lambda t: rs_s.at[p, t, rows], lambda src: rs_r.at[p, src, rows])
            groups.append(group.close())
            return sums if last else None

        def sums_out(p, parts):
            place = lax.broadcasted_iota(jnp.int32, (2 * n_mp, C), 0)
            tile = jnp.zeros((2 * n_mp, C), F32)
            for i, part in enumerate(parts):
                tile = jnp.where(place == i, jnp.sum(part, axis=0, keepdims=True), tile)
            sums_s[p] = tile
            ssem, rsem = sends[None], recv.take()
            others = [(a, k) for a in range(n_mp) for k in range(n_dp) if a or k]
            me = m * n_dp + d
            for a, k in others:
                tz, td = rem(m + a, n_mp), rem(d + k, n_dp)
                put_to(sums_s.at[p], sums_r.at[p, me], ssem, rsem, (s, td, tz))
            rest = lambda: sums_r.at[p, pl.ds(0, len(others))]
            pending[None].append(lambda: waiter(rest(), ssem, 0).wait_send())
            expected[rsem] = lambda: arrive(rest(), rsem)

            def collect_sums():
                settle(rsem)
                total = sums_s[p]
                for a, k in others:
                    total = total + sums_r[p, rem(m + a, n_mp) * n_dp + rem(d + k, n_dp)]
                sums_t[p] = total
                return total

            return collect_sums

        def rs_parts():
            p = phase["rs"]
            phase["rs"] += 1
            return p, []

        def rs_sum(handle, rows):
            p, _ = handle
            out = rs_s[p, m, rows].astype(F32)
            for k in range(1, n_mp):
                out = out + rs_r[p, rem(m + k, n_mp), rows].astype(F32)
            return out

        def coeffs_out(at, *values):
            place = lax.broadcasted_iota(jnp.int32, (8, C), 0)
            tile = jnp.zeros((8, C), F32)
            for i, v in enumerate(values):
                tile = jnp.where(place == i, jnp.broadcast_to(v, (8, C)), tile)
            co[at, m] = tile
            slot = lambda src: co.at[at, src]
            return spread("mp", lambda t: slot(m), slot, lambda: co.at[at, pl.ds(0, n_mp - 1)])

        def inner_norm(j, i, src, raw, full, hook, need, consume):
            at = 2 * j + i
            handle, mean_here = stats_start(src.at[j], C)
            push = lambda rows: rows_out(raw, j, rows, src[j, rows] - mean_here)
            groups = [push(rows) for rows in spans[:-1]]
            hook()
            stats_finish(handle, j, i)
            mu, inv, _, gain, shift = norm_of(j, i, C)
            moved = (mean_here - mu) * inv
            sent = coeffs_out(at, gain * inv, gain * moved + shift, inv, moved)
            groups.append(push(spans[-1]))
            need()
            settle(sent)
            for rows, group in zip(spans, groups):
                settle(group)
                for c in range(n_mp):
                    tile = co[at, c]
                    y = live[rows] * (raw[j, c, rows].astype(F32) * tile[0:1] + tile[1:2])
                    full[j, rows, c * C:(c + 1) * C] = gelu(y).astype(BF16)
                consume(rows)

        def norm_of(j, i, width):
            tile = keep[j, i, :, 0:width]
            if i < 2:
                gain, shift = par[j, i:i + 1, 0:width], par[j, 2 + i:3 + i, 0:width]
            else:
                gain, shift = par[j, 4:5, 0:width], par[j, 5:6, 0:width]
            return tile[0:1], tile[1:2], tile[2:3], gain, shift

        def taps_sum(src, flip, put):
            way = -1 if flip else 1
            for rows in spans:
                first_row, last_row = PAD + rows.start, PAD + rows.stop
                put(rows, lambda idx_list, lanes: sum(
                    masks[(len(MASKS) - 2 - (idx // 2) * 2 + idx % 2) if flip else idx, rows]
                    * src[first_row + way * MASKS[idx][4]:last_row + way * MASKS[idx][4], lanes]
                    for idx in idx_list
                ))

        nothing = lambda: None
        vec[...] = jnp.zeros(vec.shape, F32)

        def prepare(j):
            for i, raw in enumerate((ag_a, ag_b)):
                def inner(rows, carry):
                    for c in range(n_mp):
                        tile = co[2 * j + i, c]
                        y = live[rows] * (raw[j, c, rows].astype(F32) * tile[0:1] + tile[1:2])
                        slope[j, i, c, rows] = live[rows] * gelu_grad(y)
                    return carry

                loop(R, 64, inner)
            mu, inv, _, gain, shift = norm_of(j, 2, Wd)

            def outer(rows, carry):
                lv = wide(live[rows], Wd)
                pre = lv * (gain * ((third[j, rows] - mu) * inv) + shift)
                steep[j, rows] = lv * gelu_grad(pre + xin[j, rows].astype(F32))
                return carry

            loop(R, 32, outer)

        def forward(j, h, hooks, needs):
            hooks[0]()
            rs_finish(h, first.at[j])

            def conv(rows):
                there = slice(PAD + rows.start, PAD + rows.stop)
                ppad[there] = dot(fulla[j, rows], wsp[j].reshape(M, W9), NN)

            inner_norm(j, 0, first, ag_a, fulla, hooks[1], needs[0], conv)

            def put(rows, summed):
                second[j, rows] = sum(
                    summed([2 * k, 2 * k + 1], slice(k * C, (k + 1) * C)) for k in range(9)
                )

            taps_sum(ppad, False, put)
            if j == 0:
                pass_on(wr, 1)
            sums = []

            def expand(rows):
                out = dot(fullb[j, rows], we[j].reshape(M, Wd), NN)
                third[j, rows] = out
                sums.append(fold(out * wide(live[rows], Wd)))

            inner_norm(j, 1, second, ag_b, fullb, hooks[2], needs[1], expand)
            h, _ = stats_start(third.at[j], Wd, sum(sums))
            hooks[3]()
            stats_finish(h, j, 2)
            mu, inv, _, gain, shift = norm_of(j, 2, Wd)
            out = xin.at[1] if j == 0 else act1

            def act_c(rows):
                for r0 in range(rows.start, rows.stop, 32):
                    there = slice(r0, r0 + 32)
                    lv = wide(live[there], Wd)
                    pre = lv * (gain * ((third[j, there] - mu) * inv) + shift)
                    pre = pre + xin[j, there].astype(F32)
                    out[there] = (lv * gelu(pre)).astype(BF16)

            return act_c

        def to_section(src, hbm, j):
            sem = recv.take()

            @pl.when(s == j)
            def _():
                lsem = local.take()
                made = lambda: pltpu.make_async_copy(src(), hbm.at[0, s], lsems.at[lsem])
                made().start()
                pending[j].append(lambda: made().wait())

            @pl.when(s != j)
            def _():
                rcopy(src, lambda: hbm.at[0, s], sem, sib_dev, when=1 - j)

            expected[sem] = on(lambda: s == j, lambda: arrive(hbm.at[0, o], sem))

        grads = ((gred, sibred, rred), (gspa, sibspa, rspa), (gexp, sibexp, rexp))
        at_sib, at_dp = {}, {}

        def grad_to_sib(which, j):
            own, sib, _ = grads[which]
            sem = at_sib[which, j] = recv.take()

            @pl.when(s != j)
            def _():
                rcopy(lambda: own.at[j], lambda: sib, sem, sib_dev, when=1 - j)

            expected[sem] = on(lambda: s == j, lambda: arrive(sib, sem))

        def grad_to_dp(which, j):
            own, sib, got = grads[which]
            settle(at_sib[which, j])

            def go():
                def add(rows, carry):
                    for i in range(n_dp):
                        own[j, i, rows] = (
                            own[j, i, rows].astype(F32) + sib[i, rows].astype(F32)
                        ).astype(BF16)
                    return carry

                loop(own.shape[2], 64, add)
                base = spread(
                    "dp",
                    lambda t: own.at[j, t],
                    lambda src: got.at[src],
                    lambda: got.at[pl.ds(0, n_dp - 1)],
                    when=j,
                )
                at_dp.setdefault(which, []).append(base)

            pl.when(s == j)(go)

        def reduce_to_sib(j):
            for i in range(n_dp):
                full = dfull[j, :, i * Cd:(i + 1) * Cd]
                gred[j, i] = dot(xin[j], full, TN).astype(BF16)
                sem = at_sib[0, j, i] = recv.take()

                @pl.when(s != j)
                def _():
                    rcopy(lambda: gred.at[j, i], lambda: sibred.at[i], sem, sib_dev, when=1 - j)

                expected[sem] = on(
                    lambda: s == j, lambda i=i, sem=sem: arrive(sibred.at[i], sem)
                )

        def reduce_to_dp(j):
            group = Group("dp", lambda: rred.at[pl.ds(0, n_dp - 1)], when=j)
            for i in range(n_dp):
                settle(at_sib[0, j, i])

                @pl.when(s == j)
                def _():
                    def add(rows, carry):
                        gred[j, i, rows] = (
                            gred[j, i, rows].astype(F32) + sibred[i, rows].astype(F32)
                        ).astype(BF16)
                        return carry

                    loop(Wd, 128, add)

                    @pl.when(d != i)
                    def _():
                        put_to(gred.at[j, i], rred.at[d], group.ssem, group.rsem, dp_dev(i))

            at_dp.setdefault(0, []).append(group.close())

        def steepest(j, rows, e, carry):
            mu, inv, _, _, _ = norm_of(j, 2, Wd)
            out = steep[j, rows] * e
            dpre[rows] = out
            return carry[0] + fold(out), carry[1] + fold(out * ((third[j, rows] - mu) * inv))

        def backward(j, sums, hooks):
            mu, inv, count, gain, shift = norm_of(j, 2, Wd)
            sb, sg = sums
            total = lambda v: jnp.sum(v, axis=0, keepdims=True)
            sb, sg = total(sb), total(sg)
            h = exchange(rows_tile(sb, sg, sg))
            hooks[0]()
            tile = sum(collect(h))
            vec[j, 4:5, :] = tile[1:2]
            vec[j, 5:6, :] = tile[0:1]
            sb_n, sg_n = tile[0:1] / count, tile[1:2] / count
            scale = gain * inv

            def d_third(rows, carry):
                lv = wide(live[rows], Wd)
                xhat = (third[j, rows] - mu) * inv
                dth[rows] = (lv * scale * (dpre[rows] - sb_n - xhat * sg_n)).astype(BF16)
                return carry

            none = lambda: ([jnp.zeros((8, C), F32)] * n_mp, [jnp.zeros((8, C), F32)] * n_mp)
            h, carry = rs_parts(), none()
            for rows in halves:
                for r0 in range(rows.start, rows.stop, 32):
                    d_third(slice(r0, r0 + 32), 0)
                out = dot(dth[rows], we[j].reshape(M, Wd), NT)
                sums_of = rs_rows_sums(h, j, 1, rows, out, carry)
            for i in range(n_dp):
                full = fullb[j, :, i * Cd:(i + 1) * Cd]
                gexp[j, i] = dot(full, dth[...], TN).astype(BF16)
            grad_to_sib(2, j)
            hooks[1]()
            for group in h[1]:
                settle(group)

            def norm_sums(i, sums):
                p = sums[0]
                place = lax.broadcasted_iota(jnp.int32, (2 * n_mp, C), 0)
                row = lambda i: jnp.sum(
                    jnp.where(place == i, sums_t[p], 0.0), axis=0, keepdims=True
                )
                sb, sg = row(m), row(n_mp + m)
                vec[j, i:i + 1, 0:C] = sg
                vec[j, 2 + i:3 + i, 0:C] = sb
                return sb, sg

            sums_of()
            sb_b, sg_b = norm_sums(1, h)
            mu_b, inv_b, count_b, gain_b, _ = norm_of(j, 1, C)
            scale_b, sb_b, sg_b = gain_b * inv_b, sb_b / count_b, sg_b / count_b
            for rows in spans:
                there = slice(PAD + rows.start, PAD + rows.stop)
                xhat = (second[j, rows] - mu_b) * inv_b
                g = slope[j, 1, m, rows] * rs_sum(h, rows)
                out = live[rows] * scale_b * (g - sb_b - xhat * sg_b)
                dpad[there] = out.astype(BF16).astype(F32)

            h, carry = rs_parts(), none()
            sums_a = []

            def put(rows, summed):
                for k in range(9):
                    dbuf[rows, k * C:(k + 1) * C] = summed([2 * k, 2 * k + 1], slice(None)).astype(BF16)
                out = dot(dbuf[rows], wsp[j].reshape(M, W9), NT)
                sums_a.append(rs_rows_sums(h, j, 0, rows, out, carry))

            taps_sum(dpad, True, put)
            for i in range(n_dp):
                full = fulla[j, :, i * Cd:(i + 1) * Cd]
                gspa[j, i] = dot(full, dbuf[...], TN).astype(BF16)
            grad_to_sib(1, j)
            grad_to_dp(2, j)
            hooks[2]()
            groups = []
            for rows, part in zip(spans, h[1]):
                settle(part)
                g = slope[j, 0, m, rows] * rs_sum(h, rows)
                if not groups:
                    pivot = jnp.sum(g, axis=0, keepdims=True) / jnp.maximum(
                        jnp.sum(live[rows], axis=0, keepdims=True), 1.0
                    )
                    sent = coeffs_out(4 + j, pivot)
                groups.append(rows_out(ag_d, j, rows, g - pivot))
            hooks[3]()
            grad_to_dp(1, j)

            def d_input(rows):
                out = dot(dfull[j, rows], cat(wr.at[j], n_dp), NT) + dpre[rows]
                if j == 1:
                    out = out.astype(BF16).astype(F32)
                    evec[rows] = out
                ig[j, rows] = out

            sums = sums_a[-1]()
            norm_sums(0, h)
            if j == 0:
                hold["vec"] = recv.take()
                rcopy(lambda: vec.at[o], lambda: vsib, hold["vec"], sib_dev)
                expected[hold["vec"]] = lambda: arrive(vsib, hold["vec"])
            settle(sent)
            count = keep[j, 0, 2:3, 0:C]
            terms = []
            for c in range(n_mp):
                tile = co[2 * j, c]
                sb_n, sg_n = sums[c:c + 1] / count, sums[n_mp + c:n_mp + c + 1] / count
                scale, inv, moved = tile[0:1], tile[2:3], tile[3:4]
                offset = scale * (co[4 + j, c, 0:1] - sb_n - moved * sg_n)
                terms.append((scale, -scale * sg_n * inv, offset))
            for rows, group in zip(spans, groups):
                settle(group)
                for c, (scale, slant, offset) in enumerate(terms):
                    out = live[rows] * (
                        ag_d[j, c, rows].astype(F32) * scale
                        + ag_a[j, c, rows].astype(F32) * slant
                        + offset
                    )
                    dfull[j, rows, c * C:(c + 1) * C] = out.astype(BF16)
                if j == 1:
                    d_input(rows)
            if j == 0:
                reduce_to_sib(j)
                reduce_to_dp(j)
                for rows in spans:
                    d_input(rows)
            to_section(lambda: ig.at[j], ig_hbm, j)

        settle(l_x)

        def first_product():
            handle = rs_open()
            p, group = handle
            for k in range(n_dp):
                src = early.came_from(k) if k else d
                if k:
                    settle(early.rsem + k - 1)
                sem = recv.take()

                @pl.when(s == 0)
                def _():
                    rcopy(lambda: wr.at[0, src], lambda: wr.at[0, src], sem, sib_dev, when=0)

                expected[sem] = on(lambda: s != 0, lambda: arrive(wr.at[0, src], sem))
                settle(sem)

                def part(rows, carry):
                    rs_s[p, src, rows] = dot(xin[0, rows], wr[0, src], NN).astype(BF16)
                    return carry

                loop(R, 128, part)

                @pl.when(src != m)
                def _():
                    put_to(rs_s.at[p, src], rs_r.at[p, m], group.ssem, group.rsem, mp_dev(src))

            group.close()
            return handle

        @pl.when(s == 1)
        def _():
            pl.semaphore_wait(go, 1)

        start = first_product()
        settle(par_sem)

        def w_next():
            send_own(we, 0)
            send_own(wr, 1)

        def w_head():
            hold["heads"] = to_all(lambda t: hd.at[mine], hd)

        def f00():
            send_own(wsp, 0)

            @pl.when(s == 0)
            def _():
                pl.semaphore_signal(go, inc=1, device_id=sib_dev, device_id_type=MESH)

        hooks = (f00, w_next, lambda: send_own(wsp, 1), nothing)

        def n00():
            pass_on(wsp, 0)
            from_sib(wsp, 0)

        def n01():
            pass_on(we, 0)
            from_sib(we, 0)

        act_c = forward(0, start, hooks, (n00, n01))
        from_sib(wr, 1)
        start = rs_open()
        for rows in spans:
            act_c(rows)
            rs_rows(start, rows, dot(xin[1, rows], cat(wr.at[1], n_dp), NN))
        start[1].close()

        def f10():
            send_own(we, 1)
            pass_on(wsp, 1)
            to_section(lambda: xin.at[1], act_hbm, 0)
            prepare(0)

        def n10():
            pass_on(we, 1)
            from_sib(wsp, 1)

        hooks = (f10, w_head, nothing, nothing)
        act_c = forward(1, start, hooks, (n10, lambda: from_sib(we, 1)))

        settle(hold["heads"])
        RM = R // n_mp
        n_cls = n_sec * n_dp

        def heads_of(t):
            return hd[:, t].reshape(classes, Wd)

        logit_group = Group("mp", lambda: lg_r.at[pl.ds(0, n_mp - 1)])
        for c in range(n_mp):
            act_c(slice(c * RM, (c + 1) * RM))
            rows = act1[c * RM:(c + 1) * RM]
            for t in range(tasks):
                lg_s[c, :, t * classes:(t + 1) * classes] = dot(rows, heads_of(t), NT).astype(
                    lg_s.dtype
                )

            @pl.when(m != c)
            def _():
                put_to(
                    lg_s.at[c], lg_r.at[m], logit_group.ssem, logit_group.rsem, mp_dev(c)
                )

        base = logit_group.close()
        to_section(lambda: act1, act_hbm, 1)
        settle(l_thr)
        prepare(1)
        settle(base)
        here = pl.ds(pl.multiple_of(m * RM, RM), RM)
        lv = wide(live[here], classes)
        for t in range(tasks):
            lanes = slice(t * classes, (t + 1) * classes)
            logit = lg_s[m, :, lanes].astype(F32)
            for k in range(1, n_mp):
                logit = logit + lg_r[rem(m + k, n_mp), :, lanes].astype(F32)
            expo = jnp.exp(logit - jnp.max(logit, axis=1, keepdims=True))
            soft = expo / jnp.sum(expo, axis=1, keepdims=True)
            ids = lax.broadcasted_iota(jnp.int32, (RM, classes), 1).astype(F32)
            hot = (ids == labc[here, t:t + 1]).astype(F32)
            dl[m, :, lanes] = (LOSS_WEIGHT * lv * (soft - hot)).astype(BF16)
        group = Group(
            "mp", lambda: dl.at[pl.ds(0, n_mp - 1)], slot_of=lambda src: dl.at[src]
        )
        group.put(lambda t: dl.at[m], lambda src: dl.at[src])
        group.close()

        def merge_block(c, sums):
            for t in range(tasks):
                lanes = slice(t * classes, (t + 1) * classes)
                tg[t] = dot(dl[c, :, lanes], heads_of(t), NN)

            def merge(rows, carry):
                total = soft_sum = None
                for t in range(tasks):
                    g = tg[t, rows]
                    soft = jnp.sqrt(g * g + SIGN_FLOOR * SIGN_FLOOR) - SIGN_FLOOR
                    total = g if t == 0 else total + g
                    soft_sum = soft if t == 0 else soft_sum + soft
                purity = 0.5 * (1.0 + total / (soft_sum + SIGN_FLOOR))
                start = pl.multiple_of(rows.start + c * RM, 32)
                there = pl.ds(start, 32)
                frac = 1.0 / (1.0 + jnp.exp((thr[there] - purity) * (1.0 / KEEP_TEMPER)))
                upper, lower = 0.5 * (total + soft_sum), 0.5 * (total - soft_sum)
                return steepest(1, there, frac * upper + (1.0 - frac) * lower, carry)

            return loop(RM, 32, merge, sums)

        zero = (jnp.zeros((8, Wd), F32), jnp.zeros((8, Wd), F32))
        sums = merge_block(m, zero)
        for k in [1] + list(range(n_mp - 1, 1, -1)):
            settle(group.rsem + k - 1)
            sums = merge_block(group.came_from(k), sums)

        def b10():
            for t in range(tasks):
                lanes = slice(t * classes, (t + 1) * classes)
                delta = dl[:, :, lanes].reshape(R, classes)
                out = dot(delta, act1[...], TN).astype(BF16)
                ghead[:, t] = out.reshape(n_cls, piece, Wd)
            hold["ghead"] = to_all(lambda t: ghead.at[t], rhead)

        backward(1, sums, (nothing, b10, nothing, nothing))
        sums = loop(R, 32, lambda rows, carry: steepest(0, rows, evec[rows], carry), zero)

        backward(0, sums, (lambda: reduce_to_sib(1), lambda: reduce_to_dp(1), nothing, nothing))

        settle(hold["ghead"])
        for t in range(tasks):
            total = ghead[mine, t].astype(F32)
            for k in range(1, n_cls):
                total = total + rhead[rem(mine + k, n_cls), t].astype(F32)
            ohead[t] = total
        load(ohead, head_out)
        settle(hold["vec"])
        ovec[...] = vec[s] + vsib[...]
        load(ovec, vec_hbm)

        def total_of(own, got, rows):
            out = own[s, d, rows].astype(F32)
            for k in range(1, n_dp):
                out = out + got[rem(d + k, n_dp), rows].astype(F32)
            return out

        def finish_grad(which):
            own, _, got = grads[which]
            for key in at_dp[which]:
                settle(key)

            def finish(rows, carry):
                out = total_of(own, got, rows)
                if which == 1:
                    for k in range(9):
                        ospa[0, k, rows] = out[:, k * C:(k + 1) * C]
                else:
                    (ored if which == 0 else oexp)[0, rows] = out
                return carry

            loop(own.shape[2], 64, finish)
            load((ored, ospa, oexp)[which], (red_hbm, spa_hbm, exp_hbm)[which])

        finish_grad(2)
        finish_grad(1)
        finish_grad(0)
        for key in list(expected):
            settle(key)

        for key, waits in pending.items():
            def finish_all(waits=waits):
                for wait in waits:
                    wait()

            if key is None:
                finish_all()
            else:
                pl.when(s == key)(finish_all)

    return kernel


def fused_device(sizes, *args):
    n_dp, n_mp, R, Wd, M, C, Cd, classes, tasks, piece = sizes
    W9, n_cls = 9 * C, 2 * n_dp
    RM = R // n_mp
    vmem = lambda shape, dtype: pltpu.VMEM(shape, dtype)
    scratch = [
        pltpu.SemaphoreType.DMA((3,)),
        pltpu.SemaphoreType.DMA((95,)),
        pltpu.SemaphoreType.DMA((21,)),
        pltpu.SemaphoreType.REGULAR,
        vmem((Wd, Cd), F32),
        vmem((9, Cd, C), F32),
        vmem((Cd, Wd), F32),
        vmem((tasks, piece, Wd), F32),
        vmem((R, Wd), F32),
        vmem((2, R, Wd), BF16),
        vmem((2, n_dp, Wd, Cd), BF16),
        vmem((2, n_dp, Cd, W9), BF16),
        vmem((2, n_dp, Cd, Wd), BF16),
        vmem((n_cls, tasks, piece, Wd), BF16),
        vmem((2, 8, Wd), F32),
        vmem((R, 128), F32),
        vmem((2, R, 128), F32),
        vmem((len(MASKS), R, 128), F32),
        vmem((R, 8), F32),
        vmem((6, n_mp, R, C), BF16),
        vmem((6, n_mp, R, C), BF16),
        vmem((2, n_mp, R, C), BF16),
        vmem((2, n_mp, R, C), BF16),
        vmem((2, n_mp, R, C), BF16),
        vmem((2, R, M), BF16),
        vmem((2, R, M), BF16),
        vmem((2, R, M), BF16),
        vmem((6, n_mp, 8, C), F32),
        vmem((6, 2 * n_mp, C), F32),
        vmem((6, n_mp * n_dp, 2 * n_mp, C), F32),
        vmem((6, 2 * n_mp, C), F32),
        vmem((12, n_dp, 8, Wd), F32),
        vmem((2, 3, 8, Wd), F32),
        vmem((2, R, C), F32),
        vmem((2, R, C), F32),
        vmem((2, R, Wd), F32),
        vmem((R + 2 * PAD, W9), F32),
        vmem((R + 2 * PAD, C), F32),
        vmem((R, W9), BF16),
        vmem((n_mp, RM, tasks * classes), BF16),
        vmem((n_mp, RM, tasks * classes), BF16),
        vmem((n_mp, RM, tasks * classes), BF16),
        vmem((R, Wd), BF16),
        vmem((tasks, RM, Wd), F32),
        vmem((R, Wd), F32),
        vmem((R, Wd), F32),
        vmem((R, Wd), BF16),
        vmem((2, R, Wd), F32),
        vmem((2, 2, n_mp, R, C), F32),
        vmem((2, R, Wd), F32),
        vmem((2, n_dp, Wd, Cd), BF16),
        vmem((2, n_dp, Cd, W9), BF16),
        vmem((2, n_dp, Cd, Wd), BF16),
        vmem((n_dp, Wd, Cd), BF16),
        vmem((n_dp, Cd, W9), BF16),
        vmem((n_dp, Cd, Wd), BF16),
        vmem((n_dp, Wd, Cd), BF16),
        vmem((n_dp, Cd, W9), BF16),
        vmem((n_dp, Cd, Wd), BF16),
        vmem((n_cls, tasks, piece, Wd), BF16),
        vmem((n_cls, tasks, piece, Wd), BF16),
        vmem((2, 8, Wd), F32),
        vmem((8, Wd), F32),
        vmem((1, Wd, Cd), F32),
        vmem((1, 9, Cd, C), F32),
        vmem((1, Cd, Wd), F32),
        vmem((8, Wd), F32),
        vmem((tasks, piece, Wd), F32),
    ] + [vmem(args[i].shape, args[i].dtype) for i in (1, 5, 6, 7, 8, 10)]
    in_any = pl.BlockSpec(memory_space=pl.ANY)
    whole = lambda shape, dtype=F32: jax.ShapeDtypeStruct(shape, dtype)
    out = pl.pallas_call(
        make_kernel(sizes),
        out_shape=(
            whole((1, 2, R, Wd), BF16),
            whole((1, 2, R, Wd)),
            whole((1, Wd, Cd)),
            whole((1, 9, Cd, C)),
            whole((1, Cd, Wd)),
            whole((8, Wd)),
            whole((tasks, piece, Wd)),
        ),
        in_specs=[in_any] * len(args),
        out_specs=(in_any,) * 7,
        scratch_shapes=scratch,
        compiler_params=pltpu.CompilerParams(
            collective_id=0, has_side_effects=True, vmem_limit_bytes=60 * 2**20
        ),
    )(*args[:9], jnp.transpose(args[9], (0, 2, 1)), *args[10:])
    part, outer = C // n_dp, Wd // n_dp
    shapes = (
        whole((1, 2, R, Wd), BF16),
        whole((1, 2, R, Wd)),
        whole((1, Wd, Cd)),
        whole((1, 9, Cd, C)),
        whole((1, Cd, Wd)),
        whole((1, 2, 1, part)),
        whole((1, 2, 1, part)),
        whole((1, 1, outer)),
        whole((1, 1, outer)),
        whole((tasks, piece, Wd)),
    )
    done = pl.pallas_call(
        hand_out,
        out_shape=shapes,
        in_specs=[in_any] * 7,
        out_specs=(in_any,) * 10,
        scratch_shapes=[pltpu.VMEM(a.shape, a.dtype) for a in shapes]
        + [vmem((8, Wd), F32), pltpu.SemaphoreType.DMA((9,)), pltpu.SemaphoreType.DMA((12,))],
    )(*out)
    return done[:9] + (jnp.transpose(done[9], (0, 2, 1)),)


def hand_out(*refs):
    given, outs, held, vec, came, left = refs[:7], refs[7:17], refs[17:27], *refs[27:]
    gains, shifts, gain_out, shift_out = held[5:9]
    load_vec = pltpu.make_async_copy(given[5], vec, came.at[8])
    load_vec.start()
    pieces = []
    for src, mid, dst in zip(given[:5] + given[6:], held[:5] + held[9:], outs[:5] + outs[9:]):
        for i in range(src.shape[1]) if src.shape[1] == 2 else (None,):
            at = (lambda ref, i=i: ref) if i is None else (lambda ref, i=i: ref.at[0, i])
            n = len(pieces)
            pieces.append((
                pltpu.make_async_copy(at(src), at(mid), came.at[n]),
                pltpu.make_async_copy(at(mid), at(dst), left.at[n]),
            ))
    for fetch, _ in pieces:
        fetch.start()
    d = lax.axis_index("dp")
    part, outer = gains.shape[3], gain_out.shape[2]
    lanes = part * lax.axis_size("dp")
    load_vec.wait()
    rolled = pltpu.roll(vec[:, 0:lanes], lax.rem(lanes - d * part, lanes), 1)
    for i in range(2):
        gains[0, i] = rolled[i:i + 1, 0:part]
        shifts[0, i] = rolled[2 + i:3 + i, 0:part]
    mine = pl.ds(pl.multiple_of(d * outer, outer), outer)
    gain_out[0] = vec[4:5, mine]
    shift_out[0] = vec[5:6, mine]
    stores = [
        pltpu.make_async_copy(held[i], outs[i], left.at[len(pieces) + i - 5]) for i in range(5, 9)
    ]
    for store in stores:
        store.start()
    for fetch, store in pieces:
        fetch.wait()
        store.start()
    for store in stores + [store for _, store in pieces]:
        store.wait()


def per_device(*args):
    block_input, _, w_reduce, w_spatial = args[:4]
    n_dp, n_mp = lax.axis_size("dp"), lax.axis_size("mp")
    R, Wd = block_input.shape[1:]
    Cd, C = w_reduce.shape[2], w_spatial.shape[3]
    tasks, _, piece = args[9].shape
    sizes = (n_dp, n_mp, R, Wd, C * n_mp, C, Cd, piece * 2 * n_dp, tasks, piece)
    whole_tiles = not (C % 128 or Cd % 128 or Wd % 128 or R % 128 or piece % 16 or (R // n_mp) % 32)
    if whole_tiles and C == Cd and block_input.shape[0] == lax.axis_size("section") == 2:
        return fused_device(sizes, *args)
    return plain_device(*args)


def solution(mesh):
    return jax.shard_map(
        per_device,
        mesh=mesh,
        in_specs=(
            P(None, "dp", "mp"),
            P(None, "dp", None),
            P("section", "mp", "dp"),
            P("section", None, "dp", "mp"),
            P("section", "dp", "mp"),
            P("section", None, "mp"),
            P("section", None, "mp"),
            P("section", "mp"),
            P("section", "mp"),
            P(None, "mp", ("section", "dp")),
            P(None, None, "dp"),
            P(None, "dp", "mp"),
        ),
        out_specs=(
            P("section", None, "dp", "mp"),
            P("section", None, "dp", "mp"),
            P("section", "mp", "dp"),
            P("section", None, "dp", "mp"),
            P("section", "dp", "mp"),
            P("section", None, "mp", "dp"),
            P("section", None, "mp", "dp"),
            P("section", "mp", "dp"),
            P("section", "mp", "dp"),
            P(None, "mp", ("section", "dp")),
        ),
        check_vma=False,
    )
```

```python
import math

import jax
import jax.numpy as jnp
from jax import lax
from jax.experimental import pallas as pl
from jax.experimental.pallas import tpu as pltpu
from jax.sharding import PartitionSpec as P

NORM_EPS = 1e-05
LOSS_WEIGHT = 20.0
SIGN_FLOOR = 0.1
KEEP_TEMPER = 0.2


def shifted(value, axis, steps):
    count = lax.axis_size(axis)
    leading, last = (max(0, -steps), min(count, count - steps))
    return lax.ppermute(value, axis, [(source, source + steps) for source in range(leading, last)])


def geometry(img_sides, row_count):
    img_sizes = img_sides * img_sides
    img_ends = jnp.cumsum(img_sizes)
    img_starts = img_ends - img_sizes
    row_pos = jnp.arange(row_count, dtype=jnp.int32)[:, None]
    inside = (row_pos >= img_starts[None, :]) & (row_pos < img_ends[None, :])
    first_row = jnp.sum(jnp.where(inside, img_starts[None, :], 0), axis=1)
    side_len = jnp.sum(jnp.where(inside, img_sides[None, :], 0), axis=1)
    live_rows = jnp.any(inside, axis=1)
    offset = row_pos[:, 0] - first_row
    safe_side = jnp.maximum(side_len, 1)
    row_in = offset // safe_side
    col_in = offset % safe_side
    index_list = []
    valid_list = []
    for row_step in (-1, 0, 1):
        for col_step in (-1, 0, 1):
            new_row = row_in + row_step
            new_col = col_in + col_step
            valid = (
                live_rows
                & (new_row >= 0)
                & (new_row < side_len)
                & (new_col >= 0)
                & (new_col < side_len)
            )
            index_list.append(jnp.where(valid, first_row + new_row * side_len + new_col, 0))
            valid_list.append(valid)
    return (
        jnp.stack(index_list),
        jnp.stack(valid_list).astype(jnp.float32),
        live_rows.astype(jnp.float32),
    )


def smooth_act(values):
    return jax.nn.gelu(values, approximate=True)


def take_block(store, micro_idx):
    return lax.dynamic_index_in_dim(store, micro_idx, 0, keepdims=False)


def put_block(store, update, micro_idx, active):
    previous = take_block(store, micro_idx)
    return lax.dynamic_update_index_in_dim(store, jnp.where(active, update, previous), micro_idx, 0)


def channel_gather(values):
    return lax.all_gather(values, "mp", axis=1, tiled=True)


def channel_sum(values):
    return lax.psum_scatter(values, "mp", scatter_dimension=1, tiled=True)


def norm_stats(values, live_rows):
    masked = values * live_rows[:, None]
    total_sum, live_total = lax.psum((jnp.sum(masked, axis=0), jnp.sum(live_rows)), "dp")
    mean_val = total_sum / live_total
    centered = (values - mean_val) * live_rows[:, None]
    var_val = lax.psum(jnp.sum(centered * centered, axis=0), "dp") / live_total
    return (mean_val, lax.rsqrt(var_val + NORM_EPS), live_total)


def normalize(values, stats, live_rows, gain_vec, shift_vec):
    mean_val, inv_std, live_total = stats
    return live_rows[:, None] * (gain_vec * (values - mean_val) * inv_std + shift_vec)


def norm_backward(values, stats, live_rows, gain_vec, grad_norm):
    mean_val, inv_std, live_total = stats
    normed = (values - mean_val) * inv_std
    grad_live = grad_norm * live_rows[:, None]
    local_shift = jnp.sum(grad_live, axis=0)
    local_gain = jnp.sum(grad_live * normed, axis=0)
    sum_shift, sum_gain = lax.psum((local_shift, local_gain), "dp")
    grad_values = (
        live_rows[:, None]
        * inv_std
        * gain_vec
        * (grad_live - sum_shift / live_total - normed * sum_gain / live_total)
    )
    return (grad_values, local_gain, local_shift)


def gather_taps(values, indices, valids, tap_idx):
    return values[indices[tap_idx]] * valids[tap_idx][:, None].astype(values.dtype)


def act_backward(pre_values, grad_values):
    return jax.vjp(smooth_act, pre_values)[1](grad_values)[0]


def block_forward(x_in, layout, weights):
    indices, valids, live_rows = layout
    w_red, w_spa, w_exp, g_in, s_in, g_out, s_out = weights
    first_pre = channel_sum(jnp.dot(x_in, w_red, preferred_element_type=jnp.float32))
    stats_a = norm_stats(first_pre, live_rows)
    full_a = channel_gather(
        smooth_act(normalize(first_pre, stats_a, live_rows, g_in[0], s_in[0])).astype(jnp.bfloat16)
    )
    second_pre = jnp.zeros((x_in.shape[0], w_spa.shape[2]), jnp.float32)
    for tap_idx in range(9):
        second_pre = second_pre + jnp.dot(
            gather_taps(full_a, indices, valids, tap_idx),
            w_spa[tap_idx],
            preferred_element_type=jnp.float32,
        )
    stats_b = norm_stats(second_pre, live_rows)
    full_b = channel_gather(
        smooth_act(normalize(second_pre, stats_b, live_rows, g_in[1], s_in[1])).astype(jnp.bfloat16)
    )
    third_pre = jnp.dot(full_b, w_exp, preferred_element_type=jnp.float32)
    stats_c = norm_stats(third_pre, live_rows)
    pre_out = normalize(third_pre, stats_c, live_rows, g_out, s_out) + x_in.astype(jnp.float32)
    result = smooth_act(pre_out) * live_rows[:, None]
    return (result, (first_pre, stats_a, full_a, second_pre, stats_b, full_b, third_pre, stats_c))


def block_backward(d_out, x_in, layout, weights, saved_state):
    indices, valids, live_rows = layout
    w_red, w_spa, w_exp, g_in, s_in, g_out, s_out = weights
    first_pre, stats_a, full_a, second_pre, stats_b, full_b, third_pre, stats_c = saved_state
    pre_out = normalize(third_pre, stats_c, live_rows, g_out, s_out) + x_in.astype(jnp.float32)
    d_pre = act_backward(pre_out, d_out * live_rows[:, None])
    d_third, gain_c, shift_c = norm_backward(third_pre, stats_c, live_rows, g_out, d_pre)
    d_third = d_third.astype(jnp.bfloat16)
    grad_exp = jnp.einsum("rc,ro->co", full_b, d_third, preferred_element_type=jnp.float32)
    d_full_b = channel_sum(
        jnp.einsum("ro,co->rc", d_third, w_exp, preferred_element_type=jnp.float32)
    )
    pre_b = normalize(second_pre, stats_b, live_rows, g_in[1], s_in[1])
    d_second, gain_b, shift_b = norm_backward(
        second_pre, stats_b, live_rows, g_in[1], act_backward(pre_b, d_full_b)
    )
    d_second = d_second.astype(jnp.bfloat16)
    grad_spa = []
    back_total = jnp.zeros((x_in.shape[0], w_spa.shape[1]), jnp.float32)
    for tap_idx in range(9):
        grad_spa.append(
            jnp.einsum(
                "rc,ro->co",
                gather_taps(full_a, indices, valids, tap_idx),
                d_second,
                preferred_element_type=jnp.float32,
            )
        )
        spread = jnp.einsum(
            "ro,co->rc", d_second, w_spa[8 - tap_idx], preferred_element_type=jnp.float32
        )
        back_total = back_total + spread[indices[tap_idx]] * valids[tap_idx][:, None]
    d_full_a = channel_sum(back_total)
    pre_a = normalize(first_pre, stats_a, live_rows, g_in[0], s_in[0])
    d_first, gain_a, shift_a = norm_backward(
        first_pre, stats_a, live_rows, g_in[0], act_backward(pre_a, d_full_a)
    )
    d_first_full = channel_gather(d_first.astype(jnp.bfloat16))
    grad_red = jnp.einsum("rc,ro->co", x_in, d_first_full, preferred_element_type=jnp.float32)
    d_in = jnp.einsum("ro,co->rc", d_first_full, w_red, preferred_element_type=jnp.float32) + d_pre
    return (
        d_in,
        (
            grad_red,
            jnp.stack(grad_spa),
            grad_exp,
            jnp.stack([gain_a, gain_b]),
            jnp.stack([shift_a, shift_b]),
            gain_c,
            shift_c,
        ),
    )


def sign_merge(task_grads, thresh):
    soft_abs = jnp.sqrt(task_grads * task_grads + SIGN_FLOOR * SIGN_FLOOR) - SIGN_FLOOR
    purity = 0.5 * (1.0 + jnp.sum(task_grads, axis=0) / (jnp.sum(soft_abs, axis=0) + SIGN_FLOOR))
    keep_frac = jax.nn.sigmoid((purity - thresh) / KEEP_TEMPER)
    upper = 0.5 * jnp.sum(task_grads + soft_abs, axis=0)
    lower = 0.5 * jnp.sum(task_grads - soft_abs, axis=0)
    return keep_frac * upper + (1.0 - keep_frac) * lower


def plain_device(
    block_input,
    image_sides,
    w_reduce,
    w_spatial,
    w_expand,
    gain_inner,
    shift_inner,
    gain_outer,
    shift_outer,
    head_weight,
    labels,
    thresholds,
):
    section_idx = lax.axis_index("section")
    micro_count = block_input.shape[0]
    row_count = block_input.shape[1]
    w_red, w_spa, w_exp = (
        lax.all_gather(w_reduce[0].astype(jnp.bfloat16), "dp", axis=1, tiled=True),
        lax.all_gather(w_spatial[0].astype(jnp.bfloat16), "dp", axis=1, tiled=True),
        lax.all_gather(w_expand[0].astype(jnp.bfloat16), "dp", axis=0, tiled=True),
    )
    weights = (w_red, w_spa, w_exp, gain_inner[0], shift_inner[0], gain_outer[0], shift_outer[0])
    heads_all = lax.all_gather(
        head_weight.astype(jnp.bfloat16), ("section", "dp"), axis=2, tiled=True
    )
    class_total = heads_all.shape[2]
    class_ids = jnp.arange(class_total, dtype=jnp.int32)[None, None, :]

    def layout_for(micro_idx):
        return geometry(take_block(image_sides, micro_idx)[0], row_count)

    received = jnp.zeros(block_input.shape[1:], jnp.bfloat16)
    kept_inputs = jnp.zeros(block_input.shape, jnp.bfloat16)
    activ_store = jnp.zeros(block_input.shape, jnp.bfloat16)
    cotangents = jnp.zeros(block_input.shape, jnp.float32)
    head_grad = jnp.zeros(heads_all.shape, jnp.float32)
    for turn_idx in range(micro_count + 1):
        micro_idx = jnp.clip(turn_idx - section_idx, 0, micro_count - 1)
        active = (turn_idx - section_idx >= 0) & (turn_idx - section_idx < micro_count)
        x_in = jnp.where(section_idx == 0, block_input[min(turn_idx, micro_count - 1)], received)
        layout = layout_for(micro_idx)
        live_rows = layout[2]
        result, saved_state = block_forward(x_in, layout, weights)
        result_low = result.astype(jnp.bfloat16)
        kept_inputs = put_block(kept_inputs, x_in, micro_idx, active)
        activ_store = put_block(activ_store, result_low, micro_idx, active)
        labels_now = lax.dynamic_index_in_dim(labels, micro_idx, 1, keepdims=False)
        logits = lax.psum(
            jnp.einsum("rc,tco->tro", result_low, heads_all, preferred_element_type=jnp.float32),
            "mp",
        )
        peak_val = jnp.max(logits, axis=2, keepdims=True)
        expo = jnp.exp(logits - peak_val)
        soft_p = expo / jnp.sum(expo, axis=2, keepdims=True)
        picked = (class_ids == labels_now[:, :, None]).astype(jnp.float32)
        delta_low = (LOSS_WEIGHT * live_rows[None, :, None] * (soft_p - picked)).astype(
            jnp.bfloat16
        )
        task_grads = jnp.einsum(
            "tro,tco->trc", delta_low, heads_all, preferred_element_type=jnp.float32
        )
        merged = sign_merge(task_grads, take_block(thresholds, micro_idx))
        use_head = active & (section_idx == 1)
        head_grad = head_grad + jnp.where(
            use_head,
            jnp.einsum("rc,tro->tco", result_low, delta_low, preferred_element_type=jnp.float32),
            0.0,
        )
        cotangents = put_block(cotangents, merged, micro_idx, use_head)
        received = shifted(result_low, "section", 1)
    grad_recv = jnp.zeros(block_input.shape[1:], jnp.bfloat16)
    input_store = jnp.zeros(block_input.shape, jnp.float32)
    grad_total = None
    for turn_idx in range(micro_count + 1):
        micro_idx = jnp.clip(turn_idx - 1 + section_idx, 0, micro_count - 1)
        active = (turn_idx - 1 + section_idx >= 0) & (turn_idx - 1 + section_idx < micro_count)
        d_out = jnp.where(
            section_idx == 1, take_block(cotangents, micro_idx), grad_recv.astype(jnp.float32)
        )
        x_in = take_block(kept_inputs, micro_idx)
        layout = layout_for(micro_idx)
        saved_state = block_forward(x_in, layout, weights)[1]
        d_in, grad_set = block_backward(d_out, x_in, layout, weights, saved_state)
        masked = jax.tree.map(lambda leaf: jnp.where(active, leaf, 0.0), grad_set)
        grad_total = masked if grad_total is None else jax.tree.map(jnp.add, grad_total, masked)
        d_send = d_in.astype(jnp.bfloat16)
        input_store = put_block(
            input_store,
            jnp.where(section_idx == 1, d_send.astype(jnp.float32), d_in),
            micro_idx,
            active,
        )
        grad_recv = shifted(d_send, "section", -1)
    g_red, g_spa, g_exp, g_gain_in, g_shift_in, g_gain_out, g_shift_out = grad_total
    out_red, out_spa, out_exp, out_gain_in, out_shift_in, out_gain_out, out_shift_out = (
        lax.psum_scatter(g_red[None], "dp", scatter_dimension=2, tiled=True),
        lax.psum_scatter(g_spa[None], "dp", scatter_dimension=2, tiled=True),
        lax.psum_scatter(g_exp[None], "dp", scatter_dimension=1, tiled=True),
        lax.psum_scatter(g_gain_in[None, :, None, :], "dp", scatter_dimension=3, tiled=True),
        lax.psum_scatter(g_shift_in[None, :, None, :], "dp", scatter_dimension=3, tiled=True),
        lax.psum_scatter(g_gain_out[None, None, :], "dp", scatter_dimension=2, tiled=True),
        lax.psum_scatter(g_shift_out[None, None, :], "dp", scatter_dimension=2, tiled=True),
    )
    head_out = lax.psum_scatter(head_grad, ("section", "dp"), scatter_dimension=2, tiled=True)
    return (
        activ_store[None],
        input_store[None],
        out_red,
        out_spa,
        out_exp,
        out_gain_in,
        out_shift_in,
        out_gain_out,
        out_shift_out,
        head_out,
    )


K0 = math.sqrt(2.0 / math.pi)
K1 = 0.044715
MESH = pl.DeviceIdType.MESH
F32 = jnp.float32
BF16 = jnp.bfloat16
SIDES = (2, 7)
TAPS = [(a, b) for a in (-1, 0, 1) for b in (-1, 0, 1)]
PAD = 8
NN = (((1,), (0,)), ((), ()))
NT = (((1,), (1,)), ((), ()))
TN = (((0,), (0,)), ((), ()))


def tap_masks():
    found = []
    for tap_idx, (a, b) in enumerate(TAPS):
        for side in SIDES:
            found.append((tap_idx, a, b, side, a * side + b))
    return found


MASKS = tap_masks()


def dot(left, right, dims):
    return lax.dot_general(left, right, dims, preferred_element_type=F32)


def gelu(v):
    return 0.5 * v * (1.0 + jnp.tanh(K0 * v * (1.0 + K1 * v * v)))


def gelu_grad(v):
    sq = v * v
    t = jnp.tanh(K0 * v * (1.0 + K1 * sq))
    return 0.5 * (1.0 + t) + (0.5 * K0) * v * (1.0 - t * t) * (1.0 + 3.0 * K1 * sq)


def fold(x):
    return jnp.sum(x.reshape(x.shape[0] // 8, 8, x.shape[1]), axis=0)


def wide(x, width):
    times = width // x.shape[1]
    return x if times == 1 else jnp.concatenate([x] * times, axis=1)


def loop(total, chunk, body, init=None):
    def one(i, carry):
        return body(pl.ds(pl.multiple_of(i * chunk, chunk), chunk), carry)

    return lax.fori_loop(0, total // chunk, one, 0 if init is None else init)


def rows_tile(first, second, third):
    width = first.shape[1]
    place = lax.broadcasted_iota(jnp.int32, (8, width), 0)
    wide_of = lambda v: jnp.broadcast_to(v, (8, width))
    return jnp.where(
        place == 0, wide_of(first), jnp.where(place == 1, wide_of(second), wide_of(third))
    )


class Sems:
    def __init__(self, ref):
        self.ref, self.used, self.size = ref, 0, ref.shape[0]

    def take(self, count=1):
        first = self.used
        self.used += count
        assert self.used <= self.size, self.used
        return first


def make_kernel(sizes):
    n_dp, n_mp, R, Wd, M, C, Cd, classes, tasks, piece = sizes
    n_sec = 2
    W9 = 9 * C

    def kernel(*refs):
        (
            x_hbm, sides_hbm, wred_hbm, wspa_hbm, wexp_hbm, gin_hbm, sin_hbm, gout_hbm, sout_hbm,
            head_hbm, lab_hbm, thr_hbm,
            act_hbm, ig_hbm, red_hbm, spa_hbm, exp_hbm, vec_hbm, head_out,
            ssems, rsems, lsems, go,
            sred, sspa, sexp, shead, thr, xin, wr, wsp, we, hd, par,
            live, geo, masks, labc,
            rs_s, rs_r, ag_a, ag_b, ag_d, fulla, fullb, dfull, co, sums_s, sums_r, sums_t, st, keep, first, second, third, ppad, dpad, dbuf,
            lg_s, lg_r, dl, act1, tg, dpre, evec, dth, ig, slope, steep,
            gred, gspa, gexp, sibred, sibspa, sibexp, rred, rspa, rexp, ghead, rhead, vec, vsib,
            ored, ospa, oexp, ovec, ohead,
            sides_ref, gin_ref, sin_ref, gout_ref, sout_ref, lab_ref,
        ) = refs
        s = lax.axis_index("section")
        d = lax.axis_index("dp")
        m = lax.axis_index("mp")
        o = 1 - s
        recv, local = Sems(rsems), Sems(lsems)
        pending = {None: [], 0: [], 1: []}
        sends = {None: 0, 0: 1, 1: 2}
        rem = lax.rem
        dp_dev = lambda t: (s, t, m)
        mp_dev = lambda t: (s, d, t)
        sib_dev = (o, d, m)

        def put_to(src, dst, ssem, rsem, dev):
            pltpu.make_async_remote_copy(
                src_ref=src,
                dst_ref=dst,
                send_sem=ssems.at[ssem],
                recv_sem=rsems.at[rsem],
                device_id=dev,
                device_id_type=MESH,
            ).start()

        def waiter(ref, ssem, rsem):
            return pltpu.make_async_remote_copy(
                src_ref=ref,
                dst_ref=ref,
                send_sem=ssems.at[ssem],
                recv_sem=rsems.at[rsem],
                device_id=sib_dev,
                device_id_type=MESH,
            )

        def rcopy(src, dst, rsem, dev, when=None):
            ssem = sends[when]
            put_to(src(), dst(), ssem, rsem, dev)
            pending[when].append(lambda: waiter(src(), ssem, 0).wait_send())

        def arrive(dst, rsem):
            waiter(dst, 0, rsem).wait_recv()

        axes = {"dp": (n_dp, d, dp_dev), "mp": (n_mp, m, mp_dev)}
        expected, hold = {}, {}

        def settle(key):
            expected.pop(key)()

        def load(src, dst):
            cp = pltpu.make_async_copy(src, dst, lsems.at[local.take()])
            cp.start()
            key = ("load", local.used)
            expected[key] = cp.wait
            return key

        def on(cond, what):
            return lambda: pl.when(cond())(what)

        class Group:
            def __init__(self, axis, all_of, when=None, slot_of=None):
                self.n, self.me, self.dev = axes[axis]
                self.ssem = sends[when]
                self.rsem = recv.take(1 if slot_of is None else self.n - 1)
                self.all_of, self.when, self.slot_of = all_of, when, slot_of

            def put(self, src_of, slot_of):
                for k in range(1, self.n):
                    t = rem(self.me + k, self.n)
                    rsem = self.rsem + (0 if self.slot_of is None else k - 1)
                    put_to(src_of(t), slot_of(self.me), self.ssem, rsem, self.dev(t))

            def came_from(self, k):
                return rem(self.me + self.n - k, self.n)

            def close(self):
                ssem, all_of, when = self.ssem, self.all_of, self.when
                pending[when].append(lambda: waiter(all_of(), ssem, 0).wait_send())
                if self.slot_of is None:
                    waits = {self.rsem: lambda: arrive(all_of(), self.rsem)}
                else:
                    waits = {
                        self.rsem + k - 1: lambda k=k: arrive(
                            self.slot_of(self.came_from(k)), self.rsem + k - 1
                        )
                        for k in range(1, self.n)
                    }
                for key, wait in waits.items():
                    expected[key] = wait if when is None else on(lambda: s == when, wait)
                return self.rsem

        def spread(axis, src_of, slot_of, all_of, when=None):
            group = Group(axis, all_of, when)
            group.put(src_of, slot_of)
            return group.close()

        barrier = pltpu.get_barrier_semaphore()
        greeted = 0
        for ds_ in range(n_sec):
            for k in range(n_dp):
                if ds_ == 0 and k == 0:
                    continue
                pl.semaphore_signal(
                    barrier, inc=1,
                    device_id=(rem(s + ds_, n_sec), rem(d + k, n_dp), m),
                    device_id_type=MESH,
                )
                greeted += 1
        for k in range(1, n_mp):
            pl.semaphore_signal(
                barrier, inc=1, device_id=(s, d, rem(m + k, n_mp)), device_id_type=MESH
            )
            greeted += 1


        l_red = load(wred_hbm.at[0], sred)
        l_par = [
            load(src, dst)
            for src, dst in (
                (gin_hbm, gin_ref), (sin_hbm, sin_ref), (gout_hbm, gout_ref), (sout_hbm, sout_ref)
            )
        ]
        l_x = load(x_hbm.at[s], xin.at[0])
        l_spa = load(wspa_hbm.at[0], sspa)
        l_exp = load(wexp_hbm.at[0], sexp)
        l_small = [load(sides_hbm, sides_ref), load(lab_hbm, lab_ref)]
        l_head = load(head_hbm, shead)
        l_thr = load(thr_hbm.at[s], thr)

        settle(l_red)
        wr[s, d] = sred[...].astype(BF16)
        for key in l_par:
            settle(key)
        par[s] = jnp.zeros(par.shape[1:], F32)
        for i in range(2):
            par[s, i:i + 1, :C] = gin_ref[0, i:i + 1, :]
            par[s, 2 + i:3 + i, :C] = sin_ref[0, i:i + 1, :]
        par[s, 4:5, :] = gout_ref[...]
        par[s, 5:6, :] = sout_ref[...]
        pl.semaphore_wait(barrier, greeted)

        by_dp, by_sib = {}, {}

        def send_own(buf, j):
            def go():
                by_dp[id(buf), j] = spread(
                    "dp",
                    lambda t: buf.at[j, d],
                    lambda src: buf.at[j, src],
                    lambda: buf.at[j, pl.ds(0, n_dp - 1)],
                    when=j,
                )

            pl.when(s == j)(go)

        def pass_on(buf, j):
            settle(by_dp[id(buf), j])
            sem = by_sib[id(buf), j] = recv.take()

            @pl.when(s == j)
            def _():
                rcopy(lambda: buf.at[j], lambda: buf.at[j], sem, sib_dev, when=j)

            expected[sem] = on(lambda: s != j, lambda: arrive(buf.at[j], sem))

        def from_sib(buf, j):
            settle(by_sib[id(buf), j])

        par_sem = recv.take()
        rcopy(lambda: par.at[s], lambda: par.at[s], par_sem, sib_dev)
        expected[par_sem] = lambda: arrive(par.at[o], par_sem)
        early = Group(
            "dp",
            lambda: wr.at[0, pl.ds(0, n_dp - 1)],
            when=0,
            slot_of=lambda src: wr.at[0, src],
        )

        @pl.when(s == 0)
        def _():
            early.put(lambda t: wr.at[0, d], lambda src: wr.at[0, src])

        early.close()

        settle(l_spa)
        for k in range(9):
            wsp[s, d, :, k * C:(k + 1) * C] = sspa[k].astype(BF16)

        settle(l_exp)
        we[s, d] = sexp[...].astype(BF16)

        for key in l_small:
            settle(key)
        sides = jnp.where(s == 0, sides_ref[0], sides_ref[1]).astype(F32)
        slots = sides.shape[1]
        sq = jnp.broadcast_to(sides * sides, (8, slots)).astype(BF16)
        upper = (
            lax.broadcasted_iota(jnp.int32, (slots, slots), 0)
            <= lax.broadcasted_iota(jnp.int32, (slots, slots), 1)
        ).astype(BF16)
        ends = dot(sq, upper, NN)[0:1]
        starts = ends - sides * sides
        nloc = jnp.broadcast_to(jnp.max(ends, axis=1, keepdims=True), (1, 128))
        shape = (R, 128)
        pos = lax.broadcasted_iota(jnp.int32, (R, slots), 0).astype(F32)
        inside = (pos >= starts) & (pos < ends)
        origin = jnp.sum(jnp.where(inside, starts, 0.0), axis=1, keepdims=True)
        side = jnp.sum(jnp.where(inside, sides, 0.0), axis=1, keepdims=True)
        geo[0] = jnp.broadcast_to(origin, shape)
        geo[1] = jnp.broadcast_to(side, shape)

        def make_masks(rows, carry):
            side_b = geo[1, rows]
            here = lax.broadcasted_iota(jnp.int32, side_b.shape, 0) + rows.start
            offset = here.astype(F32) - geo[0, rows]
            row_in = jnp.floor((offset + 0.5) / jnp.maximum(side_b, 1.0))
            col_in = offset - row_in * side_b
            live[rows] = (side_b > 0.0).astype(F32)
            for idx, (_, a, b, q, _) in enumerate(MASKS):
                ra, cb = row_in + a, col_in + b
                ok = (side_b == q) & (ra >= 0.0) & (ra < q) & (cb >= 0.0) & (cb < q)
                masks[idx, rows] = ok.astype(F32)
            return carry

        loop(R, 64, make_masks)
        for buf in (ppad, dpad):
            edge = jnp.zeros((PAD, buf.shape[1]), F32)
            buf[0:PAD] = edge
            buf[PAD + R:PAD + R + PAD] = edge
        lab2 = lab_ref[...]
        lab = jnp.where(s == 0, lab2[:, 0], lab2[:, 1]).astype(F32)
        lab = jnp.concatenate([lab, jnp.zeros((8 - tasks, R), F32)], axis=0)
        labc[...] = jnp.transpose(lab)

        settle(l_head)
        mine = s * n_dp + d
        for t in range(tasks):
            hd[mine, t] = shead[t].astype(BF16)

        def to_all(src_of, buf):
            ssem, rsem = sends[None], recv.take()
            others = [(a, k) for a in range(n_sec) for k in range(n_dp) if a or k]
            for a, k in others:
                ts, td = rem(s + a, n_sec), rem(d + k, n_dp)
                put_to(src_of(ts * n_dp + td), buf.at[mine], ssem, rsem, (ts, td, m))
            rest = lambda: buf.at[pl.ds(0, len(others))]
            pending[None].append(lambda: waiter(rest(), ssem, 0).wait_send())
            expected[rsem] = lambda: arrive(rest(), rsem)
            return rsem

        def cat(buf, n):
            return jnp.concatenate([buf[i] for i in range(n)], axis=1)

        phase = {"rs": 0, "st": 0}

        def rs_open():
            p = phase["rs"]
            phase["rs"] += 1
            return p, Group("mp", lambda: rs_r.at[p, pl.ds(0, n_mp - 1)])

        def rs_rows(handle, rows, out):
            p, group = handle
            for c in range(n_mp):
                rs_s[p, c, rows] = out[:, c * C:(c + 1) * C].astype(BF16)
            group.put(lambda t: rs_s.at[p, t, rows], lambda src: rs_r.at[p, src, rows])

        def rs_finish(handle, dst):
            p, group = handle
            settle(group.rsem)

            def add(rows, carry):
                dst[rows] = rs_sum(handle, rows)
                return carry

            loop(R, 128, add)

        def exchange(tile):
            p = phase["st"]
            phase["st"] += 1
            width = tile.shape[1]
            st[p, d, :, 0:width] = tile
            slot = lambda src: st.at[p, src, :, 0:width]
            rest = lambda: st.at[p, pl.ds(0, n_dp - 1), :, 0:width]
            return p, width, spread("dp", lambda t: slot(d), slot, rest)

        def collect(handle):
            p, width, base = handle
            settle(base)
            return [st[p, i, :, 0:width] for i in range(n_dp)]

        def stats_start(buf, width, total=None):
            chunk = 128 if width <= 128 else 32
            zero = jnp.zeros((8, width), F32)

            def sum_up(rows, carry):
                return carry + fold(buf[rows] * wide(live[rows], width))

            if total is None:
                total = loop(R, chunk, sum_up, zero)
            total = jnp.sum(total, axis=0, keepdims=True)
            count = wide(nloc, width)
            mean = total / jnp.maximum(count, 1.0)

            def squares(rows, carry):
                off = (buf[rows] - mean) * wide(live[rows], width)
                return carry + fold(off * off)

            sqs = jnp.sum(loop(R, chunk, squares, zero), axis=0, keepdims=True)
            return exchange(rows_tile(total, sqs, count)), mean

        def stats_finish(handle, j, i):
            tiles = collect(handle)
            width = handle[1]
            count = sum(t[2:3] for t in tiles)
            mean = sum(t[0:1] for t in tiles) / count
            sqs = 0.0
            for t in tiles:
                local_mean = t[0:1] / jnp.maximum(t[2:3], 1.0)
                sqs = sqs + t[1:2] + t[2:3] * (local_mean - mean) * (local_mean - mean)
            inv = lax.rsqrt(sqs / count + NORM_EPS)
            keep[j, i, :, 0:width] = rows_tile(mean, inv, count)

        def parted(*twelfths):
            at = [max(32, R * n // 12 // 32 * 32) for n in twelfths]
            return [slice(a, b) for a, b in zip([0] + at, at + [R])]

        spans, halves = parted(2, 7), parted(6)

        def rows_out(buf, at, rows, values):
            buf[at, m, rows] = values.astype(BF16)
            return spread(
                "mp",
                lambda t: buf.at[at, m, rows],
                lambda src: buf.at[at, src, rows],
                lambda: buf.at[at, pl.ds(0, n_mp - 1), rows],
            )

        def rs_rows_sums(handle, j, i, rows, out, carry):
            p, groups = handle
            sb, sg = carry
            raw = (ag_a, ag_b)[i]
            for c in range(n_mp):
                part = out[:, c * C:(c + 1) * C]
                rs_s[p, c, rows] = part.astype(BF16)
                tile = co[2 * j + i, c]
                g = part * slope[j, i, c, rows]
                xhat = raw[j, c, rows].astype(F32) * tile[2:3] + tile[3:4]
                sb[c] = sb[c] + fold(g)
                sg[c] = sg[c] + fold(g * xhat)
            last = rows.stop == R
            if last:
                sums = sums_out(p, sb + sg)
            group = Group("mp", lambda: rs_r.at[p, pl.ds(0, n_mp - 1), rows])
            group.put(lambda t: rs_s.at[p, t, rows], lambda src: rs_r.at[p, src, rows])
            groups.append(group.close())
            return sums if last else None

        def sums_out(p, parts):
            place = lax.broadcasted_iota(jnp.int32, (2 * n_mp, C), 0)
            tile = jnp.zeros((2 * n_mp, C), F32)
            for i, part in enumerate(parts):
                tile = jnp.where(place == i, jnp.sum(part, axis=0, keepdims=True), tile)
            sums_s[p] = tile
            ssem, rsem = sends[None], recv.take()
            others = [(a, k) for a in range(n_mp) for k in range(n_dp) if a or k]
            me = m * n_dp + d
            for a, k in others:
                tz, td = rem(m + a, n_mp), rem(d + k, n_dp)
                put_to(sums_s.at[p], sums_r.at[p, me], ssem, rsem, (s, td, tz))
            rest = lambda: sums_r.at[p, pl.ds(0, len(others))]
            pending[None].append(lambda: waiter(rest(), ssem, 0).wait_send())
            expected[rsem] = lambda: arrive(rest(), rsem)

            def collect_sums():
                settle(rsem)
                total = sums_s[p]
                for a, k in others:
                    total = total + sums_r[p, rem(m + a, n_mp) * n_dp + rem(d + k, n_dp)]
                sums_t[p] = total
                return total

            return collect_sums

        def rs_parts():
            p = phase["rs"]
            phase["rs"] += 1
            return p, []

        def rs_sum(handle, rows):
            p, _ = handle
            out = rs_s[p, m, rows].astype(F32)
            for k in range(1, n_mp):
                out = out + rs_r[p, rem(m + k, n_mp), rows].astype(F32)
            return out

        def coeffs_out(at, *values):
            place = lax.broadcasted_iota(jnp.int32, (8, C), 0)
            tile = jnp.zeros((8, C), F32)
            for i, v in enumerate(values):
                tile = jnp.where(place == i, jnp.broadcast_to(v, (8, C)), tile)
            co[at, m] = tile
            slot = lambda src: co.at[at, src]
            return spread("mp", lambda t: slot(m), slot, lambda: co.at[at, pl.ds(0, n_mp - 1)])

        def inner_norm(j, i, src, raw, full, hook, need, consume):
            at = 2 * j + i
            handle, mean_here = stats_start(src.at[j], C)
            push = lambda rows: rows_out(raw, j, rows, src[j, rows] - mean_here)
            groups = [push(rows) for rows in spans[:-1]]
            hook()
            stats_finish(handle, j, i)
            mu, inv, _, gain, shift = norm_of(j, i, C)
            moved = (mean_here - mu) * inv
            sent = coeffs_out(at, gain * inv, gain * moved + shift, inv, moved)
            groups.append(push(spans[-1]))
            need()
            settle(sent)
            for rows, group in zip(spans, groups):
                settle(group)
                for c in range(n_mp):
                    tile = co[at, c]
                    y = live[rows] * (raw[j, c, rows].astype(F32) * tile[0:1] + tile[1:2])
                    full[j, rows, c * C:(c + 1) * C] = gelu(y).astype(BF16)
                consume(rows)

        def norm_of(j, i, width):
            tile = keep[j, i, :, 0:width]
            if i < 2:
                gain, shift = par[j, i:i + 1, 0:width], par[j, 2 + i:3 + i, 0:width]
            else:
                gain, shift = par[j, 4:5, 0:width], par[j, 5:6, 0:width]
            return tile[0:1], tile[1:2], tile[2:3], gain, shift

        def taps_sum(src, flip, put):
            way = -1 if flip else 1
            for rows in spans:
                first_row, last_row = PAD + rows.start, PAD + rows.stop
                put(rows, lambda idx_list, lanes: sum(
                    masks[(len(MASKS) - 2 - (idx // 2) * 2 + idx % 2) if flip else idx, rows]
                    * src[first_row + way * MASKS[idx][4]:last_row + way * MASKS[idx][4], lanes]
                    for idx in idx_list
                ))

        nothing = lambda: None
        vec[...] = jnp.zeros(vec.shape, F32)

        def prepare(j):
            for i, raw in enumerate((ag_a, ag_b)):
                def inner(rows, carry):
                    for c in range(n_mp):
                        tile = co[2 * j + i, c]
                        y = live[rows] * (raw[j, c, rows].astype(F32) * tile[0:1] + tile[1:2])
                        slope[j, i, c, rows] = live[rows] * gelu_grad(y)
                    return carry

                loop(R, 64, inner)
            mu, inv, _, gain, shift = norm_of(j, 2, Wd)

            def outer(rows, carry):
                lv = wide(live[rows], Wd)
                pre = lv * (gain * ((third[j, rows] - mu) * inv) + shift)
                steep[j, rows] = lv * gelu_grad(pre + xin[j, rows].astype(F32))
                return carry

            loop(R, 32, outer)

        def forward(j, h, hooks, needs):
            hooks[0]()
            rs_finish(h, first.at[j])

            def conv(rows):
                there = slice(PAD + rows.start, PAD + rows.stop)
                ppad[there] = dot(fulla[j, rows], wsp[j].reshape(M, W9), NN)

            inner_norm(j, 0, first, ag_a, fulla, hooks[1], needs[0], conv)

            def put(rows, summed):
                second[j, rows] = sum(
                    summed([2 * k, 2 * k + 1], slice(k * C, (k + 1) * C)) for k in range(9)
                )

            taps_sum(ppad, False, put)
            if j == 0:
                pass_on(wr, 1)
            sums = []

            def expand(rows):
                out = dot(fullb[j, rows], we[j].reshape(M, Wd), NN)
                third[j, rows] = out
                sums.append(fold(out * wide(live[rows], Wd)))

            inner_norm(j, 1, second, ag_b, fullb, hooks[2], needs[1], expand)
            h, _ = stats_start(third.at[j], Wd, sum(sums))
            hooks[3]()
            stats_finish(h, j, 2)
            mu, inv, _, gain, shift = norm_of(j, 2, Wd)
            out = xin.at[1] if j == 0 else act1

            def act_c(rows):
                for r0 in range(rows.start, rows.stop, 32):
                    there = slice(r0, r0 + 32)
                    lv = wide(live[there], Wd)
                    pre = lv * (gain * ((third[j, there] - mu) * inv) + shift)
                    pre = pre + xin[j, there].astype(F32)
                    out[there] = (lv * gelu(pre)).astype(BF16)

            return act_c

        def to_section(src, hbm, j):
            sem = recv.take()

            @pl.when(s == j)
            def _():
                lsem = local.take()
                made = lambda: pltpu.make_async_copy(src(), hbm.at[0, s], lsems.at[lsem])
                made().start()
                pending[j].append(lambda: made().wait())

            @pl.when(s != j)
            def _():
                rcopy(src, lambda: hbm.at[0, s], sem, sib_dev, when=1 - j)

            expected[sem] = on(lambda: s == j, lambda: arrive(hbm.at[0, o], sem))

        grads = ((gred, sibred, rred), (gspa, sibspa, rspa), (gexp, sibexp, rexp))
        at_sib, at_dp = {}, {}

        def grad_to_sib(which, j):
            own, sib, _ = grads[which]
            sem = at_sib[which, j] = recv.take()

            @pl.when(s != j)
            def _():
                rcopy(lambda: own.at[j], lambda: sib, sem, sib_dev, when=1 - j)

            expected[sem] = on(lambda: s == j, lambda: arrive(sib, sem))

        def grad_to_dp(which, j):
            own, sib, got = grads[which]
            settle(at_sib[which, j])

            def go():
                def add(rows, carry):
                    for i in range(n_dp):
                        own[j, i, rows] = (
                            own[j, i, rows].astype(F32) + sib[i, rows].astype(F32)
                        ).astype(BF16)
                    return carry

                loop(own.shape[2], 64, add)
                base = spread(
                    "dp",
                    lambda t: own.at[j, t],
                    lambda src: got.at[src],
                    lambda: got.at[pl.ds(0, n_dp - 1)],
                    when=j,
                )
                at_dp.setdefault(which, []).append(base)

            pl.when(s == j)(go)

        def reduce_to_sib(j):
            for i in range(n_dp):
                full = dfull[j, :, i * Cd:(i + 1) * Cd]
                gred[j, i] = dot(xin[j], full, TN).astype(BF16)
                sem = at_sib[0, j, i] = recv.take()

                @pl.when(s != j)
                def _():
                    rcopy(lambda: gred.at[j, i], lambda: sibred.at[i], sem, sib_dev, when=1 - j)

                expected[sem] = on(
                    lambda: s == j, lambda i=i, sem=sem: arrive(sibred.at[i], sem)
                )

        def reduce_to_dp(j):
            group = Group("dp", lambda: rred.at[pl.ds(0, n_dp - 1)], when=j)
            for i in range(n_dp):
                settle(at_sib[0, j, i])

                @pl.when(s == j)
                def _():
                    def add(rows, carry):
                        gred[j, i, rows] = (
                            gred[j, i, rows].astype(F32) + sibred[i, rows].astype(F32)
                        ).astype(BF16)
                        return carry

                    loop(Wd, 128, add)

                    @pl.when(d != i)
                    def _():
                        put_to(gred.at[j, i], rred.at[d], group.ssem, group.rsem, dp_dev(i))

            at_dp.setdefault(0, []).append(group.close())

        def steepest(j, rows, e, carry):
            mu, inv, _, _, _ = norm_of(j, 2, Wd)
            out = steep[j, rows] * e
            dpre[rows] = out
            return carry[0] + fold(out), carry[1] + fold(out * ((third[j, rows] - mu) * inv))

        def backward(j, sums, hooks):
            mu, inv, count, gain, shift = norm_of(j, 2, Wd)
            sb, sg = sums
            total = lambda v: jnp.sum(v, axis=0, keepdims=True)
            sb, sg = total(sb), total(sg)
            h = exchange(rows_tile(sb, sg, sg))
            hooks[0]()
            tile = sum(collect(h))
            vec[j, 4:5, :] = tile[1:2]
            vec[j, 5:6, :] = tile[0:1]
            sb_n, sg_n = tile[0:1] / count, tile[1:2] / count
            scale = gain * inv

            def d_third(rows, carry):
                lv = wide(live[rows], Wd)
                xhat = (third[j, rows] - mu) * inv
                dth[rows] = (lv * scale * (dpre[rows] - sb_n - xhat * sg_n)).astype(BF16)
                return carry

            none = lambda: ([jnp.zeros((8, C), F32)] * n_mp, [jnp.zeros((8, C), F32)] * n_mp)
            h, carry = rs_parts(), none()
            for rows in halves:
                for r0 in range(rows.start, rows.stop, 32):
                    d_third(slice(r0, r0 + 32), 0)
                out = dot(dth[rows], we[j].reshape(M, Wd), NT)
                sums_of = rs_rows_sums(h, j, 1, rows, out, carry)
            for i in range(n_dp):
                full = fullb[j, :, i * Cd:(i + 1) * Cd]
                gexp[j, i] = dot(full, dth[...], TN).astype(BF16)
            grad_to_sib(2, j)
            hooks[1]()
            for group in h[1]:
                settle(group)

            def norm_sums(i, sums):
                p = sums[0]
                place = lax.broadcasted_iota(jnp.int32, (2 * n_mp, C), 0)
                row = lambda i: jnp.sum(
                    jnp.where(place == i, sums_t[p], 0.0), axis=0, keepdims=True
                )
                sb, sg = row(m), row(n_mp + m)
                vec[j, i:i + 1, 0:C] = sg
                vec[j, 2 + i:3 + i, 0:C] = sb
                return sb, sg

            sums_of()
            sb_b, sg_b = norm_sums(1, h)
            mu_b, inv_b, count_b, gain_b, _ = norm_of(j, 1, C)
            scale_b, sb_b, sg_b = gain_b * inv_b, sb_b / count_b, sg_b / count_b
            for rows in spans:
                there = slice(PAD + rows.start, PAD + rows.stop)
                xhat = (second[j, rows] - mu_b) * inv_b
                g = slope[j, 1, m, rows] * rs_sum(h, rows)
                out = live[rows] * scale_b * (g - sb_b - xhat * sg_b)
                dpad[there] = out.astype(BF16).astype(F32)

            h, carry = rs_parts(), none()
            sums_a = []

            def put(rows, summed):
                for k in range(9):
                    dbuf[rows, k * C:(k + 1) * C] = summed([2 * k, 2 * k + 1], slice(None)).astype(BF16)
                out = dot(dbuf[rows], wsp[j].reshape(M, W9), NT)
                sums_a.append(rs_rows_sums(h, j, 0, rows, out, carry))

            taps_sum(dpad, True, put)
            for i in range(n_dp):
                full = fulla[j, :, i * Cd:(i + 1) * Cd]
                gspa[j, i] = dot(full, dbuf[...], TN).astype(BF16)
            grad_to_sib(1, j)
            grad_to_dp(2, j)
            hooks[2]()
            groups = []
            for rows, part in zip(spans, h[1]):
                settle(part)
                g = slope[j, 0, m, rows] * rs_sum(h, rows)
                if not groups:
                    pivot = jnp.sum(g, axis=0, keepdims=True) / jnp.maximum(
                        jnp.sum(live[rows], axis=0, keepdims=True), 1.0
                    )
                    sent = coeffs_out(4 + j, pivot)
                groups.append(rows_out(ag_d, j, rows, g - pivot))
            hooks[3]()
            grad_to_dp(1, j)

            def d_input(rows):
                out = dot(dfull[j, rows], cat(wr.at[j], n_dp), NT) + dpre[rows]
                if j == 1:
                    out = out.astype(BF16).astype(F32)
                    evec[rows] = out
                ig[j, rows] = out

            sums = sums_a[-1]()
            norm_sums(0, h)
            if j == 0:
                hold["vec"] = recv.take()
                rcopy(lambda: vec.at[o], lambda: vsib, hold["vec"], sib_dev)
                expected[hold["vec"]] = lambda: arrive(vsib, hold["vec"])
            settle(sent)
            count = keep[j, 0, 2:3, 0:C]
            terms = []
            for c in range(n_mp):
                tile = co[2 * j, c]
                sb_n, sg_n = sums[c:c + 1] / count, sums[n_mp + c:n_mp + c + 1] / count
                scale, inv, moved = tile[0:1], tile[2:3], tile[3:4]
                offset = scale * (co[4 + j, c, 0:1] - sb_n - moved * sg_n)
                terms.append((scale, -scale * sg_n * inv, offset))
            for rows, group in zip(spans, groups):
                settle(group)
                for c, (scale, slant, offset) in enumerate(terms):
                    out = live[rows] * (
                        ag_d[j, c, rows].astype(F32) * scale
                        + ag_a[j, c, rows].astype(F32) * slant
                        + offset
                    )
                    dfull[j, rows, c * C:(c + 1) * C] = out.astype(BF16)
                if j == 1:
                    d_input(rows)
            if j == 0:
                reduce_to_sib(j)
                reduce_to_dp(j)
                for rows in spans:
                    d_input(rows)
            to_section(lambda: ig.at[j], ig_hbm, j)

        settle(l_x)

        def first_product():
            handle = rs_open()
            p, group = handle
            for k in range(n_dp):
                src = early.came_from(k) if k else d
                if k:
                    settle(early.rsem + k - 1)
                sem = recv.take()

                @pl.when(s == 0)
                def _():
                    rcopy(lambda: wr.at[0, src], lambda: wr.at[0, src], sem, sib_dev, when=0)

                expected[sem] = on(lambda: s != 0, lambda: arrive(wr.at[0, src], sem))
                settle(sem)

                def part(rows, carry):
                    rs_s[p, src, rows] = dot(xin[0, rows], wr[0, src], NN).astype(BF16)
                    return carry

                loop(R, 128, part)

                @pl.when(src != m)
                def _():
                    put_to(rs_s.at[p, src], rs_r.at[p, m], group.ssem, group.rsem, mp_dev(src))

            group.close()
            return handle

        @pl.when(s == 1)
        def _():
            pl.semaphore_wait(go, 1)

        start = first_product()
        settle(par_sem)

        def w_next():
            send_own(we, 0)
            send_own(wr, 1)

        def w_head():
            hold["heads"] = to_all(lambda t: hd.at[mine], hd)

        def f00():
            send_own(wsp, 0)

            @pl.when(s == 0)
            def _():
                pl.semaphore_signal(go, inc=1, device_id=sib_dev, device_id_type=MESH)

        hooks = (f00, w_next, lambda: send_own(wsp, 1), nothing)

        def n00():
            pass_on(wsp, 0)
            from_sib(wsp, 0)

        def n01():
            pass_on(we, 0)
            from_sib(we, 0)

        act_c = forward(0, start, hooks, (n00, n01))
        from_sib(wr, 1)
        start = rs_open()
        for rows in spans:
            act_c(rows)
            rs_rows(start, rows, dot(xin[1, rows], cat(wr.at[1], n_dp), NN))
        start[1].close()

        def f10():
            send_own(we, 1)
            pass_on(wsp, 1)
            to_section(lambda: xin.at[1], act_hbm, 0)
            prepare(0)

        def n10():
            pass_on(we, 1)
            from_sib(wsp, 1)

        hooks = (f10, w_head, nothing, nothing)
        act_c = forward(1, start, hooks, (n10, lambda: from_sib(we, 1)))

        settle(hold["heads"])
        RM = R // n_mp
        n_cls = n_sec * n_dp

        def heads_of(t):
            return hd[:, t].reshape(classes, Wd)

        logit_group = Group("mp", lambda: lg_r.at[pl.ds(0, n_mp - 1)])
        for c in range(n_mp):
            act_c(slice(c * RM, (c + 1) * RM))
            rows = act1[c * RM:(c + 1) * RM]
            for t in range(tasks):
                lg_s[c, :, t * classes:(t + 1) * classes] = dot(rows, heads_of(t), NT).astype(
                    lg_s.dtype
                )

            @pl.when(m != c)
            def _():
                put_to(
                    lg_s.at[c], lg_r.at[m], logit_group.ssem, logit_group.rsem, mp_dev(c)
                )

        base = logit_group.close()
        to_section(lambda: act1, act_hbm, 1)
        settle(l_thr)
        prepare(1)
        settle(base)
        here = pl.ds(pl.multiple_of(m * RM, RM), RM)
        lv = wide(live[here], classes)
        group = Group(
            "mp", lambda: dl.at[pl.ds(0, n_mp - 1)], slot_of=lambda src: dl.at[src]
        )
        for t in range(tasks):
            lanes = slice(t * classes, (t + 1) * classes)
            logit = lg_s[m, :, lanes].astype(F32)
            for k in range(1, n_mp):
                logit = logit + lg_r[rem(m + k, n_mp), :, lanes].astype(F32)
            expo = jnp.exp(logit - jnp.max(logit, axis=1, keepdims=True))
            soft = expo / jnp.sum(expo, axis=1, keepdims=True)
            ids = lax.broadcasted_iota(jnp.int32, (RM, classes), 1).astype(F32)
            hot = (ids == labc[here, t:t + 1]).astype(F32)
            dl[m, :, lanes] = (LOSS_WEIGHT * lv * (soft - hot)).astype(BF16)
            group.put(lambda t: dl.at[m, :, lanes], lambda src: dl.at[src, :, lanes])
        group.close()

        def merge_block(c, sums):
            for t in range(tasks):
                lanes = slice(t * classes, (t + 1) * classes)
                tg[t] = dot(dl[c, :, lanes], heads_of(t), NN)

            def merge(rows, carry):
                total = soft_sum = None
                for t in range(tasks):
                    g = tg[t, rows]
                    soft = jnp.sqrt(g * g + SIGN_FLOOR * SIGN_FLOOR) - SIGN_FLOOR
                    total = g if t == 0 else total + g
                    soft_sum = soft if t == 0 else soft_sum + soft
                purity = 0.5 * (1.0 + total / (soft_sum + SIGN_FLOOR))
                start = pl.multiple_of(rows.start + c * RM, 32)
                there = pl.ds(start, 32)
                frac = 1.0 / (1.0 + jnp.exp((thr[there] - purity) * (1.0 / KEEP_TEMPER)))
                upper, lower = 0.5 * (total + soft_sum), 0.5 * (total - soft_sum)
                return steepest(1, there, frac * upper + (1.0 - frac) * lower, carry)

            return loop(RM, 32, merge, sums)

        zero = (jnp.zeros((8, Wd), F32), jnp.zeros((8, Wd), F32))
        sums = merge_block(m, zero)
        for k in [1] + list(range(n_mp - 1, 1, -1)):
            settle(group.rsem + k - 1)
            sums = merge_block(group.came_from(k), sums)

        def b10():
            for t in range(tasks):
                lanes = slice(t * classes, (t + 1) * classes)
                delta = dl[:, :, lanes].reshape(R, classes)
                out = dot(delta, act1[...], TN).astype(BF16)
                ghead[:, t] = out.reshape(n_cls, piece, Wd)
            hold["ghead"] = to_all(lambda t: ghead.at[t], rhead)

        backward(1, sums, (nothing, b10, nothing, nothing))
        sums = loop(R, 32, lambda rows, carry: steepest(0, rows, evec[rows], carry), zero)

        backward(0, sums, (lambda: reduce_to_sib(1), lambda: reduce_to_dp(1), nothing, nothing))

        settle(hold["ghead"])
        for t in range(tasks):
            total = ghead[mine, t].astype(F32)
            for k in range(1, n_cls):
                total = total + rhead[rem(mine + k, n_cls), t].astype(F32)
            ohead[t] = total
        load(ohead, head_out)
        settle(hold["vec"])
        ovec[...] = vec[s] + vsib[...]
        load(ovec, vec_hbm)

        def total_of(own, got, rows):
            out = own[s, d, rows].astype(F32)
            for k in range(1, n_dp):
                out = out + got[rem(d + k, n_dp), rows].astype(F32)
            return out

        def finish_grad(which):
            own, _, got = grads[which]
            for key in at_dp[which]:
                settle(key)

            def finish(rows, carry):
                out = total_of(own, got, rows)
                if which == 1:
                    for k in range(9):
                        ospa[0, k, rows] = out[:, k * C:(k + 1) * C]
                else:
                    (ored if which == 0 else oexp)[0, rows] = out
                return carry

            loop(own.shape[2], 64, finish)
            load((ored, ospa, oexp)[which], (red_hbm, spa_hbm, exp_hbm)[which])

        finish_grad(2)
        finish_grad(1)
        finish_grad(0)
        for key in list(expected):
            settle(key)

        for key, waits in pending.items():
            def finish_all(waits=waits):
                for wait in waits:
                    wait()

            if key is None:
                finish_all()
            else:
                pl.when(s == key)(finish_all)

    return kernel


def fused_device(sizes, *args):
    n_dp, n_mp, R, Wd, M, C, Cd, classes, tasks, piece = sizes
    W9, n_cls = 9 * C, 2 * n_dp
    RM = R // n_mp
    vmem = lambda shape, dtype: pltpu.VMEM(shape, dtype)
    scratch = [
        pltpu.SemaphoreType.DMA((3,)),
        pltpu.SemaphoreType.DMA((95,)),
        pltpu.SemaphoreType.DMA((21,)),
        pltpu.SemaphoreType.REGULAR,
        vmem((Wd, Cd), F32),
        vmem((9, Cd, C), F32),
        vmem((Cd, Wd), F32),
        vmem((tasks, piece, Wd), F32),
        vmem((R, Wd), F32),
        vmem((2, R, Wd), BF16),
        vmem((2, n_dp, Wd, Cd), BF16),
        vmem((2, n_dp, Cd, W9), BF16),
        vmem((2, n_dp, Cd, Wd), BF16),
        vmem((n_cls, tasks, piece, Wd), BF16),
        vmem((2, 8, Wd), F32),
        vmem((R, 128), F32),
        vmem((2, R, 128), F32),
        vmem((len(MASKS), R, 128), F32),
        vmem((R, 8), F32),
        vmem((6, n_mp, R, C), BF16),
        vmem((6, n_mp, R, C), BF16),
        vmem((2, n_mp, R, C), BF16),
        vmem((2, n_mp, R, C), BF16),
        vmem((2, n_mp, R, C), BF16),
        vmem((2, R, M), BF16),
        vmem((2, R, M), BF16),
        vmem((2, R, M), BF16),
        vmem((6, n_mp, 8, C), F32),
        vmem((6, 2 * n_mp, C), F32),
        vmem((6, n_mp * n_dp, 2 * n_mp, C), F32),
        vmem((6, 2 * n_mp, C), F32),
        vmem((12, n_dp, 8, Wd), F32),
        vmem((2, 3, 8, Wd), F32),
        vmem((2, R, C), F32),
        vmem((2, R, C), F32),
        vmem((2, R, Wd), F32),
        vmem((R + 2 * PAD, W9), F32),
        vmem((R + 2 * PAD, C), F32),
        vmem((R, W9), BF16),
        vmem((n_mp, RM, tasks * classes), BF16),
        vmem((n_mp, RM, tasks * classes), BF16),
        vmem((n_mp, RM, tasks * classes), BF16),
        vmem((R, Wd), BF16),
        vmem((tasks, RM, Wd), F32),
        vmem((R, Wd), F32),
        vmem((R, Wd), F32),
        vmem((R, Wd), BF16),
        vmem((2, R, Wd), F32),
        vmem((2, 2, n_mp, R, C), F32),
        vmem((2, R, Wd), F32),
        vmem((2, n_dp, Wd, Cd), BF16),
        vmem((2, n_dp, Cd, W9), BF16),
        vmem((2, n_dp, Cd, Wd), BF16),
        vmem((n_dp, Wd, Cd), BF16),
        vmem((n_dp, Cd, W9), BF16),
        vmem((n_dp, Cd, Wd), BF16),
        vmem((n_dp, Wd, Cd), BF16),
        vmem((n_dp, Cd, W9), BF16),
        vmem((n_dp, Cd, Wd), BF16),
        vmem((n_cls, tasks, piece, Wd), BF16),
        vmem((n_cls, tasks, piece, Wd), BF16),
        vmem((2, 8, Wd), F32),
        vmem((8, Wd), F32),
        vmem((1, Wd, Cd), F32),
        vmem((1, 9, Cd, C), F32),
        vmem((1, Cd, Wd), F32),
        vmem((8, Wd), F32),
        vmem((tasks, piece, Wd), F32),
    ] + [vmem(args[i].shape, args[i].dtype) for i in (1, 5, 6, 7, 8, 10)]
    in_any = pl.BlockSpec(memory_space=pl.ANY)
    whole = lambda shape, dtype=F32: jax.ShapeDtypeStruct(shape, dtype)
    out = pl.pallas_call(
        make_kernel(sizes),
        out_shape=(
            whole((1, 2, R, Wd), BF16),
            whole((1, 2, R, Wd)),
            whole((1, Wd, Cd)),
            whole((1, 9, Cd, C)),
            whole((1, Cd, Wd)),
            whole((8, Wd)),
            whole((tasks, piece, Wd)),
        ),
        in_specs=[in_any] * len(args),
        out_specs=(in_any,) * 7,
        scratch_shapes=scratch,
        compiler_params=pltpu.CompilerParams(
            collective_id=0, has_side_effects=True, vmem_limit_bytes=60 * 2**20
        ),
    )(*args[:9], jnp.transpose(args[9], (0, 2, 1)), *args[10:])
    part, outer = C // n_dp, Wd // n_dp
    shapes = (
        whole((1, 2, R, Wd), BF16),
        whole((1, 2, R, Wd)),
        whole((1, Wd, Cd)),
        whole((1, 9, Cd, C)),
        whole((1, Cd, Wd)),
        whole((1, 2, 1, part)),
        whole((1, 2, 1, part)),
        whole((1, 1, outer)),
        whole((1, 1, outer)),
        whole((tasks, piece, Wd)),
    )
    done = pl.pallas_call(
        hand_out,
        out_shape=shapes,
        in_specs=[in_any] * 7,
        out_specs=(in_any,) * 10,
        scratch_shapes=[pltpu.VMEM(a.shape, a.dtype) for a in shapes]
        + [vmem((8, Wd), F32), pltpu.SemaphoreType.DMA((9,)), pltpu.SemaphoreType.DMA((12,))],
    )(*out)
    return done[:9] + (jnp.transpose(done[9], (0, 2, 1)),)


def hand_out(*refs):
    given, outs, held, vec, came, left = refs[:7], refs[7:17], refs[17:27], *refs[27:]
    gains, shifts, gain_out, shift_out = held[5:9]
    load_vec = pltpu.make_async_copy(given[5], vec, came.at[8])
    load_vec.start()
    pieces = []
    for src, mid, dst in zip(given[:5] + given[6:], held[:5] + held[9:], outs[:5] + outs[9:]):
        for i in range(src.shape[1]) if src.shape[1] == 2 else (None,):
            at = (lambda ref, i=i: ref) if i is None else (lambda ref, i=i: ref.at[0, i])
            n = len(pieces)
            pieces.append((
                pltpu.make_async_copy(at(src), at(mid), came.at[n]),
                pltpu.make_async_copy(at(mid), at(dst), left.at[n]),
            ))
    for fetch, _ in pieces:
        fetch.start()
    d = lax.axis_index("dp")
    part, outer = gains.shape[3], gain_out.shape[2]
    lanes = part * lax.axis_size("dp")
    load_vec.wait()
    rolled = pltpu.roll(vec[:, 0:lanes], lax.rem(lanes - d * part, lanes), 1)
    for i in range(2):
        gains[0, i] = rolled[i:i + 1, 0:part]
        shifts[0, i] = rolled[2 + i:3 + i, 0:part]
    mine = pl.ds(pl.multiple_of(d * outer, outer), outer)
    gain_out[0] = vec[4:5, mine]
    shift_out[0] = vec[5:6, mine]
    stores = [
        pltpu.make_async_copy(held[i], outs[i], left.at[len(pieces) + i - 5]) for i in range(5, 9)
    ]
    for store in stores:
        store.start()
    for fetch, store in pieces:
        fetch.wait()
        store.start()
    for store in stores + [store for _, store in pieces]:
        store.wait()


def per_device(*args):
    block_input, _, w_reduce, w_spatial = args[:4]
    n_dp, n_mp = lax.axis_size("dp"), lax.axis_size("mp")
    R, Wd = block_input.shape[1:]
    Cd, C = w_reduce.shape[2], w_spatial.shape[3]
    tasks, _, piece = args[9].shape
    sizes = (n_dp, n_mp, R, Wd, C * n_mp, C, Cd, piece * 2 * n_dp, tasks, piece)
    whole_tiles = not (C % 128 or Cd % 128 or Wd % 128 or R % 128 or piece % 16 or (R // n_mp) % 32)
    if whole_tiles and C == Cd and block_input.shape[0] == lax.axis_size("section") == 2:
        return fused_device(sizes, *args)
    return plain_device(*args)


def solution(mesh):
    return jax.shard_map(
        per_device,
        mesh=mesh,
        in_specs=(
            P(None, "dp", "mp"),
            P(None, "dp", None),
            P("section", "mp", "dp"),
            P("section", None, "dp", "mp"),
            P("section", "dp", "mp"),
            P("section", None, "mp"),
            P("section", None, "mp"),
            P("section", "mp"),
            P("section", "mp"),
            P(None, "mp", ("section", "dp")),
            P(None, None, "dp"),
            P(None, "dp", "mp"),
        ),
        out_specs=(
            P("section", None, "dp", "mp"),
            P("section", None, "dp", "mp"),
            P("section", "mp", "dp"),
            P("section", None, "dp", "mp"),
            P("section", "dp", "mp"),
            P("section", None, "mp", "dp"),
            P("section", None, "mp", "dp"),
            P("section", "mp", "dp"),
            P("section", "mp", "dp"),
            P(None, "mp", ("section", "dp")),
        ),
        check_vma=False,
    )
```
